32 devices in a mesh: expert: 8 (over z, x), tensor: 4 (over y, core).
Axes of the slice: x: 2, y: 2, z: 4, core: 2. Of those that a mesh axis runs over, the one named last changes fastest.
Arguments:
- hidden_in: bfloat16 [2048, 2048], P('expert'), may hold values from -6 to 6
- attn_gain: float32 [2048], replicated, may hold values from 0.5 to 1.5
- query_weight: bfloat16 [2048, 3072], P(None, 'tensor'), may hold values from -0.125 to 0.125
- latent_weight: bfloat16 [2048, 576], replicated, may hold values from -0.125 to 0.125
- latent_gain: float32 [512], replicated, may hold values from 0.5 to 1.5
- expand_weight: bfloat16 [512, 4096], P(None, 'tensor'), may hold values from -0.25 to 0.25
- output_weight: bfloat16 [2048, 2048], P('tensor'), may hold values from -2 to 2
- moe_gain: float32 [2048], replicated, may hold values from 0.5 to 1.5
- shared_gate: bfloat16 [2048, 2816], P(None, 'tensor'), may hold values from -0.125 to 0.125
- shared_up: bfloat16 [2048, 2816], P(None, 'tensor'), may hold values from -0.125 to 0.125
- shared_down: bfloat16 [2816, 2048], P('tensor'), may hold values from -0.109375 to 0.109375
- expert_gate: bfloat16 [16, 2048, 1408], P('expert', None, 'tensor'), may hold values from -0.125 to 0.125
- expert_up: bfloat16 [16, 2048, 1408], P('expert', None, 'tensor'), may hold values from -0.125 to 0.125
- expert_down: bfloat16 [16, 1408, 2048], P('expert', 'tensor'), may hold values from -0.625 to 0.625
- gate_values: float32 [2048, 6], P('expert'), may hold values from 0.15 to 0.45
- expert_routes: int32 [2048, 6], P('expert'), may hold values from 0 to 15, all different within a row; in each aligned block of 256 rows (0 to 255, 256 to 511, ...) at most 192 rows name the same one
- segments: int32 [2048], replicated, may hold values from 0 to 4, as said below
- cotangent: bfloat16 [2048, 2048], P('expert'), may hold values from -6 to 6
Outputs:
- layer_out: bfloat16 [2048, 2048], P('expert')
- grad_hidden: float32 [2048, 2048], P('expert')
- grad_attn_gain: float32 [2048], replicated
- grad_query_weight: float32 [2048, 3072], P(None, 'tensor')
- grad_latent_weight: float32 [2048, 576], replicated
- grad_latent_gain: float32 [512], replicated
- grad_expand_weight: float32 [512, 4096], P(None, 'tensor')
- grad_output_weight: float32 [2048, 2048], P('tensor')
- grad_moe_gain: float32 [2048], replicated
- grad_shared_gate: float32 [2048, 2816], P(None, 'tensor')
- grad_shared_up: float32 [2048, 2816], P(None, 'tensor')
- grad_shared_down: float32 [2816, 2048], P('tensor')
- grad_expert_gate: float32 [16, 2048, 1408], P('expert', None, 'tensor')
- grad_expert_up: float32 [16, 2048, 1408], P('expert', None, 'tensor')
- grad_expert_down: float32 [16, 1408, 2048], P('expert', 'tensor')
The draws below stay inside these ranges and needn't reach their ends.
Inputs may be any that keep to these rules, and one draw needn't show every extreme that they name: `expert_routes`: each row names 6 different experts; among the 256 rows of one device no expert is named by more than 192 rows, and in every draw some expert reaches 192. `segments`: the first 1024 entries are 0; the rest never fall and take each of 1 to 4 at least once.
All inputs are finite; a program needn't handle non-finite values.
Results may differ from the reference program's by a relative error of at most 0.024.
Values may be sent and summed in bfloat16 or wider, within the bound.
A program may use at most 384 MiB of HBM per device.

```python
import math
import jax
import jax.numpy as jnp
import numpy as np
from jax import lax

D = 2048
HEADS = 16
NOPE = 128
ROPE = 64
VDIM = 128
LATENT = 512
FF = 1408
SHARED_FF = 2816
TOP = 6
TOK_DEV = 256
EXPERTS = 16
GROUP = 2048
CONTS = 4
CAP = 192
N_EXPERT = 8
N_TENSOR = 4


def draw_segments(key, part):
    key = jax.random.fold_in(key, 7)
    halfway = GROUP // 2
    cuts = jax.random.permutation(key, halfway - 1)[:CONTS - 1].astype(jnp.int32) + 1
    offset = jnp.arange(halfway, dtype=jnp.int32)
    later = 1 + jnp.sum((cuts[None, :] <= offset[:, None]).astype(jnp.int32), axis=1)
    return jnp.concatenate([jnp.zeros((halfway,), jnp.int32), later.astype(jnp.int32)])


def shard_levels(own_key, shape, cuts, low, top_value):
    def one(dim, parts):
        steps = jax.random.uniform(jax.random.fold_in(jax.random.fold_in(own_key, 6), dim), (parts,), jnp.float32, low / len(cuts), top_value / len(cuts))
        return jnp.repeat(jnp.exp(steps), shape[dim] // parts).reshape((-1,) + (1,) * (len(shape) - dim - 1))

    level = one(*cuts[0])
    for cut in cuts[1:]:
        level = level * one(*cut)
    return level


def deal_out(key, own, number, rows, number_of, top, bound, slope):
    ranking = jax.random.permutation(key, number_of)
    heavy_load, common = load_shares(number_of, rows * top, bound, slope, True), load_shares(number_of, rows * top, bound, slope, False)
    places = jnp.arange(number_of)

    def named(sizes, turn):
        used = int((sizes > 0).sum())
        fixed = max(1, used // 4)
        passed = fixed + (places - fixed + turn * (used - fixed)) % max(1, number_of - fixed)
        return jnp.zeros((number_of,), jnp.int32).at[ranking[jnp.where(places < fixed, places, passed)]].set(jnp.asarray(sizes, jnp.int32))

    sizes = jnp.where(number % 4 == 0, named(heavy_load, number // 4), named(common, number - number // 4 - 1))
    mixed = jax.random.permutation(jax.random.fold_in(own, 3), number_of)
    source_of, receiver = mixed[0:number_of // 2 * 2:2], mixed[1:number_of // 2 * 2:2]
    room = jnp.minimum(sizes[source_of] - 1, bound - sizes[receiver]) // 2
    room = jnp.where((source_of == ranking[0]) | (receiver == ranking[0]) | (sizes[receiver] == 0), 0, jnp.maximum(room, 0))
    passed = jax.random.randint(jax.random.fold_in(own, 4), (number_of // 2,), 0, 1 << 20) % (room + 1)
    sizes = sizes.at[source_of].add(-passed).at[receiver].add(passed)
    items = jnp.searchsorted(jnp.cumsum(sizes), jnp.arange(rows * top), side="right").astype(jnp.int32)
    listing = items.reshape(top, rows).T
    listing = listing[jax.random.permutation(jax.random.fold_in(own, 1), rows)]
    turn = jax.random.randint(jax.random.fold_in(own, 2), (rows, 1), 0, top)
    return jnp.take_along_axis(listing, (jnp.arange(top)[None, :] + turn) % top, axis=1)


def load_shares(count, total, reach, lean, full):
    weights = [(1 << 20) // math.isqrt(standing ** lean) + 1 for standing in range(1, count + 1)]
    largest = reach if full else min(reach, max(-(-total // count), total * weights[0] // sum(weights)))
    least = 1 if total - largest >= count - 1 else 0
    counts, spare = [largest] + [least] * (count - 1), total - largest - least * (count - 1)
    while spare > 0:
        free = [i for i in range(1, count) if counts[i] < largest] or [i for i in range(1, count) if counts[i] < reach]
        mass, left = sum([weights[i] for i in free]), spare
        for i in free:
            more = min(reach - counts[i], max(1, left * weights[i] // mass), spare)
            counts[i] = counts[i] + more
            spare = spare - more
    return np.array(counts)


def centred(rng, dims, width, most, shards=(), kind=jnp.bfloat16):
    values = width * jax.random.normal(rng, dims, jnp.float32)
    if shards:
        values = values * shard_levels(rng, dims, shards, -0.22, 0.18)
    return jnp.clip(values, -most, most).astype(kind)


def setup_inputs(seed: int = 0) -> dict:
    streams_of = jax.random.split(jax.random.key(seed), 19)
    hidden_in = centred(streams_of[0], (GROUP, D), 1.0, 6.0, ((0, 8),))
    attn_gain = jnp.clip(1.0 + 0.1 * jax.random.normal(streams_of[1], (D,), jnp.float32), 0.5, 1.5)
    query_weight = centred(streams_of[2], (D, HEADS * (NOPE + ROPE)), D ** -0.5, 0.125, ((1, 4),))
    latent_weight = centred(streams_of[3], (D, LATENT + ROPE), D ** -0.5, 0.125)
    latent_gain = jnp.clip(1.0 + 0.1 * jax.random.normal(streams_of[4], (LATENT,), jnp.float32), 0.5, 1.5)
    expand_weight = centred(streams_of[5], (LATENT, HEADS * (NOPE + VDIM)), LATENT ** -0.5, 0.25, ((1, 4),))
    output_weight = centred(streams_of[6], (HEADS * VDIM, D), (max(1, HEADS * VDIM // 256)) ** -0.5, 2.0, ((0, 4),))
    moe_gain = jnp.clip(1.0 + 0.1 * jax.random.normal(streams_of[7], (D,), jnp.float32), 0.5, 1.5)
    shared_gate = centred(streams_of[8], (D, SHARED_FF), D ** -0.5, 0.125, ((1, 4),))
    shared_up = centred(streams_of[9], (D, SHARED_FF), D ** -0.5, 0.125, ((1, 4),))
    shared_down = centred(streams_of[10], (SHARED_FF, D), SHARED_FF ** -0.5, 0.109375, ((0, 4),))
    expert_gate = centred(streams_of[11], (EXPERTS, D, FF), D ** -0.5, 0.125, ((0, 8), (2, 4)))
    expert_up = centred(streams_of[12], (EXPERTS, D, FF), D ** -0.5, 0.125, ((0, 8), (2, 4)))
    expert_down = centred(streams_of[13], (EXPERTS, FF, D), (max(1, FF // 16)) ** -0.5, 0.625, ((0, 8), (1, 4)))
    gate_values = jnp.clip(0.15 + 0.29999998 * jax.random.uniform(streams_of[14], (GROUP, TOP), jnp.float32) ** shard_levels(streams_of[14], (GROUP, TOP), ((0, 8),), -0.2, 0.2), 0.15, 0.45)
    expert_routes_keys = jax.random.split(jax.random.fold_in(streams_of[15], 1), GROUP // TOK_DEV)
    expert_routes_turns = jax.random.permutation(jax.random.fold_in(streams_of[15], 3), GROUP // TOK_DEV)
    expert_routes = jax.vmap(lambda own, number: deal_out(jax.random.fold_in(streams_of[15], 2), own, number, TOK_DEV, EXPERTS, TOP, CAP, 2))(expert_routes_keys, expert_routes_turns).reshape((GROUP, TOP))
    segments = draw_segments(jax.random.fold_in(streams_of[18], 71), 0)
    cotangent = centred(streams_of[17], (GROUP, D), 1.0, 6.0, ((0, 8),))
    return dict(hidden_in=hidden_in, attn_gain=attn_gain, query_weight=query_weight, latent_weight=latent_weight, latent_gain=latent_gain, expand_weight=expand_weight, output_weight=output_weight, moe_gain=moe_gain, shared_gate=shared_gate, shared_up=shared_up, shared_down=shared_down, expert_gate=expert_gate, expert_up=expert_up, expert_down=expert_down, gate_values=gate_values, expert_routes=expert_routes, segments=segments, cotangent=cotangent)


epsilon = 1e-06
masked_out = -1e+30
highest = lax.Precision.HIGHEST

@jax.custom_vjp
def low(v):
    return lax.optimization_barrier(v.astype(jnp.bfloat16)).astype(jnp.float32)

@jax.custom_vjp
def low_back(v):
    return v

def low_keep(v):
    return (low(v), None)

def low_pass(kept, grad):
    return (grad,)

def back_keep(v):
    return (v, None)

def back_low(kept, grad):
    return (low(grad),)
low.defvjp(low_keep, low_pass)
low_back.defvjp(back_keep, back_low)

def matmul(left_side, right_side):
    return jnp.dot(left_side, right_side, precision=highest)

def rms_scale(values, gain_vec):
    return values * lax.rsqrt(lax.optimization_barrier(jnp.mean(values * values, axis=-1, keepdims=True)) + epsilon) * gain_vec

def rotate(values, places):
    halfway = values.shape[-1] // 2
    frequency = 10000.0 ** (-jnp.arange(halfway, dtype=jnp.float32) / halfway)
    angles = places.astype(jnp.float32)[:, None] * frequency[None, :]
    cosine = jnp.cos(angles)
    sine_part = jnp.sin(angles)
    if values.ndim == 3:
        cosine = cosine[:, None, :]
        sine_part = sine_part[:, None, :]
    first_half = values[..., :halfway]
    second = values[..., halfway:]
    return jnp.concatenate([first_half * cosine - second * sine_part, second * cosine + first_half * sine_part], axis=-1)

def seq_places(segments):
    total_rows = segments.shape[0]
    ordinal = jnp.arange(total_rows, dtype=jnp.int32)
    starts = jnp.concatenate([jnp.ones((1,), jnp.int32), (segments[1:] != segments[:-1]).astype(jnp.int32)])
    seg_start = lax.cummax(jnp.where(starts > 0, ordinal, 0), axis=0)
    return jnp.where(segments == 0, ordinal, total_rows // 2 + ordinal - seg_start).astype(jnp.int32)

def forward(hidden_in, attn_gain, query_weight, latent_weight, latent_gain, expand_weight, output_weight, moe_gain, shared_gate, shared_up, shared_down, expert_gate, expert_up, expert_down, gate_values, expert_routes, segments):
    total_rows = hidden_in.shape[0]
    places = seq_places(segments)
    ordinal = jnp.arange(total_rows, dtype=jnp.int32)
    visible = (ordinal[None, :] <= ordinal[:, None]) & ((segments[None, :] == segments[:, None]) | (segments[None, :] == 0))
    normed = low(rms_scale(hidden_in, attn_gain))
    q_raw = low_back(matmul(normed, query_weight)).reshape(total_rows, HEADS, NOPE + ROPE)
    queries = low(jnp.concatenate([q_raw[..., :NOPE], rotate(q_raw[..., NOPE:], places)], axis=-1))
    compressed = low_back(matmul(normed, latent_weight))
    latents = low(rms_scale(compressed[:, :LATENT], latent_gain))
    key_rope = low(rotate(compressed[:, LATENT:], places))
    expanded = low(low_back(matmul(latents, expand_weight))).reshape(total_rows, HEADS, NOPE + VDIM)
    scale_factor = (NOPE + ROPE) ** (-0.5)

    def one_head(operands):
        head_query, head_key, head_value = operands
        keys_full = jnp.concatenate([head_key, key_rope], axis=-1)
        scores = low_back(scale_factor * matmul(head_query, keys_full.T))
        scores = jnp.where(visible, scores, masked_out)
        peak = lax.optimization_barrier(jnp.max(scores, axis=-1, keepdims=True))
        weights = jnp.exp(scores - peak)
        probs = weights / lax.optimization_barrier(jnp.sum(weights, axis=-1, keepdims=True))
        return low(low_back(matmul(low(probs), head_value)))
    heads_out = lax.map(jax.checkpoint(one_head), (jnp.swapaxes(queries, 0, 1), jnp.swapaxes(expanded[..., :NOPE], 0, 1), jnp.swapaxes(expanded[..., NOPE:], 0, 1)))
    merged = jnp.swapaxes(heads_out, 0, 1).reshape(total_rows, HEADS * VDIM)
    residual = hidden_in + low_back(matmul(merged, output_weight))
    moe_in = low(rms_scale(residual, moe_gain))
    gate_pre = low_back(matmul(moe_in, shared_gate))
    up_pre = low_back(matmul(moe_in, shared_up))
    shared_out = low_back(matmul(low(jax.nn.silu(gate_pre) * up_pre), shared_down))
    width_part = FF // N_TENSOR
    slots_all = N_EXPERT * CAP

    def one_expert(carry, operands):
        expert_id, weight_gate, weight_up, weight_down = operands
        hit_mask = expert_routes == expert_id
        member = jnp.any(hit_mask, axis=-1)
        weight_row = lax.optimization_barrier(jnp.sum(jnp.where(hit_mask, gate_values, 0.0), axis=-1))
        member_rank = jnp.cumsum(member.astype(jnp.int32)) - 1
        target = jnp.where(member, member_rank, slots_all).astype(jnp.int32)
        rows_at = jnp.zeros((slots_all,), jnp.int32).at[target].set(ordinal, mode='drop')
        scales = jnp.zeros((slots_all,), jnp.float32).at[target].set(weight_row, mode='drop')
        copies = low_back(jnp.broadcast_to(moe_in[rows_at], (N_TENSOR, slots_all, D)))
        gate_part = low_back(jnp.einsum('krd,dkf->krf', copies, weight_gate.reshape(D, N_TENSOR, width_part), precision=highest))
        up_part = low_back(jnp.einsum('krd,dkf->krf', copies, weight_up.reshape(D, N_TENSOR, width_part), precision=highest))
        active = low(jax.nn.silu(gate_part) * up_part)
        pieces = low_back(low(jnp.einsum('krf,kfd->krd', active, weight_down.reshape(N_TENSOR, width_part, D), precision=highest)))
        return (carry.at[rows_at].add(lax.optimization_barrier(jnp.sum(pieces, axis=0)) * scales[:, None]), None)
    routed, _ = lax.scan(jax.checkpoint(one_expert), jnp.zeros((total_rows, D), jnp.float32), (jnp.arange(EXPERTS, dtype=jnp.int32), expert_gate, expert_up, expert_down))
    return residual + shared_out + routed

def reference(hidden_in, attn_gain, query_weight, latent_weight, latent_gain, expand_weight, output_weight, moe_gain, shared_gate, shared_up, shared_down, expert_gate, expert_up, expert_down, gate_values, expert_routes, segments, cotangent):
    arrays = [array_in.astype(jnp.float32) for array_in in (hidden_in, attn_gain, query_weight, latent_weight, latent_gain, expand_weight, output_weight, moe_gain, shared_gate, shared_up, shared_down, expert_gate, expert_up, expert_down)]
    gates_f = gate_values.astype(jnp.float32)

    def run(*params):
        return forward(*params, gates_f, expert_routes, segments)
    layer_out, pull = jax.vjp(run, *arrays)
    grads = pull(cotangent.astype(jnp.float32))
    return (layer_out.astype(jnp.bfloat16), grads[0], grads[1], grads[2], grads[3], grads[4], grads[5], grads[6], grads[7], grads[8], grads[9], grads[10], grads[11], grads[12], grads[13])
```

```python
import functools
from functools import partial

import jax
import jax.numpy as jnp
from jax import lax
from jax.experimental import pallas as pl
from jax.experimental.pallas import tpu as pltpu
from jax.sharding import PartitionSpec as P

NOPE = 128
ROPE = 64
VDIM = 128
LATENT = 512
TOP = 6
EXP_DEV = 2
ALL = ("expert", "tensor")
MESH = pl.DeviceIdType.MESH

epsilon = 1e-06
masked_out = -1e30


class Grid:
    def __init__(self, expert, tensor):
        self.na = 4 if expert % 4 == 0 else 1
        self.nb = expert // self.na
        self.ny = tensor // 2
        self.size = expert * tensor

    def here(self):
        e, t = lax.axis_index("expert"), lax.axis_index("tensor")
        return (lax.div(e, self.nb), lax.rem(e, self.nb), lax.div(t, 2), lax.rem(t, 2))

    def device(self, a, b, y, c):
        return {"expert": a * self.nb + b, "tensor": y * 2 + c}

    def block(self, a, b, y, c):
        return ((a * self.nb + b) * self.ny + y) * 2 + c


def wrap(i, n):
    return lax.rem(i, n)


def greet(grid):
    a, b, y, c = grid.here()
    barrier = pltpu.get_barrier_semaphore()
    others = (
        [grid.device(wrap(a + i, grid.na), b, y, c) for i in range(1, grid.na)]
        + [grid.device(a, wrap(b + i, grid.nb), y, c) for i in range(1, grid.nb)]
        + [grid.device(a, b, wrap(y + i, grid.ny), c) for i in range(1, grid.ny)]
        + [grid.device(a, b, y, 1 - c)]
    )
    for other in others:
        pl.semaphore_signal(barrier, inc=1, device_id=other, device_id_type=MESH)
    pl.semaphore_wait(barrier, len(others))


def gather_kernel(grid, x_ref, out_ref, own_sem, send_sem, recv_sem, core_send, core_recv):
    na, nb, ny = grid.na, grid.nb, grid.ny
    a, b, y, c = grid.here()
    half = x_ref.shape[0] // 2
    greet(grid)
    waits = []

    def dst(bb, yy, cc, aa, h):
        return out_ref.at[grid.block(aa, bb, yy, cc), pl.ds(h * half, half)]

    def slot(bb, yy, aa, h):
        return ((bb * ny + yy) * na + aa) * 2 + h

    def push(src, bb, yy, aa, h, where, kind):
        copy = pltpu.make_async_remote_copy(
            src_ref=src,
            dst_ref=dst(bb, yy, c, aa, h),
            send_sem=core_send.at[slot(bb, yy, aa, h)] if kind == "c" else send_sem.at[len(waits)],
            recv_sem=(core_recv if kind == "c" else recv_sem).at[slot(bb, yy, aa, h)],
            device_id=where,
            device_id_type=MESH,
        )
        copy.start()
        if kind != "c":
            waits.append(copy)
        else:
            core_waits.append(copy)

    core_waits = []

    def onward(src, bb, yy, aa, h, dims):
        for d in dims:
            if d == "a":
                for i in range(1, na):
                    push(src, bb, yy, aa, h, grid.device(wrap(a + i, na), b, y, c), d)
            if d == "b":
                for i in range(1, nb):
                    push(src, bb, yy, aa, h, grid.device(a, wrap(b + i, nb), y, c), d)
            if d == "y":
                for i in range(1, ny):
                    push(src, bb, yy, aa, h, grid.device(a, b, wrap(y + i, ny), c), d)
        push(src, bb, yy, aa, h, grid.device(a, b, y, 1 - c), "c")

    def landed(bb, yy, cc, aa, h, sem):
        ref = dst(bb, yy, cc, aa, h)
        pltpu.make_async_copy(ref, ref, sem.at[slot(bb, yy, aa, h)]).wait()
        return ref

    own = pltpu.make_async_copy(x_ref, out_ref.at[grid.block(a, b, y, c)], own_sem)
    own.start()
    orders = (("b", "y"), ("y", "b"))
    for h in range(2):
        onward(x_ref.at[pl.ds(h * half, half)], b, y, a, h, ("a",) + orders[h])
    for i in range(1, na):
        aa = wrap(a + na - i, na)
        for h in range(2):
            onward(landed(b, y, c, aa, h, recv_sem), b, y, aa, h, orders[h])
    for i in range(na):
        aa = wrap(a + na - i, na)
        for h in range(2):
            n1 = (nb, ny)[h]
            for j in range(1, n1):
                bb, yy = (wrap(b + nb - j, nb), y) if h == 0 else (b, wrap(y + ny - j, ny))
                onward(landed(bb, yy, c, aa, h, recv_sem), bb, yy, aa, h, orders[h][1:])
    for i in range(na):
        aa = wrap(a + na - i, na)
        for h in range(2):
            for j in range(nb):
                for k in range(1, ny):
                    if h == 0:
                        bb, yy = wrap(b + nb - j, nb), wrap(y + ny - k, ny)
                        onward(landed(bb, yy, c, aa, h, recv_sem), bb, yy, aa, h, ())
            for j in range(ny):
                for k in range(1, nb):
                    if h == 1:
                        bb, yy = wrap(b + nb - k, nb), wrap(y + ny - j, ny)
                        onward(landed(bb, yy, c, aa, h, recv_sem), bb, yy, aa, h, ())
    for j in range(nb):
        for k in range(ny):
            for i in range(na):
                for h in range(2):
                    landed(wrap(b + nb - j, nb), wrap(y + ny - k, ny), 1 - c, wrap(a + na - i, na), h, core_recv)
    own.wait()
    for copy in waits + core_waits:
        copy.wait_send()


def gather_all(grid, x, collective_id):
    r, n = x.shape
    blocks = grid.na * grid.nb * grid.ny
    sends = 2 * (grid.na - 1 + grid.na * (grid.nb - 1) + grid.na * (grid.ny - 1)) + 2 * grid.na * ((grid.nb - 1) * (grid.ny - 1))
    return pl.pallas_call(
        functools.partial(gather_kernel, grid),
        out_shape=jax.ShapeDtypeStruct((grid.size, r, n), x.dtype),
        in_specs=[pl.BlockSpec(memory_space=pl.ANY)],
        out_specs=pl.BlockSpec(memory_space=pl.ANY),
        scratch_shapes=[
            pltpu.SemaphoreType.DMA,
            pltpu.SemaphoreType.DMA((sends,)),
            pltpu.SemaphoreType.DMA((2 * blocks,)),
            pltpu.SemaphoreType.DMA((2 * blocks,)),
            pltpu.SemaphoreType.DMA((2 * blocks,)),
        ],
        compiler_params=pltpu.CompilerParams(collective_id=collective_id, has_side_effects=True),
    )(x)


def scatter_kernel(grid, pieces, p_ref, out_ref, acc, core_in, d1_in0, d1_in1, d2_in0, d2_in1, a_in,
                   load_sem, core_s, core_r, s10, r10, s11, r11, s20, r20, s21, r21, sa, ra):
    na, nb, ny = grid.na, grid.nb, grid.ny
    a, b, y, c = grid.here()
    half = p_ref.shape[4] // 2
    width = p_ref.shape[5] // pieces
    greet(grid)
    pending = []

    def send(src, dst, ss, rs, where):
        copy = pltpu.make_async_remote_copy(src_ref=src, dst_ref=dst, send_sem=ss, recv_sem=rs, device_id=where, device_id_type=MESH)
        copy.start()
        pending.append(copy)

    def await_in(ref, sem):
        pltpu.make_async_copy(ref, ref, sem).wait()

    def add(dst, src):
        dst[...] = (dst[...].astype(jnp.float32) + src[...].astype(jnp.float32)).astype(dst.dtype)

    def cols(p):
        return pl.ds(p * width, width)

    spots = [(j, k) for j in reversed(range(nb)) for k in reversed(range(ny))]
    loads = {}
    for p in range(pieces):
        for n, (j, k) in enumerate(spots):
            bb, yy = wrap(b + j, nb), wrap(y + k, ny)
            send(p_ref.at[:, bb, yy, 1 - c, :, cols(p)], core_in.at[p, j, k], core_s.at[p, n], core_r.at[p, n],
                 grid.device(a, b, y, 1 - c))
            load = pltpu.make_async_copy(p_ref.at[:, bb, yy, c, :, cols(p)], acc.at[p, j, k], load_sem.at[p, n])
            load.start()
            loads[p, n] = load
    rows = (pl.ds(0, half), pl.ds(half, half))
    for p in range(pieces):
        for n, (j, k) in enumerate(spots):
            loads[p, n].wait()
            await_in(core_in.at[p, j, k], core_r.at[p, n])
            for i in range(na):
                add(acc.at[p, j, k, i], core_in.at[p, j, k, i])
            if k:
                send(acc.at[p, j, k, :, rows[0]], d1_in0.at[p, j, k - 1], s10.at[p, j, k - 1], r10.at[p, j, k - 1],
                     grid.device(a, b, wrap(y + k, ny), c))
            if j:
                send(acc.at[p, j, k, :, rows[1]], d1_in1.at[p, k, j - 1], s11.at[p, k, j - 1], r11.at[p, k, j - 1],
                     grid.device(a, wrap(b + j, nb), y, c))
    for p in range(pieces):
        for j in reversed(range(nb)):
            for k in range(1, ny):
                await_in(d1_in0.at[p, j, k - 1], r10.at[p, j, k - 1])
                for i in range(na):
                    add(acc.at[p, j, 0, i, rows[0]], d1_in0.at[p, j, k - 1, i])
            if j:
                send(acc.at[p, j, 0, :, rows[0]], d2_in0.at[p, j - 1], s20.at[p, j - 1], r20.at[p, j - 1],
                     grid.device(a, wrap(b + j, nb), y, c))
        for k in reversed(range(ny)):
            for j in range(1, nb):
                await_in(d1_in1.at[p, k, j - 1], r11.at[p, k, j - 1])
                for i in range(na):
                    add(acc.at[p, 0, k, i, rows[1]], d1_in1.at[p, k, j - 1, i])
            if k:
                send(acc.at[p, 0, k, :, rows[1]], d2_in1.at[p, k - 1], s21.at[p, k - 1], r21.at[p, k - 1],
                     grid.device(a, b, wrap(y + k, ny), c))
    for p in range(pieces):
        for j in range(1, nb):
            await_in(d2_in0.at[p, j - 1], r20.at[p, j - 1])
            for i in range(na):
                add(acc.at[p, 0, 0, i, rows[0]], d2_in0.at[p, j - 1, i])
        for k in range(1, ny):
            await_in(d2_in1.at[p, k - 1], r21.at[p, k - 1])
            for i in range(na):
                add(acc.at[p, 0, 0, i, rows[1]], d2_in1.at[p, k - 1, i])
        for i in range(1, na):
            aa = wrap(a + i, na)
            send(acc.at[p, 0, 0, aa], a_in.at[p, i - 1], sa.at[p, i - 1], ra.at[p, i - 1], grid.device(aa, b, y, c))
    for p in range(pieces):
        total = acc[p, 0, 0, a].astype(jnp.float32)
        for i in range(1, na):
            await_in(a_in.at[p, i - 1], ra.at[p, i - 1])
            total = total + a_in[p, i - 1].astype(jnp.float32)
        out_ref[:, cols(p)] = total.astype(out_ref.dtype)
    for copy in pending:
        copy.wait_send()


def scatter_all(grid, p, dtype, collective_id, pieces=2):
    r, n = p.shape[0] // grid.size, p.shape[1]
    na, nb, ny = grid.na, grid.nb, grid.ny
    half, width = r // 2, n // pieces
    sems = lambda *s: pltpu.SemaphoreType.DMA(s)
    vm = lambda *s: pltpu.VMEM(s, jnp.bfloat16)
    return pl.pallas_call(
        functools.partial(scatter_kernel, grid, pieces),
        out_shape=jax.ShapeDtypeStruct((r, n), dtype),
        in_specs=[pl.BlockSpec(memory_space=pl.ANY)],
        out_specs=pl.BlockSpec(memory_space=pltpu.VMEM),
        scratch_shapes=[
            vm(pieces, nb, ny, na, r, width),
            vm(pieces, nb, ny, na, r, width),
            vm(pieces, nb, ny - 1, na, half, width),
            vm(pieces, ny, nb - 1, na, half, width),
            vm(pieces, nb - 1, na, half, width),
            vm(pieces, ny - 1, na, half, width),
            vm(pieces, na - 1, r, width),
            sems(pieces, nb * ny), sems(pieces, nb * ny), sems(pieces, nb * ny),
            sems(pieces, nb, ny - 1), sems(pieces, nb, ny - 1),
            sems(pieces, ny, nb - 1), sems(pieces, ny, nb - 1),
            sems(pieces, nb - 1), sems(pieces, nb - 1),
            sems(pieces, ny - 1), sems(pieces, ny - 1),
            sems(pieces, na - 1), sems(pieces, na - 1),
        ],
        compiler_params=pltpu.CompilerParams(collective_id=collective_id, has_side_effects=True, vmem_limit_bytes=40 << 20),
    )(p.reshape(na, nb, ny, 2, r, n))


def greet_tensor(grid):
    a, b, y, c = grid.here()
    barrier = pltpu.get_barrier_semaphore()
    others = [grid.device(a, b, wrap(y + i, grid.ny), c) for i in range(1, grid.ny)]
    others.append(grid.device(a, b, y, 1 - c))
    for other in others:
        pl.semaphore_signal(barrier, inc=1, device_id=other, device_id_type=MESH)
    pl.semaphore_wait(barrier, len(others))


def tensor_scatter_kernel(grid, p_ref, out_ref, acc, core_in, y_in, core_s, core_r, ys, yr):
    ny = grid.ny
    a, b, y, c = grid.here()
    greet_tensor(grid)
    pending = []
    for k in reversed(range(ny)):
        copy = pltpu.make_async_remote_copy(
            src_ref=p_ref.at[wrap(y + k, ny), 1 - c], dst_ref=core_in.at[k], send_sem=core_s.at[k], recv_sem=core_r.at[k],
            device_id=grid.device(a, b, y, 1 - c), device_id_type=MESH,
        )
        copy.start()
        pending.append(copy)
    for k in reversed(range(ny)):
        pltpu.make_async_copy(core_in.at[k], core_in.at[k], core_r.at[k]).wait()
        total = p_ref[wrap(y + k, ny), c].astype(jnp.float32) + core_in[k].astype(jnp.float32)
        if k:
            acc[k - 1] = total.astype(acc.dtype)
            copy = pltpu.make_async_remote_copy(
                src_ref=acc.at[k - 1], dst_ref=y_in.at[k - 1], send_sem=ys.at[k - 1], recv_sem=yr.at[k - 1],
                device_id=grid.device(a, b, wrap(y + k, ny), c), device_id_type=MESH,
            )
            copy.start()
            pending.append(copy)
        else:
            out_ref[...] = total
    for k in range(1, ny):
        pltpu.make_async_copy(y_in.at[k - 1], y_in.at[k - 1], yr.at[k - 1]).wait()
        out_ref[...] += y_in[k - 1].astype(jnp.float32)
    for copy in pending:
        copy.wait_send()


def tensor_scatter(grid, p, collective_id):
    ny = grid.ny
    r, n = p.shape[0] // (2 * ny), p.shape[1]
    return pl.pallas_call(
        functools.partial(tensor_scatter_kernel, grid),
        out_shape=jax.ShapeDtypeStruct((r, n), jnp.float32),
        in_specs=[pl.BlockSpec(memory_space=pltpu.VMEM)],
        out_specs=pl.BlockSpec(memory_space=pltpu.VMEM),
        scratch_shapes=[
            pltpu.VMEM((max(ny - 1, 1), r, n), p.dtype),
            pltpu.VMEM((ny, r, n), p.dtype),
            pltpu.VMEM((max(ny - 1, 1), r, n), p.dtype),
            pltpu.SemaphoreType.DMA((ny,)),
            pltpu.SemaphoreType.DMA((ny,)),
            pltpu.SemaphoreType.DMA((max(ny - 1, 1),)),
            pltpu.SemaphoreType.DMA((max(ny - 1, 1),)),
        ],
        compiler_params=pltpu.CompilerParams(
            collective_id=collective_id, has_side_effects=True, vmem_limit_bytes=16 << 20
        ),
    )(p.reshape(ny, 2, r, n))


def tensor_gather_kernel(grid, x_ref, out_ref, own_sem, ys, yr, core_s, core_r):
    ny = grid.ny
    a, b, y, c = grid.here()
    greet_tensor(grid)
    own = pltpu.make_async_copy(x_ref, out_ref.at[y, c], own_sem)
    own.start()
    pending = []

    def push(src, spot, ss, rs, where):
        copy = pltpu.make_async_remote_copy(
            src_ref=src, dst_ref=out_ref.at[spot, c], send_sem=ss, recv_sem=rs, device_id=where, device_id_type=MESH
        )
        copy.start()
        pending.append(copy)

    for k in range(1, ny):
        push(x_ref, y, ys.at[k], yr.at[k], grid.device(a, b, wrap(y + k, ny), c))
    push(x_ref, y, core_s.at[0], core_r.at[0], grid.device(a, b, y, 1 - c))
    for k in range(1, ny):
        spot = wrap(y + ny - k, ny)
        ref = out_ref.at[spot, c]
        pltpu.make_async_copy(ref, ref, yr.at[k]).wait()
        push(ref, spot, core_s.at[k], core_r.at[k], grid.device(a, b, y, 1 - c))
    for k in range(ny):
        ref = out_ref.at[wrap(y + ny - k, ny), 1 - c]
        pltpu.make_async_copy(ref, ref, core_r.at[k]).wait()
    own.wait()
    for copy in pending:
        copy.wait_send()


def tensor_gather(grid, x, collective_id):
    ny = grid.ny
    r, n = x.shape
    out = pl.pallas_call(
        functools.partial(tensor_gather_kernel, grid),
        out_shape=jax.ShapeDtypeStruct((ny, 2, r, n), x.dtype),
        in_specs=[pl.BlockSpec(memory_space=pltpu.VMEM)],
        out_specs=pl.BlockSpec(memory_space=pltpu.VMEM),
        scratch_shapes=[pltpu.SemaphoreType.DMA] + [pltpu.SemaphoreType.DMA((ny,))] * 4,
        compiler_params=pltpu.CompilerParams(
            collective_id=collective_id, has_side_effects=True, vmem_limit_bytes=16 << 20
        ),
    )(x)
    return out.reshape(2 * ny * r, n)


def rms_scale(values, gain_vec):
    return (
        values * lax.rsqrt(jnp.mean(values * values, axis=-1, keepdims=True) + epsilon) * gain_vec
    )


def rotate(values, places):
    halfway = values.shape[-1] // 2
    frequency = 10000.0 ** (-jnp.arange(halfway, dtype=jnp.float32) / halfway)
    angles = places.astype(jnp.float32)[:, None] * frequency[None, :]
    cosine = jnp.cos(angles)
    sine_part = jnp.sin(angles)
    if values.ndim == 3:
        cosine = cosine[:, None, :]
        sine_part = sine_part[:, None, :]
    first_half = values[..., :halfway]
    second = values[..., halfway:]
    return jnp.concatenate(
        [first_half * cosine - second * sine_part, second * cosine + first_half * sine_part],
        axis=-1,
    )


def seq_places(segments):
    total_rows = segments.shape[0]
    ordinal = jnp.arange(total_rows, dtype=jnp.int32)
    starts = jnp.concatenate(
        [jnp.ones((1,), jnp.int32), (segments[1:] != segments[:-1]).astype(jnp.int32)]
    )
    seg_start = lax.cummax(jnp.where(starts > 0, ordinal, 0), axis=0)
    return jnp.where(segments == 0, ordinal, total_rows // 2 + ordinal - seg_start)


def silu_product(gate_pre, up_pre):
    return jax.nn.silu(gate_pre) * up_pre


def score_block(queries, key_plain, rope_all, visible):
    scale_factor = (NOPE + ROPE) ** (-0.5)
    raw_scores = jnp.einsum(
        "thc,shc->hts", queries[..., :NOPE], key_plain, preferred_element_type=jnp.float32
    )
    raw_scores = raw_scores + jnp.einsum(
        "thr,sr->hts", queries[..., NOPE:], rope_all, preferred_element_type=jnp.float32
    )
    return jnp.where(visible[None], scale_factor * raw_scores, masked_out)


def dot(left_side, right_side):
    return jnp.dot(left_side, right_side, preferred_element_type=jnp.float32)


def pad_columns(values):
    return jnp.pad(values, ((0, 0), (0, -values.shape[1] % 128)))


def low(values):
    return values.astype(jnp.bfloat16)


def shards(
    grid,
    hidden_in,
    attn_gain,
    query_weight,
    latent_weight,
    latent_gain,
    expand_weight,
    output_weight,
    moe_gain,
    shared_gate,
    shared_up,
    shared_down,
    expert_gate,
    expert_up,
    expert_down,
    gate_values,
    expert_routes,
    segments,
    cotangent,
):
    tok_rows, model_width = hidden_in.shape
    groups = lax.axis_size("expert")
    parts = lax.axis_size("tensor")
    device = lax.axis_index("expert")
    part = lax.axis_index("tensor")
    total_rows = segments.shape[0]
    few = tok_rows // parts
    start_row = device * tok_rows
    scale_factor = (NOPE + ROPE) ** (-0.5)

    def quarter(values):
        return lax.dynamic_slice_in_dim(values, part * few, few)

    def own_group(values):
        return lax.dynamic_slice_in_dim(values, start_row, tok_rows)

    places = own_group(seq_places(segments))
    own_seg = own_group(segments)
    own_ordinal = start_row + jnp.arange(tok_rows, dtype=jnp.int32)
    key_ordinal = jnp.arange(total_rows, dtype=jnp.int32)
    visible = (key_ordinal[None, :] <= own_ordinal[:, None]) & (
        (segments[None, :] == own_seg[:, None]) | (segments[None, :] == 0)
    )
    experts_all = EXP_DEV * groups
    cot_all = lax.all_gather(quarter(cotangent), ALL, axis=0, tiled=True)

    hidden_f = hidden_in.astype(jnp.float32)
    normed = low(rms_scale(hidden_f, attn_gain))
    compressed = dot(normed, latent_weight)
    latents = low(rms_scale(compressed[:, :LATENT], latent_gain))
    key_rope = low(rotate(compressed[:, LATENT:], places))
    onehot = expert_routes[:, :, None] == jnp.arange(experts_all, dtype=jnp.int32)
    gate_rows = jnp.sum(jnp.where(onehot, gate_values[:, :, None], 0.0), axis=1)
    gate_high = low(gate_rows)
    gate_low = low(gate_rows - gate_high.astype(jnp.float32))
    packed = pad_columns(jnp.concatenate([latents, key_rope, gate_high, gate_low], axis=1))
    packed_all = gather_all(grid, quarter(packed), 0).reshape(total_rows, -1)
    latents_all = packed_all[:, :LATENT]
    rope_all = packed_all[:, LATENT : LATENT + ROPE]
    first_gate = LATENT + ROPE + EXP_DEV * device
    gates_own = lax.dynamic_slice_in_dim(packed_all, first_gate, EXP_DEV, axis=1).astype(
        jnp.float32
    ) + lax.dynamic_slice_in_dim(packed_all, first_gate + experts_all, EXP_DEV, axis=1).astype(
        jnp.float32
    )
    q_raw = dot(normed, query_weight)
    heads_here = q_raw.shape[1] // (NOPE + ROPE)
    q_raw = q_raw.reshape(tok_rows, heads_here, NOPE + ROPE)
    queries = low(
        jnp.concatenate([q_raw[..., :NOPE], rotate(q_raw[..., NOPE:], places)], axis=-1)
    )
    expanded = low(dot(latents_all, expand_weight)).reshape(
        total_rows, heads_here, NOPE + VDIM
    )
    key_plain, value_part = expanded[..., :NOPE], expanded[..., NOPE:]
    scores = score_block(queries, key_plain, rope_all, visible)
    peak = jnp.max(scores, axis=-1, keepdims=True)
    weights = jnp.exp(scores - peak)
    total_weight = jnp.sum(weights, axis=-1, keepdims=True)
    log_total = peak + jnp.log(total_weight)
    context = jnp.einsum(
        "hts,shv->thv", low(weights / total_weight), value_part, preferred_element_type=jnp.float32
    )
    merged = low(context).reshape(tok_rows, heads_here * VDIM)
    attn_out = tensor_scatter(grid, low(dot(merged, output_weight)), 1)
    residual = quarter(hidden_f) + attn_out
    moe_in = low(rms_scale(residual, moe_gain))
    moe_all = gather_all(grid, moe_in, 2).reshape(total_rows, model_width)
    normed_later, _ = lax.optimization_barrier((quarter(normed), moe_all[:8]))
    normed_all = lax.all_gather(normed_later, ALL, axis=0, tiled=True)

    hidden_here = expert_gate.shape[2]
    eg = jnp.einsum("td,kdf->tkf", moe_all, expert_gate, preferred_element_type=jnp.float32)
    eu = jnp.einsum("td,kdf->tkf", moe_all, expert_up, preferred_element_type=jnp.float32)
    active, pull_expert = jax.vjp(silu_product, eg, eu)
    gated = low(gates_own[:, :, None] * active)
    d_active = jnp.einsum("td,kfd->tkf", cot_all, expert_down, preferred_element_type=jnp.float32)
    d_eg, d_eu = pull_expert(gates_own[:, :, None] * d_active)
    d_eg, d_eu = low(d_eg), low(d_eu)
    sg = dot(moe_all, shared_gate)
    su = dot(moe_all, shared_up)
    shared_act, pull_shared = jax.vjp(silu_product, sg, su)
    shared_act = low(shared_act)
    d_sg, d_su = pull_shared(dot(cot_all, shared_down.T))
    d_sg, d_su = low(d_sg), low(d_su)

    grad_in = jnp.einsum("tkf,kdf->td", d_eg, expert_gate, preferred_element_type=jnp.float32)
    grad_in = grad_in + jnp.einsum(
        "tkf,kdf->td", d_eu, expert_up, preferred_element_type=jnp.float32
    )
    grad_in_shared = dot(own_group(d_sg), shared_gate.T) + dot(own_group(d_su), shared_up.T)
    grad_in = lax.dynamic_update_slice_in_dim(
        grad_in, own_group(grad_in) + grad_in_shared, start_row, 0
    )
    grad_moe_in = scatter_all(grid, low(grad_in), jnp.float32, 3)
    out_rows = jnp.einsum("tkf,kfd->td", gated, expert_down, preferred_element_type=jnp.float32)
    out_shared = dot(own_group(shared_act), shared_down)
    out_rows = lax.dynamic_update_slice_in_dim(
        out_rows, own_group(out_rows) + out_shared, start_row, 0
    )
    moe_out = lax.psum_scatter(low(out_rows), ALL, scatter_dimension=0, tiled=True)
    layer_out = low(residual + moe_out.astype(jnp.float32))
    layer_out = tensor_gather(grid, layer_out, 4)

    grad_expert_gate = jnp.einsum("td,tkf->kdf", moe_all, d_eg, preferred_element_type=jnp.float32)
    grad_expert_up = jnp.einsum("td,tkf->kdf", moe_all, d_eu, preferred_element_type=jnp.float32)
    grad_expert_down = jnp.einsum("tkf,td->kfd", gated, cot_all, preferred_element_type=jnp.float32)
    grad_shared_gate = dot(moe_all.T, d_sg)
    grad_shared_up = dot(moe_all.T, d_su)
    grad_shared_down = dot(shared_act.T, cot_all)

    _, pull_moe = jax.vjp(rms_scale, residual, moe_gain)
    grad_residual, grad_moe_gain = pull_moe(grad_moe_in)
    grad_residual = grad_residual + quarter(cotangent).astype(jnp.float32)
    grad_res_low = tensor_gather(grid, low(grad_residual), 5)
    grad_output_weight = dot(merged.T, grad_res_low)
    grad_context = low(dot(grad_res_low, output_weight.T)).reshape(tok_rows, heads_here, VDIM)
    scores = score_block(queries, key_plain, rope_all, visible)
    probs = jnp.exp(scores - log_total)
    grad_probs = jnp.einsum(
        "thv,shv->hts", grad_context, value_part, preferred_element_type=jnp.float32
    )
    grad_values = jnp.einsum(
        "hts,thv->shv", low(probs), grad_context, preferred_element_type=jnp.float32
    )
    grad_scores = low(probs * (grad_probs - jnp.sum(probs * grad_probs, axis=-1, keepdims=True)))
    grad_q_plain = scale_factor * jnp.einsum(
        "hts,shc->thc", grad_scores, key_plain, preferred_element_type=jnp.float32
    )
    grad_q_rope = scale_factor * jnp.einsum(
        "hts,sr->thr", grad_scores, rope_all, preferred_element_type=jnp.float32
    )
    grad_k_plain = scale_factor * jnp.einsum(
        "hts,thc->shc", grad_scores, queries[..., :NOPE], preferred_element_type=jnp.float32
    )
    grad_k_rope = scale_factor * jnp.einsum(
        "hts,thr->sr", grad_scores, queries[..., NOPE:], preferred_element_type=jnp.float32
    )
    grad_expanded = low(
        jnp.concatenate([grad_k_plain, grad_values], axis=-1).reshape(
            total_rows, heads_here * (NOPE + VDIM)
        )
    )
    grad_expand_weight = dot(latents_all.T, grad_expanded)
    grad_keys = jnp.concatenate([dot(grad_expanded, expand_weight.T), grad_k_rope], axis=1)
    grad_keys = scatter_all(grid, pad_columns(low(grad_keys)), jnp.float32, 6, pieces=1)
    _, pull_qrope = jax.vjp(partial(rotate, places=places), q_raw[..., NOPE:])
    (grad_q_turned,) = pull_qrope(grad_q_rope)
    grad_q_low = low(
        jnp.concatenate([grad_q_plain, grad_q_turned], axis=-1).reshape(tok_rows, -1)
    )
    grad_q_all = lax.all_gather(grad_q_low, "expert", axis=0, tiled=True)
    grad_normed = tensor_scatter(grid, low(dot(grad_q_low, query_weight.T)), 7)

    places_few = quarter(places)
    compressed_few = quarter(compressed)
    _, pull_latent = jax.vjp(rms_scale, compressed_few[:, :LATENT], latent_gain)
    grad_plain_latent, grad_latent_gain = pull_latent(grad_keys[:, :LATENT])
    _, pull_krope = jax.vjp(partial(rotate, places=places_few), compressed_few[:, LATENT:])
    (grad_k_turned,) = pull_krope(grad_keys[:, LATENT : LATENT + ROPE])
    grad_comp_low = low(jnp.concatenate([grad_plain_latent, grad_k_turned], axis=-1))
    grad_comp_all = gather_all(grid, pad_columns(grad_comp_low), 8).reshape(total_rows, -1)
    grad_comp_all = grad_comp_all[:, : LATENT + ROPE]
    grad_latent_weight = dot(normed_all.T, grad_comp_all)
    grad_query_weight = dot(normed_all.T, grad_q_all)
    grad_normed = grad_normed + dot(grad_comp_low, latent_weight.T)
    _, pull_input = jax.vjp(rms_scale, quarter(hidden_f), attn_gain)
    grad_input_norm, grad_attn_gain = pull_input(grad_normed)
    grad_hidden = tensor_gather(grid, low(grad_residual + grad_input_norm), 9).astype(jnp.float32)

    gains = lax.psum(jnp.concatenate([grad_attn_gain, grad_latent_gain, grad_moe_gain]), ALL)
    grad_output_weight = lax.psum(low(grad_output_weight), "expert").astype(jnp.float32)
    grad_expand_weight = lax.psum(low(grad_expand_weight), "expert").astype(jnp.float32)
    return (
        layer_out,
        grad_hidden,
        gains[:model_width],
        grad_query_weight,
        grad_latent_weight,
        gains[model_width : model_width + LATENT],
        grad_expand_weight,
        grad_output_weight,
        gains[model_width + LATENT :],
        grad_shared_gate,
        grad_shared_up,
        grad_shared_down,
        grad_expert_gate,
        grad_expert_up,
        grad_expert_down,
    )


def solution(mesh):
    grid = Grid(mesh.shape["expert"], mesh.shape["tensor"])
    placed = (
        P("expert", None),
        P(),
        P(None, "tensor"),
        P(),
        P(),
        P(None, "tensor"),
        P("tensor", None),
        P(),
        P(None, "tensor"),
        P(None, "tensor"),
        P("tensor", None),
        P("expert", None, "tensor"),
        P("expert", None, "tensor"),
        P("expert", "tensor", None),
        P("expert", None),
        P("expert", None),
        P(),
        P("expert", None),
    )
    return jax.shard_map(
        partial(shards, grid),
        mesh=mesh,
        in_specs=placed,
        out_specs=(
            P("expert", None),
            P("expert", None),
            P(),
            P(None, "tensor"),
            P(),
            P(),
            P(None, "tensor"),
            P("tensor", None),
            P(),
            P(None, "tensor"),
            P(None, "tensor"),
            P("tensor", None),
            P("expert", None, "tensor"),
            P("expert", None, "tensor"),
            P("expert", "tensor", None),
        ),
        check_vma=False,
    )
```

```python
import functools
from functools import partial

import jax
import jax.numpy as jnp
from jax import lax
from jax.experimental import pallas as pl
from jax.experimental.pallas import tpu as pltpu
from jax.sharding import PartitionSpec as P

NOPE = 128
ROPE = 64
VDIM = 128
LATENT = 512
TOP = 6
EXP_DEV = 2
ALL = ("expert", "tensor")
MESH = pl.DeviceIdType.MESH

epsilon = 1e-06
masked_out = -1e30


class Grid:
    def __init__(self, expert, tensor):
        self.na = 4 if expert % 4 == 0 else 1
        self.nb = expert // self.na
        self.ny = tensor // 2
        self.size = expert * tensor

    def here(self):
        e, t = lax.axis_index("expert"), lax.axis_index("tensor")
        return (lax.div(e, self.nb), lax.rem(e, self.nb), lax.div(t, 2), lax.rem(t, 2))

    def device(self, a, b, y, c):
        return {"expert": a * self.nb + b, "tensor": y * 2 + c}

    def block(self, a, b, y, c):
        return ((a * self.nb + b) * self.ny + y) * 2 + c


def wrap(i, n):
    return lax.rem(i, n)


def greet(grid):
    a, b, y, c = grid.here()
    barrier = pltpu.get_barrier_semaphore()
    others = (
        [grid.device(wrap(a + i, grid.na), b, y, c) for i in range(1, grid.na)]
        + [grid.device(a, wrap(b + i, grid.nb), y, c) for i in range(1, grid.nb)]
        + [grid.device(a, b, wrap(y + i, grid.ny), c) for i in range(1, grid.ny)]
        + [grid.device(a, b, y, 1 - c)]
    )
    for other in others:
        pl.semaphore_signal(barrier, inc=1, device_id=other, device_id_type=MESH)
    pl.semaphore_wait(barrier, len(others))


def gather_kernel(grid, x_ref, out_ref, own_sem, send_sem, recv_sem, core_send, core_recv):
    na, nb, ny = grid.na, grid.nb, grid.ny
    a, b, y, c = grid.here()
    half = x_ref.shape[0] // 2
    greet(grid)
    waits = []

    def dst(bb, yy, cc, aa, h):
        return out_ref.at[grid.block(aa, bb, yy, cc), pl.ds(h * half, half)]

    def slot(bb, yy, aa, h):
        return ((bb * ny + yy) * na + aa) * 2 + h

    def push(src, bb, yy, aa, h, where, kind):
        copy = pltpu.make_async_remote_copy(
            src_ref=src,
            dst_ref=dst(bb, yy, c, aa, h),
            send_sem=core_send.at[slot(bb, yy, aa, h)] if kind == "c" else send_sem.at[len(waits)],
            recv_sem=(core_recv if kind == "c" else recv_sem).at[slot(bb, yy, aa, h)],
            device_id=where,
            device_id_type=MESH,
        )
        copy.start()
        if kind != "c":
            waits.append(copy)
        else:
            core_waits.append(copy)

    core_waits = []

    def onward(src, bb, yy, aa, h, dims):
        for d in dims:
            if d == "a":
                for i in range(1, na):
                    push(src, bb, yy, aa, h, grid.device(wrap(a + i, na), b, y, c), d)
            if d == "b":
                for i in range(1, nb):
                    push(src, bb, yy, aa, h, grid.device(a, wrap(b + i, nb), y, c), d)
            if d == "y":
                for i in range(1, ny):
                    push(src, bb, yy, aa, h, grid.device(a, b, wrap(y + i, ny), c), d)
        push(src, bb, yy, aa, h, grid.device(a, b, y, 1 - c), "c")

    def landed(bb, yy, cc, aa, h, sem):
        ref = dst(bb, yy, cc, aa, h)
        pltpu.make_async_copy(ref, ref, sem.at[slot(bb, yy, aa, h)]).wait()
        return ref

    own = pltpu.make_async_copy(x_ref, out_ref.at[grid.block(a, b, y, c)], own_sem)
    own.start()
    orders = (("b", "y"), ("y", "b"))
    for h in range(2):
        onward(x_ref.at[pl.ds(h * half, half)], b, y, a, h, ("a",) + orders[h])
    for i in range(1, na):
        aa = wrap(a + na - i, na)
        for h in range(2):
            onward(landed(b, y, c, aa, h, recv_sem), b, y, aa, h, orders[h])
    for i in range(na):
        aa = wrap(a + na - i, na)
        for h in range(2):
            n1 = (nb, ny)[h]
            for j in range(1, n1):
                bb, yy = (wrap(b + nb - j, nb), y) if h == 0 else (b, wrap(y + ny - j, ny))
                onward(landed(bb, yy, c, aa, h, recv_sem), bb, yy, aa, h, orders[h][1:])
    for i in range(na):
        aa = wrap(a + na - i, na)
        for h in range(2):
            for j in range(nb):
                for k in range(1, ny):
                    if h == 0:
                        bb, yy = wrap(b + nb - j, nb), wrap(y + ny - k, ny)
                        onward(landed(bb, yy, c, aa, h, recv_sem), bb, yy, aa, h, ())
            for j in range(ny):
                for k in range(1, nb):
                    if h == 1:
                        bb, yy = wrap(b + nb - k, nb), wrap(y + ny - j, ny)
                        onward(landed(bb, yy, c, aa, h, recv_sem), bb, yy, aa, h, ())
    for j in range(nb):
        for k in range(ny):
            for i in range(na):
                for h in range(2):
                    landed(wrap(b + nb - j, nb), wrap(y + ny - k, ny), 1 - c, wrap(a + na - i, na), h, core_recv)
    own.wait()
    for copy in waits + core_waits:
        copy.wait_send()


def gather_all(grid, x, collective_id):
    r, n = x.shape
    blocks = grid.na * grid.nb * grid.ny
    sends = 2 * (grid.na - 1 + grid.na * (grid.nb - 1) + grid.na * (grid.ny - 1)) + 2 * grid.na * ((grid.nb - 1) * (grid.ny - 1))
    return pl.pallas_call(
        functools.partial(gather_kernel, grid),
        out_shape=jax.ShapeDtypeStruct((grid.size, r, n), x.dtype),
        in_specs=[pl.BlockSpec(memory_space=pl.ANY)],
        out_specs=pl.BlockSpec(memory_space=pl.ANY),
        scratch_shapes=[
            pltpu.SemaphoreType.DMA,
            pltpu.SemaphoreType.DMA((sends,)),
            pltpu.SemaphoreType.DMA((2 * blocks,)),
            pltpu.SemaphoreType.DMA((2 * blocks,)),
            pltpu.SemaphoreType.DMA((2 * blocks,)),
        ],
        compiler_params=pltpu.CompilerParams(collective_id=collective_id, has_side_effects=True),
    )(x)


def scatter_kernel(grid, pieces, p_ref, out_ref, acc, core_in, d1_in0, d1_in1, d2_in0, d2_in1, a_in,
                   load_sem, core_s, core_r, s10, r10, s11, r11, s20, r20, s21, r21, sa, ra):
    na, nb, ny = grid.na, grid.nb, grid.ny
    a, b, y, c = grid.here()
    half = p_ref.shape[4] // 2
    width = p_ref.shape[5] // pieces
    greet(grid)
    pending = []

    def send(src, dst, ss, rs, where):
        copy = pltpu.make_async_remote_copy(src_ref=src, dst_ref=dst, send_sem=ss, recv_sem=rs, device_id=where, device_id_type=MESH)
        copy.start()
        pending.append(copy)

    def await_in(ref, sem):
        pltpu.make_async_copy(ref, ref, sem).wait()

    def add(dst, src):
        dst[...] = (dst[...].astype(jnp.float32) + src[...].astype(jnp.float32)).astype(dst.dtype)

    def cols(p):
        return pl.ds(p * width, width)

    spots = [(j, k) for j in reversed(range(nb)) for k in reversed(range(ny))]
    loads = {}
    for p in range(pieces):
        for n, (j, k) in enumerate(spots):
            bb, yy = wrap(b + j, nb), wrap(y + k, ny)
            send(p_ref.at[:, bb, yy, 1 - c, :, cols(p)], core_in.at[p, j, k], core_s.at[p, n], core_r.at[p, n],
                 grid.device(a, b, y, 1 - c))
            load = pltpu.make_async_copy(p_ref.at[:, bb, yy, c, :, cols(p)], acc.at[p, j, k], load_sem.at[p, n])
            load.start()
            loads[p, n] = load
    rows = (pl.ds(0, half), pl.ds(half, half))
    for p in range(pieces):
        for n, (j, k) in enumerate(spots):
            loads[p, n].wait()
            await_in(core_in.at[p, j, k], core_r.at[p, n])
            for i in range(na):
                add(acc.at[p, j, k, i], core_in.at[p, j, k, i])
            if k:
                send(acc.at[p, j, k, :, rows[0]], d1_in0.at[p, j, k - 1], s10.at[p, j, k - 1], r10.at[p, j, k - 1],
                     grid.device(a, b, wrap(y + k, ny), c))
            if j:
                send(acc.at[p, j, k, :, rows[1]], d1_in1.at[p, k, j - 1], s11.at[p, k, j - 1], r11.at[p, k, j - 1],
                     grid.device(a, wrap(b + j, nb), y, c))
    for p in range(pieces):
        for j in reversed(range(nb)):
            for k in range(1, ny):
                await_in(d1_in0.at[p, j, k - 1], r10.at[p, j, k - 1])
                for i in range(na):
                    add(acc.at[p, j, 0, i, rows[0]], d1_in0.at[p, j, k - 1, i])
            if j:
                send(acc.at[p, j, 0, :, rows[0]], d2_in0.at[p, j - 1], s20.at[p, j - 1], r20.at[p, j - 1],
                     grid.device(a, wrap(b + j, nb), y, c))
        for k in reversed(range(ny)):
            for j in range(1, nb):
                await_in(d1_in1.at[p, k, j - 1], r11.at[p, k, j - 1])
                for i in range(na):
                    add(acc.at[p, 0, k, i, rows[1]], d1_in1.at[p, k, j - 1, i])
            if k:
                send(acc.at[p, 0, k, :, rows[1]], d2_in1.at[p, k - 1], s21.at[p, k - 1], r21.at[p, k - 1],
                     grid.device(a, b, wrap(y + k, ny), c))
    for p in range(pieces):
        for j in range(1, nb):
            await_in(d2_in0.at[p, j - 1], r20.at[p, j - 1])
            for i in range(na):
                add(acc.at[p, 0, 0, i, rows[0]], d2_in0.at[p, j - 1, i])
        for k in range(1, ny):
            await_in(d2_in1.at[p, k - 1], r21.at[p, k - 1])
            for i in range(na):
                add(acc.at[p, 0, 0, i, rows[1]], d2_in1.at[p, k - 1, i])
        for i in range(1, na):
            aa = wrap(a + i, na)
            send(acc.at[p, 0, 0, aa], a_in.at[p, i - 1], sa.at[p, i - 1], ra.at[p, i - 1], grid.device(aa, b, y, c))
    for p in range(pieces):
        total = acc[p, 0, 0, a].astype(jnp.float32)
        for i in range(1, na):
            await_in(a_in.at[p, i - 1], ra.at[p, i - 1])
            total = total + a_in[p, i - 1].astype(jnp.float32)
        out_ref[:, cols(p)] = total.astype(out_ref.dtype)
    for copy in pending:
        copy.wait_send()


def scatter_all(grid, p, dtype, collective_id, pieces=2):
    r, n = p.shape[0] // grid.size, p.shape[1]
    na, nb, ny = grid.na, grid.nb, grid.ny
    half, width = r // 2, n // pieces
    sems = lambda *s: pltpu.SemaphoreType.DMA(s)
    vm = lambda *s: pltpu.VMEM(s, jnp.bfloat16)
    return pl.pallas_call(
        functools.partial(scatter_kernel, grid, pieces),
        out_shape=jax.ShapeDtypeStruct((r, n), dtype),
        in_specs=[pl.BlockSpec(memory_space=pl.ANY)],
        out_specs=pl.BlockSpec(memory_space=pltpu.VMEM),
        scratch_shapes=[
            vm(pieces, nb, ny, na, r, width),
            vm(pieces, nb, ny, na, r, width),
            vm(pieces, nb, ny - 1, na, half, width),
            vm(pieces, ny, nb - 1, na, half, width),
            vm(pieces, nb - 1, na, half, width),
            vm(pieces, ny - 1, na, half, width),
            vm(pieces, na - 1, r, width),
            sems(pieces, nb * ny), sems(pieces, nb * ny), sems(pieces, nb * ny),
            sems(pieces, nb, ny - 1), sems(pieces, nb, ny - 1),
            sems(pieces, ny, nb - 1), sems(pieces, ny, nb - 1),
            sems(pieces, nb - 1), sems(pieces, nb - 1),
            sems(pieces, ny - 1), sems(pieces, ny - 1),
            sems(pieces, na - 1), sems(pieces, na - 1),
        ],
        compiler_params=pltpu.CompilerParams(collective_id=collective_id, has_side_effects=True, vmem_limit_bytes=40 << 20),
    )(p.reshape(na, nb, ny, 2, r, n))


def greet_tensor(grid):
    a, b, y, c = grid.here()
    barrier = pltpu.get_barrier_semaphore()
    others = [grid.device(a, b, wrap(y + i, grid.ny), c) for i in range(1, grid.ny)]
    others.append(grid.device(a, b, y, 1 - c))
    for other in others:
        pl.semaphore_signal(barrier, inc=1, device_id=other, device_id_type=MESH)
    pl.semaphore_wait(barrier, len(others))


def tensor_scatter_kernel(grid, p_ref, out_ref, acc, core_in, y_in, core_s, core_r, ys, yr):
    ny = grid.ny
    a, b, y, c = grid.here()
    greet_tensor(grid)
    pending = []
    for k in reversed(range(ny)):
        copy = pltpu.make_async_remote_copy(
            src_ref=p_ref.at[wrap(y + k, ny), 1 - c], dst_ref=core_in.at[k], send_sem=core_s.at[k], recv_sem=core_r.at[k],
            device_id=grid.device(a, b, y, 1 - c), device_id_type=MESH,
        )
        copy.start()
        pending.append(copy)
    for k in reversed(range(ny)):
        pltpu.make_async_copy(core_in.at[k], core_in.at[k], core_r.at[k]).wait()
        total = p_ref[wrap(y + k, ny), c].astype(jnp.float32) + core_in[k].astype(jnp.float32)
        if k:
            acc[k - 1] = total.astype(acc.dtype)
            copy = pltpu.make_async_remote_copy(
                src_ref=acc.at[k - 1], dst_ref=y_in.at[k - 1], send_sem=ys.at[k - 1], recv_sem=yr.at[k - 1],
                device_id=grid.device(a, b, wrap(y + k, ny), c), device_id_type=MESH,
            )
            copy.start()
            pending.append(copy)
        else:
            out_ref[...] = total
    for k in range(1, ny):
        pltpu.make_async_copy(y_in.at[k - 1], y_in.at[k - 1], yr.at[k - 1]).wait()
        out_ref[...] += y_in[k - 1].astype(jnp.float32)
    for copy in pending:
        copy.wait_send()


def tensor_scatter(grid, p, collective_id):
    ny = grid.ny
    r, n = p.shape[0] // (2 * ny), p.shape[1]
    return pl.pallas_call(
        functools.partial(tensor_scatter_kernel, grid),
        out_shape=jax.ShapeDtypeStruct((r, n), jnp.float32),
        in_specs=[pl.BlockSpec(memory_space=pltpu.VMEM)],
        out_specs=pl.BlockSpec(memory_space=pltpu.VMEM),
        scratch_shapes=[
            pltpu.VMEM((max(ny - 1, 1), r, n), p.dtype),
            pltpu.VMEM((ny, r, n), p.dtype),
            pltpu.VMEM((max(ny - 1, 1), r, n), p.dtype),
            pltpu.SemaphoreType.DMA((ny,)),
            pltpu.SemaphoreType.DMA((ny,)),
            pltpu.SemaphoreType.DMA((max(ny - 1, 1),)),
            pltpu.SemaphoreType.DMA((max(ny - 1, 1),)),
        ],
        compiler_params=pltpu.CompilerParams(
            collective_id=collective_id, has_side_effects=True, vmem_limit_bytes=16 << 20
        ),
    )(p.reshape(ny, 2, r, n))


def tensor_gather_kernel(grid, x_ref, out_ref, own_sem, ys, yr, core_s, core_r):
    ny = grid.ny
    a, b, y, c = grid.here()
    greet_tensor(grid)
    own = pltpu.make_async_copy(x_ref, out_ref.at[y, c], own_sem)
    own.start()
    pending = []

    def push(src, spot, ss, rs, where):
        copy = pltpu.make_async_remote_copy(
            src_ref=src, dst_ref=out_ref.at[spot, c], send_sem=ss, recv_sem=rs, device_id=where, device_id_type=MESH
        )
        copy.start()
        pending.append(copy)

    for k in range(1, ny):
        push(x_ref, y, ys.at[k], yr.at[k], grid.device(a, b, wrap(y + k, ny), c))
    push(x_ref, y, core_s.at[0], core_r.at[0], grid.device(a, b, y, 1 - c))
    for k in range(1, ny):
        spot = wrap(y + ny - k, ny)
        ref = out_ref.at[spot, c]
        pltpu.make_async_copy(ref, ref, yr.at[k]).wait()
        push(ref, spot, core_s.at[k], core_r.at[k], grid.device(a, b, y, 1 - c))
    for k in range(ny):
        ref = out_ref.at[wrap(y + ny - k, ny), 1 - c]
        pltpu.make_async_copy(ref, ref, core_r.at[k]).wait()
    own.wait()
    for copy in pending:
        copy.wait_send()


def tensor_gather(grid, x, collective_id):
    ny = grid.ny
    r, n = x.shape
    out = pl.pallas_call(
        functools.partial(tensor_gather_kernel, grid),
        out_shape=jax.ShapeDtypeStruct((ny, 2, r, n), x.dtype),
        in_specs=[pl.BlockSpec(memory_space=pltpu.VMEM)],
        out_specs=pl.BlockSpec(memory_space=pltpu.VMEM),
        scratch_shapes=[pltpu.SemaphoreType.DMA] + [pltpu.SemaphoreType.DMA((ny,))] * 4,
        compiler_params=pltpu.CompilerParams(
            collective_id=collective_id, has_side_effects=True, vmem_limit_bytes=16 << 20
        ),
    )(x)
    return out.reshape(2 * ny * r, n)


def dot_rows(left_side, right_side):
    return lax.dot_general(
        left_side, right_side, (((1,), (1,)), ((), ())), preferred_element_type=jnp.float32
    )


def dot_plain(left_side, right_side):
    return jnp.dot(left_side, right_side, preferred_element_type=jnp.float32)


def round_up(value, unit):
    return -(-value // unit) * unit


def experts_kernel(
    grid,
    pieces,
    x_ref,
    dz_ref,
    gate_ref,
    eg_hbm,
    eu_hbm,
    ed_hbm,
    sg_hbm,
    su_hbm,
    sd_hbm,
    all_ref,
    grad_ref,
    y_ref,
    gated_ref,
    dcat_ref,
    act_ref,
    dsg_ref,
    dsu_ref,
    raw,
    egu,
    ed,
    sg,
    su,
    sd,
    dabuf,
    xbuf,
    dzbuf,
    gated,
    dcat,
    act,
    dsg,
    dsu,
    ybuf,
    dx,
    dx_out,
    core_in,
    d1_in0,
    d1_in1,
    d2_in0,
    d2_in1,
    a_in,
    raw_sem,
    weight_sem,
    own_sem,
    x_sem,
    dz_sem,
    out_sem,
    fill_sem,
    send_sem,
    recv_sem,
    share_send,
    share_recv,
    core_s,
    core_r,
    s10,
    r10,
    s11,
    r11,
    s20,
    r20,
    s21,
    r21,
    sa,
    ra,
):
    na, nb, ny = grid.na, grid.nb, grid.ny
    a, b, y, c = grid.here()
    r, n = x_ref.shape
    half, width, rows = r // 2, n // pieces, na * r
    pairs = nb * ny
    steps = 2 * pairs
    device = a * nb + b
    f, fs = eg_hbm.shape[2], sg_hbm.shape[1]
    wide = egu.shape[1] // (2 * EXP_DEV)
    ef = EXP_DEV * wide
    f32, bf = jnp.float32, jnp.bfloat16

    def raw_load(src):
        return pltpu.make_async_copy(src, raw, raw_sem)

    loads = [
        pltpu.make_async_copy(ed_hbm.at[e], ed.at[pl.ds(e * wide, f)], weight_sem.at[e])
        for e in range(EXP_DEV)
    ]
    loads += [
        pltpu.make_async_copy(src, dst, weight_sem.at[EXP_DEV + i])
        for i, (src, dst) in enumerate(((sd_hbm, sd.at[pl.ds(0, fs)]), (sg_hbm, sg), (su_hbm, su)))
    ]
    for load in loads:
        load.start()
    raw_load(eg_hbm).start()
    greet(grid)

    counts = [0]

    def place(bb, yy, cc, aa, h):
        return all_ref.at[aa, bb, yy, cc, pl.ds(h * half, half)]

    def slot(bb, yy, aa, h):
        return ((bb * ny + yy) * na + aa) * 2 + h

    def push(src, bb, yy, aa, h, where, send, recv):
        pltpu.make_async_remote_copy(
            src_ref=src,
            dst_ref=place(bb, yy, c, aa, h),
            send_sem=send,
            recv_sem=recv.at[slot(bb, yy, aa, h)],
            device_id=where,
            device_id_type=MESH,
        ).start()

    def line(i):
        if na != 4:
            return wrap(a + i, na)
        if i == 0:
            return a
        if i == 1:
            return a + 1 - 2 * lax.rem(a, 2)
        return (i - lax.div(a, 2)) if i == 2 else (3 - 3 * lax.div(a, 2))

    def onward(src, bb, yy, aa, h, dims):
        for d in dims:
            size = {"a": na, "b": nb, "y": ny}[d]
            for i in range(1, size):
                where = {
                    "a": lambda: grid.device(line(i), b, y, c),
                    "b": lambda: grid.device(a, wrap(b + i, nb), y, c),
                    "y": lambda: grid.device(a, b, wrap(y + i, ny), c),
                }[d]()
                push(src, bb, yy, aa, h, where, send_sem.at[counts[0]], recv_sem)
                counts[0] += 1
        push(
            src, bb, yy, aa, h, grid.device(a, b, y, 1 - c), share_send.at[slot(bb, yy, aa, h)], share_recv
        )

    def landed(bb, yy, cc, aa, h, sem):
        ref = place(bb, yy, cc, aa, h)
        pltpu.make_async_copy(ref, ref, sem.at[slot(bb, yy, aa, h)]).wait()
        return ref

    orders = (("b", "y"), ("y", "b"))

    def relay(j, k, i, h, dims):
        bb, yy, aa = wrap(b + j, nb), wrap(y + k, ny), line(i)
        onward(landed(bb, yy, c, aa, h, recv_sem), bb, yy, aa, h, dims)

    own = pltpu.make_async_copy(x_ref, all_ref.at[a, b, y, c], own_sem)
    own.start()
    for h in range(2):
        onward(x_ref.at[pl.ds(h * half, half)], b, y, a, h, ("a",) + orders[h])

    hooks = {}
    early = []
    for i in range(na):
        if i:
            early += [(0, 0, i, h, orders[h]) for h in range(2)]
        if i:
            early += [(j, 0, i - 1, 0, orders[0][1:]) for j in range(1, nb)]
            early += [(0, k, i - 1, 1, orders[1][1:]) for k in range(1, ny)]
    early += [(j, 0, na - 1, 0, orders[0][1:]) for j in range(1, nb)]
    early += [(0, k, na - 1, 1, orders[1][1:]) for k in range(1, ny)]
    for m, event in enumerate(early):
        place_at = 1 + m * (2 * steps - 1) // len(early)
        hooks.setdefault(("early", place_at // 2, place_at % 2), []).append(event)
    for pair in range(1, pairs):
        j, k = pair // ny, pair % ny
        late = [(j, k, i, h, ()) for i in range(na) for h in range(2) if (k if h == 0 else j)]
        for m, event in enumerate(late):
            hooks.setdefault(("main", pair, m * 3 // len(late)), []).append(event)

    def hook(stage, step, spot):
        for (when_stage, when, when_spot), events in hooks.items():
            if when_stage == stage and when_spot == spot:

                @pl.when(step == when)
                def _():
                    for event in events:
                        relay(*event)

    def spots(step):
        pair, l = lax.div(step, 2), 1 - lax.rem(step, 2)
        j, k = lax.div(pair, ny), lax.rem(pair, ny)
        return j, k, l, wrap(b + j, nb), wrap(y + k, ny), wrap(c + l, 2)

    def flat(value):
        return value.reshape(rows, value.shape[-1])

    def fold(value):
        return value.reshape(na, r, value.shape[-1])

    def dz_load(step):
        _, _, _, bb, yy, cc = spots(step)
        s = lax.rem(step, 2)
        return pltpu.make_async_copy(dz_ref.at[:, bb, yy, cc], dzbuf.at[s], dz_sem.at[s])

    dz_load(a * 0).start()
    for e in range(EXP_DEV):
        ed[e * wide + f : (e + 1) * wide] = jnp.zeros((wide - f, n), bf)
    if sd.shape[0] > fs:
        sd[fs:] = jnp.zeros((sd.shape[0] - fs, n), bf)
    for load in loads[: EXP_DEV + 1]:
        load.wait()

    def early_body(step, carry):
        s = lax.rem(step, 2)

        @pl.when(step + 1 < steps)
        def _():
            dz_load(step + 1).start()

        dz_load(step).wait()
        dz = flat(dzbuf[s])
        dabuf[step, :, :ef] = dot_rows(dz, ed[...]).astype(bf)
        hook("early", step, 0)
        dabuf[step, :, ef:] = dot_rows(dz, sd[...]).astype(bf)
        hook("early", step, 1)
        return carry

    lax.fori_loop(0, steps, early_body, 0)
    for part, src in enumerate((eg_hbm, eu_hbm)):
        raw_load(src).wait()
        for e in range(EXP_DEV):
            at = part * ef + e * wide
            if wide > f:
                egu[:, at + wide - 128 : at + wide] = jnp.zeros((n, 128), bf)
            egu[:, at : at + f] = raw[e]
        if part == 0:
            raw_load(eu_hbm).start()
    for load in loads[EXP_DEV + 1 :]:
        load.wait()
    own.wait()

    def x_load(step):
        _, _, _, bb, yy, cc = spots(step)
        return pltpu.make_async_copy(all_ref.at[:, bb, yy, cc], xbuf.at[0], x_sem.at[0])

    def stores(step):
        _, _, _, bb, yy, cc = spots(step)
        s = lax.rem(step, 2)
        return [
            pltpu.make_async_copy(gated.at[s], gated_ref.at[:, bb, yy, cc], out_sem.at[s, 0]),
            pltpu.make_async_copy(dcat.at[s], dcat_ref.at[:, bb, yy, cc], out_sem.at[s, 1]),
        ]

    def remote(src, dst, ss, rs, where):
        return pltpu.make_async_remote_copy(
            src_ref=src, dst_ref=dst, send_sem=ss, recv_sem=rs, device_id=where, device_id_type=MESH
        )

    def cols(p):
        return pl.ds(p * width, width)

    upper = (pl.ds(0, half), pl.ds(half, half))

    def send_core(pair):
        j, k = lax.div(pair, ny), lax.rem(pair, ny)
        return remote(
            dx_out.at[lax.rem(pair, 2)], core_in.at[j, k], core_s.at[lax.rem(pair, 2)],
            core_r.at[j, k], grid.device(a, b, y, 1 - c),
        )

    def send_10(p, j, k):
        return remote(
            dx.at[j, k, :, upper[0], cols(p)], d1_in0.at[p, j, k - 1], s10.at[p, j, k - 1],
            r10.at[p, j, k - 1], grid.device(a, b, wrap(y + k, ny), c),
        )

    def send_11(p, j, k):
        return remote(
            dx.at[j, k, :, upper[1], cols(p)], d1_in1.at[p, k, j - 1], s11.at[p, k, j - 1],
            r11.at[p, k, j - 1], grid.device(a, wrap(b + j, nb), y, c),
        )

    def await_in(ref, sem):
        pltpu.make_async_copy(ref, ref, sem).wait()

    def add(dst, src):
        dst[...] = (dst[...].astype(f32) + src[...].astype(f32)).astype(dst.dtype)

    def shared_front(step, x, s):
        g = dot_plain(x, sg[...])
        u = dot_plain(x, su[...])
        d = dabuf[step, :, ef : ef + fs].astype(f32)
        sig = 1.0 / (1.0 + jnp.exp(-g))
        swish = g * sig
        act[s] = fold((swish * u).astype(bf))
        dsg[s] = fold((d * u * (sig + swish * (1.0 - sig))).astype(bf))
        dsu[s] = fold((d * swish).astype(bf))

    def is_mine(bb, yy, cc):
        return lax.rem((bb * ny + yy) * 2 + cc, na * nb) == device

    chunk = min(n, 1024)

    def main_body(step, carry):
        j, k, l, bb, yy, cc = spots(step)
        s = lax.rem(step, 2)

        @pl.when(l == 1)
        def _():
            for i in range(na):
                for h in range(2):
                    landed(bb, yy, cc, line(i), h, share_recv)

        x_load(step).start()

        @pl.when(step >= 2)
        def _():
            for store in stores(step - 2):
                store.wait()

        x_load(step).wait()
        x = flat(xbuf[0])
        g = dot_plain(x, egu[:, :ef])
        u = dot_plain(x, egu[:, ef:])
        for e in range(EXP_DEV):
            at = pl.ds(e * wide, wide)
            scale = flat(gate_ref[e, :, bb, yy, cc])
            ge, ue = g[:, e * wide : (e + 1) * wide], u[:, e * wide : (e + 1) * wide]
            d = dabuf[step, :, at].astype(f32) * scale
            sig = 1.0 / (1.0 + jnp.exp(-ge))
            swish = ge * sig
            gated[s, :, :, at] = fold((scale * (swish * ue)).astype(bf))
            dcat[s, :, :, at] = fold((d * ue * (sig + swish * (1.0 - sig))).astype(bf))
            dcat[s, :, :, pl.ds(ef + e * wide, wide)] = fold((d * swish).astype(bf))
        hook("main", step, 0)
        mine = is_mine(bb, yy, cc)

        @pl.when(mine)
        def _():
            shared_front(step, x, 0)

        hook("main", step, 1)

        def column(target):
            for q in range(n // chunk):
                at = pl.ds(q * chunk, chunk)
                total = dot_rows(flat(dcat[s]), egu[at])
                target[:, :, at] = fold(total.astype(bf))

            @pl.when(mine)
            def _():
                for q in range(n // chunk):
                    at = pl.ds(q * chunk, chunk)
                    more = dot_rows(flat(dsg[0]), sg[at]) + dot_rows(flat(dsu[0]), su[at])
                    target[:, :, at] = fold((flat(target[:, :, at]).astype(f32) + more).astype(bf))

        for store in stores(step):
            store.start()

        @pl.when(l == 1)
        def _():
            pair = lax.div(step, 2)

            @pl.when(pair >= 2)
            def _():
                send_core(pair - 2).wait_send()

            column(dx_out.at[lax.rem(pair, 2)])
            send_core(pair).start()

        @pl.when(l == 0)
        def _():
            column(dx.at[j, k])
            await_in(core_in.at[j, k], core_r.at[j, k])

            def one(i, carry):
                add(dx.at[j, k, i], core_in.at[j, k, i])
                return carry

            lax.fori_loop(0, na, one, 0)

            @pl.when(k > 0)
            def _():
                for p in range(pieces):
                    send_10(p, j, k).start()

            @pl.when(j > 0)
            def _():
                for p in range(pieces):
                    send_11(p, j, k).start()

        hook("main", step, 2)
        return carry

    lax.fori_loop(0, steps, main_body, 0)
    for step in (steps - 2, steps - 1):
        for store in stores(a * 0 + step):
            store.wait()

    def send_20(p, j):
        return remote(
            dx.at[j, 0, :, upper[0], cols(p)], d2_in0.at[p, j - 1], s20.at[p, j - 1],
            r20.at[p, j - 1], grid.device(a, wrap(b + j, nb), y, c),
        )

    def send_21(p, k):
        return remote(
            dx.at[0, k, :, upper[1], cols(p)], d2_in1.at[p, k - 1], s21.at[p, k - 1],
            r21.at[p, k - 1], grid.device(a, b, wrap(y + k, ny), c),
        )

    def send_a(p, i):
        return remote(
            dx.at[0, 0, wrap(a + i, na), :, cols(p)], a_in.at[p, i - 1], sa.at[p, i - 1],
            ra.at[p, i - 1], grid.device(wrap(a + i, na), b, y, c),
        )

    def sum_first(p):
        for j in reversed(range(nb)):
            for k in range(1, ny):
                await_in(d1_in0.at[p, j, k - 1], r10.at[p, j, k - 1])
                for i in range(na):
                    add(dx.at[j, 0, i, upper[0], cols(p)], d1_in0.at[p, j, k - 1, i])
            if j:
                send_20(p, j).start()
        for k in reversed(range(ny)):
            for j in range(1, nb):
                await_in(d1_in1.at[p, k, j - 1], r11.at[p, k, j - 1])
                for i in range(na):
                    add(dx.at[0, k, i, upper[1], cols(p)], d1_in1.at[p, k, j - 1, i])
            if k:
                send_21(p, k).start()

    def sum_second(p):
        for j in range(1, nb):
            await_in(d2_in0.at[p, j - 1], r20.at[p, j - 1])
            for i in range(na):
                add(dx.at[0, 0, i, upper[0], cols(p)], d2_in0.at[p, j - 1, i])
        for k in range(1, ny):
            await_in(d2_in1.at[p, k - 1], r21.at[p, k - 1])
            for i in range(na):
                add(dx.at[0, 0, i, upper[1], cols(p)], d2_in1.at[p, k - 1, i])
        for i in range(1, na):
            send_a(p, i).start()

    def sum_last(p):
        total = dx[0, 0, a, :, cols(p)].astype(f32)
        for i in range(1, na):
            await_in(a_in.at[p, i - 1], ra.at[p, i - 1])
            total = total + a_in[p, i - 1].astype(f32)
        grad_ref[:, cols(p)] = total

    work = [(sum_first, p) for p in range(pieces)] + [(sum_second, p) for p in range(pieces)]
    turns = {}
    for m, item in enumerate(work):
        turns.setdefault(min(steps - 1, 1 + m * (steps - 1) // len(work)), []).append(item)

    def fill_loads(step):
        _, _, _, bb, yy, cc = spots(step)
        s = lax.rem(step, 2)
        return [
            pltpu.make_async_copy(all_ref.at[:, bb, yy, cc], xbuf.at[s], x_sem.at[s]),
            pltpu.make_async_copy(gated_ref.at[:, bb, yy, cc], gated.at[s], fill_sem.at[s]),
        ]

    def fill_stores(step):
        _, _, _, bb, yy, cc = spots(step)
        s = lax.rem(step, 2)
        pairs_of = [
            (act.at[s], act_ref.at[:, bb, yy, cc]),
            (dsg.at[s], dsg_ref.at[:, bb, yy, cc]),
            (dsu.at[s], dsu_ref.at[:, bb, yy, cc]),
            (ybuf.at[s], y_ref.at[:, bb, yy, cc]),
        ]
        return [
            pltpu.make_async_copy(src, dst, out_sem.at[s, i])
            for i, (src, dst) in enumerate(pairs_of)
        ]

    for load in fill_loads(a * 0):
        load.start()

    def fill_body(step, carry):
        j, k, l, bb, yy, cc = spots(step)
        s = lax.rem(step, 2)

        @pl.when(step + 1 < steps)
        def _():
            for load in fill_loads(step + 1):
                load.start()

        @pl.when(step >= 2)
        def _():
            for store in fill_stores(step - 2):
                store.wait()

        for load in fill_loads(step):
            load.wait()
        x = flat(xbuf[s])
        shared_front(step, x, s)
        for q in range(n // chunk):
            at = pl.ds(q * chunk, chunk)
            ybuf[s, :, :, at] = fold(dot_plain(flat(gated[s]), ed[:, at]).astype(bf))

        @pl.when(is_mine(bb, yy, cc))
        def _():
            for q in range(n // chunk):
                at = pl.ds(q * chunk, chunk)
                more = dot_plain(flat(act[s]), sd[:fs, at])
                ybuf[s, :, :, at] = fold((flat(ybuf[s, :, :, at]).astype(f32) + more).astype(bf))

        for store in fill_stores(step):
            store.start()
        for when, items in turns.items():

            @pl.when(step == when)
            def _():
                for item, p in items:
                    item(p)

        return carry

    lax.fori_loop(0, steps, fill_body, 0)
    for p in range(pieces):
        sum_last(p)

    for step in (steps - 2, steps - 1):
        for store in fill_stores(a * 0 + step):
            store.wait()
    some = place(b, y, c, a, 0)
    for i in range(counts[0]):
        pltpu.make_async_copy(some, some, send_sem.at[i]).wait()
    for i in range(2 * na * pairs):
        pltpu.make_async_copy(some, some, share_send.at[i]).wait()
    for pair in range(max(0, pairs - 2), pairs):
        send_core(a * 0 + pair).wait_send()
    for p in range(pieces):
        for j in range(nb):
            for k in range(ny):
                if k:
                    send_10(p, j, k).wait_send()
                if j:
                    send_11(p, j, k).wait_send()
        for j in range(1, nb):
            send_20(p, j).wait_send()
        for k in range(1, ny):
            send_21(p, k).wait_send()
        for i in range(1, na):
            send_a(p, i).wait_send()


def experts_call(
    grid, x, dz, gates, expert_gate, expert_up, expert_down, shared_gate, shared_up, shared_down,
    collective_id, pieces=2,
):
    r, n = x.shape
    na, nb, ny = grid.na, grid.nb, grid.ny
    f, fs = expert_gate.shape[2], shared_gate.shape[1]
    wide, wide_s = round_up(f, 128), round_up(fs, 128)
    ef = EXP_DEV * wide
    half, width, rows = r // 2, n // pieces, na * r
    steps = 2 * nb * ny
    lay = (na, nb, ny, 2, r)
    bf = jnp.bfloat16
    sems = lambda *s: pltpu.SemaphoreType.DMA(s)
    vm = lambda *s: pltpu.VMEM(s, bf)
    sends = 2 * (na - 1 + na * (nb - 1) + na * (ny - 1) + na * (nb - 1) * (ny - 1))
    any_space = pl.BlockSpec(memory_space=pl.ANY)
    in_vmem = pl.BlockSpec(memory_space=pltpu.VMEM)
    outs = pl.pallas_call(
        functools.partial(experts_kernel, grid, pieces),
        out_shape=[
            jax.ShapeDtypeStruct(lay + (n,), bf),
            jax.ShapeDtypeStruct((r, n), jnp.float32),
            jax.ShapeDtypeStruct(lay + (n,), bf),
            jax.ShapeDtypeStruct(lay + (ef,), bf),
            jax.ShapeDtypeStruct(lay + (2 * ef,), bf),
            jax.ShapeDtypeStruct(lay + (fs,), bf),
            jax.ShapeDtypeStruct(lay + (fs,), bf),
            jax.ShapeDtypeStruct(lay + (fs,), bf),
        ],
        in_specs=[any_space, any_space, in_vmem] + [any_space] * 6,
        out_specs=[any_space, in_vmem] + [any_space] * 6,
        scratch_shapes=[
            vm(EXP_DEV, n, f), vm(n, 2 * ef), vm(ef, n), vm(n, fs), vm(n, fs), vm(wide_s, n),
            vm(steps, rows, ef + wide_s),
            vm(2, na, r, n), vm(2, na, r, n),
            vm(2, na, r, ef), vm(2, na, r, 2 * ef),
            vm(2, na, r, fs), vm(2, na, r, fs), vm(2, na, r, fs),
            vm(2, na, r, n),
            vm(nb, ny, na, r, n),
            vm(2, na, r, n),
            vm(nb, ny, na, r, n),
            vm(pieces, nb, ny - 1, na, half, width),
            vm(pieces, ny, nb - 1, na, half, width),
            vm(pieces, nb - 1, na, half, width),
            vm(pieces, ny - 1, na, half, width),
            vm(pieces, na - 1, r, width),
            pltpu.SemaphoreType.DMA, sems(EXP_DEV + 3), pltpu.SemaphoreType.DMA, sems(2), sems(2),
            sems(2, 4), sems(2),
            sems(sends), sems(2 * na * nb * ny), sems(2 * na * nb * ny), sems(2 * na * nb * ny),
            sems(2), sems(nb, ny),
            sems(pieces, nb, ny - 1), sems(pieces, nb, ny - 1),
            sems(pieces, ny, nb - 1), sems(pieces, ny, nb - 1),
            sems(pieces, nb - 1), sems(pieces, nb - 1),
            sems(pieces, ny - 1), sems(pieces, ny - 1),
            sems(pieces, na - 1), sems(pieces, na - 1),
        ],
        compiler_params=pltpu.CompilerParams(
            collective_id=collective_id, has_side_effects=True, vmem_limit_bytes=63 << 20
        ),
    )(
        x,
        dz.reshape(lay + (n,)),
        gates.reshape((EXP_DEV,) + lay + (1,)),
        expert_gate, expert_up, expert_down, shared_gate, shared_up, shared_down,
    )
    tokens = grid.size * r
    rows_all, grad, out_rows, gated, dcat, act, d_sg, d_su = outs
    return (
        rows_all.reshape(tokens, n),
        grad,
        out_rows.reshape(tokens, n),
        gated.reshape(tokens, ef),
        dcat.reshape(tokens, 2 * ef),
        act.reshape(tokens, fs),
        d_sg.reshape(tokens, fs),
        d_su.reshape(tokens, fs),
    )


def rms_scale(values, gain_vec):
    return (
        values * lax.rsqrt(jnp.mean(values * values, axis=-1, keepdims=True) + epsilon) * gain_vec
    )


def rotate(values, places):
    halfway = values.shape[-1] // 2
    frequency = 10000.0 ** (-jnp.arange(halfway, dtype=jnp.float32) / halfway)
    angles = places.astype(jnp.float32)[:, None] * frequency[None, :]
    cosine = jnp.cos(angles)
    sine_part = jnp.sin(angles)
    if values.ndim == 3:
        cosine = cosine[:, None, :]
        sine_part = sine_part[:, None, :]
    first_half = values[..., :halfway]
    second = values[..., halfway:]
    return jnp.concatenate(
        [first_half * cosine - second * sine_part, second * cosine + first_half * sine_part],
        axis=-1,
    )


def seq_places(segments):
    total_rows = segments.shape[0]
    ordinal = jnp.arange(total_rows, dtype=jnp.int32)
    starts = jnp.concatenate(
        [jnp.ones((1,), jnp.int32), (segments[1:] != segments[:-1]).astype(jnp.int32)]
    )
    seg_start = lax.cummax(jnp.where(starts > 0, ordinal, 0), axis=0)
    return jnp.where(segments == 0, ordinal, total_rows // 2 + ordinal - seg_start)


def silu_product(gate_pre, up_pre):
    return jax.nn.silu(gate_pre) * up_pre


def score_block(queries, key_plain, rope_all, visible):
    scale_factor = (NOPE + ROPE) ** (-0.5)
    raw_scores = jnp.einsum(
        "thc,shc->hts", queries[..., :NOPE], key_plain, preferred_element_type=jnp.float32
    )
    raw_scores = raw_scores + jnp.einsum(
        "thr,sr->hts", queries[..., NOPE:], rope_all, preferred_element_type=jnp.float32
    )
    return jnp.where(visible[None], scale_factor * raw_scores, masked_out)


def dot(left_side, right_side):
    return jnp.dot(left_side, right_side, preferred_element_type=jnp.float32)


def pad_columns(values):
    return jnp.pad(values, ((0, 0), (0, -values.shape[1] % 128)))


def low(values):
    return values.astype(jnp.bfloat16)


def shards(
    grid,
    hidden_in,
    attn_gain,
    query_weight,
    latent_weight,
    latent_gain,
    expand_weight,
    output_weight,
    moe_gain,
    shared_gate,
    shared_up,
    shared_down,
    expert_gate,
    expert_up,
    expert_down,
    gate_values,
    expert_routes,
    segments,
    cotangent,
):
    tok_rows, model_width = hidden_in.shape
    groups = lax.axis_size("expert")
    parts = lax.axis_size("tensor")
    device = lax.axis_index("expert")
    part = lax.axis_index("tensor")
    total_rows = segments.shape[0]
    few = tok_rows // parts
    start_row = device * tok_rows
    scale_factor = (NOPE + ROPE) ** (-0.5)

    def quarter(values):
        return lax.dynamic_slice_in_dim(values, part * few, few)

    def own_group(values):
        return lax.dynamic_slice_in_dim(values, start_row, tok_rows)

    places = own_group(seq_places(segments))
    own_seg = own_group(segments)
    own_ordinal = start_row + jnp.arange(tok_rows, dtype=jnp.int32)
    key_ordinal = jnp.arange(total_rows, dtype=jnp.int32)
    visible = (key_ordinal[None, :] <= own_ordinal[:, None]) & (
        (segments[None, :] == own_seg[:, None]) | (segments[None, :] == 0)
    )
    experts_all = EXP_DEV * groups
    cot_all = lax.all_gather(quarter(cotangent), ALL, axis=0, tiled=True)

    hidden_f = hidden_in.astype(jnp.float32)
    normed = low(rms_scale(hidden_f, attn_gain))
    compressed = dot(normed, latent_weight)
    latents = low(rms_scale(compressed[:, :LATENT], latent_gain))
    key_rope = low(rotate(compressed[:, LATENT:], places))
    onehot = expert_routes[:, :, None] == jnp.arange(experts_all, dtype=jnp.int32)
    gate_rows = jnp.sum(jnp.where(onehot, gate_values[:, :, None], 0.0), axis=1)
    gate_high = low(gate_rows)
    gate_low = low(gate_rows - gate_high.astype(jnp.float32))
    packed = pad_columns(jnp.concatenate([latents, key_rope, gate_high, gate_low], axis=1))
    packed_all = gather_all(grid, quarter(packed), 0).reshape(total_rows, -1)
    latents_all = packed_all[:, :LATENT]
    rope_all = packed_all[:, LATENT : LATENT + ROPE]
    first_gate = LATENT + ROPE + EXP_DEV * device
    gates_own = lax.dynamic_slice_in_dim(packed_all, first_gate, EXP_DEV, axis=1).astype(
        jnp.float32
    ) + lax.dynamic_slice_in_dim(packed_all, first_gate + experts_all, EXP_DEV, axis=1).astype(
        jnp.float32
    )
    q_raw = dot(normed, query_weight)
    heads_here = q_raw.shape[1] // (NOPE + ROPE)
    q_raw = q_raw.reshape(tok_rows, heads_here, NOPE + ROPE)
    queries = low(
        jnp.concatenate([q_raw[..., :NOPE], rotate(q_raw[..., NOPE:], places)], axis=-1)
    )
    expanded = low(dot(latents_all, expand_weight)).reshape(
        total_rows, heads_here, NOPE + VDIM
    )
    key_plain, value_part = expanded[..., :NOPE], expanded[..., NOPE:]
    scores = score_block(queries, key_plain, rope_all, visible)
    peak = jnp.max(scores, axis=-1, keepdims=True)
    weights = jnp.exp(scores - peak)
    total_weight = jnp.sum(weights, axis=-1, keepdims=True)
    log_total = peak + jnp.log(total_weight)
    context = jnp.einsum(
        "hts,shv->thv", low(weights / total_weight), value_part, preferred_element_type=jnp.float32
    )
    merged = low(context).reshape(tok_rows, heads_here * VDIM)
    attn_out = tensor_scatter(grid, low(dot(merged, output_weight)), 1)
    residual = quarter(hidden_f) + attn_out
    moe_in = low(rms_scale(residual, moe_gain))
    gates_mine = jnp.swapaxes(gates_own, 0, 1)[:, :, None]
    moe_all, grad_moe_in, out_rows, gated, d_cat, shared_act, d_sg, d_su = experts_call(
        grid, moe_in, cot_all, gates_mine, expert_gate, expert_up, expert_down,
        shared_gate, shared_up, shared_down, 2,
    )
    normed_later, _ = lax.optimization_barrier((quarter(normed), moe_all[:8]))
    normed_all = lax.all_gather(normed_later, ALL, axis=0, tiled=True)
    moe_out = scatter_all(grid, out_rows, jnp.float32, 3)
    layer_out = low(residual + moe_out)
    layer_out = tensor_gather(grid, layer_out, 4)

    hidden_here = expert_gate.shape[2]
    wide = gated.shape[1] // EXP_DEV
    part_of = lambda e, first=0: slice(first + e * wide, first + e * wide + hidden_here)
    grad_expert_gate = jnp.stack([dot(moe_all.T, d_cat[:, part_of(e)]) for e in range(EXP_DEV)])
    grad_expert_up = jnp.stack(
        [dot(moe_all.T, d_cat[:, part_of(e, EXP_DEV * wide)]) for e in range(EXP_DEV)]
    )
    grad_expert_down = jnp.stack([dot(gated[:, part_of(e)].T, cot_all) for e in range(EXP_DEV)])
    grad_shared_gate = dot(moe_all.T, d_sg)
    grad_shared_up = dot(moe_all.T, d_su)
    grad_shared_down = dot(shared_act.T, cot_all)

    _, pull_moe = jax.vjp(rms_scale, residual, moe_gain)
    grad_residual, grad_moe_gain = pull_moe(grad_moe_in)
    grad_residual = grad_residual + quarter(cotangent).astype(jnp.float32)
    grad_res_low = tensor_gather(grid, low(grad_residual), 5)
    grad_output_weight = dot(merged.T, grad_res_low)
    grad_context = low(dot(grad_res_low, output_weight.T)).reshape(tok_rows, heads_here, VDIM)
    scores = score_block(queries, key_plain, rope_all, visible)
    probs = jnp.exp(scores - log_total)
    grad_probs = jnp.einsum(
        "thv,shv->hts", grad_context, value_part, preferred_element_type=jnp.float32
    )
    grad_values = jnp.einsum(
        "hts,thv->shv", low(probs), grad_context, preferred_element_type=jnp.float32
    )
    grad_scores = low(probs * (grad_probs - jnp.sum(probs * grad_probs, axis=-1, keepdims=True)))
    grad_q_plain = scale_factor * jnp.einsum(
        "hts,shc->thc", grad_scores, key_plain, preferred_element_type=jnp.float32
    )
    grad_q_rope = scale_factor * jnp.einsum(
        "hts,sr->thr", grad_scores, rope_all, preferred_element_type=jnp.float32
    )
    grad_k_plain = scale_factor * jnp.einsum(
        "hts,thc->shc", grad_scores, queries[..., :NOPE], preferred_element_type=jnp.float32
    )
    grad_k_rope = scale_factor * jnp.einsum(
        "hts,thr->sr", grad_scores, queries[..., NOPE:], preferred_element_type=jnp.float32
    )
    grad_expanded = low(
        jnp.concatenate([grad_k_plain, grad_values], axis=-1).reshape(
            total_rows, heads_here * (NOPE + VDIM)
        )
    )
    grad_expand_weight = dot(latents_all.T, grad_expanded)
    grad_keys = jnp.concatenate([dot(grad_expanded, expand_weight.T), grad_k_rope], axis=1)
    grad_keys = scatter_all(grid, pad_columns(low(grad_keys)), jnp.float32, 6, pieces=1)
    _, pull_qrope = jax.vjp(partial(rotate, places=places), q_raw[..., NOPE:])
    (grad_q_turned,) = pull_qrope(grad_q_rope)
    grad_q_low = low(
        jnp.concatenate([grad_q_plain, grad_q_turned], axis=-1).reshape(tok_rows, -1)
    )
    grad_q_all = lax.all_gather(grad_q_low, "expert", axis=0, tiled=True)
    grad_normed = tensor_scatter(grid, low(dot(grad_q_low, query_weight.T)), 7)

    places_few = quarter(places)
    compressed_few = quarter(compressed)
    _, pull_latent = jax.vjp(rms_scale, compressed_few[:, :LATENT], latent_gain)
    grad_plain_latent, grad_latent_gain = pull_latent(grad_keys[:, :LATENT])
    _, pull_krope = jax.vjp(partial(rotate, places=places_few), compressed_few[:, LATENT:])
    (grad_k_turned,) = pull_krope(grad_keys[:, LATENT : LATENT + ROPE])
    grad_comp_low = low(jnp.concatenate([grad_plain_latent, grad_k_turned], axis=-1))
    grad_comp_all = gather_all(grid, pad_columns(grad_comp_low), 8).reshape(total_rows, -1)
    grad_comp_all = grad_comp_all[:, : LATENT + ROPE]
    grad_latent_weight = dot(normed_all.T, grad_comp_all)
    grad_query_weight = dot(normed_all.T, grad_q_all)
    grad_normed = grad_normed + dot(grad_comp_low, latent_weight.T)
    _, pull_input = jax.vjp(rms_scale, quarter(hidden_f), attn_gain)
    grad_input_norm, grad_attn_gain = pull_input(grad_normed)
    grad_hidden = tensor_gather(grid, low(grad_residual + grad_input_norm), 9).astype(jnp.float32)

    gains = lax.psum(jnp.concatenate([grad_attn_gain, grad_latent_gain, grad_moe_gain]), ALL)
    grad_output_weight = lax.psum(low(grad_output_weight), "expert").astype(jnp.float32)
    grad_expand_weight = lax.psum(low(grad_expand_weight), "expert").astype(jnp.float32)
    return (
        layer_out,
        grad_hidden,
        gains[:model_width],
        grad_query_weight,
        grad_latent_weight,
        gains[model_width : model_width + LATENT],
        grad_expand_weight,
        grad_output_weight,
        gains[model_width + LATENT :],
        grad_shared_gate,
        grad_shared_up,
        grad_shared_down,
        grad_expert_gate,
        grad_expert_up,
        grad_expert_down,
    )


def solution(mesh):
    grid = Grid(mesh.shape["expert"], mesh.shape["tensor"])
    placed = (
        P("expert", None),
        P(),
        P(None, "tensor"),
        P(),
        P(),
        P(None, "tensor"),
        P("tensor", None),
        P(),
        P(None, "tensor"),
        P(None, "tensor"),
        P("tensor", None),
        P("expert", None, "tensor"),
        P("expert", None, "tensor"),
        P("expert", "tensor", None),
        P("expert", None),
        P("expert", None),
        P(),
        P("expert", None),
    )
    return jax.shard_map(
        partial(shards, grid),
        mesh=mesh,
        in_specs=placed,
        out_specs=(
            P("expert", None),
            P("expert", None),
            P(),
            P(None, "tensor"),
            P(),
            P(),
            P(None, "tensor"),
            P("tensor", None),
            P(),
            P(None, "tensor"),
            P(None, "tensor"),
            P("tensor", None),
            P("expert", None, "tensor"),
            P("expert", None, "tensor"),
            P("expert", "tensor", None),
        ),
        check_vma=False,
    )
```

```python
import functools
import math
from functools import partial

import jax
import jax.numpy as jnp
from jax import lax
from jax.experimental import pallas as pl
from jax.experimental.pallas import tpu as pltpu
from jax.sharding import PartitionSpec as P

NOPE = 128
ROPE = 64
VDIM = 128
LATENT = 512
TOP = 6
EXP_DEV = 2
ALL = ("expert", "tensor")
MESH = pl.DeviceIdType.MESH

epsilon = 1e-06
masked_out = -1e30


class Grid:
    def __init__(self, expert, tensor):
        self.na = 4 if expert % 4 == 0 else 1
        self.nb = expert // self.na
        self.ny = tensor // 2
        self.size = expert * tensor

    def here(self):
        e, t = lax.axis_index("expert"), lax.axis_index("tensor")
        return (lax.div(e, self.nb), lax.rem(e, self.nb), lax.div(t, 2), lax.rem(t, 2))

    def device(self, a, b, y, c):
        return {"expert": a * self.nb + b, "tensor": y * 2 + c}

    def block(self, a, b, y, c):
        return ((a * self.nb + b) * self.ny + y) * 2 + c


def wrap(i, n):
    return lax.rem(i, n)


def greet(grid):
    a, b, y, c = grid.here()
    barrier = pltpu.get_barrier_semaphore()
    others = (
        [grid.device(wrap(a + i, grid.na), b, y, c) for i in range(1, grid.na)]
        + [grid.device(a, wrap(b + i, grid.nb), y, c) for i in range(1, grid.nb)]
        + [grid.device(a, b, wrap(y + i, grid.ny), c) for i in range(1, grid.ny)]
        + [grid.device(a, b, y, 1 - c)]
    )
    for other in others:
        pl.semaphore_signal(barrier, inc=1, device_id=other, device_id_type=MESH)
    pl.semaphore_wait(barrier, len(others))


def gather_kernel(
    grid, x_ref, out_ref, own_sem, send_sem, recv_sem, core_send, core_recv, extra=()
):
    na, nb, ny = grid.na, grid.nb, grid.ny
    a, b, y, c = grid.here()
    half = x_ref.shape[0] // 2
    greet(grid)
    waits = []

    def dst(bb, yy, cc, aa, h):
        return out_ref.at[grid.block(aa, bb, yy, cc), pl.ds(h * half, half)]

    def slot(bb, yy, aa, h):
        return ((bb * ny + yy) * na + aa) * 2 + h

    def push(src, bb, yy, aa, h, where, kind):
        copy = pltpu.make_async_remote_copy(
            src_ref=src,
            dst_ref=dst(bb, yy, c, aa, h),
            send_sem=core_send.at[slot(bb, yy, aa, h)] if kind == "c" else send_sem.at[len(waits)],
            recv_sem=(core_recv if kind == "c" else recv_sem).at[slot(bb, yy, aa, h)],
            device_id=where,
            device_id_type=MESH,
        )
        copy.start()
        if kind != "c":
            waits.append(copy)
        else:
            core_waits.append(copy)

    core_waits = []

    def onward(src, bb, yy, aa, h, dims):
        for d in dims:
            if d == "a":
                for i in range(1, na):
                    push(src, bb, yy, aa, h, grid.device(wrap(a + i, na), b, y, c), d)
            if d == "b":
                for i in range(1, nb):
                    push(src, bb, yy, aa, h, grid.device(a, wrap(b + i, nb), y, c), d)
            if d == "y":
                for i in range(1, ny):
                    push(src, bb, yy, aa, h, grid.device(a, b, wrap(y + i, ny), c), d)
        push(src, bb, yy, aa, h, grid.device(a, b, y, 1 - c), "c")

    def landed(bb, yy, cc, aa, h, sem):
        ref = dst(bb, yy, cc, aa, h)
        pltpu.make_async_copy(ref, ref, sem.at[slot(bb, yy, aa, h)]).wait()
        return ref

    own = pltpu.make_async_copy(x_ref, out_ref.at[grid.block(a, b, y, c)], own_sem)
    own.start()
    orders = (("b", "y"), ("y", "b"))
    for h in range(2):
        onward(x_ref.at[pl.ds(h * half, half)], b, y, a, h, ("a",) + orders[h])
    for one in extra:
        one.start()
    for i in range(1, na):
        aa = wrap(a + na - i, na)
        for h in range(2):
            onward(landed(b, y, c, aa, h, recv_sem), b, y, aa, h, orders[h])
    for i in range(na):
        aa = wrap(a + na - i, na)
        for h in range(2):
            n1 = (nb, ny)[h]
            for j in range(1, n1):
                bb, yy = (wrap(b + nb - j, nb), y) if h == 0 else (b, wrap(y + ny - j, ny))
                onward(landed(bb, yy, c, aa, h, recv_sem), bb, yy, aa, h, orders[h][1:])
    for i in range(na):
        aa = wrap(a + na - i, na)
        for h in range(2):
            for j in range(nb):
                for k in range(1, ny):
                    if h == 0:
                        bb, yy = wrap(b + nb - j, nb), wrap(y + ny - k, ny)
                        onward(landed(bb, yy, c, aa, h, recv_sem), bb, yy, aa, h, ())
            for j in range(ny):
                for k in range(1, nb):
                    if h == 1:
                        bb, yy = wrap(b + nb - k, nb), wrap(y + ny - j, ny)
                        onward(landed(bb, yy, c, aa, h, recv_sem), bb, yy, aa, h, ())
    for i in range(1, na):
        for one in extra:
            one.middle(i)
    for j in range(nb):
        for k in range(ny):
            for i in range(na):
                for h in range(2):
                    landed(wrap(b + nb - j, nb), wrap(y + ny - k, ny), 1 - c, wrap(a + na - i, na), h, core_recv)
    own.wait()
    for copy in waits + core_waits:
        copy.wait_send()
    for one in extra:
        one.last()


def gather_sends(grid):
    na, nb, ny = grid.na, grid.nb, grid.ny
    return 2 * (na - 1 + na * (nb - 1) + na * (ny - 1) + na * (nb - 1) * (ny - 1))


def gather_all(grid, x, collective_id):
    r, n = x.shape
    blocks = grid.na * grid.nb * grid.ny
    return pl.pallas_call(
        functools.partial(gather_kernel, grid),
        out_shape=jax.ShapeDtypeStruct((grid.size, r, n), x.dtype),
        in_specs=[pl.BlockSpec(memory_space=pl.ANY)],
        out_specs=pl.BlockSpec(memory_space=pl.ANY),
        scratch_shapes=[
            pltpu.SemaphoreType.DMA,
            pltpu.SemaphoreType.DMA((gather_sends(grid),)),
            pltpu.SemaphoreType.DMA((2 * blocks,)),
            pltpu.SemaphoreType.DMA((2 * blocks,)),
            pltpu.SemaphoreType.DMA((2 * blocks,)),
        ],
        compiler_params=pltpu.CompilerParams(collective_id=collective_id, has_side_effects=True),
    )(x)


def scatter_kernel(grid, pieces, p_ref, out_ref, acc, core_in, d1_in0, d1_in1, d2_in0, d2_in1, a_in,
                   load_sem, core_s, core_r, s10, r10, s11, r11, s20, r20, s21, r21, sa, ra):
    na, nb, ny = grid.na, grid.nb, grid.ny
    a, b, y, c = grid.here()
    half = p_ref.shape[4] // 2
    width = p_ref.shape[5] // pieces
    greet(grid)
    pending = []

    def send(src, dst, ss, rs, where):
        copy = pltpu.make_async_remote_copy(src_ref=src, dst_ref=dst, send_sem=ss, recv_sem=rs, device_id=where, device_id_type=MESH)
        copy.start()
        pending.append(copy)

    def await_in(ref, sem):
        pltpu.make_async_copy(ref, ref, sem).wait()

    def add(dst, src):
        dst[...] = (dst[...].astype(jnp.float32) + src[...].astype(jnp.float32)).astype(dst.dtype)

    def cols(p):
        return pl.ds(p * width, width)

    spots = [(j, k) for j in reversed(range(nb)) for k in reversed(range(ny))]
    loads = {}
    for p in range(pieces):
        for n, (j, k) in enumerate(spots):
            bb, yy = wrap(b + j, nb), wrap(y + k, ny)
            send(p_ref.at[:, bb, yy, 1 - c, :, cols(p)], core_in.at[p, j, k], core_s.at[p, n], core_r.at[p, n],
                 grid.device(a, b, y, 1 - c))
            load = pltpu.make_async_copy(p_ref.at[:, bb, yy, c, :, cols(p)], acc.at[p, j, k], load_sem.at[p, n])
            load.start()
            loads[p, n] = load
    rows = (pl.ds(0, half), pl.ds(half, half))
    for p in range(pieces):
        for n, (j, k) in enumerate(spots):
            loads[p, n].wait()
            await_in(core_in.at[p, j, k], core_r.at[p, n])
            for i in range(na):
                add(acc.at[p, j, k, i], core_in.at[p, j, k, i])
            if k:
                send(acc.at[p, j, k, :, rows[0]], d1_in0.at[p, j, k - 1], s10.at[p, j, k - 1], r10.at[p, j, k - 1],
                     grid.device(a, b, wrap(y + k, ny), c))
            if j:
                send(acc.at[p, j, k, :, rows[1]], d1_in1.at[p, k, j - 1], s11.at[p, k, j - 1], r11.at[p, k, j - 1],
                     grid.device(a, wrap(b + j, nb), y, c))
    for p in range(pieces):
        for j in reversed(range(nb)):
            for k in range(1, ny):
                await_in(d1_in0.at[p, j, k - 1], r10.at[p, j, k - 1])
                for i in range(na):
                    add(acc.at[p, j, 0, i, rows[0]], d1_in0.at[p, j, k - 1, i])
            if j:
                send(acc.at[p, j, 0, :, rows[0]], d2_in0.at[p, j - 1], s20.at[p, j - 1], r20.at[p, j - 1],
                     grid.device(a, wrap(b + j, nb), y, c))
        for k in reversed(range(ny)):
            for j in range(1, nb):
                await_in(d1_in1.at[p, k, j - 1], r11.at[p, k, j - 1])
                for i in range(na):
                    add(acc.at[p, 0, k, i, rows[1]], d1_in1.at[p, k, j - 1, i])
            if k:
                send(acc.at[p, 0, k, :, rows[1]], d2_in1.at[p, k - 1], s21.at[p, k - 1], r21.at[p, k - 1],
                     grid.device(a, b, wrap(y + k, ny), c))
    for p in range(pieces):
        for j in range(1, nb):
            await_in(d2_in0.at[p, j - 1], r20.at[p, j - 1])
            for i in range(na):
                add(acc.at[p, 0, 0, i, rows[0]], d2_in0.at[p, j - 1, i])
        for k in range(1, ny):
            await_in(d2_in1.at[p, k - 1], r21.at[p, k - 1])
            for i in range(na):
                add(acc.at[p, 0, 0, i, rows[1]], d2_in1.at[p, k - 1, i])
        for i in range(1, na):
            aa = wrap(a + i, na)
            send(acc.at[p, 0, 0, aa], a_in.at[p, i - 1], sa.at[p, i - 1], ra.at[p, i - 1], grid.device(aa, b, y, c))
    for p in range(pieces):
        total = acc[p, 0, 0, a].astype(jnp.float32)
        for i in range(1, na):
            await_in(a_in.at[p, i - 1], ra.at[p, i - 1])
            total = total + a_in[p, i - 1].astype(jnp.float32)
        out_ref[:, cols(p)] = total.astype(out_ref.dtype)
    for copy in pending:
        copy.wait_send()


def scatter_all(grid, p, dtype, collective_id, pieces=2):
    r, n = p.shape[0] // grid.size, p.shape[1]
    na, nb, ny = grid.na, grid.nb, grid.ny
    half, width = r // 2, n // pieces
    sems = lambda *s: pltpu.SemaphoreType.DMA(s)
    vm = lambda *s: pltpu.VMEM(s, jnp.bfloat16)
    return pl.pallas_call(
        functools.partial(scatter_kernel, grid, pieces),
        out_shape=jax.ShapeDtypeStruct((r, n), dtype),
        in_specs=[pl.BlockSpec(memory_space=pl.ANY)],
        out_specs=pl.BlockSpec(memory_space=pltpu.VMEM),
        scratch_shapes=[
            vm(pieces, nb, ny, na, r, width),
            vm(pieces, nb, ny, na, r, width),
            vm(pieces, nb, ny - 1, na, half, width),
            vm(pieces, ny, nb - 1, na, half, width),
            vm(pieces, nb - 1, na, half, width),
            vm(pieces, ny - 1, na, half, width),
            vm(pieces, na - 1, r, width),
            sems(pieces, nb * ny), sems(pieces, nb * ny), sems(pieces, nb * ny),
            sems(pieces, nb, ny - 1), sems(pieces, nb, ny - 1),
            sems(pieces, ny, nb - 1), sems(pieces, ny, nb - 1),
            sems(pieces, nb - 1), sems(pieces, nb - 1),
            sems(pieces, ny - 1), sems(pieces, ny - 1),
            sems(pieces, na - 1), sems(pieces, na - 1),
        ],
        compiler_params=pltpu.CompilerParams(collective_id=collective_id, has_side_effects=True, vmem_limit_bytes=40 << 20),
    )(p.reshape(na, nb, ny, 2, r, n))


def greet_tensor(grid):
    a, b, y, c = grid.here()
    barrier = pltpu.get_barrier_semaphore()
    others = [grid.device(a, b, wrap(y + i, grid.ny), c) for i in range(1, grid.ny)]
    others.append(grid.device(a, b, y, 1 - c))
    for other in others:
        pl.semaphore_signal(barrier, inc=1, device_id=other, device_id_type=MESH)
    pl.semaphore_wait(barrier, len(others))


def tensor_scatter_kernel(grid, p_ref, out_ref, acc, core_in, y_in, core_s, core_r, ys, yr):
    ny = grid.ny
    a, b, y, c = grid.here()
    greet_tensor(grid)
    pending = []
    for k in reversed(range(ny)):
        copy = pltpu.make_async_remote_copy(
            src_ref=p_ref.at[wrap(y + k, ny), 1 - c], dst_ref=core_in.at[k], send_sem=core_s.at[k], recv_sem=core_r.at[k],
            device_id=grid.device(a, b, y, 1 - c), device_id_type=MESH,
        )
        copy.start()
        pending.append(copy)
    for k in reversed(range(ny)):
        pltpu.make_async_copy(core_in.at[k], core_in.at[k], core_r.at[k]).wait()
        total = p_ref[wrap(y + k, ny), c].astype(jnp.float32) + core_in[k].astype(jnp.float32)
        if k:
            acc[k - 1] = total.astype(acc.dtype)
            copy = pltpu.make_async_remote_copy(
                src_ref=acc.at[k - 1], dst_ref=y_in.at[k - 1], send_sem=ys.at[k - 1], recv_sem=yr.at[k - 1],
                device_id=grid.device(a, b, wrap(y + k, ny), c), device_id_type=MESH,
            )
            copy.start()
            pending.append(copy)
        else:
            out_ref[...] = total
    for k in range(1, ny):
        pltpu.make_async_copy(y_in.at[k - 1], y_in.at[k - 1], yr.at[k - 1]).wait()
        out_ref[...] += y_in[k - 1].astype(jnp.float32)
    for copy in pending:
        copy.wait_send()


def tensor_scatter(grid, p, collective_id):
    ny = grid.ny
    r, n = p.shape[0] // (2 * ny), p.shape[1]
    return pl.pallas_call(
        functools.partial(tensor_scatter_kernel, grid),
        out_shape=jax.ShapeDtypeStruct((r, n), jnp.float32),
        in_specs=[pl.BlockSpec(memory_space=pltpu.VMEM)],
        out_specs=pl.BlockSpec(memory_space=pltpu.VMEM),
        scratch_shapes=[
            pltpu.VMEM((max(ny - 1, 1), r, n), p.dtype),
            pltpu.VMEM((ny, r, n), p.dtype),
            pltpu.VMEM((max(ny - 1, 1), r, n), p.dtype),
            pltpu.SemaphoreType.DMA((ny,)),
            pltpu.SemaphoreType.DMA((ny,)),
            pltpu.SemaphoreType.DMA((max(ny - 1, 1),)),
            pltpu.SemaphoreType.DMA((max(ny - 1, 1),)),
        ],
        compiler_params=pltpu.CompilerParams(
            collective_id=collective_id, has_side_effects=True, vmem_limit_bytes=16 << 20
        ),
    )(p.reshape(ny, 2, r, n))


def tensor_gather_kernel(grid, x_ref, out_ref, own_sem, ys, yr, core_s, core_r):
    ny = grid.ny
    a, b, y, c = grid.here()
    greet_tensor(grid)
    own = pltpu.make_async_copy(x_ref, out_ref.at[y, c], own_sem)
    own.start()
    pending = []

    def push(src, spot, ss, rs, where):
        copy = pltpu.make_async_remote_copy(
            src_ref=src, dst_ref=out_ref.at[spot, c], send_sem=ss, recv_sem=rs, device_id=where, device_id_type=MESH
        )
        copy.start()
        pending.append(copy)

    for k in range(1, ny):
        push(x_ref, y, ys.at[k], yr.at[k], grid.device(a, b, wrap(y + k, ny), c))
    push(x_ref, y, core_s.at[0], core_r.at[0], grid.device(a, b, y, 1 - c))
    for k in range(1, ny):
        spot = wrap(y + ny - k, ny)
        ref = out_ref.at[spot, c]
        pltpu.make_async_copy(ref, ref, yr.at[k]).wait()
        push(ref, spot, core_s.at[k], core_r.at[k], grid.device(a, b, y, 1 - c))
    for k in range(ny):
        ref = out_ref.at[wrap(y + ny - k, ny), 1 - c]
        pltpu.make_async_copy(ref, ref, core_r.at[k]).wait()
    own.wait()
    for copy in pending:
        copy.wait_send()


def tensor_gather(grid, x, collective_id):
    ny = grid.ny
    r, n = x.shape
    out = pl.pallas_call(
        functools.partial(tensor_gather_kernel, grid),
        out_shape=jax.ShapeDtypeStruct((ny, 2, r, n), x.dtype),
        in_specs=[pl.BlockSpec(memory_space=pltpu.VMEM)],
        out_specs=pl.BlockSpec(memory_space=pltpu.VMEM),
        scratch_shapes=[pltpu.SemaphoreType.DMA] + [pltpu.SemaphoreType.DMA((ny,))] * 4,
        compiler_params=pltpu.CompilerParams(
            collective_id=collective_id, has_side_effects=True, vmem_limit_bytes=16 << 20
        ),
    )(x)
    return out.reshape(2 * ny * r, n)


def dot_rows(left_side, right_side):
    return lax.dot_general(
        left_side, right_side, (((1,), (1,)), ((), ())), preferred_element_type=jnp.float32
    )


def dot_plain(left_side, right_side):
    return jnp.dot(left_side, right_side, preferred_element_type=jnp.float32)


def round_up(value, unit):
    return -(-value // unit) * unit


def experts_kernel(
    grid,
    pieces,
    x_ref,
    dz_ref,
    gate_ref,
    eg_hbm,
    eu_hbm,
    ed_hbm,
    sg_hbm,
    su_hbm,
    sd_hbm,
    all_ref,
    grad_ref,
    y_ref,
    acts_ref,
    gates,
    egu,
    ed,
    sgu,
    sd,
    dabuf,
    xbuf,
    dzbuf,
    gated,
    dcat,
    act,
    dsh,
    ybuf,
    dx,
    dx_out,
    core_in,
    d1_in0,
    d1_in1,
    d2_in0,
    d2_in1,
    a_in,
    gate_sem,
    weight_sem,
    own_sem,
    x_sem,
    dz_sem,
    out_sem,
    fill_sem,
    send_sem,
    recv_sem,
    share_send,
    share_recv,
    core_s,
    core_r,
    s10,
    r10,
    s11,
    r11,
    s20,
    r20,
    s21,
    r21,
    sa,
    ra,
):
    na, nb, ny = grid.na, grid.nb, grid.ny
    a, b, y, c = grid.here()
    r, n = x_ref.shape
    half, width, rows = r // 2, n // pieces, na * r
    pairs = nb * ny
    steps = 2 * pairs
    device = a * nb + b
    f, fs = ed_hbm.shape[1], sd_hbm.shape[0]
    wide, wide_s = egu.shape[0] // (2 * EXP_DEV), sd.shape[0]
    ef = EXP_DEV * wide
    columns = columns_of(ef, wide_s)
    f32, bf = jnp.float32, jnp.bfloat16
    fills = [(ed_hbm.at[e], ed, e * wide, f, wide) for e in range(EXP_DEV)]
    fills += [(sd_hbm, sd, 0, fs, wide_s)]
    fills += [(eg_hbm.at[e], egu, e * wide, f, wide) for e in range(EXP_DEV)]
    fills += [(eu_hbm.at[e], egu, ef + e * wide, f, wide) for e in range(EXP_DEV)]
    fills += [(sg_hbm, sgu, 0, fs, wide_s), (su_hbm, sgu, wide_s, fs, wide_s)]
    loads = [
        pltpu.make_async_copy(src, dst.at[pl.ds(at, real)], weight_sem.at[i])
        for i, (src, dst, at, real, _) in enumerate(fills)
    ]
    for load in loads:
        load.start()
    gate_load = pltpu.make_async_copy(gate_ref.at[:, :, :, :, :, pl.ds(LATENT, 128)], gates, gate_sem)
    gate_load.start()
    greet(grid)

    counts = [0]

    def place(bb, yy, cc, aa, h):
        return all_ref.at[aa, bb, yy, cc, pl.ds(h * half, half)]

    def slot(bb, yy, aa, h):
        return ((bb * ny + yy) * na + aa) * 2 + h

    def push(src, bb, yy, aa, h, where, send, recv):
        pltpu.make_async_remote_copy(
            src_ref=src,
            dst_ref=place(bb, yy, c, aa, h),
            send_sem=send,
            recv_sem=recv.at[slot(bb, yy, aa, h)],
            device_id=where,
            device_id_type=MESH,
        ).start()

    def line(i):
        if na != 4:
            return wrap(a + i, na)
        if i == 0:
            return a
        if i == 1:
            return a + 1 - 2 * lax.rem(a, 2)
        return (i - lax.div(a, 2)) if i == 2 else (3 - 3 * lax.div(a, 2))

    def onward(src, bb, yy, aa, h, dims):
        for d in dims:
            size = {"a": na, "b": nb, "y": ny}[d]
            for i in range(1, size):
                where = {
                    "a": lambda: grid.device(line(i), b, y, c),
                    "b": lambda: grid.device(a, wrap(b + i, nb), y, c),
                    "y": lambda: grid.device(a, b, wrap(y + i, ny), c),
                }[d]()
                push(src, bb, yy, aa, h, where, send_sem.at[counts[0]], recv_sem)
                counts[0] += 1
        push(
            src, bb, yy, aa, h, grid.device(a, b, y, 1 - c), share_send.at[slot(bb, yy, aa, h)], share_recv
        )

    def landed(bb, yy, cc, aa, h, sem):
        ref = place(bb, yy, cc, aa, h)
        pltpu.make_async_copy(ref, ref, sem.at[slot(bb, yy, aa, h)]).wait()
        return ref

    orders = (("b", "y"), ("y", "b"))

    def relay(j, k, i, h, dims):
        bb, yy, aa = wrap(b + j, nb), wrap(y + k, ny), line(i)
        onward(landed(bb, yy, c, aa, h, recv_sem), bb, yy, aa, h, dims)

    own = pltpu.make_async_copy(x_ref, all_ref.at[a, b, y, c], own_sem)
    own.start()
    for h in range(2):
        onward(x_ref.at[pl.ds(h * half, half)], b, y, a, h, ("a",) + orders[h])

    hooks = {}
    early = []
    for i in range(na):
        if i:
            early += [(0, 0, i, h, orders[h]) for h in range(2)]
        if i:
            early += [(j, 0, i - 1, 0, orders[0][1:]) for j in range(1, nb)]
            early += [(0, k, i - 1, 1, orders[1][1:]) for k in range(1, ny)]
    early += [(j, 0, na - 1, 0, orders[0][1:]) for j in range(1, nb)]
    early += [(0, k, na - 1, 1, orders[1][1:]) for k in range(1, ny)]
    for m, event in enumerate(early):
        place_at = 1 + m * (2 * steps - 1) // len(early)
        hooks.setdefault(("early", place_at // 2, place_at % 2), []).append(event)
    for pair in range(1, pairs):
        j, k = pair // ny, pair % ny
        late = [(j, k, i, h, ()) for i in range(na) for h in range(2) if (k if h == 0 else j)]
        for m, event in enumerate(late):
            hooks.setdefault(("main", pair, m * 3 // len(late)), []).append(event)

    def hook(stage, step, spot):
        for (when_stage, when, when_spot), events in hooks.items():
            if when_stage == stage and when_spot == spot:

                @pl.when(step == when)
                def _():
                    for event in events:
                        relay(*event)

    def spots(step):
        pair, l = lax.div(step, 2), 1 - lax.rem(step, 2)
        j, k = lax.div(pair, ny), lax.rem(pair, ny)
        return j, k, l, wrap(b + j, nb), wrap(y + k, ny), wrap(c + l, 2)

    def flat(value):
        return value.reshape(rows, value.shape[-1])

    def fold(value):
        return value.reshape(na, r, value.shape[-1])

    def dz_load(step):
        _, _, _, bb, yy, cc = spots(step)
        s = lax.rem(step, 2)
        return pltpu.make_async_copy(dz_ref.at[:, bb, yy, cc], dzbuf.at[s], dz_sem.at[s])

    dz_load(a * 0).start()
    for _, dst, at, real, padded in fills:
        if padded > real:
            dst[at + real : at + padded] = jnp.zeros((padded - real, n), bf)
    for load in loads[: EXP_DEV + 1]:
        load.wait()

    def early_body(step, carry):
        s = lax.rem(step, 2)

        @pl.when(step + 1 < steps)
        def _():
            dz_load(step + 1).start()

        dz_load(step).wait()
        dz = flat(dzbuf[s])
        dabuf[step, :, :ef] = dot_rows(dz, ed[...]).astype(bf)
        hook("early", step, 0)
        dabuf[step, :, ef:] = dot_rows(dz, sd[...]).astype(bf)
        hook("early", step, 1)
        return carry

    lax.fori_loop(0, steps, early_body, 0)
    for load in loads[EXP_DEV + 1 :]:
        load.wait()
    own.wait()
    gate_load.wait()

    def x_load(step):
        _, _, _, bb, yy, cc = spots(step)
        return pltpu.make_async_copy(all_ref.at[:, bb, yy, cc], xbuf.at[0], x_sem.at[0])

    def stores(step):
        _, _, _, bb, yy, cc = spots(step)
        s = lax.rem(step, 2)
        return [
            pltpu.make_async_copy(
                gated.at[s], acts_ref.at[:, bb, yy, cc, :, pl.ds(columns[2], ef)], out_sem.at[s, 0]
            ),
            pltpu.make_async_copy(
                dcat.at[s], acts_ref.at[:, bb, yy, cc, :, pl.ds(columns[0], 2 * ef)], out_sem.at[s, 1]
            ),
        ]

    def remote(src, dst, ss, rs, where):
        return pltpu.make_async_remote_copy(
            src_ref=src, dst_ref=dst, send_sem=ss, recv_sem=rs, device_id=where, device_id_type=MESH
        )

    def cols(p):
        return pl.ds(p * width, width)

    upper = (pl.ds(0, half), pl.ds(half, half))

    def send_core(pair):
        j, k = lax.div(pair, ny), lax.rem(pair, ny)
        return remote(
            dx_out.at[lax.rem(pair, 2)], core_in.at[j, k], core_s.at[lax.rem(pair, 2)],
            core_r.at[j, k], grid.device(a, b, y, 1 - c),
        )

    def send_10(p, j, k):
        return remote(
            dx.at[j, k, :, upper[0], cols(p)], d1_in0.at[p, j, k - 1], s10.at[p, j, k - 1],
            r10.at[p, j, k - 1], grid.device(a, b, wrap(y + k, ny), c),
        )

    def send_11(p, j, k):
        return remote(
            dx.at[j, k, :, upper[1], cols(p)], d1_in1.at[p, k, j - 1], s11.at[p, k, j - 1],
            r11.at[p, k, j - 1], grid.device(a, wrap(b + j, nb), y, c),
        )

    def await_in(ref, sem):
        pltpu.make_async_copy(ref, ref, sem).wait()

    def add(dst, src):
        dst[...] = (dst[...].astype(f32) + src[...].astype(f32)).astype(dst.dtype)

    def shared_front(step, x, s):
        g = dot_rows(x, sgu[:wide_s])
        u = dot_rows(x, sgu[wide_s:])
        d = dabuf[step, :, ef:].astype(f32)
        sig = 1.0 / (1.0 + jnp.exp(-g))
        swish = g * sig
        act[s] = fold((swish * u).astype(bf))
        dsh[s, :, :, :wide_s] = fold((d * u * (sig + swish * (1.0 - sig))).astype(bf))
        dsh[s, :, :, wide_s:] = fold((d * swish).astype(bf))

    def is_mine(bb, yy, cc):
        return lax.rem((bb * ny + yy) * 2 + cc, na * nb) == device

    chunk = min(n, 1024)

    def main_body(step, carry):
        j, k, l, bb, yy, cc = spots(step)
        s = lax.rem(step, 2)

        @pl.when(l == 1)
        def _():
            for i in range(na):
                for h in range(2):
                    landed(bb, yy, cc, line(i), h, share_recv)

        x_load(step).start()

        @pl.when(step >= 2)
        def _():
            for store in stores(step - 2):
                store.wait()

        x_load(step).wait()
        x = flat(xbuf[0])
        g = dot_rows(x, egu[:ef])
        u = dot_rows(x, egu[ef:])
        gate = flat(gates[:, bb, yy, cc]).astype(f32)
        lane = lax.broadcasted_iota(jnp.int32, gate.shape, 1) - (ROPE + EXP_DEV * device)
        experts_all = EXP_DEV * na * nb
        for e in range(EXP_DEV):
            at = pl.ds(e * wide, wide)
            hit = (lane == e) | (lane == e + experts_all)
            scale = jnp.sum(jnp.where(hit, gate, 0.0), axis=-1, keepdims=True)
            ge, ue = g[:, e * wide : (e + 1) * wide], u[:, e * wide : (e + 1) * wide]
            d = dabuf[step, :, at].astype(f32) * scale
            sig = 1.0 / (1.0 + jnp.exp(-ge))
            swish = ge * sig
            gated[s, :, :, at] = fold((scale * (swish * ue)).astype(bf))
            dcat[s, :, :, at] = fold((d * ue * (sig + swish * (1.0 - sig))).astype(bf))
            dcat[s, :, :, pl.ds(ef + e * wide, wide)] = fold((d * swish).astype(bf))
        hook("main", step, 0)
        mine = is_mine(bb, yy, cc)

        @pl.when(mine)
        def _():
            shared_front(step, x, 0)

        hook("main", step, 1)

        def column(target):
            for q in range(n // chunk):
                at = pl.ds(q * chunk, chunk)
                total = dot_plain(flat(dcat[s]), egu[:, at])
                target[:, :, at] = fold(total.astype(bf))

            @pl.when(mine)
            def _():
                for q in range(n // chunk):
                    at = pl.ds(q * chunk, chunk)
                    more = dot_plain(flat(dsh[0]), sgu[:, at])
                    target[:, :, at] = fold((flat(target[:, :, at]).astype(f32) + more).astype(bf))

        for store in stores(step):
            store.start()

        @pl.when(l == 1)
        def _():
            pair = lax.div(step, 2)

            @pl.when(pair >= 2)
            def _():
                send_core(pair - 2).wait_send()

            column(dx_out.at[lax.rem(pair, 2)])
            send_core(pair).start()

        @pl.when(l == 0)
        def _():
            column(dx.at[j, k])
            await_in(core_in.at[j, k], core_r.at[j, k])

            def one(i, carry):
                add(dx.at[j, k, i], core_in.at[j, k, i])
                return carry

            lax.fori_loop(0, na, one, 0)

            @pl.when(k > 0)
            def _():
                for p in range(pieces):
                    send_10(p, j, k).start()

            @pl.when(j > 0)
            def _():
                for p in range(pieces):
                    send_11(p, j, k).start()

        hook("main", step, 2)
        return carry

    lax.fori_loop(0, steps, main_body, 0)
    for step in (steps - 2, steps - 1):
        for store in stores(a * 0 + step):
            store.wait()

    def send_20(p, j):
        return remote(
            dx.at[j, 0, :, upper[0], cols(p)], d2_in0.at[p, j - 1], s20.at[p, j - 1],
            r20.at[p, j - 1], grid.device(a, wrap(b + j, nb), y, c),
        )

    def send_21(p, k):
        return remote(
            dx.at[0, k, :, upper[1], cols(p)], d2_in1.at[p, k - 1], s21.at[p, k - 1],
            r21.at[p, k - 1], grid.device(a, b, wrap(y + k, ny), c),
        )

    def send_a(p, i):
        return remote(
            dx.at[0, 0, wrap(a + i, na), :, cols(p)], a_in.at[p, i - 1], sa.at[p, i - 1],
            ra.at[p, i - 1], grid.device(wrap(a + i, na), b, y, c),
        )

    def sum_first(p):
        for j in reversed(range(nb)):
            for k in range(1, ny):
                await_in(d1_in0.at[p, j, k - 1], r10.at[p, j, k - 1])
                for i in range(na):
                    add(dx.at[j, 0, i, upper[0], cols(p)], d1_in0.at[p, j, k - 1, i])
            if j:
                send_20(p, j).start()
        for k in reversed(range(ny)):
            for j in range(1, nb):
                await_in(d1_in1.at[p, k, j - 1], r11.at[p, k, j - 1])
                for i in range(na):
                    add(dx.at[0, k, i, upper[1], cols(p)], d1_in1.at[p, k, j - 1, i])
            if k:
                send_21(p, k).start()

    def sum_second(p):
        for j in range(1, nb):
            await_in(d2_in0.at[p, j - 1], r20.at[p, j - 1])
            for i in range(na):
                add(dx.at[0, 0, i, upper[0], cols(p)], d2_in0.at[p, j - 1, i])
        for k in range(1, ny):
            await_in(d2_in1.at[p, k - 1], r21.at[p, k - 1])
            for i in range(na):
                add(dx.at[0, 0, i, upper[1], cols(p)], d2_in1.at[p, k - 1, i])
        for i in range(1, na):
            send_a(p, i).start()

    def sum_last(p):
        total = dx[0, 0, a, :, cols(p)].astype(f32)
        for i in range(1, na):
            await_in(a_in.at[p, i - 1], ra.at[p, i - 1])
            total = total + a_in[p, i - 1].astype(f32)
        grad_ref[:, cols(p)] = total

    work = [(sum_first, p) for p in range(pieces)] + [(sum_second, p) for p in range(pieces)]
    turns = {}
    for m, item in enumerate(work):
        turns.setdefault(min(steps - 1, 1 + m * (steps - 1) // len(work)), []).append(item)

    def fill_loads(step):
        _, _, _, bb, yy, cc = spots(step)
        s = lax.rem(step, 2)
        return [
            pltpu.make_async_copy(all_ref.at[:, bb, yy, cc], xbuf.at[s], x_sem.at[s]),
            pltpu.make_async_copy(
                acts_ref.at[:, bb, yy, cc, :, pl.ds(columns[2], ef)], gated.at[s], fill_sem.at[s]
            ),
        ]

    def fill_stores(step):
        _, _, _, bb, yy, cc = spots(step)
        s = lax.rem(step, 2)
        pairs_of = [
            (act.at[s], acts_ref.at[:, bb, yy, cc, :, pl.ds(columns[3], wide_s)]),
            (dsh.at[s], acts_ref.at[:, bb, yy, cc, :, pl.ds(columns[1], 2 * wide_s)]),
            (ybuf.at[s], y_ref.at[:, bb, yy, cc]),
        ]
        return [
            pltpu.make_async_copy(src, dst, out_sem.at[s, i])
            for i, (src, dst) in enumerate(pairs_of)
        ]

    for load in fill_loads(a * 0):
        load.start()

    def fill_body(step, carry):
        j, k, l, bb, yy, cc = spots(step)
        s = lax.rem(step, 2)

        @pl.when(step + 1 < steps)
        def _():
            for load in fill_loads(step + 1):
                load.start()

        @pl.when(step >= 2)
        def _():
            for store in fill_stores(step - 2):
                store.wait()

        for load in fill_loads(step):
            load.wait()
        x = flat(xbuf[s])
        shared_front(step, x, s)
        for q in range(n // chunk):
            at = pl.ds(q * chunk, chunk)
            ybuf[s, :, :, at] = fold(dot_plain(flat(gated[s]), ed[:, at]).astype(bf))

        @pl.when(is_mine(bb, yy, cc))
        def _():
            for q in range(n // chunk):
                at = pl.ds(q * chunk, chunk)
                more = dot_plain(flat(act[s]), sd[:, at])
                ybuf[s, :, :, at] = fold((flat(ybuf[s, :, :, at]).astype(f32) + more).astype(bf))

        for store in fill_stores(step):
            store.start()
        for when, items in turns.items():

            @pl.when(step == when)
            def _():
                for item, p in items:
                    item(p)

        return carry

    lax.fori_loop(0, steps, fill_body, 0)
    for p in range(pieces):
        sum_last(p)

    for step in (steps - 2, steps - 1):
        for store in fill_stores(a * 0 + step):
            store.wait()
    some = place(b, y, c, a, 0)
    for i in range(counts[0]):
        pltpu.make_async_copy(some, some, send_sem.at[i]).wait()
    for i in range(2 * na * pairs):
        pltpu.make_async_copy(some, some, share_send.at[i]).wait()
    for pair in range(max(0, pairs - 2), pairs):
        send_core(a * 0 + pair).wait_send()
    for p in range(pieces):
        for j in range(nb):
            for k in range(ny):
                if k:
                    send_10(p, j, k).wait_send()
                if j:
                    send_11(p, j, k).wait_send()
        for j in range(1, nb):
            send_20(p, j).wait_send()
        for k in range(1, ny):
            send_21(p, k).wait_send()
        for i in range(1, na):
            send_a(p, i).wait_send()


def columns_of(ef, wide_s):
    return (0, 2 * ef, 2 * ef + 2 * wide_s, 3 * ef + 2 * wide_s, 3 * ef + 3 * wide_s)


def experts_call(
    grid, x, dz, gates, expert_gate, expert_up, expert_down, shared_gate, shared_up, shared_down,
    collective_id, pieces=2,
):
    r, n = x.shape
    na, nb, ny = grid.na, grid.nb, grid.ny
    f, fs = expert_down.shape[1], shared_down.shape[0]
    wide, wide_s = round_up(f, 128), round_up(fs, 128)
    ef = EXP_DEV * wide
    half, width, rows = r // 2, n // pieces, na * r
    steps = 2 * nb * ny
    lay = (na, nb, ny, 2, r)
    bf = jnp.bfloat16
    sems = lambda *s: pltpu.SemaphoreType.DMA(s)
    vm = lambda *s: pltpu.VMEM(s, bf)
    sends = 2 * (na - 1 + na * (nb - 1) + na * (ny - 1) + na * (nb - 1) * (ny - 1))
    any_space = pl.BlockSpec(memory_space=pl.ANY)
    in_vmem = pl.BlockSpec(memory_space=pltpu.VMEM)
    outs = pl.pallas_call(
        functools.partial(experts_kernel, grid, pieces),
        out_shape=[
            jax.ShapeDtypeStruct(lay + (n,), bf),
            jax.ShapeDtypeStruct((r, n), jnp.float32),
            jax.ShapeDtypeStruct(lay + (n,), bf),
            jax.ShapeDtypeStruct(lay + (columns_of(ef, wide_s)[-1],), bf),
        ],
        in_specs=[any_space] * 9,
        out_specs=[any_space, in_vmem] + [any_space] * 2,
        scratch_shapes=[
            vm(*lay, 128), vm(2 * ef, n), vm(ef, n), vm(2 * wide_s, n), vm(wide_s, n),
            vm(steps, rows, ef + wide_s),
            vm(2, na, r, n), vm(2, na, r, n),
            vm(2, na, r, ef), vm(2, na, r, 2 * ef),
            vm(2, na, r, wide_s), vm(2, na, r, 2 * wide_s),
            vm(2, na, r, n),
            vm(nb, ny, na, r, n),
            vm(2, na, r, n),
            vm(nb, ny, na, r, n),
            vm(pieces, nb, ny - 1, na, half, width),
            vm(pieces, ny, nb - 1, na, half, width),
            vm(pieces, nb - 1, na, half, width),
            vm(pieces, ny - 1, na, half, width),
            vm(pieces, na - 1, r, width),
            pltpu.SemaphoreType.DMA, sems(3 * EXP_DEV + 3), pltpu.SemaphoreType.DMA, sems(2), sems(2),
            sems(2, 4), sems(2),
            sems(sends), sems(2 * na * nb * ny), sems(2 * na * nb * ny), sems(2 * na * nb * ny),
            sems(2), sems(nb, ny),
            sems(pieces, nb, ny - 1), sems(pieces, nb, ny - 1),
            sems(pieces, ny, nb - 1), sems(pieces, ny, nb - 1),
            sems(pieces, nb - 1), sems(pieces, nb - 1),
            sems(pieces, ny - 1), sems(pieces, ny - 1),
            sems(pieces, na - 1), sems(pieces, na - 1),
        ],
        compiler_params=pltpu.CompilerParams(
            collective_id=collective_id, has_side_effects=True, vmem_limit_bytes=63 << 20
        ),
    )(
        x,
        dz.reshape(lay + (n,)),
        gates.reshape(lay + (gates.shape[-1],)),
        jnp.swapaxes(expert_gate, 1, 2), jnp.swapaxes(expert_up, 1, 2), expert_down,
        shared_gate.T, shared_up.T, shared_down,
    )
    tokens = grid.size * r
    rows_all, grad, out_rows, acts = outs
    return rows_all.reshape(tokens, n), grad, out_rows.reshape(tokens, n), acts.reshape(tokens, -1)


class TensorReduce:
    count = 8

    @staticmethod
    def scratch(grid, r, width):
        ny = grid.ny
        sems = lambda *s: pltpu.SemaphoreType.DMA(s)
        vm = lambda *s: pltpu.VMEM(s, jnp.bfloat16)
        return [
            vm(ny, r, width), vm(ny, r, width), vm(ny - 1, r, width),
            sems(ny), sems(ny), sems(ny), sems(ny - 1), sems(ny - 1),
        ]

    def __init__(self, grid, source, out, scratch):
        self.grid, self.source, self.out = grid, source, out
        (
            self.acc, self.core_in, self.y_in, self.load_sem, self.core_s, self.core_r, self.ys, self.yr,
        ) = scratch
        self.spot = grid.here()

    def load(self, k):
        g, (a, b, y, c) = self.grid, self.spot
        return pltpu.make_async_copy(self.source.at[wrap(y + k, g.ny), c], self.acc.at[k], self.load_sem.at[k])

    def core_copy(self, k):
        g, (a, b, y, c) = self.grid, self.spot
        return pltpu.make_async_remote_copy(
            src_ref=self.source.at[wrap(y + k, g.ny), 1 - c], dst_ref=self.core_in.at[k],
            send_sem=self.core_s.at[k], recv_sem=self.core_r.at[k],
            device_id=g.device(a, b, y, 1 - c), device_id_type=MESH,
        )

    def y_copy(self, k):
        g, (a, b, y, c) = self.grid, self.spot
        return pltpu.make_async_remote_copy(
            src_ref=self.acc.at[k], dst_ref=self.y_in.at[k - 1], send_sem=self.ys.at[k - 1],
            recv_sem=self.yr.at[k - 1], device_id=g.device(a, b, wrap(y + k, g.ny), c), device_id_type=MESH,
        )

    def start(self):
        for k in reversed(range(self.grid.ny)):
            self.core_copy(k).start()
            self.load(k).start()

    def middle(self):
        f32 = jnp.float32
        for k in reversed(range(self.grid.ny)):
            self.load(k).wait()
            ref = self.core_in.at[k]
            pltpu.make_async_copy(ref, ref, self.core_r.at[k]).wait()
            total = self.acc[k].astype(f32) + self.core_in[k].astype(f32)
            self.acc[k] = total.astype(self.acc.dtype)
            if k:
                self.y_copy(k).start()

    def last(self):
        total = self.acc[0].astype(jnp.float32)
        for k in range(1, self.grid.ny):
            ref = self.y_in.at[k - 1]
            pltpu.make_async_copy(ref, ref, self.yr.at[k - 1]).wait()
            total = total + self.y_in[k - 1].astype(jnp.float32)
        self.out[...] = total

    def finish(self):
        for k in range(self.grid.ny):
            self.core_copy(k).wait_send()
            if k:
                self.y_copy(k).wait_send()


class TensorGather:
    count = 5

    @staticmethod
    def scratch(grid):
        return [pltpu.SemaphoreType.DMA((1,))] + [pltpu.SemaphoreType.DMA((grid.ny,))] * 4

    def __init__(self, grid, x, out, scratch):
        self.grid, self.x, self.out = grid, x, out
        self.own_sem, self.ys, self.yr, self.core_s, self.core_r = scratch
        self.spot = grid.here()

    def own(self):
        return pltpu.make_async_copy(self.x, self.out.at[self.spot[2], self.spot[3]], self.own_sem.at[0])

    def y_copy(self, k):
        g, (a, b, y, c) = self.grid, self.spot
        return pltpu.make_async_remote_copy(
            src_ref=self.x, dst_ref=self.out.at[y, c], send_sem=self.ys.at[k], recv_sem=self.yr.at[k],
            device_id=g.device(a, b, wrap(y + k, g.ny), c), device_id_type=MESH,
        )

    def core_copy(self, k):
        g, (a, b, y, c) = self.grid, self.spot
        spot = wrap(y + g.ny - k, g.ny)
        return pltpu.make_async_remote_copy(
            src_ref=self.x if k == 0 else self.out.at[spot, c], dst_ref=self.out.at[spot, c],
            send_sem=self.core_s.at[k], recv_sem=self.core_r.at[k],
            device_id=g.device(a, b, y, 1 - c), device_id_type=MESH,
        )

    def start(self):
        self.own().start()
        for k in range(1, self.grid.ny):
            self.y_copy(k).start()
        self.core_copy(0).start()

    def middle(self, i):
        if i == 1:
            for k in range(1, self.grid.ny):
                pltpu.make_async_copy(self.x, self.x, self.yr.at[k]).wait()
                self.core_copy(k).start()

    def last(self):
        self.own().wait()
        for k in range(self.grid.ny):
            pltpu.make_async_copy(self.x, self.x, self.core_r.at[k]).wait()
        for k in range(self.grid.ny):
            if k:
                self.y_copy(k).wait_send()
            self.core_copy(k).wait_send()


class PlaneReduce:
    count = 9

    @staticmethod
    def scratch(grid, r, width):
        na, nb = grid.na, grid.nb
        sems = lambda *s: pltpu.SemaphoreType.DMA(s)
        vm = lambda *s: pltpu.VMEM(s, jnp.bfloat16)
        return [
            vm(na, r, width), vm(nb - 1, na, r, width), vm(na - 1, r, width),
            sems(1), sems(nb - 1), sems(nb - 1), sems(na - 1), sems(na - 1), sems(1),
        ]

    def __init__(self, grid, source, out, scratch):
        self.grid, self.source, self.out = grid, source, out
        self.acc, self.b_in, self.a_in, self.load_sem, self.sb, self.rb, self.sa, self.ra, _ = scratch
        self.spot = grid.here()

    def load(self):
        return pltpu.make_async_copy(self.source.at[:, self.spot[1]], self.acc, self.load_sem.at[0])

    def copy_b(self, i):
        g, (a, b, y, c) = self.grid, self.spot
        return pltpu.make_async_remote_copy(
            src_ref=self.source.at[:, wrap(b + i, g.nb)], dst_ref=self.b_in.at[i - 1],
            send_sem=self.sb.at[i - 1], recv_sem=self.rb.at[i - 1],
            device_id=g.device(a, wrap(b + i, g.nb), y, c), device_id_type=MESH,
        )

    def copy_a(self, i):
        g, (a, b, y, c) = self.grid, self.spot
        return pltpu.make_async_remote_copy(
            src_ref=self.acc.at[wrap(a + i, g.na)], dst_ref=self.a_in.at[i - 1],
            send_sem=self.sa.at[i - 1], recv_sem=self.ra.at[i - 1],
            device_id=g.device(wrap(a + i, g.na), b, y, c), device_id_type=MESH,
        )

    def start(self):
        for i in range(1, self.grid.nb):
            self.copy_b(i).start()
        self.load().start()

    def middle(self):
        f32 = jnp.float32
        self.load().wait()
        for i in range(1, self.grid.nb):
            ref = self.b_in.at[i - 1]
            pltpu.make_async_copy(ref, ref, self.rb.at[i - 1]).wait()

            def one(m, carry):
                self.acc[m] = (self.acc[m].astype(f32) + ref[m].astype(f32)).astype(self.acc.dtype)
                return carry

            lax.fori_loop(0, self.grid.na, one, 0)
        for i in range(1, self.grid.na):
            self.copy_a(i).start()

    def last(self):
        total = self.acc[self.spot[0]].astype(jnp.float32)
        for i in range(1, self.grid.na):
            ref = self.a_in.at[i - 1]
            pltpu.make_async_copy(ref, ref, self.ra.at[i - 1]).wait()
            total = total + self.a_in[i - 1].astype(jnp.float32)
        self.out[...] = total.astype(self.out.dtype)

    def finish(self):
        for i in range(1, self.grid.nb):
            self.copy_b(i).wait_send()
        for i in range(1, self.grid.na):
            self.copy_a(i).wait_send()


class PlaneGather:
    count = 5

    @staticmethod
    def scratch(grid):
        na, nb = grid.na, grid.nb
        sems = lambda *s: pltpu.SemaphoreType.DMA(s)
        return [sems(1), sems(na - 1), sems(na, nb - 1), sems(na), sems(na, nb - 1)]

    def __init__(self, grid, x, out, scratch):
        self.grid, self.x, self.out = grid, x, out
        self.own_sem, self.sa, self.sb, self.ra, self.rb = scratch
        self.spot = grid.here()

    def own(self):
        return pltpu.make_async_copy(self.x, self.out.at[self.spot[0], self.spot[1]], self.own_sem.at[0])

    def copy_a(self, i):
        g, (a, b, y, c) = self.grid, self.spot
        return pltpu.make_async_remote_copy(
            src_ref=self.x, dst_ref=self.out.at[a, b], send_sem=self.sa.at[i - 1], recv_sem=self.ra.at[i],
            device_id=g.device(wrap(a + i, g.na), b, y, c), device_id_type=MESH,
        )

    def copy_b(self, i, k):
        g, (a, b, y, c) = self.grid, self.spot
        aa = wrap(a + g.na - i, g.na)
        return pltpu.make_async_remote_copy(
            src_ref=self.x if i == 0 else self.out.at[aa, b], dst_ref=self.out.at[aa, b],
            send_sem=self.sb.at[i, k - 1], recv_sem=self.rb.at[i, k - 1],
            device_id=g.device(a, wrap(b + k, g.nb), y, c), device_id_type=MESH,
        )

    def start(self):
        self.own().start()
        for i in range(1, self.grid.na):
            self.copy_a(i).start()
        for k in range(1, self.grid.nb):
            self.copy_b(0, k).start()

    def middle(self, i):
        ref = self.out.at[wrap(self.spot[0] + self.grid.na - i, self.grid.na), self.spot[1]]
        pltpu.make_async_copy(ref, ref, self.ra.at[i]).wait()
        for k in range(1, self.grid.nb):
            self.copy_b(i, k).start()

    def last(self):
        self.own().wait()
        ref = self.x
        for i in range(self.grid.na):
            for k in range(1, self.grid.nb):
                pltpu.make_async_copy(ref, ref, self.rb.at[i, k - 1]).wait()
        for i in range(1, self.grid.na):
            self.copy_a(i).wait_send()
        for i in range(self.grid.na):
            for k in range(1, self.grid.nb):
                self.copy_b(i, k).wait_send()


def last_kernel(grid, x_ref, w_ref, t_ref, out_ref, w_out, t_out, own_sem, ss, rs, cs, cr, *scratch):
    gathers = [
        TensorGather(grid, t_ref, t_out, scratch[: TensorGather.count]),
        PlaneGather(grid, w_ref, w_out, scratch[TensorGather.count :]),
    ]
    gather_kernel(grid, x_ref, out_ref, own_sem, ss, rs, cs, cr, gathers)


def last_call(grid, x, w, t, collective_id):
    r, n = x.shape
    blocks = grid.na * grid.nb * grid.ny
    any_space = pl.BlockSpec(memory_space=pl.ANY)
    outs = pl.pallas_call(
        functools.partial(last_kernel, grid),
        out_shape=[
            jax.ShapeDtypeStruct((grid.size, r, n), x.dtype),
            jax.ShapeDtypeStruct((grid.na, grid.nb) + w.shape, w.dtype),
            jax.ShapeDtypeStruct((grid.ny, 2) + t.shape, t.dtype),
        ],
        in_specs=[any_space] * 3,
        out_specs=[any_space] * 3,
        scratch_shapes=[
            pltpu.SemaphoreType.DMA,
            pltpu.SemaphoreType.DMA((gather_sends(grid),)),
            pltpu.SemaphoreType.DMA((2 * blocks,)),
            pltpu.SemaphoreType.DMA((2 * blocks,)),
            pltpu.SemaphoreType.DMA((2 * blocks,)),
        ]
        + TensorGather.scratch(grid)
        + PlaneGather.scratch(grid),
        compiler_params=pltpu.CompilerParams(collective_id=collective_id, has_side_effects=True),
    )(x, w, t)
    whole = lambda v: v.reshape(-1, v.shape[-1])
    return outs[0], whole(outs[1]), whole(outs[2])


class Reduce:
    @staticmethod
    def scratch(grid, r, width):
        na, nb, ny = grid.na, grid.nb, grid.ny
        head = Reduce.head(r)
        sems = lambda *s: pltpu.SemaphoreType.DMA(s)
        vm = lambda *s: pltpu.VMEM(s, jnp.bfloat16)
        return [
            vm(nb, ny, na, r, width), vm(nb, ny, na, r, width),
            vm(nb, ny - 1, na, head, width), vm(ny, nb - 1, na, r - head, width),
            vm(nb - 1, na, head, width), vm(ny - 1, na, r - head, width), vm(na - 1, r, width),
            sems(nb, ny), sems(nb, ny), sems(nb, ny),
            sems(nb, ny - 1), sems(nb, ny - 1), sems(ny, nb - 1), sems(ny, nb - 1),
            sems(nb - 1), sems(nb - 1), sems(ny - 1), sems(ny - 1), sems(na - 1), sems(na - 1),
        ]

    count = 20

    @staticmethod
    def head(r):
        return max(16, r * 3 // 4 // 16 * 16)

    def __init__(self, grid, source, out, scratch):
        self.grid, self.source, self.out = grid, source, out
        (
            self.acc, self.core_in, self.in10, self.in11, self.in20, self.in21, self.a_in,
            self.load_sem, self.core_s, self.core_r, self.s10, self.r10, self.s11, self.r11,
            self.s20, self.r20, self.s21, self.r21, self.sa, self.ra,
        ) = scratch
        self.spot = grid.here()
        r = self.acc.shape[3]
        head = Reduce.head(r)
        self.upper = (pl.ds(0, head), pl.ds(head, r - head))
        self.spots = [(j, k) for j in reversed(range(grid.nb)) for k in reversed(range(grid.ny))]

    def remote(self, src, dst, ss, rs, where):
        return pltpu.make_async_remote_copy(
            src_ref=src, dst_ref=dst, send_sem=ss, recv_sem=rs, device_id=where, device_id_type=MESH
        )

    def core_copy(self, j, k):
        g, (a, b, y, c) = self.grid, self.spot
        return self.remote(
            self.source.at[:, wrap(b + j, g.nb), wrap(y + k, g.ny), 1 - c], self.core_in.at[j, k],
            self.core_s.at[j, k], self.core_r.at[j, k], g.device(a, b, y, 1 - c),
        )

    def load(self, j, k):
        g, (a, b, y, c) = self.grid, self.spot
        return pltpu.make_async_copy(
            self.source.at[:, wrap(b + j, g.nb), wrap(y + k, g.ny), c], self.acc.at[j, k], self.load_sem.at[j, k]
        )

    def copy10(self, j, k):
        g, (a, b, y, c) = self.grid, self.spot
        return self.remote(
            self.acc.at[j, k, :, self.upper[0]], self.in10.at[j, k - 1], self.s10.at[j, k - 1],
            self.r10.at[j, k - 1], g.device(a, b, wrap(y + k, g.ny), c),
        )

    def copy11(self, j, k):
        g, (a, b, y, c) = self.grid, self.spot
        return self.remote(
            self.acc.at[j, k, :, self.upper[1]], self.in11.at[k, j - 1], self.s11.at[k, j - 1],
            self.r11.at[k, j - 1], g.device(a, wrap(b + j, g.nb), y, c),
        )

    def copy20(self, j):
        g, (a, b, y, c) = self.grid, self.spot
        return self.remote(
            self.acc.at[j, 0, :, self.upper[0]], self.in20.at[j - 1], self.s20.at[j - 1],
            self.r20.at[j - 1], g.device(a, wrap(b + j, g.nb), y, c),
        )

    def copy21(self, k):
        g, (a, b, y, c) = self.grid, self.spot
        return self.remote(
            self.acc.at[0, k, :, self.upper[1]], self.in21.at[k - 1], self.s21.at[k - 1],
            self.r21.at[k - 1], g.device(a, b, wrap(y + k, g.ny), c),
        )

    def copy_a(self, i):
        g, (a, b, y, c) = self.grid, self.spot
        return self.remote(
            self.acc.at[0, 0, wrap(a + i, g.na)], self.a_in.at[i - 1], self.sa.at[i - 1],
            self.ra.at[i - 1], g.device(wrap(a + i, g.na), b, y, c),
        )

    def add(self, into, rows, ref, sem):
        pltpu.make_async_copy(ref, ref, sem).wait()
        f32 = jnp.float32

        def one(i, carry):
            total = into[i, rows].astype(f32) + ref[i].astype(f32)
            into[i, rows] = total.astype(into.dtype)
            return carry

        lax.fori_loop(0, self.grid.na, one, 0)

    def start(self):
        for j, k in self.spots:
            self.core_copy(j, k).start()
            self.load(j, k).start()

    def core(self):
        whole = pl.ds(0, self.acc.shape[3])
        for j, k in self.spots:
            self.load(j, k).wait()
            self.add(self.acc.at[j, k], whole, self.core_in.at[j, k], self.core_r.at[j, k])
            if k:
                self.copy10(j, k).start()
            if j:
                self.copy11(j, k).start()

    def first(self):
        nb, ny = self.grid.nb, self.grid.ny
        for j in reversed(range(nb)):
            for k in range(1, ny):
                self.add(self.acc.at[j, 0], self.upper[0], self.in10.at[j, k - 1], self.r10.at[j, k - 1])
            if j:
                self.copy20(j).start()
        for k in reversed(range(ny)):
            for j in range(1, nb):
                self.add(self.acc.at[0, k], self.upper[1], self.in11.at[k, j - 1], self.r11.at[k, j - 1])
            if k:
                self.copy21(k).start()

    def second(self):
        for j in range(1, self.grid.nb):
            self.add(self.acc.at[0, 0], self.upper[0], self.in20.at[j - 1], self.r20.at[j - 1])
        for k in range(1, self.grid.ny):
            self.add(self.acc.at[0, 0], self.upper[1], self.in21.at[k - 1], self.r21.at[k - 1])
        for i in range(1, self.grid.na):
            self.copy_a(i).start()

    def last(self):
        total = self.acc[0, 0, self.spot[0]].astype(jnp.float32)
        for i in range(1, self.grid.na):
            pltpu.make_async_copy(self.a_in.at[i - 1], self.a_in.at[i - 1], self.ra.at[i - 1]).wait()
            total = total + self.a_in[i - 1].astype(jnp.float32)
        self.out[...] = total.astype(self.out.dtype)

    def finish(self):
        for j, k in self.spots:
            self.core_copy(j, k).wait_send()
            if k:
                self.copy10(j, k).wait_send()
            if j:
                self.copy11(j, k).wait_send()
        for j in range(1, self.grid.nb):
            self.copy20(j).wait_send()
        for k in range(1, self.grid.ny):
            self.copy21(k).wait_send()
        for i in range(1, self.grid.na):
            self.copy_a(i).wait_send()


W_PIECES = 3


def gradients_kernel(grid, pieces, unit, places, *refs):
    (y_ref, k_ref, w_ref, t_ref, q_ref, x_ref, dz_ref, acts_ref), refs = refs[:8], refs[8:]
    (y_out, k_out, w_out, t_out, q_out), refs = refs[:5], refs[5:]
    outs, refs = refs[:6], refs[6:]
    (big, left, right, big_sem, left_sem, out_sem), refs = refs[:6], refs[6:]
    width = y_ref.shape[-1] // pieces
    sources = [(k_ref, k_out)]
    for p in range(pieces):
        at = pl.ds(p * width, width)
        sources.append((y_ref.at[:, :, :, :, :, at], y_out.at[:, at]))
    sums = [
        Reduce(grid, src, out, refs[m * Reduce.count : (m + 1) * Reduce.count])
        for m, (src, out) in enumerate(sources)
    ]
    refs = refs[len(sums) * Reduce.count :]
    w_width = w_ref.shape[-1] // W_PIECES
    flat_sums = []
    for p in range(W_PIECES):
        at = pl.ds(p * w_width, w_width)
        part = refs[p * PlaneReduce.count : (p + 1) * PlaneReduce.count]
        flat_sums.append(PlaneReduce(grid, w_ref.at[:, :, :, at], w_out.at[:, at], part))
    refs = refs[W_PIECES * PlaneReduce.count :]
    flat_sums.append(TensorReduce(grid, t_ref, t_out, refs[: TensorReduce.count]))
    q_gather = PlaneGather(grid, q_ref, q_out, refs[TensorReduce.count :])
    tiles = len(places)
    turn = sum(1 for place in places if place[0] != 2 and place[0] != 5)
    slots = big.shape[0]

    def left_load(m):
        s = lax.rem(m, 2)
        at = pl.ds(pl.multiple_of(m * unit, unit), unit)
        return pltpu.make_async_copy(acts_ref.at[:, at], left.at[s], left_sem.at[s])

    big_loads = [
        pltpu.make_async_copy(src, big.at[s % slots], big_sem.at[s]) for s, src in enumerate((x_ref, dz_ref))
    ]
    big_loads[0].start()
    greet(grid)
    for one in sums + flat_sums + [q_gather]:
        one.start()
    left_load(grid.here()[0] * 0).start()
    if slots > 1:
        big_loads[1].start()
    big_loads[0].wait()

    stages = [[one.core, one.first, one.second] for one in sums]
    work = []
    for beat in range(len(sums) + 2):
        for back in range(3):
            if 0 <= beat - back < len(sums):
                work.append(stages[beat - back][back])
    for p, one in enumerate(flat_sums):
        work.insert(min(len(work), 3 + 3 * p), one.middle)
    for i in range(1, grid.na):
        work.insert(min(len(work), 3 + 3 * i), functools.partial(q_gather.middle, i))
    turns = {}
    for n, item in enumerate(work):
        turns.setdefault(n * tiles // len(work), []).append(item)

    def store(m):
        which, head, first, rows = places[m]
        dst = outs[which]
        dst = dst.at[pl.ds(first, rows)] if head is None else dst.at[head, pl.ds(first, rows)]
        return pltpu.make_async_copy(right.at[m % 2, pl.ds(0, rows)], dst, out_sem.at[m % 2])

    def tile_body(m, carry):
        s = lax.rem(m, 2)

        @pl.when(m + 1 < tiles)
        def _():
            left_load(m + 1).start()

        for n in range(2, tiles):

            @pl.when(m == n)
            def _():
                store(n - 2).wait()

        @pl.when(m == turn)
        def _():
            if slots == 1:
                big_loads[1].start()
            big_loads[1].wait()

        left_load(m).wait()
        operand = big.at[lax.div(m, turn) if slots > 1 else 0]
        right[s] = lax.dot_general(
            left[s], operand[...], (((0,), (0,)), ((), ())), preferred_element_type=jnp.float32
        ).astype(right.dtype)
        for n in range(tiles):

            @pl.when(m == n)
            def _():
                store(n).start()
                for item in turns.get(n, ()):
                    item()

        return carry

    lax.fori_loop(0, tiles, tile_body, 0)
    for one in sums + flat_sums:
        one.last()
    for n in range(max(0, tiles - 2), tiles):
        store(n).wait()
    for one in sums + flat_sums:
        one.finish()
    q_gather.last()


def gradients_call(grid, out_rows, key_rows, weight_rows, tensor_rows, query_rows, x, dz, acts, f, fs, collective_id, pieces=4):
    tokens, n = x.shape
    r = tokens // grid.size
    lay = (grid.na, grid.nb, grid.ny, 2, r)
    wide, wide_s = round_up(f, 128), round_up(fs, 128)
    unit = math.gcd(wide, wide_s)
    places = []
    for which, heads, real, padded in (
        (0, EXP_DEV, f, wide), (1, EXP_DEV, f, wide), (3, 0, fs, wide_s), (4, 0, fs, wide_s),
        (2, EXP_DEV, f, wide), (5, 0, fs, wide_s),
    ):
        for head in range(max(heads, 1)):
            for first in range(0, padded, unit):
                places.append((which, head if heads else None, first, min(unit, real - first)))
    slots = 2 if 2 * tokens * n * 2 <= (24 << 20) else 1
    any_space = pl.BlockSpec(memory_space=pl.ANY)
    in_vmem = pl.BlockSpec(memory_space=pltpu.VMEM)
    f32 = jnp.float32
    scratch = [
        pltpu.VMEM((slots, tokens, n), x.dtype),
        pltpu.VMEM((2, tokens, unit), x.dtype),
        pltpu.VMEM((2, unit, n), x.dtype),
        pltpu.SemaphoreType.DMA((2,)),
        pltpu.SemaphoreType.DMA((2,)),
        pltpu.SemaphoreType.DMA((2,)),
    ]
    kw = key_rows.shape[1]
    for width in [kw] + [n // pieces] * pieces:
        scratch += Reduce.scratch(grid, r, width)
    wr, ww = weight_rows.shape[0] // (grid.na * grid.nb), weight_rows.shape[1]
    scratch += PlaneReduce.scratch(grid, wr, ww // W_PIECES) * W_PIECES
    tr, tw = tensor_rows.shape[0] // (2 * grid.ny), tensor_rows.shape[1]
    scratch += TensorReduce.scratch(grid, tr, tw) + PlaneGather.scratch(grid)
    outs = pl.pallas_call(
        functools.partial(gradients_kernel, grid, pieces, unit, places),
        out_shape=[
            jax.ShapeDtypeStruct((r, n), f32),
            jax.ShapeDtypeStruct((r, kw), f32),
            jax.ShapeDtypeStruct((wr, ww), x.dtype),
            jax.ShapeDtypeStruct((tr, tw), f32),
            jax.ShapeDtypeStruct((grid.na, grid.nb) + query_rows.shape, x.dtype),
            jax.ShapeDtypeStruct((EXP_DEV, f, n), x.dtype),
            jax.ShapeDtypeStruct((EXP_DEV, f, n), x.dtype),
            jax.ShapeDtypeStruct((EXP_DEV, f, n), x.dtype),
            jax.ShapeDtypeStruct((fs, n), x.dtype),
            jax.ShapeDtypeStruct((fs, n), x.dtype),
            jax.ShapeDtypeStruct((fs, n), x.dtype),
        ],
        in_specs=[any_space] * 8,
        out_specs=[in_vmem] * 4 + [any_space] * 7,
        scratch_shapes=scratch,
        compiler_params=pltpu.CompilerParams(
            collective_id=collective_id, has_side_effects=True, vmem_limit_bytes=62 << 20
        ),
    )(
        out_rows.reshape(lay + (n,)),
        key_rows.reshape(lay + (kw,)),
        weight_rows.reshape(grid.na, grid.nb, wr, ww),
        tensor_rows.reshape(grid.ny, 2, tr, tw),
        query_rows,
        x,
        dz,
        acts,
    )
    y_sum, k_sum, w_sum, t_sum, q_all = outs[:5]
    eg, eu, ed, sg, su, sd = (out.astype(f32) for out in outs[5:])
    q_all = q_all.reshape(tokens, -1)
    weights = (jnp.swapaxes(eg, 1, 2), jnp.swapaxes(eu, 1, 2), ed, sg.T, su.T, sd)
    return y_sum, k_sum, w_sum, t_sum, q_all, weights


def rms_scale(values, gain_vec):
    return (
        values * lax.rsqrt(jnp.mean(values * values, axis=-1, keepdims=True) + epsilon) * gain_vec
    )


def rotate(values, places):
    halfway = values.shape[-1] // 2
    frequency = 10000.0 ** (-jnp.arange(halfway, dtype=jnp.float32) / halfway)
    angles = places.astype(jnp.float32)[:, None] * frequency[None, :]
    cosine = jnp.cos(angles)
    sine_part = jnp.sin(angles)
    if values.ndim == 3:
        cosine = cosine[:, None, :]
        sine_part = sine_part[:, None, :]
    first_half = values[..., :halfway]
    second = values[..., halfway:]
    return jnp.concatenate(
        [first_half * cosine - second * sine_part, second * cosine + first_half * sine_part],
        axis=-1,
    )


def seq_places(segments):
    total_rows = segments.shape[0]
    ordinal = jnp.arange(total_rows, dtype=jnp.int32)
    starts = jnp.concatenate(
        [jnp.ones((1,), jnp.int32), (segments[1:] != segments[:-1]).astype(jnp.int32)]
    )
    seg_start = lax.cummax(jnp.where(starts > 0, ordinal, 0), axis=0)
    return jnp.where(segments == 0, ordinal, total_rows // 2 + ordinal - seg_start)


def silu_product(gate_pre, up_pre):
    return jax.nn.silu(gate_pre) * up_pre


def score_block(queries, key_plain, rope_all, visible):
    scale_factor = (NOPE + ROPE) ** (-0.5)
    raw_scores = jnp.einsum(
        "thc,shc->hts", queries[..., :NOPE], key_plain, preferred_element_type=jnp.float32
    )
    raw_scores = raw_scores + jnp.einsum(
        "thr,sr->hts", queries[..., NOPE:], rope_all, preferred_element_type=jnp.float32
    )
    return jnp.where(visible[None], scale_factor * raw_scores, masked_out)


def dot(left_side, right_side):
    return jnp.dot(left_side, right_side, preferred_element_type=jnp.float32)


def pad_columns(values):
    return jnp.pad(values, ((0, 0), (0, -values.shape[1] % 128)))


def low(values):
    return values.astype(jnp.bfloat16)


def shards(
    grid,
    hidden_in,
    attn_gain,
    query_weight,
    latent_weight,
    latent_gain,
    expand_weight,
    output_weight,
    moe_gain,
    shared_gate,
    shared_up,
    shared_down,
    expert_gate,
    expert_up,
    expert_down,
    gate_values,
    expert_routes,
    segments,
    cotangent,
):
    tok_rows, model_width = hidden_in.shape
    groups = lax.axis_size("expert")
    parts = lax.axis_size("tensor")
    device = lax.axis_index("expert")
    part = lax.axis_index("tensor")
    total_rows = segments.shape[0]
    few = tok_rows // parts
    start_row = device * tok_rows
    scale_factor = (NOPE + ROPE) ** (-0.5)

    def quarter(values):
        return lax.dynamic_slice_in_dim(values, part * few, few)

    def own_group(values):
        return lax.dynamic_slice_in_dim(values, start_row, tok_rows)

    places = own_group(seq_places(segments))
    own_seg = own_group(segments)
    own_ordinal = start_row + jnp.arange(tok_rows, dtype=jnp.int32)
    key_ordinal = jnp.arange(total_rows, dtype=jnp.int32)
    visible = (key_ordinal[None, :] <= own_ordinal[:, None]) & (
        (segments[None, :] == own_seg[:, None]) | (segments[None, :] == 0)
    )
    experts_all = EXP_DEV * groups
    cot_all = lax.all_gather(quarter(cotangent), ALL, axis=0, tiled=True)

    hidden_f = hidden_in.astype(jnp.float32)
    normed = low(rms_scale(hidden_f, attn_gain))
    compressed = dot(normed, latent_weight)
    latents = low(rms_scale(compressed[:, :LATENT], latent_gain))
    key_rope = low(rotate(compressed[:, LATENT:], places))
    onehot = expert_routes[:, :, None] == jnp.arange(experts_all, dtype=jnp.int32)
    gate_rows = jnp.sum(jnp.where(onehot, gate_values[:, :, None], 0.0), axis=1)
    gate_high = low(gate_rows)
    gate_low = low(gate_rows - gate_high.astype(jnp.float32))
    packed = pad_columns(jnp.concatenate([latents, key_rope, gate_high, gate_low], axis=1))
    packed_all = gather_all(grid, quarter(packed), 0).reshape(total_rows, -1)
    latents_all = packed_all[:, :LATENT]
    rope_all = packed_all[:, LATENT : LATENT + ROPE]
    q_raw = dot(normed, query_weight)
    heads_here = q_raw.shape[1] // (NOPE + ROPE)
    q_raw = q_raw.reshape(tok_rows, heads_here, NOPE + ROPE)
    queries = low(
        jnp.concatenate([q_raw[..., :NOPE], rotate(q_raw[..., NOPE:], places)], axis=-1)
    )
    expanded = low(dot(latents_all, expand_weight)).reshape(
        total_rows, heads_here, NOPE + VDIM
    )
    key_plain, value_part = expanded[..., :NOPE], expanded[..., NOPE:]
    scores = score_block(queries, key_plain, rope_all, visible)
    peak = jnp.max(scores, axis=-1, keepdims=True)
    weights = jnp.exp(scores - peak)
    total_weight = jnp.sum(weights, axis=-1, keepdims=True)
    log_total = peak + jnp.log(total_weight)
    context = jnp.einsum(
        "hts,shv->thv", low(weights / total_weight), value_part, preferred_element_type=jnp.float32
    )
    merged = low(context).reshape(tok_rows, heads_here * VDIM)
    attn_out = tensor_scatter(grid, low(dot(merged, output_weight)), 1)
    residual = quarter(hidden_f) + attn_out
    moe_in = low(rms_scale(residual, moe_gain))
    moe_all, grad_moe_in, out_rows, acts = experts_call(
        grid, moe_in, cot_all, packed_all, expert_gate, expert_up, expert_down,
        shared_gate, shared_up, shared_down, 2,
    )
    normed_later, _ = lax.optimization_barrier((quarter(normed), moe_in[:8]))
    normed_all = lax.all_gather(normed_later, ALL, axis=0, tiled=True)

    grad_moe_in, normed_all = lax.optimization_barrier((grad_moe_in, normed_all))
    _, pull_moe = jax.vjp(rms_scale, residual, moe_gain)
    grad_residual, grad_moe_gain = pull_moe(grad_moe_in)
    grad_residual = grad_residual + quarter(cotangent).astype(jnp.float32)
    grad_res_low = tensor_gather(grid, low(grad_residual), 5)
    output_part = low(dot(merged.T, grad_res_low))
    grad_context = low(dot(grad_res_low, output_weight.T)).reshape(tok_rows, heads_here, VDIM)
    scores = score_block(queries, key_plain, rope_all, visible)
    probs = jnp.exp(scores - log_total)
    grad_probs = jnp.einsum(
        "thv,shv->hts", grad_context, value_part, preferred_element_type=jnp.float32
    )
    grad_values = jnp.einsum(
        "hts,thv->shv", low(probs), grad_context, preferred_element_type=jnp.float32
    )
    grad_scores = low(probs * (grad_probs - jnp.sum(probs * grad_probs, axis=-1, keepdims=True)))
    grad_q_plain = scale_factor * jnp.einsum(
        "hts,shc->thc", grad_scores, key_plain, preferred_element_type=jnp.float32
    )
    grad_q_rope = scale_factor * jnp.einsum(
        "hts,sr->thr", grad_scores, rope_all, preferred_element_type=jnp.float32
    )
    grad_k_plain = scale_factor * jnp.einsum(
        "hts,thc->shc", grad_scores, queries[..., :NOPE], preferred_element_type=jnp.float32
    )
    grad_k_rope = scale_factor * jnp.einsum(
        "hts,thr->sr", grad_scores, queries[..., NOPE:], preferred_element_type=jnp.float32
    )
    grad_expanded = low(
        jnp.concatenate([grad_k_plain, grad_values], axis=-1).reshape(
            total_rows, heads_here * (NOPE + VDIM)
        )
    )
    expand_part = low(dot(latents_all.T, grad_expanded))
    grad_keys = jnp.concatenate([dot(grad_expanded, expand_weight.T), grad_k_rope], axis=1)
    _, pull_qrope = jax.vjp(partial(rotate, places=places), q_raw[..., NOPE:])
    (grad_q_turned,) = pull_qrope(grad_q_rope)
    grad_q_low = low(
        jnp.concatenate([grad_q_plain, grad_q_turned], axis=-1).reshape(tok_rows, -1)
    )
    normed_rows = low(dot(grad_q_low, query_weight.T))

    weight_rows = jnp.concatenate(
        [output_part.reshape(LATENT, -1), expand_part], axis=1
    )
    moe_out, grad_keys, weight_rows, grad_normed, grad_q_all, expert_grads = gradients_call(
        grid, out_rows, pad_columns(low(grad_keys)), weight_rows, normed_rows, grad_q_low, moe_all, cot_all, acts,
        expert_down.shape[1], shared_down.shape[0], 3,
    )
    grad_expert_gate, grad_expert_up, grad_expert_down = expert_grads[:3]
    grad_shared_gate, grad_shared_up, grad_shared_down = expert_grads[3:]
    layer_out = low(residual + moe_out)
    places_few = quarter(places)
    compressed_few = quarter(compressed)
    _, pull_latent = jax.vjp(rms_scale, compressed_few[:, :LATENT], latent_gain)
    grad_plain_latent, grad_latent_gain = pull_latent(grad_keys[:, :LATENT])
    _, pull_krope = jax.vjp(partial(rotate, places=places_few), compressed_few[:, LATENT:])
    (grad_k_turned,) = pull_krope(grad_keys[:, LATENT : LATENT + ROPE])
    grad_comp_low = low(jnp.concatenate([grad_plain_latent, grad_k_turned], axis=-1))
    grad_normed = grad_normed + dot(grad_comp_low, latent_weight.T)
    _, pull_input = jax.vjp(rms_scale, quarter(hidden_f), attn_gain)
    grad_input_norm, grad_attn_gain = pull_input(grad_normed)
    gains = jnp.concatenate([grad_attn_gain, grad_latent_gain, grad_moe_gain])
    gains = jnp.pad(gains, (0, -gains.shape[0] % few)).reshape(few, -1)
    gains_high = low(gains)
    gains_low = low(gains - gains_high.astype(jnp.float32))
    spread = gains.shape[1]
    both = jnp.concatenate([layer_out, low(grad_residual + grad_input_norm)], axis=1)
    last, weight_rows, both = last_call(
        grid,
        pad_columns(jnp.concatenate([grad_comp_low, gains_high, gains_low], axis=1)),
        weight_rows,
        both,
        8,
    )
    grad_comp_all = last.reshape(total_rows, -1)[:, : LATENT + ROPE]
    gains = jnp.sum(last[:, :, LATENT + ROPE : LATENT + ROPE + 2 * spread].astype(jnp.float32), axis=0)
    gains = (gains[:, :spread] + gains[:, spread:]).reshape(-1)
    grad_latent_weight = dot(normed_all.T, grad_comp_all)
    grad_query_weight = dot(normed_all.T, grad_q_all)
    layer_out, grad_hidden = both[:, :model_width], both[:, model_width:].astype(jnp.float32)
    split = weight_rows.shape[1] - expand_weight.shape[1]
    grad_output_weight = weight_rows[:, :split].reshape(output_weight.shape).astype(jnp.float32)
    grad_expand_weight = weight_rows[:, split:].astype(jnp.float32)
    return (
        layer_out,
        grad_hidden,
        gains[:model_width],
        grad_query_weight,
        grad_latent_weight,
        gains[model_width : model_width + LATENT],
        grad_expand_weight,
        grad_output_weight,
        gains[model_width + LATENT : 2 * model_width + LATENT],
        grad_shared_gate,
        grad_shared_up,
        grad_shared_down,
        grad_expert_gate,
        grad_expert_up,
        grad_expert_down,
    )


def solution(mesh):
    grid = Grid(mesh.shape["expert"], mesh.shape["tensor"])
    placed = (
        P("expert", None),
        P(),
        P(None, "tensor"),
        P(),
        P(),
        P(None, "tensor"),
        P("tensor", None),
        P(),
        P(None, "tensor"),
        P(None, "tensor"),
        P("tensor", None),
        P("expert", None, "tensor"),
        P("expert", None, "tensor"),
        P("expert", "tensor", None),
        P("expert", None),
        P("expert", None),
        P(),
        P("expert", None),
    )
    return jax.shard_map(
        partial(shards, grid),
        mesh=mesh,
        in_specs=placed,
        out_specs=(
            P("expert", None),
            P("expert", None),
            P(),
            P(None, "tensor"),
            P(),
            P(),
            P(None, "tensor"),
            P("tensor", None),
            P(),
            P(None, "tensor"),
            P(None, "tensor"),
            P("tensor", None),
            P("expert", None, "tensor"),
            P("expert", None, "tensor"),
            P("expert", "tensor", None),
        ),
        check_vma=False,
    )
```

```python
import functools
import math
from functools import partial

import jax
import jax.numpy as jnp
from jax import lax
from jax.experimental import pallas as pl
from jax.experimental.pallas import tpu as pltpu
from jax.sharding import PartitionSpec as P

NOPE = 128
ROPE = 64
VDIM = 128
LATENT = 512
TOP = 6
EXP_DEV = 2
ALL = ("expert", "tensor")
MESH = pl.DeviceIdType.MESH

epsilon = 1e-06
masked_out = -1e30


class Grid:
    def __init__(self, expert, tensor):
        self.na = 4 if expert % 4 == 0 else 1
        self.nb = expert // self.na
        self.ny = tensor // 2
        self.size = expert * tensor

    def here(self):
        e, t = lax.axis_index("expert"), lax.axis_index("tensor")
        return (lax.div(e, self.nb), lax.rem(e, self.nb), lax.div(t, 2), lax.rem(t, 2))

    def device(self, a, b, y, c):
        return {"expert": a * self.nb + b, "tensor": y * 2 + c}

    def block(self, a, b, y, c):
        return ((a * self.nb + b) * self.ny + y) * 2 + c


def wrap(i, n):
    return lax.rem(i, n)


def greet(grid):
    a, b, y, c = grid.here()
    barrier = pltpu.get_barrier_semaphore()
    others = (
        [grid.device(wrap(a + i, grid.na), b, y, c) for i in range(1, grid.na)]
        + [grid.device(a, wrap(b + i, grid.nb), y, c) for i in range(1, grid.nb)]
        + [grid.device(a, b, wrap(y + i, grid.ny), c) for i in range(1, grid.ny)]
        + [grid.device(a, b, y, 1 - c)]
    )
    for other in others:
        pl.semaphore_signal(barrier, inc=1, device_id=other, device_id_type=MESH)
    pl.semaphore_wait(barrier, len(others))


def gather_kernel(
    grid, x_ref, out_ref, own_sem, send_sem, recv_sem, core_send, core_recv, extra=()
):
    na, nb, ny = grid.na, grid.nb, grid.ny
    a, b, y, c = grid.here()
    half = x_ref.shape[0] // 2
    greet(grid)
    waits = []

    def dst(bb, yy, cc, aa, h):
        return out_ref.at[grid.block(aa, bb, yy, cc), pl.ds(h * half, half)]

    def slot(bb, yy, aa, h):
        return ((bb * ny + yy) * na + aa) * 2 + h

    def push(src, bb, yy, aa, h, where, kind):
        copy = pltpu.make_async_remote_copy(
            src_ref=src,
            dst_ref=dst(bb, yy, c, aa, h),
            send_sem=core_send.at[slot(bb, yy, aa, h)] if kind == "c" else send_sem.at[len(waits)],
            recv_sem=(core_recv if kind == "c" else recv_sem).at[slot(bb, yy, aa, h)],
            device_id=where,
            device_id_type=MESH,
        )
        copy.start()
        if kind != "c":
            waits.append(copy)
        else:
            core_waits.append(copy)

    core_waits = []

    def onward(src, bb, yy, aa, h, dims):
        for d in dims:
            if d == "a":
                for i in range(1, na):
                    push(src, bb, yy, aa, h, grid.device(wrap(a + i, na), b, y, c), d)
            if d == "b":
                for i in range(1, nb):
                    push(src, bb, yy, aa, h, grid.device(a, wrap(b + i, nb), y, c), d)
            if d == "y":
                for i in range(1, ny):
                    push(src, bb, yy, aa, h, grid.device(a, b, wrap(y + i, ny), c), d)
        push(src, bb, yy, aa, h, grid.device(a, b, y, 1 - c), "c")

    def landed(bb, yy, cc, aa, h, sem):
        ref = dst(bb, yy, cc, aa, h)
        pltpu.make_async_copy(ref, ref, sem.at[slot(bb, yy, aa, h)]).wait()
        return ref

    own = pltpu.make_async_copy(x_ref, out_ref.at[grid.block(a, b, y, c)], own_sem)
    own.start()
    orders = (("b", "y"), ("y", "b"))
    for h in range(2):
        onward(x_ref.at[pl.ds(h * half, half)], b, y, a, h, ("a",) + orders[h])
    for one in extra:
        one.start()
    for i in range(1, na):
        aa = wrap(a + na - i, na)
        for h in range(2):
            onward(landed(b, y, c, aa, h, recv_sem), b, y, aa, h, orders[h])
    for i in range(na):
        aa = wrap(a + na - i, na)
        for h in range(2):
            n1 = (nb, ny)[h]
            for j in range(1, n1):
                bb, yy = (wrap(b + nb - j, nb), y) if h == 0 else (b, wrap(y + ny - j, ny))
                onward(landed(bb, yy, c, aa, h, recv_sem), bb, yy, aa, h, orders[h][1:])
    for i in range(na):
        aa = wrap(a + na - i, na)
        for h in range(2):
            for j in range(nb):
                for k in range(1, ny):
                    if h == 0:
                        bb, yy = wrap(b + nb - j, nb), wrap(y + ny - k, ny)
                        onward(landed(bb, yy, c, aa, h, recv_sem), bb, yy, aa, h, ())
            for j in range(ny):
                for k in range(1, nb):
                    if h == 1:
                        bb, yy = wrap(b + nb - k, nb), wrap(y + ny - j, ny)
                        onward(landed(bb, yy, c, aa, h, recv_sem), bb, yy, aa, h, ())
    for i in range(1, na):
        for one in extra:
            one.middle(i)
    for j in range(nb):
        for k in range(ny):
            for i in range(na):
                for h in range(2):
                    landed(wrap(b + nb - j, nb), wrap(y + ny - k, ny), 1 - c, wrap(a + na - i, na), h, core_recv)
    own.wait()
    for copy in waits + core_waits:
        copy.wait_send()
    for one in extra:
        one.last()


def gather_sends(grid):
    na, nb, ny = grid.na, grid.nb, grid.ny
    return 2 * (na - 1 + na * (nb - 1) + na * (ny - 1) + na * (nb - 1) * (ny - 1))


def gather_all(grid, x, collective_id):
    r, n = x.shape
    blocks = grid.na * grid.nb * grid.ny
    return pl.pallas_call(
        functools.partial(gather_kernel, grid),
        out_shape=jax.ShapeDtypeStruct((grid.size, r, n), x.dtype),
        in_specs=[pl.BlockSpec(memory_space=pl.ANY)],
        out_specs=pl.BlockSpec(memory_space=pl.ANY),
        scratch_shapes=[
            pltpu.SemaphoreType.DMA,
            pltpu.SemaphoreType.DMA((gather_sends(grid),)),
            pltpu.SemaphoreType.DMA((2 * blocks,)),
            pltpu.SemaphoreType.DMA((2 * blocks,)),
            pltpu.SemaphoreType.DMA((2 * blocks,)),
        ],
        compiler_params=pltpu.CompilerParams(collective_id=collective_id, has_side_effects=True),
    )(x)


def scatter_kernel(grid, pieces, p_ref, out_ref, acc, core_in, d1_in0, d1_in1, d2_in0, d2_in1, a_in,
                   load_sem, core_s, core_r, s10, r10, s11, r11, s20, r20, s21, r21, sa, ra):
    na, nb, ny = grid.na, grid.nb, grid.ny
    a, b, y, c = grid.here()
    half = p_ref.shape[4] // 2
    width = p_ref.shape[5] // pieces
    greet(grid)
    pending = []

    def send(src, dst, ss, rs, where):
        copy = pltpu.make_async_remote_copy(src_ref=src, dst_ref=dst, send_sem=ss, recv_sem=rs, device_id=where, device_id_type=MESH)
        copy.start()
        pending.append(copy)

    def await_in(ref, sem):
        pltpu.make_async_copy(ref, ref, sem).wait()

    def add(dst, src):
        dst[...] = (dst[...].astype(jnp.float32) + src[...].astype(jnp.float32)).astype(dst.dtype)

    def cols(p):
        return pl.ds(p * width, width)

    spots = [(j, k) for j in reversed(range(nb)) for k in reversed(range(ny))]
    loads = {}
    for p in range(pieces):
        for n, (j, k) in enumerate(spots):
            bb, yy = wrap(b + j, nb), wrap(y + k, ny)
            send(p_ref.at[:, bb, yy, 1 - c, :, cols(p)], core_in.at[p, j, k], core_s.at[p, n], core_r.at[p, n],
                 grid.device(a, b, y, 1 - c))
            load = pltpu.make_async_copy(p_ref.at[:, bb, yy, c, :, cols(p)], acc.at[p, j, k], load_sem.at[p, n])
            load.start()
            loads[p, n] = load
    rows = (pl.ds(0, half), pl.ds(half, half))
    for p in range(pieces):
        for n, (j, k) in enumerate(spots):
            loads[p, n].wait()
            await_in(core_in.at[p, j, k], core_r.at[p, n])
            for i in range(na):
                add(acc.at[p, j, k, i], core_in.at[p, j, k, i])
            if k:
                send(acc.at[p, j, k, :, rows[0]], d1_in0.at[p, j, k - 1], s10.at[p, j, k - 1], r10.at[p, j, k - 1],
                     grid.device(a, b, wrap(y + k, ny), c))
            if j:
                send(acc.at[p, j, k, :, rows[1]], d1_in1.at[p, k, j - 1], s11.at[p, k, j - 1], r11.at[p, k, j - 1],
                     grid.device(a, wrap(b + j, nb), y, c))
    for p in range(pieces):
        for j in reversed(range(nb)):
            for k in range(1, ny):
                await_in(d1_in0.at[p, j, k - 1], r10.at[p, j, k - 1])
                for i in range(na):
                    add(acc.at[p, j, 0, i, rows[0]], d1_in0.at[p, j, k - 1, i])
            if j:
                send(acc.at[p, j, 0, :, rows[0]], d2_in0.at[p, j - 1], s20.at[p, j - 1], r20.at[p, j - 1],
                     grid.device(a, wrap(b + j, nb), y, c))
        for k in reversed(range(ny)):
            for j in range(1, nb):
                await_in(d1_in1.at[p, k, j - 1], r11.at[p, k, j - 1])
                for i in range(na):
                    add(acc.at[p, 0, k, i, rows[1]], d1_in1.at[p, k, j - 1, i])
            if k:
                send(acc.at[p, 0, k, :, rows[1]], d2_in1.at[p, k - 1], s21.at[p, k - 1], r21.at[p, k - 1],
                     grid.device(a, b, wrap(y + k, ny), c))
    for p in range(pieces):
        for j in range(1, nb):
            await_in(d2_in0.at[p, j - 1], r20.at[p, j - 1])
            for i in range(na):
                add(acc.at[p, 0, 0, i, rows[0]], d2_in0.at[p, j - 1, i])
        for k in range(1, ny):
            await_in(d2_in1.at[p, k - 1], r21.at[p, k - 1])
            for i in range(na):
                add(acc.at[p, 0, 0, i, rows[1]], d2_in1.at[p, k - 1, i])
        for i in range(1, na):
            aa = wrap(a + i, na)
            send(acc.at[p, 0, 0, aa], a_in.at[p, i - 1], sa.at[p, i - 1], ra.at[p, i - 1], grid.device(aa, b, y, c))
    for p in range(pieces):
        total = acc[p, 0, 0, a].astype(jnp.float32)
        for i in range(1, na):
            await_in(a_in.at[p, i - 1], ra.at[p, i - 1])
            total = total + a_in[p, i - 1].astype(jnp.float32)
        out_ref[:, cols(p)] = total.astype(out_ref.dtype)
    for copy in pending:
        copy.wait_send()


def scatter_all(grid, p, dtype, collective_id, pieces=2):
    r, n = p.shape[0] // grid.size, p.shape[1]
    na, nb, ny = grid.na, grid.nb, grid.ny
    half, width = r // 2, n // pieces
    sems = lambda *s: pltpu.SemaphoreType.DMA(s)
    vm = lambda *s: pltpu.VMEM(s, jnp.bfloat16)
    return pl.pallas_call(
        functools.partial(scatter_kernel, grid, pieces),
        out_shape=jax.ShapeDtypeStruct((r, n), dtype),
        in_specs=[pl.BlockSpec(memory_space=pl.ANY)],
        out_specs=pl.BlockSpec(memory_space=pltpu.VMEM),
        scratch_shapes=[
            vm(pieces, nb, ny, na, r, width),
            vm(pieces, nb, ny, na, r, width),
            vm(pieces, nb, ny - 1, na, half, width),
            vm(pieces, ny, nb - 1, na, half, width),
            vm(pieces, nb - 1, na, half, width),
            vm(pieces, ny - 1, na, half, width),
            vm(pieces, na - 1, r, width),
            sems(pieces, nb * ny), sems(pieces, nb * ny), sems(pieces, nb * ny),
            sems(pieces, nb, ny - 1), sems(pieces, nb, ny - 1),
            sems(pieces, ny, nb - 1), sems(pieces, ny, nb - 1),
            sems(pieces, nb - 1), sems(pieces, nb - 1),
            sems(pieces, ny - 1), sems(pieces, ny - 1),
            sems(pieces, na - 1), sems(pieces, na - 1),
        ],
        compiler_params=pltpu.CompilerParams(collective_id=collective_id, has_side_effects=True, vmem_limit_bytes=40 << 20),
    )(p.reshape(na, nb, ny, 2, r, n))


def greet_tensor(grid):
    a, b, y, c = grid.here()
    barrier = pltpu.get_barrier_semaphore()
    others = [grid.device(a, b, wrap(y + i, grid.ny), c) for i in range(1, grid.ny)]
    others.append(grid.device(a, b, y, 1 - c))
    for other in others:
        pl.semaphore_signal(barrier, inc=1, device_id=other, device_id_type=MESH)
    pl.semaphore_wait(barrier, len(others))


def tensor_scatter_kernel(grid, p_ref, out_ref, acc, core_in, y_in, core_s, core_r, ys, yr):
    ny = grid.ny
    a, b, y, c = grid.here()
    greet_tensor(grid)
    pending = []
    for k in reversed(range(ny)):
        copy = pltpu.make_async_remote_copy(
            src_ref=p_ref.at[wrap(y + k, ny), 1 - c], dst_ref=core_in.at[k], send_sem=core_s.at[k], recv_sem=core_r.at[k],
            device_id=grid.device(a, b, y, 1 - c), device_id_type=MESH,
        )
        copy.start()
        pending.append(copy)
    for k in reversed(range(ny)):
        pltpu.make_async_copy(core_in.at[k], core_in.at[k], core_r.at[k]).wait()
        total = p_ref[wrap(y + k, ny), c].astype(jnp.float32) + core_in[k].astype(jnp.float32)
        if k:
            acc[k - 1] = total.astype(acc.dtype)
            copy = pltpu.make_async_remote_copy(
                src_ref=acc.at[k - 1], dst_ref=y_in.at[k - 1], send_sem=ys.at[k - 1], recv_sem=yr.at[k - 1],
                device_id=grid.device(a, b, wrap(y + k, ny), c), device_id_type=MESH,
            )
            copy.start()
            pending.append(copy)
        else:
            out_ref[...] = total
    for k in range(1, ny):
        pltpu.make_async_copy(y_in.at[k - 1], y_in.at[k - 1], yr.at[k - 1]).wait()
        out_ref[...] += y_in[k - 1].astype(jnp.float32)
    for copy in pending:
        copy.wait_send()


def tensor_scatter(grid, p, collective_id):
    ny = grid.ny
    r, n = p.shape[0] // (2 * ny), p.shape[1]
    return pl.pallas_call(
        functools.partial(tensor_scatter_kernel, grid),
        out_shape=jax.ShapeDtypeStruct((r, n), jnp.float32),
        in_specs=[pl.BlockSpec(memory_space=pltpu.VMEM)],
        out_specs=pl.BlockSpec(memory_space=pltpu.VMEM),
        scratch_shapes=[
            pltpu.VMEM((max(ny - 1, 1), r, n), p.dtype),
            pltpu.VMEM((ny, r, n), p.dtype),
            pltpu.VMEM((max(ny - 1, 1), r, n), p.dtype),
            pltpu.SemaphoreType.DMA((ny,)),
            pltpu.SemaphoreType.DMA((ny,)),
            pltpu.SemaphoreType.DMA((max(ny - 1, 1),)),
            pltpu.SemaphoreType.DMA((max(ny - 1, 1),)),
        ],
        compiler_params=pltpu.CompilerParams(
            collective_id=collective_id, has_side_effects=True, vmem_limit_bytes=16 << 20
        ),
    )(p.reshape(ny, 2, r, n))


def tensor_gather_kernel(grid, x_ref, out_ref, own_sem, ys, yr, core_s, core_r):
    ny = grid.ny
    a, b, y, c = grid.here()
    greet_tensor(grid)
    own = pltpu.make_async_copy(x_ref, out_ref.at[y, c], own_sem)
    own.start()
    pending = []

    def push(src, spot, ss, rs, where):
        copy = pltpu.make_async_remote_copy(
            src_ref=src, dst_ref=out_ref.at[spot, c], send_sem=ss, recv_sem=rs, device_id=where, device_id_type=MESH
        )
        copy.start()
        pending.append(copy)

    for k in range(1, ny):
        push(x_ref, y, ys.at[k], yr.at[k], grid.device(a, b, wrap(y + k, ny), c))
    push(x_ref, y, core_s.at[0], core_r.at[0], grid.device(a, b, y, 1 - c))
    for k in range(1, ny):
        spot = wrap(y + ny - k, ny)
        ref = out_ref.at[spot, c]
        pltpu.make_async_copy(ref, ref, yr.at[k]).wait()
        push(ref, spot, core_s.at[k], core_r.at[k], grid.device(a, b, y, 1 - c))
    for k in range(ny):
        ref = out_ref.at[wrap(y + ny - k, ny), 1 - c]
        pltpu.make_async_copy(ref, ref, core_r.at[k]).wait()
    own.wait()
    for copy in pending:
        copy.wait_send()


def tensor_gather(grid, x, collective_id):
    ny = grid.ny
    r, n = x.shape
    out = pl.pallas_call(
        functools.partial(tensor_gather_kernel, grid),
        out_shape=jax.ShapeDtypeStruct((ny, 2, r, n), x.dtype),
        in_specs=[pl.BlockSpec(memory_space=pltpu.VMEM)],
        out_specs=pl.BlockSpec(memory_space=pltpu.VMEM),
        scratch_shapes=[pltpu.SemaphoreType.DMA] + [pltpu.SemaphoreType.DMA((ny,))] * 4,
        compiler_params=pltpu.CompilerParams(
            collective_id=collective_id, has_side_effects=True, vmem_limit_bytes=16 << 20
        ),
    )(x)
    return out.reshape(2 * ny * r, n)


class TensorReduce:
    count = 8

    @staticmethod
    def scratch(grid, r, width):
        ny = grid.ny
        sems = lambda *s: pltpu.SemaphoreType.DMA(s)
        vm = lambda *s: pltpu.VMEM(s, jnp.bfloat16)
        return [
            vm(ny, r, width), vm(ny, r, width), vm(ny - 1, r, width),
            sems(ny), sems(ny), sems(ny), sems(ny - 1), sems(ny - 1),
        ]

    def __init__(self, grid, source, out, scratch):
        self.grid, self.source, self.out = grid, source, out
        (
            self.acc, self.core_in, self.y_in, self.load_sem, self.core_s, self.core_r, self.ys, self.yr,
        ) = scratch
        self.spot = grid.here()

    def load(self, k):
        g, (a, b, y, c) = self.grid, self.spot
        return pltpu.make_async_copy(self.source.at[wrap(y + k, g.ny), c], self.acc.at[k], self.load_sem.at[k])

    def core_copy(self, k):
        g, (a, b, y, c) = self.grid, self.spot
        return pltpu.make_async_remote_copy(
            src_ref=self.source.at[wrap(y + k, g.ny), 1 - c], dst_ref=self.core_in.at[k],
            send_sem=self.core_s.at[k], recv_sem=self.core_r.at[k],
            device_id=g.device(a, b, y, 1 - c), device_id_type=MESH,
        )

    def y_copy(self, k):
        g, (a, b, y, c) = self.grid, self.spot
        return pltpu.make_async_remote_copy(
            src_ref=self.acc.at[k], dst_ref=self.y_in.at[k - 1], send_sem=self.ys.at[k - 1],
            recv_sem=self.yr.at[k - 1], device_id=g.device(a, b, wrap(y + k, g.ny), c), device_id_type=MESH,
        )

    def start(self):
        for k in reversed(range(self.grid.ny)):
            self.core_copy(k).start()
            self.load(k).start()

    def middle(self):
        f32 = jnp.float32
        for k in reversed(range(self.grid.ny)):
            self.load(k).wait()
            ref = self.core_in.at[k]
            pltpu.make_async_copy(ref, ref, self.core_r.at[k]).wait()
            total = self.acc[k].astype(f32) + self.core_in[k].astype(f32)
            self.acc[k] = total.astype(self.acc.dtype)
            if k:
                self.y_copy(k).start()

    def last(self):
        total = self.acc[0].astype(jnp.float32)
        for k in range(1, self.grid.ny):
            ref = self.y_in.at[k - 1]
            pltpu.make_async_copy(ref, ref, self.yr.at[k - 1]).wait()
            total = total + self.y_in[k - 1].astype(jnp.float32)
        self.out[...] = total

    def finish(self):
        for k in range(self.grid.ny):
            self.core_copy(k).wait_send()
            if k:
                self.y_copy(k).wait_send()


class TensorGather:
    count = 5

    @staticmethod
    def scratch(grid):
        return [pltpu.SemaphoreType.DMA((1,))] + [pltpu.SemaphoreType.DMA((grid.ny,))] * 4

    def __init__(self, grid, x, out, scratch):
        self.grid, self.x, self.out = grid, x, out
        self.own_sem, self.ys, self.yr, self.core_s, self.core_r = scratch
        self.spot = grid.here()

    def own(self):
        return pltpu.make_async_copy(self.x, self.out.at[self.spot[2], self.spot[3]], self.own_sem.at[0])

    def y_copy(self, k):
        g, (a, b, y, c) = self.grid, self.spot
        return pltpu.make_async_remote_copy(
            src_ref=self.x, dst_ref=self.out.at[y, c], send_sem=self.ys.at[k], recv_sem=self.yr.at[k],
            device_id=g.device(a, b, wrap(y + k, g.ny), c), device_id_type=MESH,
        )

    def core_copy(self, k):
        g, (a, b, y, c) = self.grid, self.spot
        spot = wrap(y + g.ny - k, g.ny)
        return pltpu.make_async_remote_copy(
            src_ref=self.x if k == 0 else self.out.at[spot, c], dst_ref=self.out.at[spot, c],
            send_sem=self.core_s.at[k], recv_sem=self.core_r.at[k],
            device_id=g.device(a, b, y, 1 - c), device_id_type=MESH,
        )

    def start(self):
        self.own().start()
        for k in range(1, self.grid.ny):
            self.y_copy(k).start()
        self.core_copy(0).start()

    def middle(self, i):
        if i == 1:
            for k in range(1, self.grid.ny):
                pltpu.make_async_copy(self.x, self.x, self.yr.at[k]).wait()
                self.core_copy(k).start()

    def last(self):
        self.own().wait()
        for k in range(self.grid.ny):
            pltpu.make_async_copy(self.x, self.x, self.core_r.at[k]).wait()
        for k in range(self.grid.ny):
            if k:
                self.y_copy(k).wait_send()
            self.core_copy(k).wait_send()


class PlaneReduce:
    count = 9

    @staticmethod
    def scratch(grid, r, width):
        na, nb = grid.na, grid.nb
        sems = lambda *s: pltpu.SemaphoreType.DMA(s)
        vm = lambda *s: pltpu.VMEM(s, jnp.bfloat16)
        return [
            vm(na, r, width), vm(nb - 1, na, r, width), vm(na - 1, r, width),
            sems(1), sems(nb - 1), sems(nb - 1), sems(na - 1), sems(na - 1), sems(1),
        ]

    def __init__(self, grid, source, out, scratch):
        self.grid, self.source, self.out = grid, source, out
        self.acc, self.b_in, self.a_in, self.load_sem, self.sb, self.rb, self.sa, self.ra, _ = scratch
        self.spot = grid.here()

    def load(self):
        return pltpu.make_async_copy(self.source.at[:, self.spot[1]], self.acc, self.load_sem.at[0])

    def copy_b(self, i):
        g, (a, b, y, c) = self.grid, self.spot
        return pltpu.make_async_remote_copy(
            src_ref=self.source.at[:, wrap(b + i, g.nb)], dst_ref=self.b_in.at[i - 1],
            send_sem=self.sb.at[i - 1], recv_sem=self.rb.at[i - 1],
            device_id=g.device(a, wrap(b + i, g.nb), y, c), device_id_type=MESH,
        )

    def copy_a(self, i):
        g, (a, b, y, c) = self.grid, self.spot
        return pltpu.make_async_remote_copy(
            src_ref=self.acc.at[wrap(a + i, g.na)], dst_ref=self.a_in.at[i - 1],
            send_sem=self.sa.at[i - 1], recv_sem=self.ra.at[i - 1],
            device_id=g.device(wrap(a + i, g.na), b, y, c), device_id_type=MESH,
        )

    def start(self):
        for i in range(1, self.grid.nb):
            self.copy_b(i).start()
        self.load().start()

    def middle(self):
        f32 = jnp.float32
        self.load().wait()
        for i in range(1, self.grid.nb):
            ref = self.b_in.at[i - 1]
            pltpu.make_async_copy(ref, ref, self.rb.at[i - 1]).wait()

            def one(m, carry):
                self.acc[m] = (self.acc[m].astype(f32) + ref[m].astype(f32)).astype(self.acc.dtype)
                return carry

            lax.fori_loop(0, self.grid.na, one, 0)
        for i in range(1, self.grid.na):
            self.copy_a(i).start()

    def last(self):
        total = self.acc[self.spot[0]].astype(jnp.float32)
        for i in range(1, self.grid.na):
            ref = self.a_in.at[i - 1]
            pltpu.make_async_copy(ref, ref, self.ra.at[i - 1]).wait()
            total = total + self.a_in[i - 1].astype(jnp.float32)
        self.out[...] = total.astype(self.out.dtype)

    def finish(self):
        for i in range(1, self.grid.nb):
            self.copy_b(i).wait_send()
        for i in range(1, self.grid.na):
            self.copy_a(i).wait_send()


class PlaneGather:
    count = 5

    @staticmethod
    def scratch(grid):
        na, nb = grid.na, grid.nb
        sems = lambda *s: pltpu.SemaphoreType.DMA(s)
        return [sems(1), sems(na - 1), sems(na, nb - 1), sems(na), sems(na, nb - 1)]

    def __init__(self, grid, x, out, scratch):
        self.grid, self.x, self.out = grid, x, out
        self.own_sem, self.sa, self.sb, self.ra, self.rb = scratch
        self.spot = grid.here()

    def own(self):
        return pltpu.make_async_copy(self.x, self.out.at[self.spot[0], self.spot[1]], self.own_sem.at[0])

    def copy_a(self, i):
        g, (a, b, y, c) = self.grid, self.spot
        return pltpu.make_async_remote_copy(
            src_ref=self.x, dst_ref=self.out.at[a, b], send_sem=self.sa.at[i - 1], recv_sem=self.ra.at[i],
            device_id=g.device(wrap(a + i, g.na), b, y, c), device_id_type=MESH,
        )

    def copy_b(self, i, k):
        g, (a, b, y, c) = self.grid, self.spot
        aa = wrap(a + g.na - i, g.na)
        return pltpu.make_async_remote_copy(
            src_ref=self.x if i == 0 else self.out.at[aa, b], dst_ref=self.out.at[aa, b],
            send_sem=self.sb.at[i, k - 1], recv_sem=self.rb.at[i, k - 1],
            device_id=g.device(a, wrap(b + k, g.nb), y, c), device_id_type=MESH,
        )

    def start(self):
        self.own().start()
        for i in range(1, self.grid.na):
            self.copy_a(i).start()
        for k in range(1, self.grid.nb):
            self.copy_b(0, k).start()

    def middle(self, i):
        ref = self.out.at[wrap(self.spot[0] + self.grid.na - i, self.grid.na), self.spot[1]]
        pltpu.make_async_copy(ref, ref, self.ra.at[i]).wait()
        for k in range(1, self.grid.nb):
            self.copy_b(i, k).start()

    def last(self):
        self.own().wait()
        ref = self.x
        for i in range(self.grid.na):
            for k in range(1, self.grid.nb):
                pltpu.make_async_copy(ref, ref, self.rb.at[i, k - 1]).wait()
        for i in range(1, self.grid.na):
            self.copy_a(i).wait_send()
        for i in range(self.grid.na):
            for k in range(1, self.grid.nb):
                self.copy_b(i, k).wait_send()


def last_kernel(
    grid, x_ref, w_ref, o_ref, t_ref, out_ref, w_out, o_out, t_out, own_sem, ss, rs, cs, cr, *scratch
):
    plane = TensorGather.count + PlaneGather.count
    gathers = [
        TensorGather(grid, t_ref, t_out, scratch[: TensorGather.count]),
        PlaneGather(grid, o_ref, o_out, scratch[TensorGather.count : plane]),
        PlaneGather(grid, w_ref, w_out, scratch[plane:]),
    ]
    gather_kernel(grid, x_ref, out_ref, own_sem, ss, rs, cs, cr, gathers)


def last_call(grid, x, w, o, t, collective_id):
    r, n = x.shape
    blocks = grid.na * grid.nb * grid.ny
    any_space = pl.BlockSpec(memory_space=pl.ANY)
    plane = (grid.na, grid.nb)
    outs = pl.pallas_call(
        functools.partial(last_kernel, grid),
        out_shape=[
            jax.ShapeDtypeStruct((grid.size, r, n), x.dtype),
            jax.ShapeDtypeStruct(plane + w.shape, w.dtype),
            jax.ShapeDtypeStruct(plane + o.shape, o.dtype),
            jax.ShapeDtypeStruct((grid.ny, 2) + t.shape, t.dtype),
        ],
        in_specs=[any_space] * 4,
        out_specs=[any_space] * 4,
        scratch_shapes=[
            pltpu.SemaphoreType.DMA,
            pltpu.SemaphoreType.DMA((gather_sends(grid),)),
            pltpu.SemaphoreType.DMA((2 * blocks,)),
            pltpu.SemaphoreType.DMA((2 * blocks,)),
            pltpu.SemaphoreType.DMA((2 * blocks,)),
        ]
        + TensorGather.scratch(grid)
        + PlaneGather.scratch(grid) * 2,
        compiler_params=pltpu.CompilerParams(collective_id=collective_id, has_side_effects=True),
    )(x, w, o, t)
    whole = lambda v: v.reshape(-1, v.shape[-1])
    return outs[0], whole(outs[1]), whole(outs[2]), whole(outs[3])


def dot_rows(left_side, right_side):
    return lax.dot_general(
        left_side, right_side, (((1,), (1,)), ((), ())), preferred_element_type=jnp.float32
    )


def dot_plain(left_side, right_side):
    return jnp.dot(left_side, right_side, preferred_element_type=jnp.float32)


def round_up(value, unit):
    return -(-value // unit) * unit


def experts_kernel(
    grid,
    pieces,
    x_ref,
    dz_ref,
    gate_ref,
    eg_hbm,
    eu_hbm,
    ed_hbm,
    sg_hbm,
    su_hbm,
    sd_hbm,
    all_ref,
    grad_ref,
    y_ref,
    acts_ref,
    gates,
    egu,
    ed,
    sgu,
    sd,
    dabuf,
    xbuf,
    dzbuf,
    gated,
    dcat,
    act,
    dsh,
    ybuf,
    dx,
    dx_out,
    core_in,
    d1_in0,
    d1_in1,
    d2_in0,
    d2_in1,
    a_in,
    gate_sem,
    weight_sem,
    own_sem,
    x_sem,
    dz_sem,
    out_sem,
    fill_sem,
    send_sem,
    recv_sem,
    share_send,
    share_recv,
    core_s,
    core_r,
    s10,
    r10,
    s11,
    r11,
    s20,
    r20,
    s21,
    r21,
    sa,
    ra,
):
    na, nb, ny = grid.na, grid.nb, grid.ny
    a, b, y, c = grid.here()
    r, n = x_ref.shape
    half, width, rows = r // 2, n // pieces, na * r
    pairs = nb * ny
    steps = 2 * pairs
    device = a * nb + b
    f, fs = ed_hbm.shape[1], sd_hbm.shape[0]
    wide, wide_s = egu.shape[0] // (2 * EXP_DEV), sd.shape[0]
    ef = EXP_DEV * wide
    columns = columns_of(ef, wide_s)
    f32, bf = jnp.float32, jnp.bfloat16
    fills = [(ed_hbm.at[e], ed, e * wide, f, wide) for e in range(EXP_DEV)]
    fills += [(sd_hbm, sd, 0, fs, wide_s)]
    fills += [(eg_hbm.at[e], egu, e * wide, f, wide) for e in range(EXP_DEV)]
    fills += [(eu_hbm.at[e], egu, ef + e * wide, f, wide) for e in range(EXP_DEV)]
    fills += [(sg_hbm, sgu, 0, fs, wide_s), (su_hbm, sgu, wide_s, fs, wide_s)]
    loads = [
        pltpu.make_async_copy(src, dst.at[pl.ds(at, real)], weight_sem.at[i])
        for i, (src, dst, at, real, _) in enumerate(fills)
    ]
    for load in loads:
        load.start()
    gate_load = pltpu.make_async_copy(gate_ref.at[:, :, :, :, :, pl.ds(LATENT, 128)], gates, gate_sem)
    gate_load.start()
    greet(grid)

    counts = [0]

    def place(bb, yy, cc, aa, h):
        return all_ref.at[aa, bb, yy, cc, pl.ds(h * half, half)]

    def slot(bb, yy, aa, h):
        return ((bb * ny + yy) * na + aa) * 2 + h

    def push(src, bb, yy, aa, h, where, send, recv):
        pltpu.make_async_remote_copy(
            src_ref=src,
            dst_ref=place(bb, yy, c, aa, h),
            send_sem=send,
            recv_sem=recv.at[slot(bb, yy, aa, h)],
            device_id=where,
            device_id_type=MESH,
        ).start()

    def line(i):
        if na != 4:
            return wrap(a + i, na)
        if i == 0:
            return a
        if i == 1:
            return a + 1 - 2 * lax.rem(a, 2)
        return (i - lax.div(a, 2)) if i == 2 else (3 - 3 * lax.div(a, 2))

    def onward(src, bb, yy, aa, h, dims):
        for d in dims:
            size = {"a": na, "b": nb, "y": ny}[d]
            for i in range(1, size):
                where = {
                    "a": lambda: grid.device(line(i), b, y, c),
                    "b": lambda: grid.device(a, wrap(b + i, nb), y, c),
                    "y": lambda: grid.device(a, b, wrap(y + i, ny), c),
                }[d]()
                push(src, bb, yy, aa, h, where, send_sem.at[counts[0]], recv_sem)
                counts[0] += 1
        push(
            src, bb, yy, aa, h, grid.device(a, b, y, 1 - c), share_send.at[slot(bb, yy, aa, h)], share_recv
        )

    def landed(bb, yy, cc, aa, h, sem):
        ref = place(bb, yy, cc, aa, h)
        pltpu.make_async_copy(ref, ref, sem.at[slot(bb, yy, aa, h)]).wait()
        return ref

    orders = (("b", "y"), ("y", "b"))

    def relay(j, k, i, h, dims):
        bb, yy, aa = wrap(b + j, nb), wrap(y + k, ny), line(i)
        onward(landed(bb, yy, c, aa, h, recv_sem), bb, yy, aa, h, dims)

    own = pltpu.make_async_copy(x_ref, all_ref.at[a, b, y, c], own_sem)
    own.start()
    for h in range(2):
        onward(x_ref.at[pl.ds(h * half, half)], b, y, a, h, ("a",) + orders[h])

    hooks = {}
    early = []
    for i in range(na):
        if i:
            early += [(0, 0, i, h, orders[h]) for h in range(2)]
        if i:
            early += [(j, 0, i - 1, 0, orders[0][1:]) for j in range(1, nb)]
            early += [(0, k, i - 1, 1, orders[1][1:]) for k in range(1, ny)]
    early += [(j, 0, na - 1, 0, orders[0][1:]) for j in range(1, nb)]
    early += [(0, k, na - 1, 1, orders[1][1:]) for k in range(1, ny)]
    for m, event in enumerate(early):
        place_at = 1 + m * (2 * steps - 1) // len(early)
        hooks.setdefault(("early", place_at // 2, place_at % 2), []).append(event)
    for pair in range(1, pairs):
        j, k = pair // ny, pair % ny
        late = [(j, k, i, h, ()) for i in range(na) for h in range(2) if (k if h == 0 else j)]
        for m, event in enumerate(late):
            hooks.setdefault(("main", pair, m * 3 // len(late)), []).append(event)

    def hook(stage, step, spot):
        for (when_stage, when, when_spot), events in hooks.items():
            if when_stage == stage and when_spot == spot:

                @pl.when(step == when)
                def _():
                    for event in events:
                        relay(*event)

    def spots(step):
        pair, l = lax.div(step, 2), 1 - lax.rem(step, 2)
        j, k = lax.div(pair, ny), lax.rem(pair, ny)
        return j, k, l, wrap(b + j, nb), wrap(y + k, ny), wrap(c + l, 2)

    def flat(value):
        return value.reshape(rows, value.shape[-1])

    def fold(value):
        return value.reshape(na, r, value.shape[-1])

    def dz_load(step):
        _, _, _, bb, yy, cc = spots(step)
        s = lax.rem(step, 2)
        return pltpu.make_async_copy(dz_ref.at[:, bb, yy, cc], dzbuf.at[s], dz_sem.at[s])

    dz_load(a * 0).start()
    for _, dst, at, real, padded in fills:
        if padded > real:
            dst[at + real : at + padded] = jnp.zeros((padded - real, n), bf)
    for load in loads[: EXP_DEV + 1]:
        load.wait()

    def early_body(step, carry):
        s = lax.rem(step, 2)

        @pl.when(step + 1 < steps)
        def _():
            dz_load(step + 1).start()

        dz_load(step).wait()
        dz = flat(dzbuf[s])
        dabuf[step, :, :ef] = dot_rows(dz, ed[...]).astype(bf)
        hook("early", step, 0)
        dabuf[step, :, ef:] = dot_rows(dz, sd[...]).astype(bf)
        hook("early", step, 1)
        return carry

    lax.fori_loop(0, steps, early_body, 0)
    for load in loads[EXP_DEV + 1 :]:
        load.wait()
    own.wait()
    gate_load.wait()

    def x_load(step):
        _, _, _, bb, yy, cc = spots(step)
        return pltpu.make_async_copy(all_ref.at[:, bb, yy, cc], xbuf.at[0], x_sem.at[0])

    def stores(step):
        _, _, _, bb, yy, cc = spots(step)
        s = lax.rem(step, 2)
        return [
            pltpu.make_async_copy(
                gated.at[s], acts_ref.at[:, bb, yy, cc, :, pl.ds(columns[2], ef)], out_sem.at[s, 0]
            ),
            pltpu.make_async_copy(
                dcat.at[s], acts_ref.at[:, bb, yy, cc, :, pl.ds(columns[0], 2 * ef)], out_sem.at[s, 1]
            ),
        ]

    def remote(src, dst, ss, rs, where):
        return pltpu.make_async_remote_copy(
            src_ref=src, dst_ref=dst, send_sem=ss, recv_sem=rs, device_id=where, device_id_type=MESH
        )

    def cols(p):
        return pl.ds(p * width, width)

    upper = (pl.ds(0, half), pl.ds(half, half))

    def send_core(pair):
        j, k = lax.div(pair, ny), lax.rem(pair, ny)
        return remote(
            dx_out.at[lax.rem(pair, 2)], core_in.at[j, k], core_s.at[lax.rem(pair, 2)],
            core_r.at[j, k], grid.device(a, b, y, 1 - c),
        )

    def send_10(p, j, k):
        return remote(
            dx.at[j, k, :, upper[0], cols(p)], d1_in0.at[p, j, k - 1], s10.at[p, j, k - 1],
            r10.at[p, j, k - 1], grid.device(a, b, wrap(y + k, ny), c),
        )

    def send_11(p, j, k):
        return remote(
            dx.at[j, k, :, upper[1], cols(p)], d1_in1.at[p, k, j - 1], s11.at[p, k, j - 1],
            r11.at[p, k, j - 1], grid.device(a, wrap(b + j, nb), y, c),
        )

    def await_in(ref, sem):
        pltpu.make_async_copy(ref, ref, sem).wait()

    def add(dst, src):
        dst[...] = (dst[...].astype(f32) + src[...].astype(f32)).astype(dst.dtype)

    def shared_front(step, x, s):
        g = dot_rows(x, sgu[:wide_s])
        u = dot_rows(x, sgu[wide_s:])
        d = dabuf[step, :, ef:].astype(f32)
        sig = 1.0 / (1.0 + jnp.exp(-g))
        swish = g * sig
        act[s] = fold((swish * u).astype(bf))
        dsh[s, :, :, :wide_s] = fold((d * u * (sig + swish * (1.0 - sig))).astype(bf))
        dsh[s, :, :, wide_s:] = fold((d * swish).astype(bf))

    def is_mine(bb, yy, cc):
        return lax.rem((bb * ny + yy) * 2 + cc, na * nb) == device

    chunk = min(n, 1024)

    def main_body(step, carry):
        j, k, l, bb, yy, cc = spots(step)
        s = lax.rem(step, 2)

        @pl.when(l == 1)
        def _():
            for i in range(na):
                for h in range(2):
                    landed(bb, yy, cc, line(i), h, share_recv)

        x_load(step).start()

        @pl.when(step >= 2)
        def _():
            for store in stores(step - 2):
                store.wait()

        x_load(step).wait()
        x = flat(xbuf[0])
        g = dot_rows(x, egu[:ef])
        u = dot_rows(x, egu[ef:])
        gate = flat(gates[:, bb, yy, cc]).astype(f32)
        lane = lax.broadcasted_iota(jnp.int32, gate.shape, 1) - (ROPE + EXP_DEV * device)
        experts_all = EXP_DEV * na * nb
        for e in range(EXP_DEV):
            at = pl.ds(e * wide, wide)
            hit = (lane == e) | (lane == e + experts_all)
            scale = jnp.sum(jnp.where(hit, gate, 0.0), axis=-1, keepdims=True)
            ge, ue = g[:, e * wide : (e + 1) * wide], u[:, e * wide : (e + 1) * wide]
            d = dabuf[step, :, at].astype(f32) * scale
            sig = 1.0 / (1.0 + jnp.exp(-ge))
            swish = ge * sig
            gated[s, :, :, at] = fold((scale * (swish * ue)).astype(bf))
            dcat[s, :, :, at] = fold((d * ue * (sig + swish * (1.0 - sig))).astype(bf))
            dcat[s, :, :, pl.ds(ef + e * wide, wide)] = fold((d * swish).astype(bf))
        hook("main", step, 0)
        mine = is_mine(bb, yy, cc)

        @pl.when(mine)
        def _():
            shared_front(step, x, 0)

        hook("main", step, 1)

        def column(target):
            for q in range(n // chunk):
                at = pl.ds(q * chunk, chunk)
                total = dot_plain(flat(dcat[s]), egu[:, at])
                target[:, :, at] = fold(total.astype(bf))

            @pl.when(mine)
            def _():
                for q in range(n // chunk):
                    at = pl.ds(q * chunk, chunk)
                    more = dot_plain(flat(dsh[0]), sgu[:, at])
                    target[:, :, at] = fold((flat(target[:, :, at]).astype(f32) + more).astype(bf))

        for store in stores(step):
            store.start()

        @pl.when(l == 1)
        def _():
            pair = lax.div(step, 2)

            @pl.when(pair >= 2)
            def _():
                send_core(pair - 2).wait_send()

            column(dx_out.at[lax.rem(pair, 2)])
            send_core(pair).start()

        @pl.when(l == 0)
        def _():
            column(dx.at[j, k])
            await_in(core_in.at[j, k], core_r.at[j, k])

            def one(i, carry):
                add(dx.at[j, k, i], core_in.at[j, k, i])
                return carry

            lax.fori_loop(0, na, one, 0)

            @pl.when(k > 0)
            def _():
                for p in range(pieces):
                    send_10(p, j, k).start()

            @pl.when(j > 0)
            def _():
                for p in range(pieces):
                    send_11(p, j, k).start()

        hook("main", step, 2)
        return carry

    lax.fori_loop(0, steps, main_body, 0)
    for step in (steps - 2, steps - 1):
        for store in stores(a * 0 + step):
            store.wait()

    def send_20(p, j):
        return remote(
            dx.at[j, 0, :, upper[0], cols(p)], d2_in0.at[p, j - 1], s20.at[p, j - 1],
            r20.at[p, j - 1], grid.device(a, wrap(b + j, nb), y, c),
        )

    def send_21(p, k):
        return remote(
            dx.at[0, k, :, upper[1], cols(p)], d2_in1.at[p, k - 1], s21.at[p, k - 1],
            r21.at[p, k - 1], grid.device(a, b, wrap(y + k, ny), c),
        )

    def send_a(p, i):
        return remote(
            dx.at[0, 0, wrap(a + i, na), :, cols(p)], a_in.at[p, i - 1], sa.at[p, i - 1],
            ra.at[p, i - 1], grid.device(wrap(a + i, na), b, y, c),
        )

    def sum_first(p):
        for j in reversed(range(nb)):
            for k in range(1, ny):
                await_in(d1_in0.at[p, j, k - 1], r10.at[p, j, k - 1])
                for i in range(na):
                    add(dx.at[j, 0, i, upper[0], cols(p)], d1_in0.at[p, j, k - 1, i])
            if j:
                send_20(p, j).start()
        for k in reversed(range(ny)):
            for j in range(1, nb):
                await_in(d1_in1.at[p, k, j - 1], r11.at[p, k, j - 1])
                for i in range(na):
                    add(dx.at[0, k, i, upper[1], cols(p)], d1_in1.at[p, k, j - 1, i])
            if k:
                send_21(p, k).start()

    def sum_second(p):
        for j in range(1, nb):
            await_in(d2_in0.at[p, j - 1], r20.at[p, j - 1])
            for i in range(na):
                add(dx.at[0, 0, i, upper[0], cols(p)], d2_in0.at[p, j - 1, i])
        for k in range(1, ny):
            await_in(d2_in1.at[p, k - 1], r21.at[p, k - 1])
            for i in range(na):
                add(dx.at[0, 0, i, upper[1], cols(p)], d2_in1.at[p, k - 1, i])
        for i in range(1, na):
            send_a(p, i).start()

    def sum_last(p):
        total = dx[0, 0, a, :, cols(p)].astype(f32)
        for i in range(1, na):
            await_in(a_in.at[p, i - 1], ra.at[p, i - 1])
            total = total + a_in[p, i - 1].astype(f32)
        grad_ref[:, cols(p)] = total

    work = [(sum_first, p) for p in range(pieces)] + [(sum_second, p) for p in range(pieces)]
    turns = {}
    for m, item in enumerate(work):
        turns.setdefault(min(steps - 1, 1 + m * (steps - 1) // len(work)), []).append(item)

    def fill_loads(step):
        _, _, _, bb, yy, cc = spots(step)
        s = lax.rem(step, 2)
        return [
            pltpu.make_async_copy(all_ref.at[:, bb, yy, cc], xbuf.at[s], x_sem.at[s]),
            pltpu.make_async_copy(
                acts_ref.at[:, bb, yy, cc, :, pl.ds(columns[2], ef)], gated.at[s], fill_sem.at[s]
            ),
        ]

    def fill_stores(step):
        _, _, _, bb, yy, cc = spots(step)
        s = lax.rem(step, 2)
        pairs_of = [
            (act.at[s], acts_ref.at[:, bb, yy, cc, :, pl.ds(columns[3], wide_s)]),
            (dsh.at[s], acts_ref.at[:, bb, yy, cc, :, pl.ds(columns[1], 2 * wide_s)]),
            (ybuf.at[s], y_ref.at[:, bb, yy, cc]),
        ]
        return [
            pltpu.make_async_copy(src, dst, out_sem.at[s, i])
            for i, (src, dst) in enumerate(pairs_of)
        ]

    for load in fill_loads(a * 0):
        load.start()

    def fill_body(step, carry):
        j, k, l, bb, yy, cc = spots(step)
        s = lax.rem(step, 2)

        @pl.when(step + 1 < steps)
        def _():
            for load in fill_loads(step + 1):
                load.start()

        @pl.when(step >= 2)
        def _():
            for store in fill_stores(step - 2):
                store.wait()

        for load in fill_loads(step):
            load.wait()
        x = flat(xbuf[s])
        shared_front(step, x, s)
        for q in range(n // chunk):
            at = pl.ds(q * chunk, chunk)
            ybuf[s, :, :, at] = fold(dot_plain(flat(gated[s]), ed[:, at]).astype(bf))

        @pl.when(is_mine(bb, yy, cc))
        def _():
            for q in range(n // chunk):
                at = pl.ds(q * chunk, chunk)
                more = dot_plain(flat(act[s]), sd[:, at])
                ybuf[s, :, :, at] = fold((flat(ybuf[s, :, :, at]).astype(f32) + more).astype(bf))

        for store in fill_stores(step):
            store.start()
        for when, items in turns.items():

            @pl.when(step == when)
            def _():
                for item, p in items:
                    item(p)

        return carry

    lax.fori_loop(0, steps, fill_body, 0)
    for p in range(pieces):
        sum_last(p)

    for step in (steps - 2, steps - 1):
        for store in fill_stores(a * 0 + step):
            store.wait()
    some = place(b, y, c, a, 0)
    for i in range(counts[0]):
        pltpu.make_async_copy(some, some, send_sem.at[i]).wait()
    for i in range(2 * na * pairs):
        pltpu.make_async_copy(some, some, share_send.at[i]).wait()
    for pair in range(max(0, pairs - 2), pairs):
        send_core(a * 0 + pair).wait_send()
    for p in range(pieces):
        for j in range(nb):
            for k in range(ny):
                if k:
                    send_10(p, j, k).wait_send()
                if j:
                    send_11(p, j, k).wait_send()
        for j in range(1, nb):
            send_20(p, j).wait_send()
        for k in range(1, ny):
            send_21(p, k).wait_send()
        for i in range(1, na):
            send_a(p, i).wait_send()


def columns_of(ef, wide_s):
    return (0, 2 * ef, 2 * ef + 2 * wide_s, 3 * ef + 2 * wide_s, 3 * ef + 3 * wide_s)


def experts_call(
    grid, x, dz, gates, expert_gate, expert_up, expert_down, shared_gate, shared_up, shared_down,
    collective_id, pieces=2,
):
    r, n = x.shape
    na, nb, ny = grid.na, grid.nb, grid.ny
    f, fs = expert_down.shape[1], shared_down.shape[0]
    wide, wide_s = round_up(f, 128), round_up(fs, 128)
    ef = EXP_DEV * wide
    half, width, rows = r // 2, n // pieces, na * r
    steps = 2 * nb * ny
    lay = (na, nb, ny, 2, r)
    bf = jnp.bfloat16
    sems = lambda *s: pltpu.SemaphoreType.DMA(s)
    vm = lambda *s: pltpu.VMEM(s, bf)
    sends = 2 * (na - 1 + na * (nb - 1) + na * (ny - 1) + na * (nb - 1) * (ny - 1))
    any_space = pl.BlockSpec(memory_space=pl.ANY)
    in_vmem = pl.BlockSpec(memory_space=pltpu.VMEM)
    outs = pl.pallas_call(
        functools.partial(experts_kernel, grid, pieces),
        out_shape=[
            jax.ShapeDtypeStruct(lay + (n,), bf),
            jax.ShapeDtypeStruct((r, n), jnp.float32),
            jax.ShapeDtypeStruct(lay + (n,), bf),
            jax.ShapeDtypeStruct(lay + (columns_of(ef, wide_s)[-1],), bf),
        ],
        in_specs=[any_space] * 9,
        out_specs=[any_space, in_vmem] + [any_space] * 2,
        scratch_shapes=[
            vm(*lay, 128), vm(2 * ef, n), vm(ef, n), vm(2 * wide_s, n), vm(wide_s, n),
            vm(steps, rows, ef + wide_s),
            vm(2, na, r, n), vm(2, na, r, n),
            vm(2, na, r, ef), vm(2, na, r, 2 * ef),
            vm(2, na, r, wide_s), vm(2, na, r, 2 * wide_s),
            vm(2, na, r, n),
            vm(nb, ny, na, r, n),
            vm(2, na, r, n),
            vm(nb, ny, na, r, n),
            vm(pieces, nb, ny - 1, na, half, width),
            vm(pieces, ny, nb - 1, na, half, width),
            vm(pieces, nb - 1, na, half, width),
            vm(pieces, ny - 1, na, half, width),
            vm(pieces, na - 1, r, width),
            pltpu.SemaphoreType.DMA, sems(3 * EXP_DEV + 3), pltpu.SemaphoreType.DMA, sems(2), sems(2),
            sems(2, 4), sems(2),
            sems(sends), sems(2 * na * nb * ny), sems(2 * na * nb * ny), sems(2 * na * nb * ny),
            sems(2), sems(nb, ny),
            sems(pieces, nb, ny - 1), sems(pieces, nb, ny - 1),
            sems(pieces, ny, nb - 1), sems(pieces, ny, nb - 1),
            sems(pieces, nb - 1), sems(pieces, nb - 1),
            sems(pieces, ny - 1), sems(pieces, ny - 1),
            sems(pieces, na - 1), sems(pieces, na - 1),
        ],
        compiler_params=pltpu.CompilerParams(
            collective_id=collective_id, has_side_effects=True, vmem_limit_bytes=63 << 20
        ),
    )(
        x,
        dz.reshape(lay + (n,)),
        gates.reshape(lay + (gates.shape[-1],)),
        jnp.swapaxes(expert_gate, 1, 2), jnp.swapaxes(expert_up, 1, 2), expert_down,
        shared_gate.T, shared_up.T, shared_down,
    )
    tokens = grid.size * r
    rows_all, grad, out_rows, acts = outs
    return rows_all.reshape(tokens, n), grad, out_rows.reshape(tokens, n), acts.reshape(tokens, -1)


class Reduce:
    @staticmethod
    def scratch(grid, r, width):
        na, nb, ny = grid.na, grid.nb, grid.ny
        head = Reduce.head(r)
        sems = lambda *s: pltpu.SemaphoreType.DMA(s)
        vm = lambda *s: pltpu.VMEM(s, jnp.bfloat16)
        return [
            vm(nb, ny, na, r, width), vm(nb, ny, na, r, width),
            vm(nb, ny - 1, na, head, width), vm(ny, nb - 1, na, r - head, width),
            vm(nb - 1, na, head, width), vm(ny - 1, na, r - head, width), vm(na - 1, r, width),
            sems(nb, ny), sems(nb, ny), sems(nb, ny),
            sems(nb, ny - 1), sems(nb, ny - 1), sems(ny, nb - 1), sems(ny, nb - 1),
            sems(nb - 1), sems(nb - 1), sems(ny - 1), sems(ny - 1), sems(na - 1), sems(na - 1),
        ]

    count = 20

    @staticmethod
    def head(r):
        return max(16, r * 3 // 4 // 16 * 16)

    def __init__(self, grid, source, out, scratch):
        self.grid, self.source, self.out = grid, source, out
        (
            self.acc, self.core_in, self.in10, self.in11, self.in20, self.in21, self.a_in,
            self.load_sem, self.core_s, self.core_r, self.s10, self.r10, self.s11, self.r11,
            self.s20, self.r20, self.s21, self.r21, self.sa, self.ra,
        ) = scratch
        self.spot = grid.here()
        r = self.acc.shape[3]
        head = Reduce.head(r)
        self.upper = (pl.ds(0, head), pl.ds(head, r - head))
        self.spots = [(j, k) for j in reversed(range(grid.nb)) for k in reversed(range(grid.ny))]

    def remote(self, src, dst, ss, rs, where):
        return pltpu.make_async_remote_copy(
            src_ref=src, dst_ref=dst, send_sem=ss, recv_sem=rs, device_id=where, device_id_type=MESH
        )

    def core_copy(self, j, k):
        g, (a, b, y, c) = self.grid, self.spot
        return self.remote(
            self.source.at[:, wrap(b + j, g.nb), wrap(y + k, g.ny), 1 - c], self.core_in.at[j, k],
            self.core_s.at[j, k], self.core_r.at[j, k], g.device(a, b, y, 1 - c),
        )

    def load(self, j, k):
        g, (a, b, y, c) = self.grid, self.spot
        return pltpu.make_async_copy(
            self.source.at[:, wrap(b + j, g.nb), wrap(y + k, g.ny), c], self.acc.at[j, k], self.load_sem.at[j, k]
        )

    def copy10(self, j, k):
        g, (a, b, y, c) = self.grid, self.spot
        return self.remote(
            self.acc.at[j, k, :, self.upper[0]], self.in10.at[j, k - 1], self.s10.at[j, k - 1],
            self.r10.at[j, k - 1], g.device(a, b, wrap(y + k, g.ny), c),
        )

    def copy11(self, j, k):
        g, (a, b, y, c) = self.grid, self.spot
        return self.remote(
            self.acc.at[j, k, :, self.upper[1]], self.in11.at[k, j - 1], self.s11.at[k, j - 1],
            self.r11.at[k, j - 1], g.device(a, wrap(b + j, g.nb), y, c),
        )

    def copy20(self, j):
        g, (a, b, y, c) = self.grid, self.spot
        return self.remote(
            self.acc.at[j, 0, :, self.upper[0]], self.in20.at[j - 1], self.s20.at[j - 1],
            self.r20.at[j - 1], g.device(a, wrap(b + j, g.nb), y, c),
        )

    def copy21(self, k):
        g, (a, b, y, c) = self.grid, self.spot
        return self.remote(
            self.acc.at[0, k, :, self.upper[1]], self.in21.at[k - 1], self.s21.at[k - 1],
            self.r21.at[k - 1], g.device(a, b, wrap(y + k, g.ny), c),
        )

    def copy_a(self, i):
        g, (a, b, y, c) = self.grid, self.spot
        return self.remote(
            self.acc.at[0, 0, wrap(a + i, g.na)], self.a_in.at[i - 1], self.sa.at[i - 1],
            self.ra.at[i - 1], g.device(wrap(a + i, g.na), b, y, c),
        )

    def add(self, into, rows, ref, sem):
        pltpu.make_async_copy(ref, ref, sem).wait()
        f32 = jnp.float32

        def one(i, carry):
            total = into[i, rows].astype(f32) + ref[i].astype(f32)
            into[i, rows] = total.astype(into.dtype)
            return carry

        lax.fori_loop(0, self.grid.na, one, 0)

    def start(self):
        for j, k in self.spots:
            self.core_copy(j, k).start()
            self.load(j, k).start()

    def core(self):
        whole = pl.ds(0, self.acc.shape[3])
        for j, k in self.spots:
            self.load(j, k).wait()
            self.add(self.acc.at[j, k], whole, self.core_in.at[j, k], self.core_r.at[j, k])
            if k:
                self.copy10(j, k).start()
            if j:
                self.copy11(j, k).start()

    def first(self):
        nb, ny = self.grid.nb, self.grid.ny
        for j in reversed(range(nb)):
            for k in range(1, ny):
                self.add(self.acc.at[j, 0], self.upper[0], self.in10.at[j, k - 1], self.r10.at[j, k - 1])
            if j:
                self.copy20(j).start()
        for k in reversed(range(ny)):
            for j in range(1, nb):
                self.add(self.acc.at[0, k], self.upper[1], self.in11.at[k, j - 1], self.r11.at[k, j - 1])
            if k:
                self.copy21(k).start()

    def second(self):
        for j in range(1, self.grid.nb):
            self.add(self.acc.at[0, 0], self.upper[0], self.in20.at[j - 1], self.r20.at[j - 1])
        for k in range(1, self.grid.ny):
            self.add(self.acc.at[0, 0], self.upper[1], self.in21.at[k - 1], self.r21.at[k - 1])
        for i in range(1, self.grid.na):
            self.copy_a(i).start()

    def last(self):
        total = self.acc[0, 0, self.spot[0]].astype(jnp.float32)
        for i in range(1, self.grid.na):
            pltpu.make_async_copy(self.a_in.at[i - 1], self.a_in.at[i - 1], self.ra.at[i - 1]).wait()
            total = total + self.a_in[i - 1].astype(jnp.float32)
        self.out[...] = total.astype(self.out.dtype)

    def finish(self):
        for j, k in self.spots:
            self.core_copy(j, k).wait_send()
            if k:
                self.copy10(j, k).wait_send()
            if j:
                self.copy11(j, k).wait_send()
        for j in range(1, self.grid.nb):
            self.copy20(j).wait_send()
        for k in range(1, self.grid.ny):
            self.copy21(k).wait_send()
        for i in range(1, self.grid.na):
            self.copy_a(i).wait_send()


W_PIECES = 1


def gradients_kernel(grid, pieces, unit, places, *refs):
    (y_ref, k_ref, w_ref, t_ref, q_ref, x_ref, dz_ref, acts_ref), refs = refs[:8], refs[8:]
    (y_out, k_out, w_out, t_out, q_out), refs = refs[:5], refs[5:]
    outs, refs = refs[:6], refs[6:]
    (big, left, right, big_sem, left_sem, out_sem), refs = refs[:6], refs[6:]
    width = y_ref.shape[-1] // pieces
    sources = [(k_ref, k_out)]
    for p in range(pieces):
        at = pl.ds(p * width, width)
        sources.append((y_ref.at[:, :, :, :, :, at], y_out.at[:, at]))
    sums = [
        Reduce(grid, src, out, refs[m * Reduce.count : (m + 1) * Reduce.count])
        for m, (src, out) in enumerate(sources)
    ]
    refs = refs[len(sums) * Reduce.count :]
    w_width = w_ref.shape[-1] // W_PIECES
    flat_sums = []
    for p in range(W_PIECES):
        at = pl.ds(p * w_width, w_width)
        part = refs[p * PlaneReduce.count : (p + 1) * PlaneReduce.count]
        flat_sums.append(PlaneReduce(grid, w_ref.at[:, :, :, at], w_out.at[:, at], part))
    refs = refs[W_PIECES * PlaneReduce.count :]
    flat_sums.append(TensorReduce(grid, t_ref, t_out, refs[: TensorReduce.count]))
    q_gather = PlaneGather(grid, q_ref, q_out, refs[TensorReduce.count :])
    tiles = len(places)
    turn = sum(1 for place in places if place[0] != 2 and place[0] != 5)
    slots = big.shape[0]

    def left_load(m):
        s = lax.rem(m, 2)
        at = pl.ds(pl.multiple_of(m * unit, unit), unit)
        return pltpu.make_async_copy(acts_ref.at[:, at], left.at[s], left_sem.at[s])

    big_loads = [
        pltpu.make_async_copy(src, big.at[s % slots], big_sem.at[s]) for s, src in enumerate((x_ref, dz_ref))
    ]
    big_loads[0].start()
    greet(grid)
    for one in sums + flat_sums + [q_gather]:
        one.start()
    left_load(grid.here()[0] * 0).start()
    if slots > 1:
        big_loads[1].start()
    big_loads[0].wait()

    stages = [[one.core, one.first, one.second] for one in sums]
    work = []
    for beat in range(len(sums) + 2):
        for back in range(3):
            if 0 <= beat - back < len(sums):
                work.append(stages[beat - back][back])
    for p, one in enumerate(flat_sums):
        work.insert(min(len(work), 3 + 3 * p), one.middle)
    for i in range(1, grid.na):
        work.insert(min(len(work), 3 + 3 * i), functools.partial(q_gather.middle, i))
    turns = {}
    for n, item in enumerate(work):
        turns.setdefault(n * tiles // len(work), []).append(item)

    def store(m):
        which, head, first, rows = places[m]
        dst = outs[which]
        dst = dst.at[pl.ds(first, rows)] if head is None else dst.at[head, pl.ds(first, rows)]
        return pltpu.make_async_copy(right.at[m % 2, pl.ds(0, rows)], dst, out_sem.at[m % 2])

    def tile_body(m, carry):
        s = lax.rem(m, 2)

        @pl.when(m + 1 < tiles)
        def _():
            left_load(m + 1).start()

        for n in range(2, tiles):

            @pl.when(m == n)
            def _():
                store(n - 2).wait()

        @pl.when(m == turn)
        def _():
            if slots == 1:
                big_loads[1].start()
            big_loads[1].wait()

        left_load(m).wait()
        operand = big.at[lax.div(m, turn) if slots > 1 else 0]
        right[s] = lax.dot_general(
            left[s], operand[...], (((0,), (0,)), ((), ())), preferred_element_type=jnp.float32
        ).astype(right.dtype)
        for n in range(tiles):

            @pl.when(m == n)
            def _():
                store(n).start()
                for item in turns.get(n, ()):
                    item()

        return carry

    lax.fori_loop(0, tiles, tile_body, 0)
    for one in sums + flat_sums:
        one.last()
    for n in range(max(0, tiles - 2), tiles):
        store(n).wait()
    for one in sums + flat_sums:
        one.finish()
    q_gather.last()


def gradients_call(grid, out_rows, key_rows, weight_rows, tensor_rows, query_rows, x, dz, acts, f, fs, collective_id, pieces=4):
    tokens, n = x.shape
    r = tokens // grid.size
    lay = (grid.na, grid.nb, grid.ny, 2, r)
    wide, wide_s = round_up(f, 128), round_up(fs, 128)
    unit = math.gcd(wide, wide_s)
    places = []
    for which, heads, real, padded in (
        (0, EXP_DEV, f, wide), (1, EXP_DEV, f, wide), (3, 0, fs, wide_s), (4, 0, fs, wide_s),
        (2, EXP_DEV, f, wide), (5, 0, fs, wide_s),
    ):
        for head in range(max(heads, 1)):
            for first in range(0, padded, unit):
                places.append((which, head if heads else None, first, min(unit, real - first)))
    slots = 2 if 2 * tokens * n * 2 <= (24 << 20) else 1
    any_space = pl.BlockSpec(memory_space=pl.ANY)
    in_vmem = pl.BlockSpec(memory_space=pltpu.VMEM)
    f32 = jnp.float32
    scratch = [
        pltpu.VMEM((slots, tokens, n), x.dtype),
        pltpu.VMEM((2, tokens, unit), x.dtype),
        pltpu.VMEM((2, unit, n), x.dtype),
        pltpu.SemaphoreType.DMA((2,)),
        pltpu.SemaphoreType.DMA((2,)),
        pltpu.SemaphoreType.DMA((2,)),
    ]
    kw = key_rows.shape[1]
    for width in [kw] + [n // pieces] * pieces:
        scratch += Reduce.scratch(grid, r, width)
    wr, ww = weight_rows.shape[0] // (grid.na * grid.nb), weight_rows.shape[1]
    scratch += PlaneReduce.scratch(grid, wr, ww // W_PIECES) * W_PIECES
    tr, tw = tensor_rows.shape[0] // (2 * grid.ny), tensor_rows.shape[1]
    scratch += TensorReduce.scratch(grid, tr, tw) + PlaneGather.scratch(grid)
    outs = pl.pallas_call(
        functools.partial(gradients_kernel, grid, pieces, unit, places),
        out_shape=[
            jax.ShapeDtypeStruct((r, n), f32),
            jax.ShapeDtypeStruct((r, kw), f32),
            jax.ShapeDtypeStruct((wr, ww), x.dtype),
            jax.ShapeDtypeStruct((tr, tw), f32),
            jax.ShapeDtypeStruct((grid.na, grid.nb) + query_rows.shape, x.dtype),
            jax.ShapeDtypeStruct((EXP_DEV, f, n), x.dtype),
            jax.ShapeDtypeStruct((EXP_DEV, f, n), x.dtype),
            jax.ShapeDtypeStruct((EXP_DEV, f, n), x.dtype),
            jax.ShapeDtypeStruct((fs, n), x.dtype),
            jax.ShapeDtypeStruct((fs, n), x.dtype),
            jax.ShapeDtypeStruct((fs, n), x.dtype),
        ],
        in_specs=[any_space] * 8,
        out_specs=[in_vmem] * 4 + [any_space] * 7,
        scratch_shapes=scratch,
        compiler_params=pltpu.CompilerParams(
            collective_id=collective_id, has_side_effects=True, vmem_limit_bytes=62 << 20
        ),
    )(
        out_rows.reshape(lay + (n,)),
        key_rows.reshape(lay + (kw,)),
        weight_rows.reshape(grid.na, grid.nb, wr, ww),
        tensor_rows.reshape(grid.ny, 2, tr, tw),
        query_rows,
        x,
        dz,
        acts,
    )
    y_sum, k_sum, w_sum, t_sum, q_all = outs[:5]
    eg, eu, ed, sg, su, sd = (out.astype(f32) for out in outs[5:])
    q_all = q_all.reshape(tokens, -1)
    weights = (jnp.swapaxes(eg, 1, 2), jnp.swapaxes(eu, 1, 2), ed, sg.T, su.T, sd)
    return y_sum, k_sum, w_sum, t_sum, q_all, weights


class GatherAll:
    @staticmethod
    def scratch(grid):
        blocks = 2 * grid.na * grid.nb * grid.ny
        sems = lambda n: pltpu.SemaphoreType.DMA((n,))
        return [sems(1), sems(gather_sends(grid)), sems(blocks), sems(blocks), sems(blocks)]

    def __init__(self, grid, x, out, scratch, halves=2):
        self.grid, self.x, self.out, self.halves = grid, x, out, halves
        self.own_sem, self.sends, self.recvs, self.share_s, self.share_r = scratch
        self.spot = grid.here()
        self.half = x.shape[0] // halves
        self.count = 0
        na, nb, ny = grid.na, grid.nb, grid.ny
        self.orders = (("b", "y"), ("y", "b"))
        near = [(0, k, 0, 0, ()) for k in range(1, ny)] + [(0, k, 0, 1, ("b",)) for k in range(1, ny)]
        first = [(0, 0, i, h, self.orders[h]) for i in range(1, na) for h in range(2)]
        second = []
        for i in range(na):
            second += [(j, 0, i, 0, ("y",)) for j in range(1, nb)]
            second += [(0, k, i, 1, ("b",)) for k in range(1, ny) if i]
        third = []
        for i in range(na):
            third += [(0, k, i, 0, ()) for k in range(1, ny) if i]
            third += [(j, 0, i, 1, ()) for j in range(1, nb)]
        for i in range(na):
            third += [(j, k, i, h, ()) for j in range(1, nb) for k in range(1, ny) for h in range(2)]
        self.near = [event for event in near if event[3] < halves]
        self.others = [event for event in first + second + third if event[3] < halves]

    def line(self, i):
        a = self.spot[0]
        if self.grid.na != 4:
            return wrap(a + i, self.grid.na)
        if i == 0:
            return a
        if i == 1:
            return a + 1 - 2 * lax.rem(a, 2)
        return (i - lax.div(a, 2)) if i == 2 else (3 - 3 * lax.div(a, 2))

    def place(self, bb, yy, cc, aa, h):
        return self.out.at[aa, bb, yy, cc, pl.ds(h * self.half, self.half)]

    def slot(self, bb, yy, aa, h):
        return ((bb * self.grid.ny + yy) * self.grid.na + aa) * 2 + h

    def push(self, src, bb, yy, aa, h, where, send, recv):
        pltpu.make_async_remote_copy(
            src_ref=src, dst_ref=self.place(bb, yy, self.spot[3], aa, h), send_sem=send,
            recv_sem=recv.at[self.slot(bb, yy, aa, h)], device_id=where, device_id_type=MESH,
        ).start()

    def onward(self, src, bb, yy, aa, h, dims):
        g, (a, b, y, c) = self.grid, self.spot
        for d in dims:
            for i in range(1, {"a": g.na, "b": g.nb, "y": g.ny}[d]):
                if d == "a":
                    where = g.device(self.line(i), b, y, c)
                elif d == "b":
                    where = g.device(a, wrap(b + i, g.nb), y, c)
                else:
                    where = g.device(a, b, wrap(y + i, g.ny), c)
                self.push(src, bb, yy, aa, h, where, self.sends.at[self.count], self.recvs)
                self.count += 1
        where = g.device(a, b, y, 1 - c)
        self.push(src, bb, yy, aa, h, where, self.share_s.at[self.slot(bb, yy, aa, h)], self.share_r)

    def landed(self, bb, yy, cc, aa, h, sem):
        ref = self.place(bb, yy, cc, aa, h)
        pltpu.make_async_copy(ref, ref, sem.at[self.slot(bb, yy, aa, h)]).wait()
        return ref

    def own(self):
        a, b, y, c = self.spot
        return pltpu.make_async_copy(self.x, self.out.at[a, b, y, c], self.own_sem.at[0])

    def start(self):
        a, b, y, c = self.spot
        self.own().start()
        for h in range(self.halves):
            src = self.x.at[pl.ds(h * self.half, self.half)]
            self.onward(src, b, y, a, h, ("y", "a", "b") if h == 0 else ("y", "b", "a"))

    def relay(self, j, k, i, h, dims):
        g, (a, b, y, c) = self.grid, self.spot
        bb, yy, aa = wrap(b + j, g.nb), wrap(y + k, g.ny), self.line(i)
        self.onward(self.landed(bb, yy, c, aa, h, self.recvs), bb, yy, aa, h, dims)

    def shared(self, j, k, i):
        g, (a, b, y, c) = self.grid, self.spot
        for h in range(self.halves):
            self.landed(wrap(b + j, g.nb), wrap(y + k, g.ny), 1 - c, self.line(i), h, self.share_r)

    def group(self):
        for event in self.near:
            self.relay(*event)
        for k in range(self.grid.ny):
            self.shared(0, k, 0)
        self.own().wait()

    def finish(self):
        g, (a, b, y, c) = self.grid, self.spot
        for j in range(g.nb):
            for k in range(g.ny):
                for i in range(g.na):
                    if i or j:
                        self.shared(j, k, i)
        some = self.place(b, y, c, a, 0)
        for i in range(self.count):
            pltpu.make_async_copy(some, some, self.sends.at[i]).wait()
        for i in range(g.na * g.nb * g.ny):
            for h in range(self.halves):
                pltpu.make_async_copy(some, some, self.share_s.at[2 * i + h]).wait()


def turn_back(values, cosines, sines):
    quarter = ROPE // 2
    lane = lax.broadcasted_iota(jnp.int32, values.shape, 1)
    swapped = jnp.where(
        lane < quarter,
        pltpu.roll(values, values.shape[1] - quarter, 1),
        pltpu.roll(values, quarter, 1),
    )
    return values * cosines + swapped * sines


def attention_back_kernel(
    grid,
    pieces,
    x_ref,
    wo_hbm,
    q_hbm,
    kv_hbm,
    packed_hbm,
    we_hbm,
    ctx_ref,
    log_ref,
    seg_ref,
    own_seg_ref,
    cos_ref,
    sin_ref,
    dq_ref,
    keys_ref,
    part_ref,
    wo_ref,
    wo,
    q,
    kv,
    packed,
    we,
    grads,
    kcat,
    bias,
    dkv,
    drope,
    wo_part,
    load_sem,
    *scratch,
):
    f32, bf = jnp.float32, jnp.bfloat16
    rows, tokens = q.shape[0], kv.shape[0]
    heads = q.shape[1] // 256
    scale = (NOPE + ROPE) ** (-0.5)
    a, b, y, c = grid.here()
    pairs = ((wo_hbm, wo), (q_hbm, q), (kv_hbm, kv), (packed_hbm, packed), (we_hbm, we))
    loads = [pltpu.make_async_copy(src, dst, load_sem.at[i]) for i, (src, dst) in enumerate(pairs)]
    for load in loads:
        load.start()
    greet(grid)
    group = TensorGather(grid, x_ref, grads, scratch[: TensorGather.count])
    group.start()
    sums = []
    width = wo.shape[1] // pieces
    for p in range(pieces):
        first = TensorGather.count + p * PlaneReduce.count
        at = pl.ds(p * width, width)
        sums.append(
            PlaneReduce(
                grid, wo_part.at[:, :, :, at], wo_ref.at[:, at], scratch[first : first + PlaneReduce.count]
            )
        )
    first_row = (a * grid.nb + b) * rows
    ordinal = first_row + lax.broadcasted_iota(jnp.int32, (rows, tokens), 0)
    key = lax.broadcasted_iota(jnp.int32, (rows, tokens), 1)
    seg = seg_ref[...]
    seen = (key <= ordinal) & ((seg == own_seg_ref[...]) | (seg == 0))
    bias[...] = jnp.where(seen, 0.0, masked_out)
    for load in loads:
        load.wait()
    kcat[:, NOPE:] = packed[:, LATENT : LATENT + 128]
    lane = lax.broadcasted_iota(jnp.int32, (tokens, 128), 1)
    kcat[:, NOPE:] = jnp.where(lane < ROPE, kcat[:, NOPE:].astype(f32), 0.0).astype(bf)

    group.middle(1)
    group.last()
    rows_in = grads[...].reshape(rows, grads.shape[-1])
    for p in range(pieces):
        at = pl.ds(p * width, width)
        wo_part[:, :, :, at] = (
            lax.dot_general(
                ctx_ref[...], rows_in[:, p * width : (p + 1) * width], (((0,), (0,)), ((), ())),
                preferred_element_type=f32,
            )
            .astype(bf)
            .reshape(wo_part.shape[:3] + (width,))
        )
        sums[p].start()
    dctx = dot_rows(rows_in, wo[...]).astype(bf)

    points = 3 * heads + 1
    at_point = {}
    for p in range(pieces):
        at_point.setdefault((p + 1) * points // (pieces + 2), []).append(sums[p].middle)
    done = [0]

    def hook():
        for event in at_point.get(done[0], ()):
            event()
        done[0] += 1

    hook()
    for h in range(heads):
        qh = q[:, h * 256 : (h + 1) * 256]
        kcat[:, :NOPE] = kv[:, h * 256 : h * 256 + NOPE]
        s = dot_rows(qh, kcat[...]) * scale + bias[...]
        p = jnp.exp(s - log_ref[h])
        dh = dctx[:, h * VDIM : (h + 1) * VDIM]
        dp = dot_rows(dh, kv[:, h * 256 + NOPE : (h + 1) * 256])
        ds = (p * (dp - jnp.sum(p * dp, axis=-1, keepdims=True))).astype(bf)
        p = p.astype(bf)
        hook()
        dq = dot_plain(ds, kcat[...]) * scale
        dq_ref[:, h * 256 : h * 256 + NOPE] = dq[:, :NOPE].astype(bf)
        dq_ref[:, h * 256 + NOPE : (h + 1) * 256] = turn_back(
            dq[:, NOPE:], cos_ref[...], sin_ref[...]
        ).astype(bf)
        hook()
        dkv[:, h * 256 + NOPE : (h + 1) * 256] = lax.dot_general(
            p, dh, (((0,), (0,)), ((), ())), preferred_element_type=f32
        ).astype(bf)
        dk = scale * lax.dot_general(ds, qh, (((0,), (0,)), ((), ())), preferred_element_type=f32)
        dkv[:, h * 256 : h * 256 + NOPE] = dk[:, :NOPE].astype(bf)
        if h == 0:
            drope[...] = dk[:, NOPE:]
        else:
            drope[...] += dk[:, NOPE:]
        hook()
    keys_ref[:, :LATENT] = dot_rows(dkv[...], we[...]).astype(bf)
    keys_ref[:, LATENT:] = drope[...].astype(bf)
    part_ref[...] = lax.dot_general(
        packed[:, :LATENT], dkv[...], (((0,), (0,)), ((), ())), preferred_element_type=f32
    ).astype(bf)
    for one in sums:
        one.last()
    for one in sums:
        one.finish()


def attention_back_call(
    grid, x, wo, q, kv, packed, we, context, log_total, seg, own_seg, cosines, sines, collective_id, pieces=4
):
    r, n = x.shape
    rows, tokens, heads = q.shape[0], kv.shape[0], q.shape[1] // 256
    bf, f32 = jnp.bfloat16, jnp.float32
    any_space = pl.BlockSpec(memory_space=pl.ANY)
    in_vmem = pl.BlockSpec(memory_space=pltpu.VMEM)
    share = wo.shape[0] // (grid.na * grid.nb)
    return pl.pallas_call(
        functools.partial(attention_back_kernel, grid, pieces),
        out_shape=[
            jax.ShapeDtypeStruct(q.shape, bf),
            jax.ShapeDtypeStruct((tokens, LATENT + 128), bf),
            jax.ShapeDtypeStruct(we.shape, bf),
            jax.ShapeDtypeStruct((share, n), bf),
        ],
        in_specs=[any_space] * 6 + [in_vmem] * 6,
        out_specs=[in_vmem] * 4,
        scratch_shapes=[
            pltpu.VMEM(wo.shape, bf),
            pltpu.VMEM(q.shape, bf),
            pltpu.VMEM(kv.shape, bf),
            pltpu.VMEM(packed.shape, bf),
            pltpu.VMEM(we.shape, bf),
            pltpu.VMEM((grid.ny, 2, r, n), bf),
            pltpu.VMEM((tokens, 256), bf),
            pltpu.VMEM((rows, tokens), f32),
            pltpu.VMEM(kv.shape, bf),
            pltpu.VMEM((tokens, 128), f32),
            pltpu.VMEM((grid.na, grid.nb, share, n), bf),
            pltpu.SemaphoreType.DMA((5,)),
        ]
        + TensorGather.scratch(grid)
        + PlaneReduce.scratch(grid, share, n // pieces) * pieces,
        compiler_params=pltpu.CompilerParams(
            collective_id=collective_id, has_side_effects=True, vmem_limit_bytes=62 << 20
        ),
    )(x, wo, q, kv, packed, we, context, log_total, seg, own_seg, cosines, sines)


def first_kernel(
    grid,
    hidden_ref,
    gain_ref,
    wl_hbm,
    lgain_ref,
    wq_hbm,
    gate_ref,
    route_ref,
    cos_ref,
    sin_ref,
    packed_ref,
    q_ref,
    normed_ref,
    comp_ref,
    wl,
    wq,
    normed,
    mine,
    load_sem,
    *scratch,
):
    f32, bf = jnp.float32, jnp.bfloat16
    rows, few = hidden_ref.shape[0], mine.shape[0]
    heads = q_ref.shape[1] // 256
    a, b, y, c = grid.here()
    pairs = ((wl_hbm, wl.at[pl.ds(0, LATENT + ROPE)]), (wq_hbm, wq))
    loads = [pltpu.make_async_copy(src, dst, load_sem.at[i]) for i, (src, dst) in enumerate(pairs)]
    for load in loads:
        load.start()
    wl[LATENT + ROPE :] = jnp.zeros((wl.shape[0] - LATENT - ROPE, wl.shape[1]), bf)
    greet(grid)
    at = pl.ds(pl.multiple_of((y * 2 + c) * few, few), few)

    def rms(v, gain):
        return v * lax.rsqrt(jnp.mean(v * v, axis=-1, keepdims=True) + epsilon) * gain

    normed_few = rms(hidden_ref[at].astype(f32), gain_ref[...]).astype(bf)
    normed_ref[...] = normed_few
    loads[0].wait()
    comp = dot_rows(normed_few, wl[...])
    comp_ref[...] = comp
    mine[:, :LATENT] = rms(comp[:, :LATENT], lgain_ref[...]).astype(bf)
    tail = turn_back(comp[:, LATENT:], cos_ref[at], -sin_ref[at])
    lane = lax.broadcasted_iota(jnp.int32, tail.shape, 1) - ROPE
    routes, gates = route_ref[at], gate_ref[at]
    for k in range(TOP):
        expert, gate = routes[:, k : k + 1], gates[:, k : k + 1]
        high = gate.astype(bf).astype(f32)
        tail += jnp.where(lane == expert, high, 0.0)
        tail += jnp.where(lane == expert + EXP_DEV * grid.na * grid.nb, gate - high, 0.0)
    mine[:, LATENT:] = tail.astype(bf)
    gather = GatherAll(grid, mine, packed_ref, scratch, halves=1)
    gather.start()
    normed[...] = rms(hidden_ref[...].astype(f32), gain_ref[...]).astype(bf)
    loads[1].wait()
    gather.group()
    for event in gather.others[: len(gather.others) // 3]:
        gather.relay(*event)
    raw = dot_plain(normed[...], wq[...])
    total = raw.shape[1]
    for h in range(heads):
        step = h * (NOPE + ROPE)
        moved = raw if step == 0 else pltpu.roll(raw, total - step, 1)
        q_ref[:, h * 256 : h * 256 + NOPE] = moved[:, :NOPE].astype(bf)
        q_ref[:, h * 256 + NOPE : (h + 1) * 256] = turn_back(
            moved[:, NOPE : NOPE + 128], cos_ref[...], -sin_ref[...]
        ).astype(bf)
    for event in gather.others[len(gather.others) // 3 :]:
        gather.relay(*event)
    gather.finish()


def first_call(
    grid, hidden, attn_gain, latent_weight, latent_gain, query_weight, gates, routes, cosines, sines,
    collective_id,
):
    rows, n = hidden.shape
    few = rows // (2 * grid.ny)
    heads = query_weight.shape[1] // (NOPE + ROPE)
    bf, f32 = jnp.bfloat16, jnp.float32
    any_space = pl.BlockSpec(memory_space=pl.ANY)
    in_vmem = pl.BlockSpec(memory_space=pltpu.VMEM)
    width = LATENT + 128
    outs = pl.pallas_call(
        functools.partial(first_kernel, grid),
        out_shape=[
            jax.ShapeDtypeStruct((grid.na, grid.nb, grid.ny, 2, few, width), bf),
            jax.ShapeDtypeStruct((rows, heads * 256), bf),
            jax.ShapeDtypeStruct((few, n), bf),
            jax.ShapeDtypeStruct((few, width), f32),
        ],
        in_specs=[in_vmem, in_vmem, any_space, in_vmem, any_space] + [in_vmem] * 4,
        out_specs=[any_space] + [in_vmem] * 3,
        scratch_shapes=[
            pltpu.VMEM((width, n), bf),
            pltpu.VMEM(query_weight.shape, bf),
            pltpu.VMEM((rows, n), bf),
            pltpu.VMEM((few, width), bf),
            pltpu.SemaphoreType.DMA((2,)),
        ]
        + GatherAll.scratch(grid),
        compiler_params=pltpu.CompilerParams(
            collective_id=collective_id, has_side_effects=True, vmem_limit_bytes=40 << 20
        ),
    )(
        hidden, attn_gain[None], latent_weight.T, latent_gain[None], query_weight, gates, routes,
        cosines, sines,
    )
    return outs[0].reshape(-1, width), outs[1], outs[2], outs[3]


def attention_kernel(
    grid,
    hidden_ref,
    gain_ref,
    q_hbm,
    packed_hbm,
    we_hbm,
    wo_hbm,
    seg_ref,
    own_seg_ref,
    kv_ref,
    log_ref,
    ctx_ref,
    res_ref,
    moe_ref,
    q,
    packed,
    we,
    wo,
    kv,
    kcat,
    bias,
    part,
    total,
    load_sem,
    kv_sem,
    *scratch,
):
    f32, bf = jnp.float32, jnp.bfloat16
    rows, tokens = q.shape[0], kv.shape[0]
    heads = q.shape[1] // 256
    few = res_ref.shape[0]
    scale = (NOPE + ROPE) ** (-0.5)
    a, b, y, c = grid.here()
    pairs = ((packed_hbm, packed), (we_hbm, we), (q_hbm, q), (wo_hbm, wo))
    loads = [pltpu.make_async_copy(src, dst, load_sem.at[i]) for i, (src, dst) in enumerate(pairs)]
    for load in loads:
        load.start()
    greet_tensor(grid)
    ordinal = (a * grid.nb + b) * rows + lax.broadcasted_iota(jnp.int32, (rows, tokens), 0)
    key = lax.broadcasted_iota(jnp.int32, (rows, tokens), 1)
    seg = seg_ref[...]
    seen = (key <= ordinal) & ((seg == own_seg_ref[...]) | (seg == 0))
    bias[...] = jnp.where(seen, 0.0, masked_out)
    for load in loads:
        load.wait()
    lane = lax.broadcasted_iota(jnp.int32, (tokens, 128), 1)
    kcat[:, NOPE:] = jnp.where(lane < ROPE, packed[:, LATENT:].astype(f32), 0.0).astype(bf)
    kv[...] = dot_plain(packed[:, :LATENT], we[...]).astype(bf)
    store = pltpu.make_async_copy(kv, kv_ref, kv_sem)
    store.start()
    for h in range(heads):
        kcat[:, :NOPE] = kv[:, h * 256 : h * 256 + NOPE]
        s = dot_rows(q[:, h * 256 : (h + 1) * 256], kcat[...]) * scale + bias[...]
        peak = jnp.max(s, axis=-1, keepdims=True)
        w = jnp.exp(s - peak)
        tot = jnp.sum(w, axis=-1, keepdims=True)
        log_ref[h] = peak + jnp.log(tot)
        p = (w * (1.0 / tot)).astype(bf)
        ctx_ref[:, h * VDIM : (h + 1) * VDIM] = dot_plain(
            p, kv[:, h * 256 + NOPE : (h + 1) * 256]
        ).astype(bf)
    part[...] = dot_plain(ctx_ref[...], wo[...]).astype(bf).reshape(part.shape)
    reduce = TensorReduce(grid, part, total, scratch)
    reduce.start()
    reduce.middle()
    reduce.last()
    residual = hidden_ref[...].astype(f32) + total[...]
    res_ref[...] = residual
    inverse = lax.rsqrt(jnp.mean(residual * residual, axis=-1, keepdims=True) + epsilon)
    moe_ref[...] = (residual * inverse * gain_ref[...]).astype(bf)
    store.wait()
    reduce.finish()


def attention_call(grid, hidden, gain, q, packed, we, wo, seg, own_seg, collective_id):
    few, n = hidden.shape
    rows, tokens, heads = q.shape[0], packed.shape[0], q.shape[1] // 256
    bf, f32 = jnp.bfloat16, jnp.float32
    any_space = pl.BlockSpec(memory_space=pl.ANY)
    in_vmem = pl.BlockSpec(memory_space=pltpu.VMEM)
    return pl.pallas_call(
        functools.partial(attention_kernel, grid),
        out_shape=[
            jax.ShapeDtypeStruct((tokens, heads * 256), bf),
            jax.ShapeDtypeStruct((heads, rows, 1), f32),
            jax.ShapeDtypeStruct((rows, heads * VDIM), bf),
            jax.ShapeDtypeStruct((few, n), f32),
            jax.ShapeDtypeStruct((few, n), bf),
        ],
        in_specs=[in_vmem] * 2 + [any_space] * 4 + [in_vmem] * 2,
        out_specs=[any_space] + [in_vmem] * 4,
        scratch_shapes=[
            pltpu.VMEM(q.shape, bf),
            pltpu.VMEM(packed.shape, bf),
            pltpu.VMEM(we.shape, bf),
            pltpu.VMEM(wo.shape, bf),
            pltpu.VMEM((tokens, heads * 256), bf),
            pltpu.VMEM((tokens, 256), bf),
            pltpu.VMEM((rows, tokens), f32),
            pltpu.VMEM((grid.ny, 2, few, n), bf),
            pltpu.VMEM((few, n), f32),
            pltpu.SemaphoreType.DMA((4,)),
            pltpu.SemaphoreType.DMA,
        ]
        + TensorReduce.scratch(grid, few, n),
        compiler_params=pltpu.CompilerParams(
            collective_id=collective_id, has_side_effects=True, vmem_limit_bytes=62 << 20
        ),
    )(hidden, gain[None], q, packed, we, wo, seg, own_seg)


def rms_scale(values, gain_vec):
    return (
        values * lax.rsqrt(jnp.mean(values * values, axis=-1, keepdims=True) + epsilon) * gain_vec
    )


def rotate(values, places):
    halfway = values.shape[-1] // 2
    frequency = 10000.0 ** (-jnp.arange(halfway, dtype=jnp.float32) / halfway)
    angles = places.astype(jnp.float32)[:, None] * frequency[None, :]
    cosine = jnp.cos(angles)
    sine_part = jnp.sin(angles)
    if values.ndim == 3:
        cosine = cosine[:, None, :]
        sine_part = sine_part[:, None, :]
    first_half = values[..., :halfway]
    second = values[..., halfway:]
    return jnp.concatenate(
        [first_half * cosine - second * sine_part, second * cosine + first_half * sine_part],
        axis=-1,
    )


def seq_places(segments):
    total_rows = segments.shape[0]
    ordinal = jnp.arange(total_rows, dtype=jnp.int32)
    starts = jnp.concatenate(
        [jnp.ones((1,), jnp.int32), (segments[1:] != segments[:-1]).astype(jnp.int32)]
    )
    seg_start = lax.cummax(jnp.where(starts > 0, ordinal, 0), axis=0)
    return jnp.where(segments == 0, ordinal, total_rows // 2 + ordinal - seg_start)


def silu_product(gate_pre, up_pre):
    return jax.nn.silu(gate_pre) * up_pre


def score_block(queries, key_plain, rope_all, visible):
    scale_factor = (NOPE + ROPE) ** (-0.5)
    raw_scores = jnp.einsum(
        "thc,shc->hts", queries[..., :NOPE], key_plain, preferred_element_type=jnp.float32
    )
    raw_scores = raw_scores + jnp.einsum(
        "thr,sr->hts", queries[..., NOPE:], rope_all, preferred_element_type=jnp.float32
    )
    return jnp.where(visible[None], scale_factor * raw_scores, masked_out)


def dot(left_side, right_side):
    return jnp.dot(left_side, right_side, preferred_element_type=jnp.float32)


def pad_columns(values):
    return jnp.pad(values, ((0, 0), (0, -values.shape[1] % 128)))


def low(values):
    return values.astype(jnp.bfloat16)


def shards(
    grid,
    hidden_in,
    attn_gain,
    query_weight,
    latent_weight,
    latent_gain,
    expand_weight,
    output_weight,
    moe_gain,
    shared_gate,
    shared_up,
    shared_down,
    expert_gate,
    expert_up,
    expert_down,
    gate_values,
    expert_routes,
    segments,
    cotangent,
):
    tok_rows, model_width = hidden_in.shape
    groups = lax.axis_size("expert")
    parts = lax.axis_size("tensor")
    device = lax.axis_index("expert")
    part = lax.axis_index("tensor")
    total_rows = segments.shape[0]
    few = tok_rows // parts
    start_row = device * tok_rows
    scale_factor = (NOPE + ROPE) ** (-0.5)

    def quarter(values):
        return lax.dynamic_slice_in_dim(values, part * few, few)

    def own_group(values):
        return lax.dynamic_slice_in_dim(values, start_row, tok_rows)

    places = own_group(seq_places(segments))
    own_seg = own_group(segments)
    halfway = ROPE // 2
    frequency = 10000.0 ** (-jnp.arange(halfway, dtype=jnp.float32) / halfway)
    angles = places.astype(jnp.float32)[:, None] * frequency[None, :]
    nothing = jnp.zeros((tok_rows, 128 - ROPE), jnp.float32)
    cosines, sines = jnp.cos(angles), jnp.sin(angles)
    cosines = jnp.concatenate([cosines, cosines, nothing], axis=1)
    sines = jnp.concatenate([sines, -sines, nothing], axis=1)
    hidden_few = quarter(hidden_in)
    cot_all = lax.all_gather(quarter(cotangent), ALL, axis=0, tiled=True)

    packed_all, queries, normed_few, compressed = first_call(
        grid, hidden_in, attn_gain, latent_weight, latent_gain, query_weight, gate_values,
        expert_routes, cosines, sines, 0,
    )
    expanded, log_total, merged, residual, moe_in = attention_call(
        grid, hidden_few, moe_gain, queries, packed_all, expand_weight, output_weight,
        segments[None, :], own_seg[:, None], 1,
    )
    hidden_f = hidden_few.astype(jnp.float32)

    moe_all, grad_moe_in, out_rows, acts = experts_call(
        grid, moe_in, cot_all, packed_all, expert_gate, expert_up, expert_down,
        shared_gate, shared_up, shared_down, 2,
    )
    normed_later, _ = lax.optimization_barrier((normed_few, moe_in[:8]))
    normed_all = lax.all_gather(normed_later, ALL, axis=0, tiled=True)

    _, pull_moe = jax.vjp(rms_scale, residual, moe_gain)
    grad_residual, grad_moe_gain = pull_moe(grad_moe_in)
    grad_residual = grad_residual + quarter(cotangent).astype(jnp.float32)
    grad_q, key_rows, expand_part, output_rows = attention_back_call(
        grid,
        low(grad_residual),
        output_weight,
        queries,
        expanded,
        packed_all,
        expand_weight,
        merged,
        log_total,
        segments[None, :],
        own_seg[:, None],
        cosines,
        sines,
        5,
    )
    grad_q_low = grad_q.reshape(tok_rows, -1, 256)[:, :, : NOPE + ROPE].reshape(tok_rows, -1)
    normed_rows = low(dot(grad_q_low, query_weight.T))

    moe_out, grad_keys, weight_rows, grad_normed, grad_q_all, expert_grads = gradients_call(
        grid, out_rows, key_rows, expand_part, normed_rows, grad_q_low, moe_all, cot_all, acts,
        expert_down.shape[1], shared_down.shape[0], 3,
    )
    grad_expert_gate, grad_expert_up, grad_expert_down = expert_grads[:3]
    grad_shared_gate, grad_shared_up, grad_shared_down = expert_grads[3:]
    layer_out = low(residual + moe_out)
    places_few = quarter(places)
    compressed_few = compressed[:, : LATENT + ROPE]
    _, pull_latent = jax.vjp(rms_scale, compressed_few[:, :LATENT], latent_gain)
    grad_plain_latent, grad_latent_gain = pull_latent(grad_keys[:, :LATENT])
    _, pull_krope = jax.vjp(partial(rotate, places=places_few), compressed_few[:, LATENT:])
    (grad_k_turned,) = pull_krope(grad_keys[:, LATENT : LATENT + ROPE])
    grad_comp_low = low(jnp.concatenate([grad_plain_latent, grad_k_turned], axis=-1))
    grad_normed = grad_normed + dot(grad_comp_low, latent_weight.T)
    _, pull_input = jax.vjp(rms_scale, hidden_f, attn_gain)
    grad_input_norm, grad_attn_gain = pull_input(grad_normed)
    gains = jnp.concatenate([grad_attn_gain, grad_latent_gain, grad_moe_gain])
    gains = jnp.pad(gains, (0, -gains.shape[0] % few)).reshape(few, -1)
    gains_high = low(gains)
    gains_low = low(gains - gains_high.astype(jnp.float32))
    spread = gains.shape[1]
    both = jnp.concatenate([layer_out, low(grad_residual + grad_input_norm)], axis=1)
    last, weight_rows, output_rows, both = last_call(
        grid,
        pad_columns(jnp.concatenate([grad_comp_low, gains_high, gains_low], axis=1)),
        weight_rows,
        output_rows,
        both,
        8,
    )
    grad_comp_all = last.reshape(total_rows, -1)[:, : LATENT + ROPE]
    gains = jnp.sum(last[:, :, LATENT + ROPE : LATENT + ROPE + 2 * spread].astype(jnp.float32), axis=0)
    gains = (gains[:, :spread] + gains[:, spread:]).reshape(-1)
    grad_latent_weight = dot(normed_all.T, grad_comp_all)
    grad_query_weight = dot(normed_all.T, grad_q_all)
    layer_out, grad_hidden = both[:, :model_width], both[:, model_width:].astype(jnp.float32)
    grad_output_weight = output_rows.astype(jnp.float32)
    grad_expand_weight = weight_rows.astype(jnp.float32)
    return (
        layer_out,
        grad_hidden,
        gains[:model_width],
        grad_query_weight,
        grad_latent_weight,
        gains[model_width : model_width + LATENT],
        grad_expand_weight,
        grad_output_weight,
        gains[model_width + LATENT : 2 * model_width + LATENT],
        grad_shared_gate,
        grad_shared_up,
        grad_shared_down,
        grad_expert_gate,
        grad_expert_up,
        grad_expert_down,
    )


def solution(mesh):
    grid = Grid(mesh.shape["expert"], mesh.shape["tensor"])
    placed = (
        P("expert", None),
        P(),
        P(None, "tensor"),
        P(),
        P(),
        P(None, "tensor"),
        P("tensor", None),
        P(),
        P(None, "tensor"),
        P(None, "tensor"),
        P("tensor", None),
        P("expert", None, "tensor"),
        P("expert", None, "tensor"),
        P("expert", "tensor", None),
        P("expert", None),
        P("expert", None),
        P(),
        P("expert", None),
    )
    return jax.shard_map(
        partial(shards, grid),
        mesh=mesh,
        in_specs=placed,
        out_specs=(
            P("expert", None),
            P("expert", None),
            P(),
            P(None, "tensor"),
            P(),
            P(),
            P(None, "tensor"),
            P("tensor", None),
            P(),
            P(None, "tensor"),
            P(None, "tensor"),
            P("tensor", None),
            P("expert", None, "tensor"),
            P("expert", None, "tensor"),
            P("expert", "tensor", None),
        ),
        check_vma=False,
    )
```

```python
import functools
import math
from functools import partial

import jax
import jax.numpy as jnp
from jax import lax
from jax.experimental import pallas as pl
from jax.experimental.pallas import tpu as pltpu
from jax.sharding import PartitionSpec as P

NOPE = 128
ROPE = 64
VDIM = 128
LATENT = 512
TOP = 6
EXP_DEV = 2
ALL = ("expert", "tensor")
MESH = pl.DeviceIdType.MESH

epsilon = 1e-06
masked_out = -1e30


class Grid:
    def __init__(self, expert, tensor):
        self.na = 4 if expert % 4 == 0 else 1
        self.nb = expert // self.na
        self.ny = tensor // 2
        self.size = expert * tensor

    def here(self):
        e, t = lax.axis_index("expert"), lax.axis_index("tensor")
        return (lax.div(e, self.nb), lax.rem(e, self.nb), lax.div(t, 2), lax.rem(t, 2))

    def device(self, a, b, y, c):
        return {"expert": a * self.nb + b, "tensor": y * 2 + c}

    def block(self, a, b, y, c):
        return ((a * self.nb + b) * self.ny + y) * 2 + c


def microseconds(time):
    return pl.CostEstimate(flops=time * 1000**3, bytes_accessed=0, transcendentals=0)


def wrap(i, n):
    return lax.rem(i, n)


def greet(grid):
    a, b, y, c = grid.here()
    barrier = pltpu.get_barrier_semaphore()
    others = (
        [grid.device(wrap(a + i, grid.na), b, y, c) for i in range(1, grid.na)]
        + [grid.device(a, wrap(b + i, grid.nb), y, c) for i in range(1, grid.nb)]
        + [grid.device(a, b, wrap(y + i, grid.ny), c) for i in range(1, grid.ny)]
        + [grid.device(a, b, y, 1 - c)]
    )
    for other in others:
        pl.semaphore_signal(barrier, inc=1, device_id=other, device_id_type=MESH)
    pl.semaphore_wait(barrier, len(others))


def gather_kernel(
    grid, x_ref, out_ref, own_sem, send_sem, recv_sem, core_send, core_recv, extra=()
):
    na, nb, ny = grid.na, grid.nb, grid.ny
    a, b, y, c = grid.here()
    half = x_ref.shape[0] // 2
    greet(grid)
    waits = []

    def dst(bb, yy, cc, aa, h):
        return out_ref.at[grid.block(aa, bb, yy, cc), pl.ds(h * half, half)]

    def slot(bb, yy, aa, h):
        return ((bb * ny + yy) * na + aa) * 2 + h

    def push(src, bb, yy, aa, h, where, kind):
        copy = pltpu.make_async_remote_copy(
            src_ref=src,
            dst_ref=dst(bb, yy, c, aa, h),
            send_sem=core_send.at[slot(bb, yy, aa, h)] if kind == "c" else send_sem.at[len(waits)],
            recv_sem=(core_recv if kind == "c" else recv_sem).at[slot(bb, yy, aa, h)],
            device_id=where,
            device_id_type=MESH,
        )
        copy.start()
        if kind != "c":
            waits.append(copy)
        else:
            core_waits.append(copy)

    core_waits = []

    def onward(src, bb, yy, aa, h, dims):
        for d in dims:
            if d == "a":
                for i in range(1, na):
                    push(src, bb, yy, aa, h, grid.device(wrap(a + i, na), b, y, c), d)
            if d == "b":
                for i in range(1, nb):
                    push(src, bb, yy, aa, h, grid.device(a, wrap(b + i, nb), y, c), d)
            if d == "y":
                for i in range(1, ny):
                    push(src, bb, yy, aa, h, grid.device(a, b, wrap(y + i, ny), c), d)
        push(src, bb, yy, aa, h, grid.device(a, b, y, 1 - c), "c")

    def landed(bb, yy, cc, aa, h, sem):
        ref = dst(bb, yy, cc, aa, h)
        pltpu.make_async_copy(ref, ref, sem.at[slot(bb, yy, aa, h)]).wait()
        return ref

    own = pltpu.make_async_copy(x_ref, out_ref.at[grid.block(a, b, y, c)], own_sem)
    own.start()
    orders = (("b", "y"), ("y", "b"))
    for h in range(2):
        onward(x_ref.at[pl.ds(h * half, half)], b, y, a, h, ("a",) + orders[h])
    for one in extra:
        one.start()
    for i in range(1, na):
        aa = wrap(a + na - i, na)
        for h in range(2):
            onward(landed(b, y, c, aa, h, recv_sem), b, y, aa, h, orders[h])
    for i in range(na):
        aa = wrap(a + na - i, na)
        for h in range(2):
            n1 = (nb, ny)[h]
            for j in range(1, n1):
                bb, yy = (wrap(b + nb - j, nb), y) if h == 0 else (b, wrap(y + ny - j, ny))
                onward(landed(bb, yy, c, aa, h, recv_sem), bb, yy, aa, h, orders[h][1:])
    for i in range(na):
        aa = wrap(a + na - i, na)
        for h in range(2):
            for j in range(nb):
                for k in range(1, ny):
                    if h == 0:
                        bb, yy = wrap(b + nb - j, nb), wrap(y + ny - k, ny)
                        onward(landed(bb, yy, c, aa, h, recv_sem), bb, yy, aa, h, ())
            for j in range(ny):
                for k in range(1, nb):
                    if h == 1:
                        bb, yy = wrap(b + nb - k, nb), wrap(y + ny - j, ny)
                        onward(landed(bb, yy, c, aa, h, recv_sem), bb, yy, aa, h, ())
    for i in range(1, na):
        for one in extra:
            one.middle(i)
    for j in range(nb):
        for k in range(ny):
            for i in range(na):
                for h in range(2):
                    landed(wrap(b + nb - j, nb), wrap(y + ny - k, ny), 1 - c, wrap(a + na - i, na), h, core_recv)
    own.wait()
    for copy in waits + core_waits:
        copy.wait_send()
    for one in extra:
        one.last()


def gather_sends(grid):
    na, nb, ny = grid.na, grid.nb, grid.ny
    return 2 * (na - 1 + na * (nb - 1) + na * (ny - 1) + na * (nb - 1) * (ny - 1))


def gather_all(grid, x, collective_id):
    r, n = x.shape
    blocks = grid.na * grid.nb * grid.ny
    return pl.pallas_call(
        functools.partial(gather_kernel, grid),
        out_shape=jax.ShapeDtypeStruct((grid.size, r, n), x.dtype),
        in_specs=[pl.BlockSpec(memory_space=pl.ANY)],
        out_specs=pl.BlockSpec(memory_space=pl.ANY),
        scratch_shapes=[
            pltpu.SemaphoreType.DMA,
            pltpu.SemaphoreType.DMA((gather_sends(grid),)),
            pltpu.SemaphoreType.DMA((2 * blocks,)),
            pltpu.SemaphoreType.DMA((2 * blocks,)),
            pltpu.SemaphoreType.DMA((2 * blocks,)),
        ],
        compiler_params=pltpu.CompilerParams(collective_id=collective_id, has_side_effects=True),
    )(x)


def scatter_kernel(grid, pieces, p_ref, out_ref, acc, core_in, d1_in0, d1_in1, d2_in0, d2_in1, a_in,
                   load_sem, core_s, core_r, s10, r10, s11, r11, s20, r20, s21, r21, sa, ra):
    na, nb, ny = grid.na, grid.nb, grid.ny
    a, b, y, c = grid.here()
    half = p_ref.shape[4] // 2
    width = p_ref.shape[5] // pieces
    greet(grid)
    pending = []

    def send(src, dst, ss, rs, where):
        copy = pltpu.make_async_remote_copy(src_ref=src, dst_ref=dst, send_sem=ss, recv_sem=rs, device_id=where, device_id_type=MESH)
        copy.start()
        pending.append(copy)

    def await_in(ref, sem):
        pltpu.make_async_copy(ref, ref, sem).wait()

    def add(dst, src):
        dst[...] = (dst[...].astype(jnp.float32) + src[...].astype(jnp.float32)).astype(dst.dtype)

    def cols(p):
        return pl.ds(p * width, width)

    spots = [(j, k) for j in reversed(range(nb)) for k in reversed(range(ny))]
    loads = {}
    for p in range(pieces):
        for n, (j, k) in enumerate(spots):
            bb, yy = wrap(b + j, nb), wrap(y + k, ny)
            send(p_ref.at[:, bb, yy, 1 - c, :, cols(p)], core_in.at[p, j, k], core_s.at[p, n], core_r.at[p, n],
                 grid.device(a, b, y, 1 - c))
            load = pltpu.make_async_copy(p_ref.at[:, bb, yy, c, :, cols(p)], acc.at[p, j, k], load_sem.at[p, n])
            load.start()
            loads[p, n] = load
    rows = (pl.ds(0, half), pl.ds(half, half))
    for p in range(pieces):
        for n, (j, k) in enumerate(spots):
            loads[p, n].wait()
            await_in(core_in.at[p, j, k], core_r.at[p, n])
            for i in range(na):
                add(acc.at[p, j, k, i], core_in.at[p, j, k, i])
            if k:
                send(acc.at[p, j, k, :, rows[0]], d1_in0.at[p, j, k - 1], s10.at[p, j, k - 1], r10.at[p, j, k - 1],
                     grid.device(a, b, wrap(y + k, ny), c))
            if j:
                send(acc.at[p, j, k, :, rows[1]], d1_in1.at[p, k, j - 1], s11.at[p, k, j - 1], r11.at[p, k, j - 1],
                     grid.device(a, wrap(b + j, nb), y, c))
    for p in range(pieces):
        for j in reversed(range(nb)):
            for k in range(1, ny):
                await_in(d1_in0.at[p, j, k - 1], r10.at[p, j, k - 1])
                for i in range(na):
                    add(acc.at[p, j, 0, i, rows[0]], d1_in0.at[p, j, k - 1, i])
            if j:
                send(acc.at[p, j, 0, :, rows[0]], d2_in0.at[p, j - 1], s20.at[p, j - 1], r20.at[p, j - 1],
                     grid.device(a, wrap(b + j, nb), y, c))
        for k in reversed(range(ny)):
            for j in range(1, nb):
                await_in(d1_in1.at[p, k, j - 1], r11.at[p, k, j - 1])
                for i in range(na):
                    add(acc.at[p, 0, k, i, rows[1]], d1_in1.at[p, k, j - 1, i])
            if k:
                send(acc.at[p, 0, k, :, rows[1]], d2_in1.at[p, k - 1], s21.at[p, k - 1], r21.at[p, k - 1],
                     grid.device(a, b, wrap(y + k, ny), c))
    for p in range(pieces):
        for j in range(1, nb):
            await_in(d2_in0.at[p, j - 1], r20.at[p, j - 1])
            for i in range(na):
                add(acc.at[p, 0, 0, i, rows[0]], d2_in0.at[p, j - 1, i])
        for k in range(1, ny):
            await_in(d2_in1.at[p, k - 1], r21.at[p, k - 1])
            for i in range(na):
                add(acc.at[p, 0, 0, i, rows[1]], d2_in1.at[p, k - 1, i])
        for i in range(1, na):
            aa = wrap(a + i, na)
            send(acc.at[p, 0, 0, aa], a_in.at[p, i - 1], sa.at[p, i - 1], ra.at[p, i - 1], grid.device(aa, b, y, c))
    for p in range(pieces):
        total = acc[p, 0, 0, a].astype(jnp.float32)
        for i in range(1, na):
            await_in(a_in.at[p, i - 1], ra.at[p, i - 1])
            total = total + a_in[p, i - 1].astype(jnp.float32)
        out_ref[:, cols(p)] = total.astype(out_ref.dtype)
    for copy in pending:
        copy.wait_send()


def scatter_all(grid, p, dtype, collective_id, pieces=2):
    r, n = p.shape[0] // grid.size, p.shape[1]
    na, nb, ny = grid.na, grid.nb, grid.ny
    half, width = r // 2, n // pieces
    sems = lambda *s: pltpu.SemaphoreType.DMA(s)
    vm = lambda *s: pltpu.VMEM(s, jnp.bfloat16)
    return pl.pallas_call(
        functools.partial(scatter_kernel, grid, pieces),
        out_shape=jax.ShapeDtypeStruct((r, n), dtype),
        in_specs=[pl.BlockSpec(memory_space=pl.ANY)],
        out_specs=pl.BlockSpec(memory_space=pltpu.VMEM),
        scratch_shapes=[
            vm(pieces, nb, ny, na, r, width),
            vm(pieces, nb, ny, na, r, width),
            vm(pieces, nb, ny - 1, na, half, width),
            vm(pieces, ny, nb - 1, na, half, width),
            vm(pieces, nb - 1, na, half, width),
            vm(pieces, ny - 1, na, half, width),
            vm(pieces, na - 1, r, width),
            sems(pieces, nb * ny), sems(pieces, nb * ny), sems(pieces, nb * ny),
            sems(pieces, nb, ny - 1), sems(pieces, nb, ny - 1),
            sems(pieces, ny, nb - 1), sems(pieces, ny, nb - 1),
            sems(pieces, nb - 1), sems(pieces, nb - 1),
            sems(pieces, ny - 1), sems(pieces, ny - 1),
            sems(pieces, na - 1), sems(pieces, na - 1),
        ],
        compiler_params=pltpu.CompilerParams(collective_id=collective_id, has_side_effects=True, vmem_limit_bytes=40 << 20),
    )(p.reshape(na, nb, ny, 2, r, n))


def greet_tensor(grid):
    a, b, y, c = grid.here()
    barrier = pltpu.get_barrier_semaphore()
    others = [grid.device(a, b, wrap(y + i, grid.ny), c) for i in range(1, grid.ny)]
    others.append(grid.device(a, b, y, 1 - c))
    for other in others:
        pl.semaphore_signal(barrier, inc=1, device_id=other, device_id_type=MESH)
    pl.semaphore_wait(barrier, len(others))


def tensor_scatter_kernel(grid, p_ref, out_ref, acc, core_in, y_in, core_s, core_r, ys, yr):
    ny = grid.ny
    a, b, y, c = grid.here()
    greet_tensor(grid)
    pending = []
    for k in reversed(range(ny)):
        copy = pltpu.make_async_remote_copy(
            src_ref=p_ref.at[wrap(y + k, ny), 1 - c], dst_ref=core_in.at[k], send_sem=core_s.at[k], recv_sem=core_r.at[k],
            device_id=grid.device(a, b, y, 1 - c), device_id_type=MESH,
        )
        copy.start()
        pending.append(copy)
    for k in reversed(range(ny)):
        pltpu.make_async_copy(core_in.at[k], core_in.at[k], core_r.at[k]).wait()
        total = p_ref[wrap(y + k, ny), c].astype(jnp.float32) + core_in[k].astype(jnp.float32)
        if k:
            acc[k - 1] = total.astype(acc.dtype)
            copy = pltpu.make_async_remote_copy(
                src_ref=acc.at[k - 1], dst_ref=y_in.at[k - 1], send_sem=ys.at[k - 1], recv_sem=yr.at[k - 1],
                device_id=grid.device(a, b, wrap(y + k, ny), c), device_id_type=MESH,
            )
            copy.start()
            pending.append(copy)
        else:
            out_ref[...] = total
    for k in range(1, ny):
        pltpu.make_async_copy(y_in.at[k - 1], y_in.at[k - 1], yr.at[k - 1]).wait()
        out_ref[...] += y_in[k - 1].astype(jnp.float32)
    for copy in pending:
        copy.wait_send()


def tensor_scatter(grid, p, collective_id):
    ny = grid.ny
    r, n = p.shape[0] // (2 * ny), p.shape[1]
    return pl.pallas_call(
        functools.partial(tensor_scatter_kernel, grid),
        out_shape=jax.ShapeDtypeStruct((r, n), jnp.float32),
        in_specs=[pl.BlockSpec(memory_space=pltpu.VMEM)],
        out_specs=pl.BlockSpec(memory_space=pltpu.VMEM),
        scratch_shapes=[
            pltpu.VMEM((max(ny - 1, 1), r, n), p.dtype),
            pltpu.VMEM((ny, r, n), p.dtype),
            pltpu.VMEM((max(ny - 1, 1), r, n), p.dtype),
            pltpu.SemaphoreType.DMA((ny,)),
            pltpu.SemaphoreType.DMA((ny,)),
            pltpu.SemaphoreType.DMA((max(ny - 1, 1),)),
            pltpu.SemaphoreType.DMA((max(ny - 1, 1),)),
        ],
        compiler_params=pltpu.CompilerParams(
            collective_id=collective_id, has_side_effects=True, vmem_limit_bytes=16 << 20
        ),
    )(p.reshape(ny, 2, r, n))


def tensor_gather_kernel(grid, x_ref, out_ref, own_sem, ys, yr, core_s, core_r):
    ny = grid.ny
    a, b, y, c = grid.here()
    greet_tensor(grid)
    own = pltpu.make_async_copy(x_ref, out_ref.at[y, c], own_sem)
    own.start()
    pending = []

    def push(src, spot, ss, rs, where):
        copy = pltpu.make_async_remote_copy(
            src_ref=src, dst_ref=out_ref.at[spot, c], send_sem=ss, recv_sem=rs, device_id=where, device_id_type=MESH
        )
        copy.start()
        pending.append(copy)

    for k in range(1, ny):
        push(x_ref, y, ys.at[k], yr.at[k], grid.device(a, b, wrap(y + k, ny), c))
    push(x_ref, y, core_s.at[0], core_r.at[0], grid.device(a, b, y, 1 - c))
    for k in range(1, ny):
        spot = wrap(y + ny - k, ny)
        ref = out_ref.at[spot, c]
        pltpu.make_async_copy(ref, ref, yr.at[k]).wait()
        push(ref, spot, core_s.at[k], core_r.at[k], grid.device(a, b, y, 1 - c))
    for k in range(ny):
        ref = out_ref.at[wrap(y + ny - k, ny), 1 - c]
        pltpu.make_async_copy(ref, ref, core_r.at[k]).wait()
    own.wait()
    for copy in pending:
        copy.wait_send()


def tensor_gather(grid, x, collective_id):
    ny = grid.ny
    r, n = x.shape
    out = pl.pallas_call(
        functools.partial(tensor_gather_kernel, grid),
        out_shape=jax.ShapeDtypeStruct((ny, 2, r, n), x.dtype),
        in_specs=[pl.BlockSpec(memory_space=pltpu.VMEM)],
        out_specs=pl.BlockSpec(memory_space=pltpu.VMEM),
        scratch_shapes=[pltpu.SemaphoreType.DMA] + [pltpu.SemaphoreType.DMA((ny,))] * 4,
        compiler_params=pltpu.CompilerParams(
            collective_id=collective_id, has_side_effects=True, vmem_limit_bytes=16 << 20
        ),
    )(x)
    return out.reshape(2 * ny * r, n)


class TensorReduce:
    count = 8

    @staticmethod
    def scratch(grid, r, width):
        ny = grid.ny
        sems = lambda *s: pltpu.SemaphoreType.DMA(s)
        vm = lambda *s: pltpu.VMEM(s, jnp.bfloat16)
        return [
            vm(ny, r, width), vm(ny, r, width), vm(ny - 1, r, width),
            sems(ny), sems(ny), sems(ny), sems(ny - 1), sems(ny - 1),
        ]

    def __init__(self, grid, source, out, scratch):
        self.grid, self.source, self.out = grid, source, out
        (
            self.acc, self.core_in, self.y_in, self.load_sem, self.core_s, self.core_r, self.ys, self.yr,
        ) = scratch
        self.spot = grid.here()

    def load(self, k):
        g, (a, b, y, c) = self.grid, self.spot
        return pltpu.make_async_copy(self.source.at[wrap(y + k, g.ny), c], self.acc.at[k], self.load_sem.at[k])

    def core_copy(self, k):
        g, (a, b, y, c) = self.grid, self.spot
        return pltpu.make_async_remote_copy(
            src_ref=self.source.at[wrap(y + k, g.ny), 1 - c], dst_ref=self.core_in.at[k],
            send_sem=self.core_s.at[k], recv_sem=self.core_r.at[k],
            device_id=g.device(a, b, y, 1 - c), device_id_type=MESH,
        )

    def y_copy(self, k):
        g, (a, b, y, c) = self.grid, self.spot
        return pltpu.make_async_remote_copy(
            src_ref=self.acc.at[k], dst_ref=self.y_in.at[k - 1], send_sem=self.ys.at[k - 1],
            recv_sem=self.yr.at[k - 1], device_id=g.device(a, b, wrap(y + k, g.ny), c), device_id_type=MESH,
        )

    def start(self):
        for k in reversed(range(self.grid.ny)):
            self.core_copy(k).start()
            self.load(k).start()

    def middle(self):
        f32 = jnp.float32
        for k in reversed(range(self.grid.ny)):
            self.load(k).wait()
            ref = self.core_in.at[k]
            pltpu.make_async_copy(ref, ref, self.core_r.at[k]).wait()
            total = self.acc[k].astype(f32) + self.core_in[k].astype(f32)
            self.acc[k] = total.astype(self.acc.dtype)
            if k:
                self.y_copy(k).start()

    def last(self):
        total = self.acc[0].astype(jnp.float32)
        for k in range(1, self.grid.ny):
            ref = self.y_in.at[k - 1]
            pltpu.make_async_copy(ref, ref, self.yr.at[k - 1]).wait()
            total = total + self.y_in[k - 1].astype(jnp.float32)
        self.out[...] = total

    def finish(self):
        for k in range(self.grid.ny):
            self.core_copy(k).wait_send()
            if k:
                self.y_copy(k).wait_send()


class TensorGather:
    count = 5

    @staticmethod
    def scratch(grid):
        return [pltpu.SemaphoreType.DMA((1,))] + [pltpu.SemaphoreType.DMA((grid.ny,))] * 4

    def __init__(self, grid, x, out, scratch):
        self.grid, self.x, self.out = grid, x, out
        self.own_sem, self.ys, self.yr, self.core_s, self.core_r = scratch
        self.spot = grid.here()

    def own(self):
        return pltpu.make_async_copy(self.x, self.out.at[self.spot[2], self.spot[3]], self.own_sem.at[0])

    def y_copy(self, k):
        g, (a, b, y, c) = self.grid, self.spot
        return pltpu.make_async_remote_copy(
            src_ref=self.x, dst_ref=self.out.at[y, c], send_sem=self.ys.at[k], recv_sem=self.yr.at[k],
            device_id=g.device(a, b, wrap(y + k, g.ny), c), device_id_type=MESH,
        )

    def core_copy(self, k):
        g, (a, b, y, c) = self.grid, self.spot
        spot = wrap(y + g.ny - k, g.ny)
        return pltpu.make_async_remote_copy(
            src_ref=self.x if k == 0 else self.out.at[spot, c], dst_ref=self.out.at[spot, c],
            send_sem=self.core_s.at[k], recv_sem=self.core_r.at[k],
            device_id=g.device(a, b, y, 1 - c), device_id_type=MESH,
        )

    def start(self):
        self.own().start()
        for k in range(1, self.grid.ny):
            self.y_copy(k).start()
        self.core_copy(0).start()

    def middle(self, i):
        if i == 1:
            for k in range(1, self.grid.ny):
                pltpu.make_async_copy(self.x, self.x, self.yr.at[k]).wait()
                self.core_copy(k).start()

    def last(self):
        self.own().wait()
        for k in range(self.grid.ny):
            pltpu.make_async_copy(self.x, self.x, self.core_r.at[k]).wait()
        for k in range(self.grid.ny):
            if k:
                self.y_copy(k).wait_send()
            self.core_copy(k).wait_send()


class PlaneReduce:
    count = 9

    @staticmethod
    def scratch(grid, r, width):
        na, nb = grid.na, grid.nb
        sems = lambda *s: pltpu.SemaphoreType.DMA(s)
        vm = lambda *s: pltpu.VMEM(s, jnp.bfloat16)
        return [
            vm(na, r, width), vm(nb - 1, na, r, width), vm(na - 1, r, width),
            sems(1), sems(nb - 1), sems(nb - 1), sems(na - 1), sems(na - 1), sems(1),
        ]

    def __init__(self, grid, source, out, scratch):
        self.grid, self.source, self.out = grid, source, out
        self.acc, self.b_in, self.a_in, self.load_sem, self.sb, self.rb, self.sa, self.ra, _ = scratch
        self.spot = grid.here()

    def load(self):
        return pltpu.make_async_copy(self.source.at[:, self.spot[1]], self.acc, self.load_sem.at[0])

    def copy_b(self, i):
        g, (a, b, y, c) = self.grid, self.spot
        return pltpu.make_async_remote_copy(
            src_ref=self.source.at[:, wrap(b + i, g.nb)], dst_ref=self.b_in.at[i - 1],
            send_sem=self.sb.at[i - 1], recv_sem=self.rb.at[i - 1],
            device_id=g.device(a, wrap(b + i, g.nb), y, c), device_id_type=MESH,
        )

    def copy_a(self, i):
        g, (a, b, y, c) = self.grid, self.spot
        return pltpu.make_async_remote_copy(
            src_ref=self.acc.at[wrap(a + i, g.na)], dst_ref=self.a_in.at[i - 1],
            send_sem=self.sa.at[i - 1], recv_sem=self.ra.at[i - 1],
            device_id=g.device(wrap(a + i, g.na), b, y, c), device_id_type=MESH,
        )

    def start(self):
        for i in range(1, self.grid.nb):
            self.copy_b(i).start()
        self.load().start()

    def middle(self):
        f32 = jnp.float32
        self.load().wait()
        for i in range(1, self.grid.nb):
            ref = self.b_in.at[i - 1]
            pltpu.make_async_copy(ref, ref, self.rb.at[i - 1]).wait()

            def one(m, carry):
                self.acc[m] = (self.acc[m].astype(f32) + ref[m].astype(f32)).astype(self.acc.dtype)
                return carry

            lax.fori_loop(0, self.grid.na, one, 0)
        for i in range(1, self.grid.na):
            self.copy_a(i).start()

    def last(self):
        total = self.acc[self.spot[0]].astype(jnp.float32)
        for i in range(1, self.grid.na):
            ref = self.a_in.at[i - 1]
            pltpu.make_async_copy(ref, ref, self.ra.at[i - 1]).wait()
            total = total + self.a_in[i - 1].astype(jnp.float32)
        self.out[...] = total.astype(self.out.dtype)

    def finish(self):
        for i in range(1, self.grid.nb):
            self.copy_b(i).wait_send()
        for i in range(1, self.grid.na):
            self.copy_a(i).wait_send()


class PlaneGather:
    count = 5

    @staticmethod
    def scratch(grid):
        na, nb = grid.na, grid.nb
        sems = lambda *s: pltpu.SemaphoreType.DMA(s)
        return [sems(1), sems(na - 1), sems(na, nb - 1), sems(na), sems(na, nb - 1)]

    def __init__(self, grid, x, out, scratch):
        self.grid, self.x, self.out = grid, x, out
        self.own_sem, self.sa, self.sb, self.ra, self.rb = scratch
        self.spot = grid.here()

    def own(self):
        return pltpu.make_async_copy(self.x, self.out.at[self.spot[0], self.spot[1]], self.own_sem.at[0])

    def copy_a(self, i):
        g, (a, b, y, c) = self.grid, self.spot
        return pltpu.make_async_remote_copy(
            src_ref=self.x, dst_ref=self.out.at[a, b], send_sem=self.sa.at[i - 1], recv_sem=self.ra.at[i],
            device_id=g.device(wrap(a + i, g.na), b, y, c), device_id_type=MESH,
        )

    def copy_b(self, i, k):
        g, (a, b, y, c) = self.grid, self.spot
        aa = wrap(a + g.na - i, g.na)
        return pltpu.make_async_remote_copy(
            src_ref=self.x if i == 0 else self.out.at[aa, b], dst_ref=self.out.at[aa, b],
            send_sem=self.sb.at[i, k - 1], recv_sem=self.rb.at[i, k - 1],
            device_id=g.device(a, wrap(b + k, g.nb), y, c), device_id_type=MESH,
        )

    def start(self):
        self.own().start()
        for i in range(1, self.grid.na):
            self.copy_a(i).start()
        for k in range(1, self.grid.nb):
            self.copy_b(0, k).start()

    def middle(self, i):
        ref = self.out.at[wrap(self.spot[0] + self.grid.na - i, self.grid.na), self.spot[1]]
        pltpu.make_async_copy(ref, ref, self.ra.at[i]).wait()
        for k in range(1, self.grid.nb):
            self.copy_b(i, k).start()

    def last(self):
        self.own().wait()
        ref = self.x
        for i in range(self.grid.na):
            for k in range(1, self.grid.nb):
                pltpu.make_async_copy(ref, ref, self.rb.at[i, k - 1]).wait()
        for i in range(1, self.grid.na):
            self.copy_a(i).wait_send()
        for i in range(self.grid.na):
            for k in range(1, self.grid.nb):
                self.copy_b(i, k).wait_send()


def last_kernel(grid, x_ref, t_ref, out_ref, t_out, own_sem, ss, rs, cs, cr, *scratch):
    gather_kernel(grid, x_ref, out_ref, own_sem, ss, rs, cs, cr, [TensorGather(grid, t_ref, t_out, scratch)])


def last_call(grid, x, t, collective_id):
    r, n = x.shape
    blocks = grid.na * grid.nb * grid.ny
    any_space = pl.BlockSpec(memory_space=pl.ANY)
    outs = pl.pallas_call(
        functools.partial(last_kernel, grid),
        out_shape=[
            jax.ShapeDtypeStruct((grid.size, r, n), x.dtype),
            jax.ShapeDtypeStruct((grid.ny, 2) + t.shape, t.dtype),
        ],
        in_specs=[any_space] * 2,
        out_specs=[any_space] * 2,
        scratch_shapes=[
            pltpu.SemaphoreType.DMA,
            pltpu.SemaphoreType.DMA((gather_sends(grid),)),
            pltpu.SemaphoreType.DMA((2 * blocks,)),
            pltpu.SemaphoreType.DMA((2 * blocks,)),
            pltpu.SemaphoreType.DMA((2 * blocks,)),
        ]
        + TensorGather.scratch(grid),
        cost_estimate=microseconds(32),
        compiler_params=pltpu.CompilerParams(collective_id=collective_id, has_side_effects=True),
    )(x, t)
    return outs[0], outs[1].reshape(-1, t.shape[-1])


def dot_rows(left_side, right_side):
    return lax.dot_general(
        left_side, right_side, (((1,), (1,)), ((), ())), preferred_element_type=jnp.float32
    )


def dot_plain(left_side, right_side):
    return jnp.dot(left_side, right_side, preferred_element_type=jnp.float32)


def round_up(value, unit):
    return -(-value // unit) * unit


def experts_kernel(
    grid,
    pieces,
    x_ref,
    dz_ref,
    gate_ref,
    eg_hbm,
    eu_hbm,
    ed_hbm,
    sg_hbm,
    su_hbm,
    sd_hbm,
    all_ref,
    grad_ref,
    y_ref,
    acts_ref,
    gates,
    egu,
    ed,
    sgu,
    sd,
    dabuf,
    xbuf,
    dzbuf,
    gated,
    dcat,
    act,
    dsh,
    ybuf,
    dx,
    dx_out,
    core_in,
    d1_in0,
    d1_in1,
    d2_in0,
    d2_in1,
    a_in,
    gate_sem,
    weight_sem,
    own_sem,
    x_sem,
    dz_sem,
    out_sem,
    fill_sem,
    send_sem,
    recv_sem,
    share_send,
    share_recv,
    core_s,
    core_r,
    s10,
    r10,
    s11,
    r11,
    s20,
    r20,
    s21,
    r21,
    sa,
    ra,
):
    na, nb, ny = grid.na, grid.nb, grid.ny
    a, b, y, c = grid.here()
    r, n = x_ref.shape
    half, width, rows = r // 2, n // pieces, na * r
    pairs = nb * ny
    steps = 2 * pairs
    device = a * nb + b
    f, fs = ed_hbm.shape[1], sd_hbm.shape[0]
    wide, wide_s = egu.shape[0] // (2 * EXP_DEV), sd.shape[0]
    ef = EXP_DEV * wide
    columns = columns_of(ef, wide_s)
    f32, bf = jnp.float32, jnp.bfloat16
    fills = [(ed_hbm.at[e], ed, e * wide, f, wide) for e in range(EXP_DEV)]
    fills += [(sd_hbm, sd, 0, fs, wide_s)]
    fills += [(eg_hbm.at[e], egu, e * wide, f, wide) for e in range(EXP_DEV)]
    fills += [(eu_hbm.at[e], egu, ef + e * wide, f, wide) for e in range(EXP_DEV)]
    fills += [(sg_hbm, sgu, 0, fs, wide_s), (su_hbm, sgu, wide_s, fs, wide_s)]
    loads = [
        pltpu.make_async_copy(src, dst.at[pl.ds(at, real)], weight_sem.at[i])
        for i, (src, dst, at, real, _) in enumerate(fills)
    ]
    for load in loads:
        load.start()
    gate_load = pltpu.make_async_copy(gate_ref.at[:, :, :, :, :, pl.ds(LATENT, 128)], gates, gate_sem)
    gate_load.start()
    greet(grid)

    counts = [0]

    def place(bb, yy, cc, aa, h):
        return all_ref.at[aa, bb, yy, cc, pl.ds(h * half, half)]

    def slot(bb, yy, aa, h):
        return ((bb * ny + yy) * na + aa) * 2 + h

    def push(src, bb, yy, aa, h, where, send, recv):
        pltpu.make_async_remote_copy(
            src_ref=src,
            dst_ref=place(bb, yy, c, aa, h),
            send_sem=send,
            recv_sem=recv.at[slot(bb, yy, aa, h)],
            device_id=where,
            device_id_type=MESH,
        ).start()

    def line(i):
        if na != 4:
            return wrap(a + i, na)
        if i == 0:
            return a
        if i == 1:
            return a + 1 - 2 * lax.rem(a, 2)
        return (i - lax.div(a, 2)) if i == 2 else (3 - 3 * lax.div(a, 2))

    def onward(src, bb, yy, aa, h, dims):
        for d in dims:
            size = {"a": na, "b": nb, "y": ny}[d]
            for i in range(1, size):
                where = {
                    "a": lambda: grid.device(line(i), b, y, c),
                    "b": lambda: grid.device(a, wrap(b + i, nb), y, c),
                    "y": lambda: grid.device(a, b, wrap(y + i, ny), c),
                }[d]()
                push(src, bb, yy, aa, h, where, send_sem.at[counts[0]], recv_sem)
                counts[0] += 1
        push(
            src, bb, yy, aa, h, grid.device(a, b, y, 1 - c), share_send.at[slot(bb, yy, aa, h)], share_recv
        )

    def landed(bb, yy, cc, aa, h, sem):
        ref = place(bb, yy, cc, aa, h)
        pltpu.make_async_copy(ref, ref, sem.at[slot(bb, yy, aa, h)]).wait()
        return ref

    orders = (("b", "y"), ("y", "b"))

    def relay(j, k, i, h, dims):
        bb, yy, aa = wrap(b + j, nb), wrap(y + k, ny), line(i)
        onward(landed(bb, yy, c, aa, h, recv_sem), bb, yy, aa, h, dims)

    own = pltpu.make_async_copy(x_ref, all_ref.at[a, b, y, c], own_sem)
    own.start()
    for h in range(2):
        onward(x_ref.at[pl.ds(h * half, half)], b, y, a, h, ("a",) + orders[h])

    hooks = {}
    early = []
    for i in range(na):
        if i:
            early += [(0, 0, i, h, orders[h]) for h in range(2)]
        if i:
            early += [(j, 0, i - 1, 0, orders[0][1:]) for j in range(1, nb)]
            early += [(0, k, i - 1, 1, orders[1][1:]) for k in range(1, ny)]
    early += [(j, 0, na - 1, 0, orders[0][1:]) for j in range(1, nb)]
    early += [(0, k, na - 1, 1, orders[1][1:]) for k in range(1, ny)]
    for m, event in enumerate(early):
        place_at = 1 + m * (2 * steps - 1) // len(early)
        hooks.setdefault(("early", place_at // 2, place_at % 2), []).append(event)
    for pair in range(1, pairs):
        j, k = pair // ny, pair % ny
        late = [(j, k, i, h, ()) for i in range(na) for h in range(2) if (k if h == 0 else j)]
        for m, event in enumerate(late):
            hooks.setdefault(("main", pair, m * 3 // len(late)), []).append(event)

    def hook(stage, step, spot):
        for (when_stage, when, when_spot), events in hooks.items():
            if when_stage == stage and when_spot == spot:

                @pl.when(step == when)
                def _():
                    for event in events:
                        relay(*event)

    def spots(step):
        pair, l = lax.div(step, 2), 1 - lax.rem(step, 2)
        j, k = lax.div(pair, ny), lax.rem(pair, ny)
        return j, k, l, wrap(b + j, nb), wrap(y + k, ny), wrap(c + l, 2)

    def flat(value):
        return value.reshape(rows, value.shape[-1])

    def fold(value):
        return value.reshape(na, r, value.shape[-1])

    def dz_load(step):
        _, _, _, bb, yy, cc = spots(step)
        s = lax.rem(step, 2)
        return pltpu.make_async_copy(dz_ref.at[:, bb, yy, cc], dzbuf.at[s], dz_sem.at[s])

    dz_load(a * 0).start()
    for _, dst, at, real, padded in fills:
        if padded > real:
            dst[at + real : at + padded] = jnp.zeros((padded - real, n), bf)
    for load in loads[: EXP_DEV + 1]:
        load.wait()

    def early_body(step, carry):
        s = lax.rem(step, 2)

        @pl.when(step + 1 < steps)
        def _():
            dz_load(step + 1).start()

        dz_load(step).wait()
        dz = flat(dzbuf[s])
        dabuf[step, :, :ef] = dot_rows(dz, ed[...]).astype(bf)
        hook("early", step, 0)
        dabuf[step, :, ef:] = dot_rows(dz, sd[...]).astype(bf)
        hook("early", step, 1)
        return carry

    lax.fori_loop(0, steps, early_body, 0)
    for load in loads[EXP_DEV + 1 :]:
        load.wait()
    own.wait()
    gate_load.wait()

    def x_load(step):
        _, _, _, bb, yy, cc = spots(step)
        return pltpu.make_async_copy(all_ref.at[:, bb, yy, cc], xbuf.at[0], x_sem.at[0])

    def stores(step):
        _, _, _, bb, yy, cc = spots(step)
        s = lax.rem(step, 2)
        return [
            pltpu.make_async_copy(
                gated.at[s], acts_ref.at[:, bb, yy, cc, :, pl.ds(columns[2], ef)], out_sem.at[s, 0]
            ),
            pltpu.make_async_copy(
                dcat.at[s], acts_ref.at[:, bb, yy, cc, :, pl.ds(columns[0], 2 * ef)], out_sem.at[s, 1]
            ),
        ]

    def remote(src, dst, ss, rs, where):
        return pltpu.make_async_remote_copy(
            src_ref=src, dst_ref=dst, send_sem=ss, recv_sem=rs, device_id=where, device_id_type=MESH
        )

    def cols(p):
        return pl.ds(p * width, width)

    upper = (pl.ds(0, half), pl.ds(half, half))

    def send_core(pair):
        j, k = lax.div(pair, ny), lax.rem(pair, ny)
        return remote(
            dx_out.at[lax.rem(pair, 2)], core_in.at[j, k], core_s.at[lax.rem(pair, 2)],
            core_r.at[j, k], grid.device(a, b, y, 1 - c),
        )

    def send_10(p, j, k):
        return remote(
            dx.at[j, k, :, upper[0], cols(p)], d1_in0.at[p, j, k - 1], s10.at[p, j, k - 1],
            r10.at[p, j, k - 1], grid.device(a, b, wrap(y + k, ny), c),
        )

    def send_11(p, j, k):
        return remote(
            dx.at[j, k, :, upper[1], cols(p)], d1_in1.at[p, k, j - 1], s11.at[p, k, j - 1],
            r11.at[p, k, j - 1], grid.device(a, wrap(b + j, nb), y, c),
        )

    def await_in(ref, sem):
        pltpu.make_async_copy(ref, ref, sem).wait()

    def add(dst, src):
        dst[...] = (dst[...].astype(f32) + src[...].astype(f32)).astype(dst.dtype)

    def shared_front(step, x, s):
        g = dot_rows(x, sgu[:wide_s])
        u = dot_rows(x, sgu[wide_s:])
        d = dabuf[step, :, ef:].astype(f32)
        sig = 1.0 / (1.0 + jnp.exp(-g))
        swish = g * sig
        act[s] = fold((swish * u).astype(bf))
        dsh[s, :, :, :wide_s] = fold((d * u * (sig + swish * (1.0 - sig))).astype(bf))
        dsh[s, :, :, wide_s:] = fold((d * swish).astype(bf))

    def is_mine(bb, yy, cc):
        return lax.rem((bb * ny + yy) * 2 + cc, na * nb) == device

    chunk = min(n, 1024)

    def main_body(step, carry):
        j, k, l, bb, yy, cc = spots(step)
        s = lax.rem(step, 2)

        @pl.when(l == 1)
        def _():
            for i in range(na):
                for h in range(2):
                    landed(bb, yy, cc, line(i), h, share_recv)

        x_load(step).start()

        @pl.when(step >= 2)
        def _():
            for store in stores(step - 2):
                store.wait()

        x_load(step).wait()
        x = flat(xbuf[0])
        g = dot_rows(x, egu[:ef])
        u = dot_rows(x, egu[ef:])
        gate = flat(gates[:, bb, yy, cc]).astype(f32)
        lane = lax.broadcasted_iota(jnp.int32, gate.shape, 1) - (ROPE + EXP_DEV * device)
        experts_all = EXP_DEV * na * nb
        for e in range(EXP_DEV):
            at = pl.ds(e * wide, wide)
            hit = (lane == e) | (lane == e + experts_all)
            scale = jnp.sum(jnp.where(hit, gate, 0.0), axis=-1, keepdims=True)
            ge, ue = g[:, e * wide : (e + 1) * wide], u[:, e * wide : (e + 1) * wide]
            d = dabuf[step, :, at].astype(f32) * scale
            sig = 1.0 / (1.0 + jnp.exp(-ge))
            swish = ge * sig
            gated[s, :, :, at] = fold((scale * (swish * ue)).astype(bf))
            dcat[s, :, :, at] = fold((d * ue * (sig + swish * (1.0 - sig))).astype(bf))
            dcat[s, :, :, pl.ds(ef + e * wide, wide)] = fold((d * swish).astype(bf))
        hook("main", step, 0)
        mine = is_mine(bb, yy, cc)

        @pl.when(mine)
        def _():
            shared_front(step, x, 0)

        hook("main", step, 1)

        def column(target):
            for q in range(n // chunk):
                at = pl.ds(q * chunk, chunk)
                total = dot_plain(flat(dcat[s]), egu[:, at])
                target[:, :, at] = fold(total.astype(bf))

            @pl.when(mine)
            def _():
                for q in range(n // chunk):
                    at = pl.ds(q * chunk, chunk)
                    more = dot_plain(flat(dsh[0]), sgu[:, at])
                    target[:, :, at] = fold((flat(target[:, :, at]).astype(f32) + more).astype(bf))

        for store in stores(step):
            store.start()

        @pl.when(l == 1)
        def _():
            pair = lax.div(step, 2)

            @pl.when(pair >= 2)
            def _():
                send_core(pair - 2).wait_send()

            column(dx_out.at[lax.rem(pair, 2)])
            send_core(pair).start()

        @pl.when(l == 0)
        def _():
            column(dx.at[j, k])
            await_in(core_in.at[j, k], core_r.at[j, k])

            def one(i, carry):
                add(dx.at[j, k, i], core_in.at[j, k, i])
                return carry

            lax.fori_loop(0, na, one, 0)

            @pl.when(k > 0)
            def _():
                for p in range(pieces):
                    send_10(p, j, k).start()

            @pl.when(j > 0)
            def _():
                for p in range(pieces):
                    send_11(p, j, k).start()

        hook("main", step, 2)
        return carry

    lax.fori_loop(0, steps, main_body, 0)
    for step in (steps - 2, steps - 1):
        for store in stores(a * 0 + step):
            store.wait()

    def send_20(p, j):
        return remote(
            dx.at[j, 0, :, upper[0], cols(p)], d2_in0.at[p, j - 1], s20.at[p, j - 1],
            r20.at[p, j - 1], grid.device(a, wrap(b + j, nb), y, c),
        )

    def send_21(p, k):
        return remote(
            dx.at[0, k, :, upper[1], cols(p)], d2_in1.at[p, k - 1], s21.at[p, k - 1],
            r21.at[p, k - 1], grid.device(a, b, wrap(y + k, ny), c),
        )

    def send_a(p, i):
        return remote(
            dx.at[0, 0, wrap(a + i, na), :, cols(p)], a_in.at[p, i - 1], sa.at[p, i - 1],
            ra.at[p, i - 1], grid.device(wrap(a + i, na), b, y, c),
        )

    def sum_first(p):
        for j in reversed(range(nb)):
            for k in range(1, ny):
                await_in(d1_in0.at[p, j, k - 1], r10.at[p, j, k - 1])
                for i in range(na):
                    add(dx.at[j, 0, i, upper[0], cols(p)], d1_in0.at[p, j, k - 1, i])
            if j:
                send_20(p, j).start()
        for k in reversed(range(ny)):
            for j in range(1, nb):
                await_in(d1_in1.at[p, k, j - 1], r11.at[p, k, j - 1])
                for i in range(na):
                    add(dx.at[0, k, i, upper[1], cols(p)], d1_in1.at[p, k, j - 1, i])
            if k:
                send_21(p, k).start()

    def sum_second(p):
        for j in range(1, nb):
            await_in(d2_in0.at[p, j - 1], r20.at[p, j - 1])
            for i in range(na):
                add(dx.at[0, 0, i, upper[0], cols(p)], d2_in0.at[p, j - 1, i])
        for k in range(1, ny):
            await_in(d2_in1.at[p, k - 1], r21.at[p, k - 1])
            for i in range(na):
                add(dx.at[0, 0, i, upper[1], cols(p)], d2_in1.at[p, k - 1, i])
        for i in range(1, na):
            send_a(p, i).start()

    def sum_last(p):
        total = dx[0, 0, a, :, cols(p)].astype(f32)
        for i in range(1, na):
            await_in(a_in.at[p, i - 1], ra.at[p, i - 1])
            total = total + a_in[p, i - 1].astype(f32)
        grad_ref[:, cols(p)] = total

    work = [(sum_first, p) for p in range(pieces)] + [(sum_second, p) for p in range(pieces)]
    turns = {}
    for m, item in enumerate(work):
        turns.setdefault(min(steps - 1, 1 + m * (steps - 1) // len(work)), []).append(item)

    def fill_loads(step):
        _, _, _, bb, yy, cc = spots(step)
        s = lax.rem(step, 2)
        return [
            pltpu.make_async_copy(all_ref.at[:, bb, yy, cc], xbuf.at[s], x_sem.at[s]),
            pltpu.make_async_copy(
                acts_ref.at[:, bb, yy, cc, :, pl.ds(columns[2], ef)], gated.at[s], fill_sem.at[s]
            ),
        ]

    def fill_stores(step):
        _, _, _, bb, yy, cc = spots(step)
        s = lax.rem(step, 2)
        pairs_of = [
            (act.at[s], acts_ref.at[:, bb, yy, cc, :, pl.ds(columns[3], wide_s)]),
            (dsh.at[s], acts_ref.at[:, bb, yy, cc, :, pl.ds(columns[1], 2 * wide_s)]),
            (ybuf.at[s], y_ref.at[:, bb, yy, cc]),
        ]
        return [
            pltpu.make_async_copy(src, dst, out_sem.at[s, i])
            for i, (src, dst) in enumerate(pairs_of)
        ]

    for load in fill_loads(a * 0):
        load.start()

    def fill_body(step, carry):
        j, k, l, bb, yy, cc = spots(step)
        s = lax.rem(step, 2)

        @pl.when(step + 1 < steps)
        def _():
            for load in fill_loads(step + 1):
                load.start()

        @pl.when(step >= 2)
        def _():
            for store in fill_stores(step - 2):
                store.wait()

        for load in fill_loads(step):
            load.wait()
        x = flat(xbuf[s])
        shared_front(step, x, s)
        for q in range(n // chunk):
            at = pl.ds(q * chunk, chunk)
            ybuf[s, :, :, at] = fold(dot_plain(flat(gated[s]), ed[:, at]).astype(bf))

        @pl.when(is_mine(bb, yy, cc))
        def _():
            for q in range(n // chunk):
                at = pl.ds(q * chunk, chunk)
                more = dot_plain(flat(act[s]), sd[:, at])
                ybuf[s, :, :, at] = fold((flat(ybuf[s, :, :, at]).astype(f32) + more).astype(bf))

        for store in fill_stores(step):
            store.start()
        for when, items in turns.items():

            @pl.when(step == when)
            def _():
                for item, p in items:
                    item(p)

        return carry

    lax.fori_loop(0, steps, fill_body, 0)
    for p in range(pieces):
        sum_last(p)

    for step in (steps - 2, steps - 1):
        for store in fill_stores(a * 0 + step):
            store.wait()
    some = place(b, y, c, a, 0)
    for i in range(counts[0]):
        pltpu.make_async_copy(some, some, send_sem.at[i]).wait()
    for i in range(2 * na * pairs):
        pltpu.make_async_copy(some, some, share_send.at[i]).wait()
    for pair in range(max(0, pairs - 2), pairs):
        send_core(a * 0 + pair).wait_send()
    for p in range(pieces):
        for j in range(nb):
            for k in range(ny):
                if k:
                    send_10(p, j, k).wait_send()
                if j:
                    send_11(p, j, k).wait_send()
        for j in range(1, nb):
            send_20(p, j).wait_send()
        for k in range(1, ny):
            send_21(p, k).wait_send()
        for i in range(1, na):
            send_a(p, i).wait_send()


def columns_of(ef, wide_s):
    return (0, 2 * ef, 2 * ef + 2 * wide_s, 3 * ef + 2 * wide_s, 3 * ef + 3 * wide_s)


def experts_call(
    grid, x, dz, gates, expert_gate, expert_up, expert_down, shared_gate, shared_up, shared_down,
    collective_id, pieces=2,
):
    r, n = x.shape
    na, nb, ny = grid.na, grid.nb, grid.ny
    f, fs = expert_down.shape[1], shared_down.shape[0]
    wide, wide_s = round_up(f, 128), round_up(fs, 128)
    ef = EXP_DEV * wide
    half, width, rows = r // 2, n // pieces, na * r
    steps = 2 * nb * ny
    lay = (na, nb, ny, 2, r)
    bf = jnp.bfloat16
    sems = lambda *s: pltpu.SemaphoreType.DMA(s)
    vm = lambda *s: pltpu.VMEM(s, bf)
    sends = 2 * (na - 1 + na * (nb - 1) + na * (ny - 1) + na * (nb - 1) * (ny - 1))
    any_space = pl.BlockSpec(memory_space=pl.ANY)
    in_vmem = pl.BlockSpec(memory_space=pltpu.VMEM)
    outs = pl.pallas_call(
        functools.partial(experts_kernel, grid, pieces),
        out_shape=[
            jax.ShapeDtypeStruct(lay + (n,), bf),
            jax.ShapeDtypeStruct((r, n), jnp.float32),
            jax.ShapeDtypeStruct(lay + (n,), bf),
            jax.ShapeDtypeStruct(lay + (columns_of(ef, wide_s)[-1],), bf),
        ],
        in_specs=[any_space] * 9,
        out_specs=[any_space, in_vmem] + [any_space] * 2,
        scratch_shapes=[
            vm(*lay, 128), vm(2 * ef, n), vm(ef, n), vm(2 * wide_s, n), vm(wide_s, n),
            vm(steps, rows, ef + wide_s),
            vm(2, na, r, n), vm(2, na, r, n),
            vm(2, na, r, ef), vm(2, na, r, 2 * ef),
            vm(2, na, r, wide_s), vm(2, na, r, 2 * wide_s),
            vm(2, na, r, n),
            vm(nb, ny, na, r, n),
            vm(2, na, r, n),
            vm(nb, ny, na, r, n),
            vm(pieces, nb, ny - 1, na, half, width),
            vm(pieces, ny, nb - 1, na, half, width),
            vm(pieces, nb - 1, na, half, width),
            vm(pieces, ny - 1, na, half, width),
            vm(pieces, na - 1, r, width),
            pltpu.SemaphoreType.DMA, sems(3 * EXP_DEV + 3), pltpu.SemaphoreType.DMA, sems(2), sems(2),
            sems(2, 4), sems(2),
            sems(sends), sems(2 * na * nb * ny), sems(2 * na * nb * ny), sems(2 * na * nb * ny),
            sems(2), sems(nb, ny),
            sems(pieces, nb, ny - 1), sems(pieces, nb, ny - 1),
            sems(pieces, ny, nb - 1), sems(pieces, ny, nb - 1),
            sems(pieces, nb - 1), sems(pieces, nb - 1),
            sems(pieces, ny - 1), sems(pieces, ny - 1),
            sems(pieces, na - 1), sems(pieces, na - 1),
        ],
        cost_estimate=microseconds(130),
        compiler_params=pltpu.CompilerParams(
            collective_id=collective_id, has_side_effects=True, vmem_limit_bytes=63 << 20
        ),
    )(
        x,
        dz.reshape(lay + (n,)),
        gates.reshape(lay + (gates.shape[-1],)),
        jnp.swapaxes(expert_gate, 1, 2), jnp.swapaxes(expert_up, 1, 2), expert_down,
        shared_gate.T, shared_up.T, shared_down,
    )
    tokens = grid.size * r
    rows_all, grad, out_rows, acts = outs
    return rows_all.reshape(tokens, n), grad, out_rows.reshape(tokens, n), acts.reshape(tokens, -1)


class Reduce:
    @staticmethod
    def scratch(grid, r, width):
        na, nb, ny = grid.na, grid.nb, grid.ny
        head = Reduce.head(r)
        sems = lambda *s: pltpu.SemaphoreType.DMA(s)
        vm = lambda *s: pltpu.VMEM(s, jnp.bfloat16)
        return [
            vm(nb, ny, na, r, width), vm(nb, ny, na, r, width),
            vm(nb, ny - 1, na, head, width), vm(ny, nb - 1, na, max(16, r - head), width),
            vm(nb - 1, na, head, width), vm(ny - 1, na, max(16, r - head), width), vm(na - 1, r, width),
            sems(nb, ny), sems(nb, ny), sems(nb, ny),
            sems(nb, ny - 1), sems(nb, ny - 1), sems(ny, nb - 1), sems(ny, nb - 1),
            sems(nb - 1), sems(nb - 1), sems(ny - 1), sems(ny - 1), sems(na - 1), sems(na - 1),
        ]

    count = 20

    @staticmethod
    def head(r):
        return r

    @staticmethod
    def schedule(sums):
        stages = [[one.core, one.first, one.second] for one in sums]
        work = []
        for beat in range(len(sums) + 2):
            for back in range(3):
                if 0 <= beat - back < len(sums):
                    work.append(stages[beat - back][back])
        return work

    def __init__(self, grid, source, out, scratch):
        self.grid, self.source, self.out = grid, source, out
        (
            self.acc, self.core_in, self.in10, self.in11, self.in20, self.in21, self.a_in,
            self.load_sem, self.core_s, self.core_r, self.s10, self.r10, self.s11, self.r11,
            self.s20, self.r20, self.s21, self.r21, self.sa, self.ra,
        ) = scratch
        self.spot = grid.here()
        r = self.acc.shape[3]
        head = Reduce.head(r)
        self.both = head < r
        self.upper = (pl.ds(0, head), pl.ds(head, r - head) if self.both else None)
        self.spots = [(j, k) for j in reversed(range(grid.nb)) for k in reversed(range(grid.ny))]

    def remote(self, src, dst, ss, rs, where):
        return pltpu.make_async_remote_copy(
            src_ref=src, dst_ref=dst, send_sem=ss, recv_sem=rs, device_id=where, device_id_type=MESH
        )

    def core_copy(self, j, k):
        g, (a, b, y, c) = self.grid, self.spot
        return self.remote(
            self.source.at[:, wrap(b + j, g.nb), wrap(y + k, g.ny), 1 - c], self.core_in.at[j, k],
            self.core_s.at[j, k], self.core_r.at[j, k], g.device(a, b, y, 1 - c),
        )

    def load(self, j, k):
        g, (a, b, y, c) = self.grid, self.spot
        return pltpu.make_async_copy(
            self.source.at[:, wrap(b + j, g.nb), wrap(y + k, g.ny), c], self.acc.at[j, k], self.load_sem.at[j, k]
        )

    def copy10(self, j, k):
        g, (a, b, y, c) = self.grid, self.spot
        return self.remote(
            self.acc.at[j, k, :, self.upper[0]], self.in10.at[j, k - 1], self.s10.at[j, k - 1],
            self.r10.at[j, k - 1], g.device(a, b, wrap(y + k, g.ny), c),
        )

    def copy11(self, j, k):
        g, (a, b, y, c) = self.grid, self.spot
        return self.remote(
            self.acc.at[j, k, :, self.upper[1]], self.in11.at[k, j - 1], self.s11.at[k, j - 1],
            self.r11.at[k, j - 1], g.device(a, wrap(b + j, g.nb), y, c),
        )

    def copy20(self, j):
        g, (a, b, y, c) = self.grid, self.spot
        return self.remote(
            self.acc.at[j, 0, :, self.upper[0]], self.in20.at[j - 1], self.s20.at[j - 1],
            self.r20.at[j - 1], g.device(a, wrap(b + j, g.nb), y, c),
        )

    def copy21(self, k):
        g, (a, b, y, c) = self.grid, self.spot
        return self.remote(
            self.acc.at[0, k, :, self.upper[1]], self.in21.at[k - 1], self.s21.at[k - 1],
            self.r21.at[k - 1], g.device(a, b, wrap(y + k, g.ny), c),
        )

    def copy_a(self, i):
        g, (a, b, y, c) = self.grid, self.spot
        return self.remote(
            self.acc.at[0, 0, wrap(a + i, g.na)], self.a_in.at[i - 1], self.sa.at[i - 1],
            self.ra.at[i - 1], g.device(wrap(a + i, g.na), b, y, c),
        )

    def add(self, into, rows, ref, sem):
        pltpu.make_async_copy(ref, ref, sem).wait()
        f32 = jnp.float32

        def one(i, carry):
            total = into[i, rows].astype(f32) + ref[i].astype(f32)
            into[i, rows] = total.astype(into.dtype)
            return carry

        lax.fori_loop(0, self.grid.na, one, 0)

    def start(self):
        for j, k in self.spots:
            self.core_copy(j, k).start()
            self.load(j, k).start()

    def core(self):
        whole = pl.ds(0, self.acc.shape[3])
        for j, k in self.spots:
            self.load(j, k).wait()
            self.add(self.acc.at[j, k], whole, self.core_in.at[j, k], self.core_r.at[j, k])
            if k:
                self.copy10(j, k).start()
            if j and self.both:
                self.copy11(j, k).start()

    def first(self):
        nb, ny = self.grid.nb, self.grid.ny
        for j in reversed(range(nb)):
            for k in range(1, ny):
                self.add(self.acc.at[j, 0], self.upper[0], self.in10.at[j, k - 1], self.r10.at[j, k - 1])
            if j:
                self.copy20(j).start()
        for k in reversed(range(ny if self.both else 0)):
            for j in range(1, nb):
                self.add(self.acc.at[0, k], self.upper[1], self.in11.at[k, j - 1], self.r11.at[k, j - 1])
            if k:
                self.copy21(k).start()

    def second(self):
        for j in range(1, self.grid.nb):
            self.add(self.acc.at[0, 0], self.upper[0], self.in20.at[j - 1], self.r20.at[j - 1])
        for k in range(1, self.grid.ny if self.both else 0):
            self.add(self.acc.at[0, 0], self.upper[1], self.in21.at[k - 1], self.r21.at[k - 1])
        for i in range(1, self.grid.na):
            self.copy_a(i).start()

    def last(self):
        total = self.acc[0, 0, self.spot[0]].astype(jnp.float32)
        for i in range(1, self.grid.na):
            pltpu.make_async_copy(self.a_in.at[i - 1], self.a_in.at[i - 1], self.ra.at[i - 1]).wait()
            total = total + self.a_in[i - 1].astype(jnp.float32)
        self.out[...] = total.astype(self.out.dtype)

    def finish(self):
        for j, k in self.spots:
            self.core_copy(j, k).wait_send()
            if k:
                self.copy10(j, k).wait_send()
            if j and self.both:
                self.copy11(j, k).wait_send()
        for j in range(1, self.grid.nb):
            self.copy20(j).wait_send()
        for k in range(1, self.grid.ny if self.both else 0):
            self.copy21(k).wait_send()
        for i in range(1, self.grid.na):
            self.copy_a(i).wait_send()


W_PIECES = 1


def gradients_kernel(grid, pieces, unit, places, *refs):
    (y_ref, k_ref, w_ref, t_ref, q_ref, x_ref, dz_ref, acts_ref), refs = refs[:8], refs[8:]
    (y_out, k_out, w_out, t_out, q_out), refs = refs[:5], refs[5:]
    outs, refs = refs[:6], refs[6:]
    (big, left, right, big_sem, left_sem, out_sem), refs = refs[:6], refs[6:]
    width = y_ref.shape[-1] // pieces
    sources = [(k_ref, k_out)]
    for p in range(pieces):
        at = pl.ds(p * width, width)
        sources.append((y_ref.at[:, :, :, :, :, at], y_out.at[:, at]))
    sums = [
        Reduce(grid, src, out, refs[m * Reduce.count : (m + 1) * Reduce.count])
        for m, (src, out) in enumerate(sources)
    ]
    refs = refs[len(sums) * Reduce.count :]
    w_width = w_ref.shape[-1] // W_PIECES
    flat_sums = []
    for p in range(W_PIECES):
        at = pl.ds(p * w_width, w_width)
        part = refs[p * PlaneReduce.count : (p + 1) * PlaneReduce.count]
        flat_sums.append(PlaneReduce(grid, w_ref.at[:, :, :, at], w_out.at[:, at], part))
    refs = refs[W_PIECES * PlaneReduce.count :]
    flat_sums.append(TensorReduce(grid, t_ref, t_out, refs[: TensorReduce.count]))
    q_gather = PlaneGather(grid, q_ref, q_out, refs[TensorReduce.count :])
    tiles = len(places)
    turn = sum(1 for place in places if place[0] != 2 and place[0] != 5)
    slots = big.shape[0]

    def left_load(m):
        s = lax.rem(m, 2)
        at = pl.ds(pl.multiple_of(m * unit, unit), unit)
        return pltpu.make_async_copy(acts_ref.at[:, at], left.at[s], left_sem.at[s])

    big_loads = [
        pltpu.make_async_copy(src, big.at[s % slots], big_sem.at[s]) for s, src in enumerate((x_ref, dz_ref))
    ]
    big_loads[0].start()
    greet(grid)
    for one in sums + flat_sums + [q_gather]:
        one.start()
    left_load(grid.here()[0] * 0).start()
    if slots > 1:
        big_loads[1].start()
    big_loads[0].wait()

    work = Reduce.schedule(sums)
    for p, one in enumerate(flat_sums):
        work.insert(min(len(work), 3 + 3 * p), one.middle)
    for i in range(1, grid.na):
        work.insert(min(len(work), 3 + 3 * i), functools.partial(q_gather.middle, i))
    turns = {}
    for n, item in enumerate(work):
        turns.setdefault(n * tiles // len(work), []).append(item)

    def store(m):
        which, head, first, rows = places[m]
        dst = outs[which]
        dst = dst.at[pl.ds(first, rows)] if head is None else dst.at[head, pl.ds(first, rows)]
        return pltpu.make_async_copy(right.at[m % 2, pl.ds(0, rows)], dst, out_sem.at[m % 2])

    def tile_body(m, carry):
        s = lax.rem(m, 2)

        @pl.when(m + 1 < tiles)
        def _():
            left_load(m + 1).start()

        for n in range(2, tiles):

            @pl.when(m == n)
            def _():
                store(n - 2).wait()

        @pl.when(m == turn)
        def _():
            if slots == 1:
                big_loads[1].start()
            big_loads[1].wait()

        left_load(m).wait()
        operand = big.at[lax.div(m, turn) if slots > 1 else 0]
        right[s] = lax.dot_general(
            left[s], operand[...], (((0,), (0,)), ((), ())), preferred_element_type=jnp.float32
        ).astype(right.dtype)
        for n in range(tiles):

            @pl.when(m == n)
            def _():
                store(n).start()
                for item in turns.get(n, ()):
                    item()

        return carry

    lax.fori_loop(0, tiles, tile_body, 0)
    for one in sums + flat_sums:
        one.last()
    for n in range(max(0, tiles - 2), tiles):
        store(n).wait()
    for one in sums + flat_sums:
        one.finish()
    q_gather.last()


def gradients_call(grid, out_rows, key_rows, weight_rows, tensor_rows, query_rows, x, dz, acts, f, fs, collective_id, pieces=4):
    tokens, n = x.shape
    r = tokens // grid.size
    lay = (grid.na, grid.nb, grid.ny, 2, r)
    wide, wide_s = round_up(f, 128), round_up(fs, 128)
    unit = math.gcd(wide, wide_s)
    places = []
    for which, heads, real, padded in (
        (0, EXP_DEV, f, wide), (1, EXP_DEV, f, wide), (3, 0, fs, wide_s), (4, 0, fs, wide_s),
        (2, EXP_DEV, f, wide), (5, 0, fs, wide_s),
    ):
        for head in range(max(heads, 1)):
            for first in range(0, padded, unit):
                places.append((which, head if heads else None, first, min(unit, real - first)))
    slots = 2 if 2 * tokens * n * 2 <= (24 << 20) else 1
    any_space = pl.BlockSpec(memory_space=pl.ANY)
    in_vmem = pl.BlockSpec(memory_space=pltpu.VMEM)
    f32 = jnp.float32
    scratch = [
        pltpu.VMEM((slots, tokens, n), x.dtype),
        pltpu.VMEM((2, tokens, unit), x.dtype),
        pltpu.VMEM((2, unit, n), x.dtype),
        pltpu.SemaphoreType.DMA((2,)),
        pltpu.SemaphoreType.DMA((2,)),
        pltpu.SemaphoreType.DMA((2,)),
    ]
    kw = key_rows.shape[1]
    for width in [kw] + [n // pieces] * pieces:
        scratch += Reduce.scratch(grid, r, width)
    wr, ww = weight_rows.shape[0] // (grid.na * grid.nb), weight_rows.shape[1]
    scratch += PlaneReduce.scratch(grid, wr, ww // W_PIECES) * W_PIECES
    tr, tw = tensor_rows.shape[0] // (2 * grid.ny), tensor_rows.shape[1]
    scratch += TensorReduce.scratch(grid, tr, tw) + PlaneGather.scratch(grid)
    outs = pl.pallas_call(
        functools.partial(gradients_kernel, grid, pieces, unit, places),
        out_shape=[
            jax.ShapeDtypeStruct((r, n), f32),
            jax.ShapeDtypeStruct((r, kw), f32),
            jax.ShapeDtypeStruct((wr, ww), x.dtype),
            jax.ShapeDtypeStruct((tr, tw), f32),
            jax.ShapeDtypeStruct((grid.na, grid.nb) + query_rows.shape, x.dtype),
            jax.ShapeDtypeStruct((EXP_DEV, f, n), x.dtype),
            jax.ShapeDtypeStruct((EXP_DEV, f, n), x.dtype),
            jax.ShapeDtypeStruct((EXP_DEV, f, n), x.dtype),
            jax.ShapeDtypeStruct((fs, n), x.dtype),
            jax.ShapeDtypeStruct((fs, n), x.dtype),
            jax.ShapeDtypeStruct((fs, n), x.dtype),
        ],
        in_specs=[any_space] * 8,
        out_specs=[in_vmem] * 4 + [any_space] * 7,
        scratch_shapes=scratch,
        cost_estimate=microseconds(90),
        compiler_params=pltpu.CompilerParams(
            collective_id=collective_id, has_side_effects=True, vmem_limit_bytes=62 << 20
        ),
    )(
        out_rows.reshape(lay + (n,)),
        key_rows.reshape(lay + (kw,)),
        weight_rows.reshape(grid.na, grid.nb, wr, ww),
        tensor_rows.reshape(grid.ny, 2, tr, tw),
        query_rows,
        x,
        dz,
        acts,
    )
    y_sum, k_sum, w_sum, t_sum, q_all = outs[:5]
    eg, eu, ed, sg, su, sd = (out.astype(f32) for out in outs[5:])
    q_all = q_all.reshape(tokens, -1)
    weights = (jnp.swapaxes(eg, 1, 2), jnp.swapaxes(eu, 1, 2), ed, sg.T, su.T, sd)
    return y_sum, k_sum, w_sum, t_sum, q_all, weights


class GatherAll:
    @staticmethod
    def scratch(grid):
        blocks = 2 * grid.na * grid.nb * grid.ny
        sems = lambda n: pltpu.SemaphoreType.DMA((n,))
        return [sems(1), sems(gather_sends(grid)), sems(blocks), sems(blocks), sems(blocks)]

    def __init__(self, grid, x, out, scratch, halves=2):
        self.grid, self.x, self.out, self.halves = grid, x, out, halves
        self.own_sem, self.sends, self.recvs, self.share_s, self.share_r = scratch
        self.spot = grid.here()
        self.half = x.shape[0] // halves
        self.count = 0
        na, nb, ny = grid.na, grid.nb, grid.ny
        self.orders = (("b", "y"), ("y", "b"))
        near = [(0, k, 0, 0, ()) for k in range(1, ny)] + [(0, k, 0, 1, ("b",)) for k in range(1, ny)]
        first = [(0, 0, i, h, self.orders[h]) for i in range(1, na) for h in range(2)]
        second = []
        for i in range(na):
            second += [(j, 0, i, 0, ("y",)) for j in range(1, nb)]
            second += [(0, k, i, 1, ("b",)) for k in range(1, ny) if i]
        third = []
        for i in range(na):
            third += [(0, k, i, 0, ()) for k in range(1, ny) if i]
            third += [(j, 0, i, 1, ()) for j in range(1, nb)]
        for i in range(na):
            third += [(j, k, i, h, ()) for j in range(1, nb) for k in range(1, ny) for h in range(2)]
        self.near = [event for event in near if event[3] < halves]
        self.others = [event for event in first + second + third if event[3] < halves]

    def line(self, i):
        a = self.spot[0]
        if self.grid.na != 4:
            return wrap(a + i, self.grid.na)
        if i == 0:
            return a
        if i == 1:
            return a + 1 - 2 * lax.rem(a, 2)
        return (i - lax.div(a, 2)) if i == 2 else (3 - 3 * lax.div(a, 2))

    def place(self, bb, yy, cc, aa, h):
        return self.out.at[aa, bb, yy, cc, pl.ds(h * self.half, self.half)]

    def slot(self, bb, yy, aa, h):
        return ((bb * self.grid.ny + yy) * self.grid.na + aa) * 2 + h

    def push(self, src, bb, yy, aa, h, where, send, recv):
        pltpu.make_async_remote_copy(
            src_ref=src, dst_ref=self.place(bb, yy, self.spot[3], aa, h), send_sem=send,
            recv_sem=recv.at[self.slot(bb, yy, aa, h)], device_id=where, device_id_type=MESH,
        ).start()

    def onward(self, src, bb, yy, aa, h, dims):
        g, (a, b, y, c) = self.grid, self.spot
        for d in dims:
            for i in range(1, {"a": g.na, "b": g.nb, "y": g.ny}[d]):
                if d == "a":
                    where = g.device(self.line(i), b, y, c)
                elif d == "b":
                    where = g.device(a, wrap(b + i, g.nb), y, c)
                else:
                    where = g.device(a, b, wrap(y + i, g.ny), c)
                self.push(src, bb, yy, aa, h, where, self.sends.at[self.count], self.recvs)
                self.count += 1
        where = g.device(a, b, y, 1 - c)
        self.push(src, bb, yy, aa, h, where, self.share_s.at[self.slot(bb, yy, aa, h)], self.share_r)

    def landed(self, bb, yy, cc, aa, h, sem):
        ref = self.place(bb, yy, cc, aa, h)
        pltpu.make_async_copy(ref, ref, sem.at[self.slot(bb, yy, aa, h)]).wait()
        return ref

    def own(self):
        a, b, y, c = self.spot
        return pltpu.make_async_copy(self.x, self.out.at[a, b, y, c], self.own_sem.at[0])

    def start(self):
        a, b, y, c = self.spot
        self.own().start()
        for h in range(self.halves):
            src = self.x.at[pl.ds(h * self.half, self.half)]
            self.onward(src, b, y, a, h, ("y", "a", "b") if h == 0 else ("y", "b", "a"))

    def relay(self, j, k, i, h, dims):
        g, (a, b, y, c) = self.grid, self.spot
        bb, yy, aa = wrap(b + j, g.nb), wrap(y + k, g.ny), self.line(i)
        self.onward(self.landed(bb, yy, c, aa, h, self.recvs), bb, yy, aa, h, dims)

    def shared(self, j, k, i):
        g, (a, b, y, c) = self.grid, self.spot
        for h in range(self.halves):
            self.landed(wrap(b + j, g.nb), wrap(y + k, g.ny), 1 - c, self.line(i), h, self.share_r)

    def group(self):
        for event in self.near:
            self.relay(*event)
        for k in range(self.grid.ny):
            self.shared(0, k, 0)
        self.own().wait()

    def finish(self):
        g, (a, b, y, c) = self.grid, self.spot
        for j in range(g.nb):
            for k in range(g.ny):
                for i in range(g.na):
                    if i or j:
                        self.shared(j, k, i)
        some = self.place(b, y, c, a, 0)
        for i in range(self.count):
            pltpu.make_async_copy(some, some, self.sends.at[i]).wait()
        for i in range(g.na * g.nb * g.ny):
            for h in range(self.halves):
                pltpu.make_async_copy(some, some, self.share_s.at[2 * i + h]).wait()


def turn_back(values, cosines, sines):
    quarter = ROPE // 2
    lane = lax.broadcasted_iota(jnp.int32, values.shape, 1)
    swapped = jnp.where(
        lane < quarter,
        pltpu.roll(values, values.shape[1] - quarter, 1),
        pltpu.roll(values, quarter, 1),
    )
    return values * cosines + swapped * sines


def attention_back_kernel(
    grid,
    pieces,
    x_ref,
    wo_hbm,
    q_hbm,
    kv_hbm,
    packed_hbm,
    we_hbm,
    ctx_ref,
    log_ref,
    seg_ref,
    own_seg_ref,
    cos_ref,
    sin_ref,
    dq_ref,
    keys_ref,
    part_ref,
    wo_ref,
    wo,
    q,
    kv,
    packed,
    we,
    grads,
    kcat,
    bias,
    dkv,
    drope,
    wo_part,
    load_sem,
    *scratch,
):
    f32, bf = jnp.float32, jnp.bfloat16
    rows, tokens = q.shape[0], kv.shape[0]
    heads = q.shape[1] // 256
    scale = (NOPE + ROPE) ** (-0.5)
    a, b, y, c = grid.here()
    pairs = ((wo_hbm, wo), (q_hbm, q), (kv_hbm, kv), (packed_hbm, packed), (we_hbm, we))
    loads = [pltpu.make_async_copy(src, dst, load_sem.at[i]) for i, (src, dst) in enumerate(pairs)]
    for load in loads:
        load.start()
    greet(grid)
    group = TensorGather(grid, x_ref, grads, scratch[: TensorGather.count])
    group.start()
    sums = []
    width = wo.shape[1] // pieces
    for p in range(pieces):
        first = TensorGather.count + p * PlaneReduce.count
        at = pl.ds(p * width, width)
        sums.append(
            PlaneReduce(
                grid, wo_part.at[:, :, :, at], wo_ref.at[:, at], scratch[first : first + PlaneReduce.count]
            )
        )
    first_row = (a * grid.nb + b) * rows
    ordinal = first_row + lax.broadcasted_iota(jnp.int32, (rows, tokens), 0)
    key = lax.broadcasted_iota(jnp.int32, (rows, tokens), 1)
    seg = seg_ref[...]
    seen = (key <= ordinal) & ((seg == own_seg_ref[...]) | (seg == 0))
    bias[...] = jnp.where(seen, 0.0, masked_out)
    for load in loads:
        load.wait()
    kcat[:, NOPE:] = packed[:, LATENT : LATENT + 128]
    lane = lax.broadcasted_iota(jnp.int32, (tokens, 128), 1)
    kcat[:, NOPE:] = jnp.where(lane < ROPE, kcat[:, NOPE:].astype(f32), 0.0).astype(bf)

    group.middle(1)
    group.last()
    rows_in = grads[...].reshape(rows, grads.shape[-1])
    for p in range(pieces):
        at = pl.ds(p * width, width)
        wo_part[:, :, :, at] = (
            lax.dot_general(
                ctx_ref[...], rows_in[:, p * width : (p + 1) * width], (((0,), (0,)), ((), ())),
                preferred_element_type=f32,
            )
            .astype(bf)
            .reshape(wo_part.shape[:3] + (width,))
        )
        sums[p].start()
    dctx = dot_rows(rows_in, wo[...]).astype(bf)

    points = 3 * heads + 1
    at_point = {}
    for p in range(pieces):
        at_point.setdefault((p + 1) * points // (pieces + 2), []).append(sums[p].middle)
    done = [0]

    def hook():
        for event in at_point.get(done[0], ()):
            event()
        done[0] += 1

    hook()
    for h in range(heads):
        qh = q[:, h * 256 : (h + 1) * 256]
        kcat[:, :NOPE] = kv[:, h * 256 : h * 256 + NOPE]
        s = dot_rows(qh, kcat[...]) * scale + bias[...]
        p = jnp.exp(s - log_ref[h])
        dh = dctx[:, h * VDIM : (h + 1) * VDIM]
        dp = dot_rows(dh, kv[:, h * 256 + NOPE : (h + 1) * 256])
        ds = (p * (dp - jnp.sum(p * dp, axis=-1, keepdims=True))).astype(bf)
        p = p.astype(bf)
        hook()
        dq = dot_plain(ds, kcat[...]) * scale
        dq_ref[:, h * 256 : h * 256 + NOPE] = dq[:, :NOPE].astype(bf)
        dq_ref[:, h * 256 + NOPE : (h + 1) * 256] = turn_back(
            dq[:, NOPE:], cos_ref[...], sin_ref[...]
        ).astype(bf)
        hook()
        dkv[:, h * 256 + NOPE : (h + 1) * 256] = lax.dot_general(
            p, dh, (((0,), (0,)), ((), ())), preferred_element_type=f32
        ).astype(bf)
        dk = scale * lax.dot_general(ds, qh, (((0,), (0,)), ((), ())), preferred_element_type=f32)
        dkv[:, h * 256 : h * 256 + NOPE] = dk[:, :NOPE].astype(bf)
        if h == 0:
            drope[...] = dk[:, NOPE:]
        else:
            drope[...] += dk[:, NOPE:]
        hook()
    keys_ref[:, :LATENT] = dot_rows(dkv[...], we[...]).astype(bf)
    keys_ref[:, LATENT:] = drope[...].astype(bf)
    part_ref[...] = lax.dot_general(
        packed[:, :LATENT], dkv[...], (((0,), (0,)), ((), ())), preferred_element_type=f32
    ).astype(bf)
    for one in sums:
        one.last()
    for one in sums:
        one.finish()


def attention_back_call(
    grid, x, wo, q, kv, packed, we, context, log_total, seg, own_seg, cosines, sines, collective_id, pieces=4
):
    r, n = x.shape
    rows, tokens, heads = q.shape[0], kv.shape[0], q.shape[1] // 256
    bf, f32 = jnp.bfloat16, jnp.float32
    any_space = pl.BlockSpec(memory_space=pl.ANY)
    in_vmem = pl.BlockSpec(memory_space=pltpu.VMEM)
    share = wo.shape[0] // (grid.na * grid.nb)
    return pl.pallas_call(
        functools.partial(attention_back_kernel, grid, pieces),
        out_shape=[
            jax.ShapeDtypeStruct(q.shape, bf),
            jax.ShapeDtypeStruct((tokens, LATENT + 128), bf),
            jax.ShapeDtypeStruct(we.shape, bf),
            jax.ShapeDtypeStruct((share, n), bf),
        ],
        in_specs=[any_space] * 6 + [in_vmem] * 6,
        out_specs=[in_vmem] * 4,
        scratch_shapes=[
            pltpu.VMEM(wo.shape, bf),
            pltpu.VMEM(q.shape, bf),
            pltpu.VMEM(kv.shape, bf),
            pltpu.VMEM(packed.shape, bf),
            pltpu.VMEM(we.shape, bf),
            pltpu.VMEM((grid.ny, 2, r, n), bf),
            pltpu.VMEM((tokens, 256), bf),
            pltpu.VMEM((rows, tokens), f32),
            pltpu.VMEM(kv.shape, bf),
            pltpu.VMEM((tokens, 128), f32),
            pltpu.VMEM((grid.na, grid.nb, share, n), bf),
            pltpu.SemaphoreType.DMA((5,)),
        ]
        + TensorGather.scratch(grid)
        + PlaneReduce.scratch(grid, share, n // pieces) * pieces,
        cost_estimate=microseconds(50),
        compiler_params=pltpu.CompilerParams(
            collective_id=collective_id, has_side_effects=True, vmem_limit_bytes=62 << 20
        ),
    )(x, wo, q, kv, packed, we, context, log_total, seg, own_seg, cosines, sines)


def front_kernel(
    grid,
    hidden_ref,
    gain_ref,
    lgain_ref,
    mgain_ref,
    gate_ref,
    route_ref,
    cos_ref,
    sin_ref,
    seg_ref,
    own_seg_ref,
    cot_hbm,
    wl_hbm,
    wq_hbm,
    we_hbm,
    wo_hbm,
    packed_hbm,
    cot_all,
    kv_ref,
    q,
    normed_ref,
    comp_ref,
    log_ref,
    ctx_ref,
    res_ref,
    moe_ref,
    wl,
    wq,
    we,
    wo,
    normed,
    mine,
    packed,
    kv,
    kcat,
    bias,
    part,
    total,
    load_sem,
    kv_sem,
    packed_sem,
    *scratch,
):
    f32, bf = jnp.float32, jnp.bfloat16
    rows, few, tokens = hidden_ref.shape[0], mine.shape[0], kv.shape[0]
    heads = q.shape[1] // 256
    scale = (NOPE + ROPE) ** (-0.5)
    a, b, y, c = grid.here()
    pairs = (
        (wl_hbm, wl.at[pl.ds(0, LATENT + ROPE)]), (wq_hbm, wq), (we_hbm, we), (wo_hbm, wo),
    )
    loads = [pltpu.make_async_copy(src, dst, load_sem.at[i]) for i, (src, dst) in enumerate(pairs)]
    for load in loads:
        load.start()
    wl[LATENT + ROPE :] = jnp.zeros((wl.shape[0] - LATENT - ROPE, wl.shape[1]), bf)
    greet(grid)
    at = pl.ds(pl.multiple_of((y * 2 + c) * few, few), few)

    def rms(v, gain):
        return v * lax.rsqrt(jnp.mean(v * v, axis=-1, keepdims=True) + epsilon) * gain

    hidden_few = hidden_ref[at].astype(f32)
    normed_few = rms(hidden_few, gain_ref[...]).astype(bf)
    normed_ref[...] = normed_few
    loads[0].wait()
    comp = dot_rows(normed_few, wl[...])
    comp_ref[...] = comp
    mine[:, :LATENT] = rms(comp[:, :LATENT], lgain_ref[...]).astype(bf)
    tail = turn_back(comp[:, LATENT:], cos_ref[at], -sin_ref[at])
    lane = lax.broadcasted_iota(jnp.int32, tail.shape, 1) - ROPE
    routes, gates = route_ref[at], gate_ref[at]
    for k in range(TOP):
        expert, gate = routes[:, k : k + 1], gates[:, k : k + 1]
        high = gate.astype(bf).astype(f32)
        tail += jnp.where(lane == expert, high, 0.0)
        tail += jnp.where(lane == expert + EXP_DEV * grid.na * grid.nb, gate - high, 0.0)
    mine[:, LATENT:] = tail.astype(bf)
    gather = GatherAll(grid, mine, packed_hbm, scratch[:5], halves=1)
    gather.start()
    cots = GatherAll(grid, cot_hbm.at[at], cot_all, scratch[5:10])
    cots.start()
    normed[...] = rms(hidden_ref[...].astype(f32), gain_ref[...]).astype(bf)
    loads[1].wait()
    gather.group()
    third = len(gather.others) // 3
    for event in gather.others[:third]:
        gather.relay(*event)
    raw = dot_plain(normed[...], wq[...])
    width = raw.shape[1]
    for h in range(heads):
        step = h * (NOPE + ROPE)
        moved = raw if step == 0 else pltpu.roll(raw, width - step, 1)
        q[:, h * 256 : h * 256 + NOPE] = moved[:, :NOPE].astype(bf)
        q[:, h * 256 + NOPE : (h + 1) * 256] = turn_back(
            moved[:, NOPE : NOPE + 128], cos_ref[...], -sin_ref[...]
        ).astype(bf)
    for event in gather.others[third:]:
        gather.relay(*event)
    early = 2 * (grid.na - 1)
    for event in cots.near + cots.others[:early]:
        cots.relay(*event)
    ordinal = (a * grid.nb + b) * rows + lax.broadcasted_iota(jnp.int32, (rows, tokens), 0)
    key = lax.broadcasted_iota(jnp.int32, (rows, tokens), 1)
    seg = seg_ref[...]
    seen = (key <= ordinal) & ((seg == own_seg_ref[...]) | (seg == 0))
    bias[...] = jnp.where(seen, 0.0, masked_out)
    gather.finish()
    load = pltpu.make_async_copy(packed_hbm, packed, packed_sem)
    load.start()

    passing = [functools.partial(cots.relay, *event) for event in cots.others[early:]]
    at_point = {}
    for m, event in enumerate(passing):
        at_point.setdefault(m * (heads + 1) // len(passing), []).append(event)

    def hook(point):
        for event in at_point.get(point, ()):
            event()

    load.wait()
    hook(0)
    flat = packed[...].reshape(tokens, packed.shape[-1])
    lane = lax.broadcasted_iota(jnp.int32, (tokens, 128), 1)
    kcat[:, NOPE:] = jnp.where(lane < ROPE, flat[:, LATENT:].astype(f32), 0.0).astype(bf)
    loads[2].wait()
    kv[...] = dot_plain(flat[:, :LATENT], we[...]).astype(bf)
    store = pltpu.make_async_copy(kv, kv_ref, kv_sem)
    store.start()
    hook(1)
    for h in range(heads):
        kcat[:, :NOPE] = kv[:, h * 256 : h * 256 + NOPE]
        s = dot_rows(q[:, h * 256 : (h + 1) * 256], kcat[...]) * scale + bias[...]
        peak = jnp.max(s, axis=-1, keepdims=True)
        w = jnp.exp(s - peak)
        tot = jnp.sum(w, axis=-1, keepdims=True)
        log_ref[h] = peak + jnp.log(tot)
        p = (w * (1.0 / tot)).astype(bf)
        ctx_ref[:, h * VDIM : (h + 1) * VDIM] = dot_plain(
            p, kv[:, h * 256 + NOPE : (h + 1) * 256]
        ).astype(bf)
        hook(2 + h)
    loads[3].wait()
    part[...] = dot_plain(ctx_ref[...], wo[...]).astype(bf).reshape(part.shape)
    reduce = TensorReduce(grid, part, total, scratch[10:])
    reduce.start()
    reduce.middle()
    reduce.last()
    residual = hidden_ref[at].astype(f32) + total[...]
    res_ref[...] = residual
    moe_ref[...] = rms(residual, mgain_ref[...]).astype(bf)
    store.wait()
    for k in range(grid.ny):
        cots.shared(0, k, 0)
    cots.own().wait()
    cots.finish()
    reduce.finish()


def front_call(
    grid, hidden, cotangent, attn_gain, latent_gain, moe_gain, gates, routes, cosines, sines, seg, own_seg,
    latent_weight, query_weight, expand_weight, output_weight, collective_id,
):
    rows, n = hidden.shape
    few = rows // (2 * grid.ny)
    tokens = grid.size * few
    heads = query_weight.shape[1] // (NOPE + ROPE)
    bf, f32 = jnp.bfloat16, jnp.float32
    any_space = pl.BlockSpec(memory_space=pl.ANY)
    in_vmem = pl.BlockSpec(memory_space=pltpu.VMEM)
    width = LATENT + 128
    lay = (grid.na, grid.nb, grid.ny, 2, few)
    outs = pl.pallas_call(
        functools.partial(front_kernel, grid),
        out_shape=[
            jax.ShapeDtypeStruct(lay + (width,), bf),
            jax.ShapeDtypeStruct(lay + (n,), bf),
            jax.ShapeDtypeStruct((tokens, heads * 256), bf),
            jax.ShapeDtypeStruct((rows, heads * 256), bf),
            jax.ShapeDtypeStruct((few, n), bf),
            jax.ShapeDtypeStruct((few, width), f32),
            jax.ShapeDtypeStruct((heads, rows, 1), f32),
            jax.ShapeDtypeStruct((rows, heads * VDIM), bf),
            jax.ShapeDtypeStruct((few, n), f32),
            jax.ShapeDtypeStruct((few, n), bf),
        ],
        in_specs=[in_vmem] * 10 + [any_space] * 5,
        out_specs=[any_space] * 3 + [in_vmem] * 7,
        scratch_shapes=[
            pltpu.VMEM((width, n), bf),
            pltpu.VMEM(query_weight.shape, bf),
            pltpu.VMEM(expand_weight.shape, bf),
            pltpu.VMEM(output_weight.shape, bf),
            pltpu.VMEM((rows, n), bf),
            pltpu.VMEM((few, width), bf),
            pltpu.VMEM(lay + (width,), bf),
            pltpu.VMEM((tokens, heads * 256), bf),
            pltpu.VMEM((tokens, 256), bf),
            pltpu.VMEM((rows, tokens), f32),
            pltpu.VMEM((grid.ny, 2, few, n), bf),
            pltpu.VMEM((few, n), f32),
            pltpu.SemaphoreType.DMA((4,)),
            pltpu.SemaphoreType.DMA,
            pltpu.SemaphoreType.DMA,
        ]
        + GatherAll.scratch(grid) * 2
        + TensorReduce.scratch(grid, few, n),
        cost_estimate=microseconds(74),
        compiler_params=pltpu.CompilerParams(
            collective_id=collective_id, has_side_effects=True, vmem_limit_bytes=62 << 20
        ),
    )(
        hidden, attn_gain[None], latent_gain[None], moe_gain[None], gates, routes, cosines, sines,
        seg, own_seg, cotangent, latent_weight.T, query_weight, expand_weight, output_weight,
    )
    return [outs[0].reshape(tokens, width), outs[1].reshape(tokens, n), *outs[2:]]


def rms_scale(values, gain_vec):
    return (
        values * lax.rsqrt(jnp.mean(values * values, axis=-1, keepdims=True) + epsilon) * gain_vec
    )


def rotate(values, places):
    halfway = values.shape[-1] // 2
    frequency = 10000.0 ** (-jnp.arange(halfway, dtype=jnp.float32) / halfway)
    angles = places.astype(jnp.float32)[:, None] * frequency[None, :]
    cosine = jnp.cos(angles)
    sine_part = jnp.sin(angles)
    if values.ndim == 3:
        cosine = cosine[:, None, :]
        sine_part = sine_part[:, None, :]
    first_half = values[..., :halfway]
    second = values[..., halfway:]
    return jnp.concatenate(
        [first_half * cosine - second * sine_part, second * cosine + first_half * sine_part],
        axis=-1,
    )


def seq_places(segments):
    total_rows = segments.shape[0]
    ordinal = jnp.arange(total_rows, dtype=jnp.int32)
    starts = jnp.concatenate(
        [jnp.ones((1,), jnp.int32), (segments[1:] != segments[:-1]).astype(jnp.int32)]
    )
    seg_start = lax.cummax(jnp.where(starts > 0, ordinal, 0), axis=0)
    return jnp.where(segments == 0, ordinal, total_rows // 2 + ordinal - seg_start)


def silu_product(gate_pre, up_pre):
    return jax.nn.silu(gate_pre) * up_pre


def score_block(queries, key_plain, rope_all, visible):
    scale_factor = (NOPE + ROPE) ** (-0.5)
    raw_scores = jnp.einsum(
        "thc,shc->hts", queries[..., :NOPE], key_plain, preferred_element_type=jnp.float32
    )
    raw_scores = raw_scores + jnp.einsum(
        "thr,sr->hts", queries[..., NOPE:], rope_all, preferred_element_type=jnp.float32
    )
    return jnp.where(visible[None], scale_factor * raw_scores, masked_out)


def dot(left_side, right_side):
    return jnp.dot(left_side, right_side, preferred_element_type=jnp.float32)


def pad_columns(values):
    return jnp.pad(values, ((0, 0), (0, -values.shape[1] % 128)))


def low(values):
    return values.astype(jnp.bfloat16)


def shards(
    grid,
    hidden_in,
    attn_gain,
    query_weight,
    latent_weight,
    latent_gain,
    expand_weight,
    output_weight,
    moe_gain,
    shared_gate,
    shared_up,
    shared_down,
    expert_gate,
    expert_up,
    expert_down,
    gate_values,
    expert_routes,
    segments,
    cotangent,
):
    tok_rows, model_width = hidden_in.shape
    groups = lax.axis_size("expert")
    parts = lax.axis_size("tensor")
    device = lax.axis_index("expert")
    part = lax.axis_index("tensor")
    total_rows = segments.shape[0]
    few = tok_rows // parts
    start_row = device * tok_rows
    scale_factor = (NOPE + ROPE) ** (-0.5)

    def quarter(values):
        return lax.dynamic_slice_in_dim(values, part * few, few)

    def own_group(values):
        return lax.dynamic_slice_in_dim(values, start_row, tok_rows)

    places = own_group(seq_places(segments))
    own_seg = own_group(segments)
    halfway = ROPE // 2
    frequency = 10000.0 ** (-jnp.arange(halfway, dtype=jnp.float32) / halfway)
    angles = places.astype(jnp.float32)[:, None] * frequency[None, :]
    nothing = jnp.zeros((tok_rows, 128 - ROPE), jnp.float32)
    cosines, sines = jnp.cos(angles), jnp.sin(angles)
    cosines = jnp.concatenate([cosines, cosines, nothing], axis=1)
    sines = jnp.concatenate([sines, -sines, nothing], axis=1)
    hidden_few = quarter(hidden_in)

    (
        packed_all, cot_all, expanded, queries, normed_few, compressed, log_total, merged, residual, moe_in,
    ) = front_call(
        grid, hidden_in, cotangent, attn_gain, latent_gain, moe_gain, gate_values, expert_routes,
        cosines, sines, segments[None, :], own_seg[:, None],
        latent_weight, query_weight, expand_weight, output_weight, 0,
    )
    hidden_f = hidden_few.astype(jnp.float32)

    moe_all, grad_moe_in, out_rows, acts = experts_call(
        grid, moe_in, cot_all, packed_all, expert_gate, expert_up, expert_down,
        shared_gate, shared_up, shared_down, 2,
    )
    normed_later, _ = lax.optimization_barrier((normed_few, moe_in[:8]))
    normed_all = lax.all_gather(normed_later, ALL, axis=0, tiled=True)

    grad_moe_in, normed_all = lax.optimization_barrier((grad_moe_in, normed_all))
    _, pull_moe = jax.vjp(rms_scale, residual, moe_gain)
    grad_residual, grad_moe_gain = pull_moe(grad_moe_in)
    grad_residual = grad_residual + quarter(cotangent).astype(jnp.float32)
    grad_q, key_rows, expand_part, output_rows = attention_back_call(
        grid,
        low(grad_residual),
        output_weight,
        queries,
        expanded,
        packed_all,
        expand_weight,
        merged,
        log_total,
        segments[None, :],
        own_seg[:, None],
        cosines,
        sines,
        5,
    )
    grad_q_low = grad_q.reshape(tok_rows, -1, 256)[:, :, : NOPE + ROPE].reshape(tok_rows, -1)
    normed_rows = low(dot(grad_q_low, query_weight.T))

    moe_out, grad_keys, weight_rows, grad_normed, grad_q_all, expert_grads = gradients_call(
        grid, out_rows, key_rows, expand_part, normed_rows, grad_q_low, moe_all, cot_all, acts,
        expert_down.shape[1], shared_down.shape[0], 3,
    )
    output_rows, weight_rows = lax.optimization_barrier((output_rows, weight_rows))
    output_rows = lax.all_gather(output_rows, "expert", axis=0, tiled=True)
    weight_rows = lax.all_gather(weight_rows, "expert", axis=0, tiled=True)
    grad_expert_gate, grad_expert_up, grad_expert_down = expert_grads[:3]
    grad_shared_gate, grad_shared_up, grad_shared_down = expert_grads[3:]
    layer_out = low(residual + moe_out)
    places_few = quarter(places)
    compressed_few = compressed[:, : LATENT + ROPE]
    _, pull_latent = jax.vjp(rms_scale, compressed_few[:, :LATENT], latent_gain)
    grad_plain_latent, grad_latent_gain = pull_latent(grad_keys[:, :LATENT])
    _, pull_krope = jax.vjp(partial(rotate, places=places_few), compressed_few[:, LATENT:])
    (grad_k_turned,) = pull_krope(grad_keys[:, LATENT : LATENT + ROPE])
    grad_comp_low = low(jnp.concatenate([grad_plain_latent, grad_k_turned], axis=-1))
    grad_normed = grad_normed + dot(grad_comp_low, latent_weight.T)
    _, pull_input = jax.vjp(rms_scale, hidden_f, attn_gain)
    grad_input_norm, grad_attn_gain = pull_input(grad_normed)
    gains = jnp.concatenate([grad_attn_gain, grad_latent_gain, grad_moe_gain])
    gains = jnp.pad(gains, (0, -gains.shape[0] % few)).reshape(few, -1)
    gains_high = low(gains)
    gains_low = low(gains - gains_high.astype(jnp.float32))
    spread = gains.shape[1]
    both = jnp.concatenate([layer_out, low(grad_residual + grad_input_norm)], axis=1)
    last, both = last_call(
        grid,
        pad_columns(jnp.concatenate([grad_comp_low, gains_high, gains_low], axis=1)),
        both,
        8,
    )
    grad_comp_all = last.reshape(total_rows, -1)[:, : LATENT + ROPE]
    gains = jnp.sum(last[:, :, LATENT + ROPE : LATENT + ROPE + 2 * spread].astype(jnp.float32), axis=0)
    gains = (gains[:, :spread] + gains[:, spread:]).reshape(-1)
    grad_latent_weight = dot(normed_all.T, grad_comp_all)
    grad_query_weight = dot(normed_all.T, grad_q_all)
    layer_out, grad_hidden = both[:, :model_width], both[:, model_width:].astype(jnp.float32)
    grad_output_weight = output_rows.astype(jnp.float32)
    grad_expand_weight = weight_rows.astype(jnp.float32)
    return (
        layer_out,
        grad_hidden,
        gains[:model_width],
        grad_query_weight,
        grad_latent_weight,
        gains[model_width : model_width + LATENT],
        grad_expand_weight,
        grad_output_weight,
        gains[model_width + LATENT : 2 * model_width + LATENT],
        grad_shared_gate,
        grad_shared_up,
        grad_shared_down,
        grad_expert_gate,
        grad_expert_up,
        grad_expert_down,
    )


def solution(mesh):
    grid = Grid(mesh.shape["expert"], mesh.shape["tensor"])
    placed = (
        P("expert", None),
        P(),
        P(None, "tensor"),
        P(),
        P(),
        P(None, "tensor"),
        P("tensor", None),
        P(),
        P(None, "tensor"),
        P(None, "tensor"),
        P("tensor", None),
        P("expert", None, "tensor"),
        P("expert", None, "tensor"),
        P("expert", "tensor", None),
        P("expert", None),
        P("expert", None),
        P(),
        P("expert", None),
    )
    return jax.shard_map(
        partial(shards, grid),
        mesh=mesh,
        in_specs=placed,
        out_specs=(
            P("expert", None),
            P("expert", None),
            P(),
            P(None, "tensor"),
            P(),
            P(),
            P(None, "tensor"),
            P("tensor", None),
            P(),
            P(None, "tensor"),
            P(None, "tensor"),
            P("tensor", None),
            P("expert", None, "tensor"),
            P("expert", None, "tensor"),
            P("expert", "tensor", None),
        ),
        check_vma=False,
    )
```

```python
import functools
import math
from functools import partial

import jax
import jax.numpy as jnp
from jax import lax
from jax.experimental import pallas as pl
from jax.experimental.pallas import tpu as pltpu
from jax.sharding import PartitionSpec as P

NOPE = 128
ROPE = 64
VDIM = 128
LATENT = 512
TOP = 6
EXP_DEV = 2
ALL = ("expert", "tensor")
MESH = pl.DeviceIdType.MESH

epsilon = 1e-06
masked_out = -1e30


class Grid:
    def __init__(self, expert, tensor):
        self.na = 4 if expert % 4 == 0 else 1
        self.nb = expert // self.na
        self.ny = tensor // 2
        self.size = expert * tensor

    def here(self):
        e, t = lax.axis_index("expert"), lax.axis_index("tensor")
        return (lax.div(e, self.nb), lax.rem(e, self.nb), lax.div(t, 2), lax.rem(t, 2))

    def device(self, a, b, y, c):
        return {"expert": a * self.nb + b, "tensor": y * 2 + c}

    def block(self, a, b, y, c):
        return ((a * self.nb + b) * self.ny + y) * 2 + c


def microseconds(time):
    return pl.CostEstimate(flops=time * 1000**3, bytes_accessed=0, transcendentals=0)


def wrap(i, n):
    return lax.rem(i, n)


def greet(grid):
    a, b, y, c = grid.here()
    barrier = pltpu.get_barrier_semaphore()
    others = (
        [grid.device(wrap(a + i, grid.na), b, y, c) for i in range(1, grid.na)]
        + [grid.device(a, wrap(b + i, grid.nb), y, c) for i in range(1, grid.nb)]
        + [grid.device(a, b, wrap(y + i, grid.ny), c) for i in range(1, grid.ny)]
        + [grid.device(a, b, y, 1 - c)]
    )
    for other in others:
        pl.semaphore_signal(barrier, inc=1, device_id=other, device_id_type=MESH)
    pl.semaphore_wait(barrier, len(others))


def gather_kernel(
    grid, x_ref, out_ref, own_sem, send_sem, recv_sem, core_send, core_recv, extra=()
):
    na, nb, ny = grid.na, grid.nb, grid.ny
    a, b, y, c = grid.here()
    half = x_ref.shape[0] // 2
    greet(grid)
    waits = []

    def dst(bb, yy, cc, aa, h):
        return out_ref.at[grid.block(aa, bb, yy, cc), pl.ds(h * half, half)]

    def slot(bb, yy, aa, h):
        return ((bb * ny + yy) * na + aa) * 2 + h

    def push(src, bb, yy, aa, h, where, kind):
        copy = pltpu.make_async_remote_copy(
            src_ref=src,
            dst_ref=dst(bb, yy, c, aa, h),
            send_sem=core_send.at[slot(bb, yy, aa, h)] if kind == "c" else send_sem.at[len(waits)],
            recv_sem=(core_recv if kind == "c" else recv_sem).at[slot(bb, yy, aa, h)],
            device_id=where,
            device_id_type=MESH,
        )
        copy.start()
        if kind != "c":
            waits.append(copy)
        else:
            core_waits.append(copy)

    core_waits = []

    def onward(src, bb, yy, aa, h, dims):
        for d in dims:
            if d == "a":
                for i in range(1, na):
                    push(src, bb, yy, aa, h, grid.device(wrap(a + i, na), b, y, c), d)
            if d == "b":
                for i in range(1, nb):
                    push(src, bb, yy, aa, h, grid.device(a, wrap(b + i, nb), y, c), d)
            if d == "y":
                for i in range(1, ny):
                    push(src, bb, yy, aa, h, grid.device(a, b, wrap(y + i, ny), c), d)
        push(src, bb, yy, aa, h, grid.device(a, b, y, 1 - c), "c")

    def landed(bb, yy, cc, aa, h, sem):
        ref = dst(bb, yy, cc, aa, h)
        pltpu.make_async_copy(ref, ref, sem.at[slot(bb, yy, aa, h)]).wait()
        return ref

    own = pltpu.make_async_copy(x_ref, out_ref.at[grid.block(a, b, y, c)], own_sem)
    own.start()
    orders = (("b", "y"), ("y", "b"))
    for h in range(2):
        onward(x_ref.at[pl.ds(h * half, half)], b, y, a, h, ("a",) + orders[h])
    for one in extra:
        one.start()
    for i in range(1, na):
        aa = wrap(a + na - i, na)
        for h in range(2):
            onward(landed(b, y, c, aa, h, recv_sem), b, y, aa, h, orders[h])
    for i in range(na):
        aa = wrap(a + na - i, na)
        for h in range(2):
            n1 = (nb, ny)[h]
            for j in range(1, n1):
                bb, yy = (wrap(b + nb - j, nb), y) if h == 0 else (b, wrap(y + ny - j, ny))
                onward(landed(bb, yy, c, aa, h, recv_sem), bb, yy, aa, h, orders[h][1:])
    for i in range(na):
        aa = wrap(a + na - i, na)
        for h in range(2):
            for j in range(nb):
                for k in range(1, ny):
                    if h == 0:
                        bb, yy = wrap(b + nb - j, nb), wrap(y + ny - k, ny)
                        onward(landed(bb, yy, c, aa, h, recv_sem), bb, yy, aa, h, ())
            for j in range(ny):
                for k in range(1, nb):
                    if h == 1:
                        bb, yy = wrap(b + nb - k, nb), wrap(y + ny - j, ny)
                        onward(landed(bb, yy, c, aa, h, recv_sem), bb, yy, aa, h, ())
    for i in range(1, na):
        for one in extra:
            one.middle(i)
    for j in range(nb):
        for k in range(ny):
            for i in range(na):
                for h in range(2):
                    landed(wrap(b + nb - j, nb), wrap(y + ny - k, ny), 1 - c, wrap(a + na - i, na), h, core_recv)
    own.wait()
    for copy in waits + core_waits:
        copy.wait_send()
    for one in extra:
        one.last()


def gather_sends(grid):
    na, nb, ny = grid.na, grid.nb, grid.ny
    return 2 * (na - 1 + na * (nb - 1) + na * (ny - 1) + na * (nb - 1) * (ny - 1))


def gather_all(grid, x, collective_id):
    r, n = x.shape
    blocks = grid.na * grid.nb * grid.ny
    return pl.pallas_call(
        functools.partial(gather_kernel, grid),
        out_shape=jax.ShapeDtypeStruct((grid.size, r, n), x.dtype),
        in_specs=[pl.BlockSpec(memory_space=pl.ANY)],
        out_specs=pl.BlockSpec(memory_space=pl.ANY),
        scratch_shapes=[
            pltpu.SemaphoreType.DMA,
            pltpu.SemaphoreType.DMA((gather_sends(grid),)),
            pltpu.SemaphoreType.DMA((2 * blocks,)),
            pltpu.SemaphoreType.DMA((2 * blocks,)),
            pltpu.SemaphoreType.DMA((2 * blocks,)),
        ],
        compiler_params=pltpu.CompilerParams(collective_id=collective_id, has_side_effects=True),
    )(x)


def scatter_kernel(grid, pieces, p_ref, out_ref, acc, core_in, d1_in0, d1_in1, d2_in0, d2_in1, a_in,
                   load_sem, core_s, core_r, s10, r10, s11, r11, s20, r20, s21, r21, sa, ra):
    na, nb, ny = grid.na, grid.nb, grid.ny
    a, b, y, c = grid.here()
    half = p_ref.shape[4] // 2
    width = p_ref.shape[5] // pieces
    greet(grid)
    pending = []

    def send(src, dst, ss, rs, where):
        copy = pltpu.make_async_remote_copy(src_ref=src, dst_ref=dst, send_sem=ss, recv_sem=rs, device_id=where, device_id_type=MESH)
        copy.start()
        pending.append(copy)

    def await_in(ref, sem):
        pltpu.make_async_copy(ref, ref, sem).wait()

    def add(dst, src):
        dst[...] = (dst[...].astype(jnp.float32) + src[...].astype(jnp.float32)).astype(dst.dtype)

    def cols(p):
        return pl.ds(p * width, width)

    spots = [(j, k) for j in reversed(range(nb)) for k in reversed(range(ny))]
    loads = {}
    for p in range(pieces):
        for n, (j, k) in enumerate(spots):
            bb, yy = wrap(b + j, nb), wrap(y + k, ny)
            send(p_ref.at[:, bb, yy, 1 - c, :, cols(p)], core_in.at[p, j, k], core_s.at[p, n], core_r.at[p, n],
                 grid.device(a, b, y, 1 - c))
            load = pltpu.make_async_copy(p_ref.at[:, bb, yy, c, :, cols(p)], acc.at[p, j, k], load_sem.at[p, n])
            load.start()
            loads[p, n] = load
    rows = (pl.ds(0, half), pl.ds(half, half))
    for p in range(pieces):
        for n, (j, k) in enumerate(spots):
            loads[p, n].wait()
            await_in(core_in.at[p, j, k], core_r.at[p, n])
            for i in range(na):
                add(acc.at[p, j, k, i], core_in.at[p, j, k, i])
            if k:
                send(acc.at[p, j, k, :, rows[0]], d1_in0.at[p, j, k - 1], s10.at[p, j, k - 1], r10.at[p, j, k - 1],
                     grid.device(a, b, wrap(y + k, ny), c))
            if j:
                send(acc.at[p, j, k, :, rows[1]], d1_in1.at[p, k, j - 1], s11.at[p, k, j - 1], r11.at[p, k, j - 1],
                     grid.device(a, wrap(b + j, nb), y, c))
    for p in range(pieces):
        for j in reversed(range(nb)):
            for k in range(1, ny):
                await_in(d1_in0.at[p, j, k - 1], r10.at[p, j, k - 1])
                for i in range(na):
                    add(acc.at[p, j, 0, i, rows[0]], d1_in0.at[p, j, k - 1, i])
            if j:
                send(acc.at[p, j, 0, :, rows[0]], d2_in0.at[p, j - 1], s20.at[p, j - 1], r20.at[p, j - 1],
                     grid.device(a, wrap(b + j, nb), y, c))
        for k in reversed(range(ny)):
            for j in range(1, nb):
                await_in(d1_in1.at[p, k, j - 1], r11.at[p, k, j - 1])
                for i in range(na):
                    add(acc.at[p, 0, k, i, rows[1]], d1_in1.at[p, k, j - 1, i])
            if k:
                send(acc.at[p, 0, k, :, rows[1]], d2_in1.at[p, k - 1], s21.at[p, k - 1], r21.at[p, k - 1],
                     grid.device(a, b, wrap(y + k, ny), c))
    for p in range(pieces):
        for j in range(1, nb):
            await_in(d2_in0.at[p, j - 1], r20.at[p, j - 1])
            for i in range(na):
                add(acc.at[p, 0, 0, i, rows[0]], d2_in0.at[p, j - 1, i])
        for k in range(1, ny):
            await_in(d2_in1.at[p, k - 1], r21.at[p, k - 1])
            for i in range(na):
                add(acc.at[p, 0, 0, i, rows[1]], d2_in1.at[p, k - 1, i])
        for i in range(1, na):
            aa = wrap(a + i, na)
            send(acc.at[p, 0, 0, aa], a_in.at[p, i - 1], sa.at[p, i - 1], ra.at[p, i - 1], grid.device(aa, b, y, c))
    for p in range(pieces):
        total = acc[p, 0, 0, a].astype(jnp.float32)
        for i in range(1, na):
            await_in(a_in.at[p, i - 1], ra.at[p, i - 1])
            total = total + a_in[p, i - 1].astype(jnp.float32)
        out_ref[:, cols(p)] = total.astype(out_ref.dtype)
    for copy in pending:
        copy.wait_send()


def scatter_all(grid, p, dtype, collective_id, pieces=2):
    r, n = p.shape[0] // grid.size, p.shape[1]
    na, nb, ny = grid.na, grid.nb, grid.ny
    half, width = r // 2, n // pieces
    sems = lambda *s: pltpu.SemaphoreType.DMA(s)
    vm = lambda *s: pltpu.VMEM(s, jnp.bfloat16)
    return pl.pallas_call(
        functools.partial(scatter_kernel, grid, pieces),
        out_shape=jax.ShapeDtypeStruct((r, n), dtype),
        in_specs=[pl.BlockSpec(memory_space=pl.ANY)],
        out_specs=pl.BlockSpec(memory_space=pltpu.VMEM),
        scratch_shapes=[
            vm(pieces, nb, ny, na, r, width),
            vm(pieces, nb, ny, na, r, width),
            vm(pieces, nb, ny - 1, na, half, width),
            vm(pieces, ny, nb - 1, na, half, width),
            vm(pieces, nb - 1, na, half, width),
            vm(pieces, ny - 1, na, half, width),
            vm(pieces, na - 1, r, width),
            sems(pieces, nb * ny), sems(pieces, nb * ny), sems(pieces, nb * ny),
            sems(pieces, nb, ny - 1), sems(pieces, nb, ny - 1),
            sems(pieces, ny, nb - 1), sems(pieces, ny, nb - 1),
            sems(pieces, nb - 1), sems(pieces, nb - 1),
            sems(pieces, ny - 1), sems(pieces, ny - 1),
            sems(pieces, na - 1), sems(pieces, na - 1),
        ],
        compiler_params=pltpu.CompilerParams(collective_id=collective_id, has_side_effects=True, vmem_limit_bytes=40 << 20),
    )(p.reshape(na, nb, ny, 2, r, n))


def greet_tensor(grid):
    a, b, y, c = grid.here()
    barrier = pltpu.get_barrier_semaphore()
    others = [grid.device(a, b, wrap(y + i, grid.ny), c) for i in range(1, grid.ny)]
    others.append(grid.device(a, b, y, 1 - c))
    for other in others:
        pl.semaphore_signal(barrier, inc=1, device_id=other, device_id_type=MESH)
    pl.semaphore_wait(barrier, len(others))


def tensor_scatter_kernel(grid, p_ref, out_ref, acc, core_in, y_in, core_s, core_r, ys, yr):
    ny = grid.ny
    a, b, y, c = grid.here()
    greet_tensor(grid)
    pending = []
    for k in reversed(range(ny)):
        copy = pltpu.make_async_remote_copy(
            src_ref=p_ref.at[wrap(y + k, ny), 1 - c], dst_ref=core_in.at[k], send_sem=core_s.at[k], recv_sem=core_r.at[k],
            device_id=grid.device(a, b, y, 1 - c), device_id_type=MESH,
        )
        copy.start()
        pending.append(copy)
    for k in reversed(range(ny)):
        pltpu.make_async_copy(core_in.at[k], core_in.at[k], core_r.at[k]).wait()
        total = p_ref[wrap(y + k, ny), c].astype(jnp.float32) + core_in[k].astype(jnp.float32)
        if k:
            acc[k - 1] = total.astype(acc.dtype)
            copy = pltpu.make_async_remote_copy(
                src_ref=acc.at[k - 1], dst_ref=y_in.at[k - 1], send_sem=ys.at[k - 1], recv_sem=yr.at[k - 1],
                device_id=grid.device(a, b, wrap(y + k, ny), c), device_id_type=MESH,
            )
            copy.start()
            pending.append(copy)
        else:
            out_ref[...] = total
    for k in range(1, ny):
        pltpu.make_async_copy(y_in.at[k - 1], y_in.at[k - 1], yr.at[k - 1]).wait()
        out_ref[...] += y_in[k - 1].astype(jnp.float32)
    for copy in pending:
        copy.wait_send()


def tensor_scatter(grid, p, collective_id):
    ny = grid.ny
    r, n = p.shape[0] // (2 * ny), p.shape[1]
    return pl.pallas_call(
        functools.partial(tensor_scatter_kernel, grid),
        out_shape=jax.ShapeDtypeStruct((r, n), jnp.float32),
        in_specs=[pl.BlockSpec(memory_space=pltpu.VMEM)],
        out_specs=pl.BlockSpec(memory_space=pltpu.VMEM),
        scratch_shapes=[
            pltpu.VMEM((max(ny - 1, 1), r, n), p.dtype),
            pltpu.VMEM((ny, r, n), p.dtype),
            pltpu.VMEM((max(ny - 1, 1), r, n), p.dtype),
            pltpu.SemaphoreType.DMA((ny,)),
            pltpu.SemaphoreType.DMA((ny,)),
            pltpu.SemaphoreType.DMA((max(ny - 1, 1),)),
            pltpu.SemaphoreType.DMA((max(ny - 1, 1),)),
        ],
        compiler_params=pltpu.CompilerParams(
            collective_id=collective_id, has_side_effects=True, vmem_limit_bytes=16 << 20
        ),
    )(p.reshape(ny, 2, r, n))


def tensor_gather_kernel(grid, x_ref, out_ref, own_sem, ys, yr, core_s, core_r):
    ny = grid.ny
    a, b, y, c = grid.here()
    greet_tensor(grid)
    own = pltpu.make_async_copy(x_ref, out_ref.at[y, c], own_sem)
    own.start()
    pending = []

    def push(src, spot, ss, rs, where):
        copy = pltpu.make_async_remote_copy(
            src_ref=src, dst_ref=out_ref.at[spot, c], send_sem=ss, recv_sem=rs, device_id=where, device_id_type=MESH
        )
        copy.start()
        pending.append(copy)

    for k in range(1, ny):
        push(x_ref, y, ys.at[k], yr.at[k], grid.device(a, b, wrap(y + k, ny), c))
    push(x_ref, y, core_s.at[0], core_r.at[0], grid.device(a, b, y, 1 - c))
    for k in range(1, ny):
        spot = wrap(y + ny - k, ny)
        ref = out_ref.at[spot, c]
        pltpu.make_async_copy(ref, ref, yr.at[k]).wait()
        push(ref, spot, core_s.at[k], core_r.at[k], grid.device(a, b, y, 1 - c))
    for k in range(ny):
        ref = out_ref.at[wrap(y + ny - k, ny), 1 - c]
        pltpu.make_async_copy(ref, ref, core_r.at[k]).wait()
    own.wait()
    for copy in pending:
        copy.wait_send()


def tensor_gather(grid, x, collective_id):
    ny = grid.ny
    r, n = x.shape
    out = pl.pallas_call(
        functools.partial(tensor_gather_kernel, grid),
        out_shape=jax.ShapeDtypeStruct((ny, 2, r, n), x.dtype),
        in_specs=[pl.BlockSpec(memory_space=pltpu.VMEM)],
        out_specs=pl.BlockSpec(memory_space=pltpu.VMEM),
        scratch_shapes=[pltpu.SemaphoreType.DMA] + [pltpu.SemaphoreType.DMA((ny,))] * 4,
        compiler_params=pltpu.CompilerParams(
            collective_id=collective_id, has_side_effects=True, vmem_limit_bytes=16 << 20
        ),
    )(x)
    return out.reshape(2 * ny * r, n)


class TensorReduce:
    count = 8

    @staticmethod
    def scratch(grid, r, width):
        ny = grid.ny
        sems = lambda *s: pltpu.SemaphoreType.DMA(s)
        vm = lambda *s: pltpu.VMEM(s, jnp.bfloat16)
        return [
            vm(ny, r, width), vm(ny, r, width), vm(ny - 1, r, width),
            sems(ny), sems(ny), sems(ny), sems(ny - 1), sems(ny - 1),
        ]

    def __init__(self, grid, source, out, scratch):
        self.grid, self.source, self.out = grid, source, out
        (
            self.acc, self.core_in, self.y_in, self.load_sem, self.core_s, self.core_r, self.ys, self.yr,
        ) = scratch
        self.spot = grid.here()

    def load(self, k):
        g, (a, b, y, c) = self.grid, self.spot
        return pltpu.make_async_copy(self.source.at[wrap(y + k, g.ny), c], self.acc.at[k], self.load_sem.at[k])

    def core_copy(self, k):
        g, (a, b, y, c) = self.grid, self.spot
        return pltpu.make_async_remote_copy(
            src_ref=self.source.at[wrap(y + k, g.ny), 1 - c], dst_ref=self.core_in.at[k],
            send_sem=self.core_s.at[k], recv_sem=self.core_r.at[k],
            device_id=g.device(a, b, y, 1 - c), device_id_type=MESH,
        )

    def y_copy(self, k):
        g, (a, b, y, c) = self.grid, self.spot
        return pltpu.make_async_remote_copy(
            src_ref=self.acc.at[k], dst_ref=self.y_in.at[k - 1], send_sem=self.ys.at[k - 1],
            recv_sem=self.yr.at[k - 1], device_id=g.device(a, b, wrap(y + k, g.ny), c), device_id_type=MESH,
        )

    def start(self):
        for k in reversed(range(self.grid.ny)):
            self.core_copy(k).start()
            self.load(k).start()

    def middle(self):
        f32 = jnp.float32
        for k in reversed(range(self.grid.ny)):
            self.load(k).wait()
            ref = self.core_in.at[k]
            pltpu.make_async_copy(ref, ref, self.core_r.at[k]).wait()
            total = self.acc[k].astype(f32) + self.core_in[k].astype(f32)
            self.acc[k] = total.astype(self.acc.dtype)
            if k:
                self.y_copy(k).start()

    def last(self):
        total = self.acc[0].astype(jnp.float32)
        for k in range(1, self.grid.ny):
            ref = self.y_in.at[k - 1]
            pltpu.make_async_copy(ref, ref, self.yr.at[k - 1]).wait()
            total = total + self.y_in[k - 1].astype(jnp.float32)
        self.out[...] = total

    def finish(self):
        for k in range(self.grid.ny):
            self.core_copy(k).wait_send()
            if k:
                self.y_copy(k).wait_send()


class TensorGather:
    count = 5

    @staticmethod
    def scratch(grid):
        return [pltpu.SemaphoreType.DMA((1,))] + [pltpu.SemaphoreType.DMA((grid.ny,))] * 4

    def __init__(self, grid, x, out, scratch):
        self.grid, self.x, self.out = grid, x, out
        self.own_sem, self.ys, self.yr, self.core_s, self.core_r = scratch
        self.spot = grid.here()

    def own(self):
        return pltpu.make_async_copy(self.x, self.out.at[self.spot[2], self.spot[3]], self.own_sem.at[0])

    def y_copy(self, k):
        g, (a, b, y, c) = self.grid, self.spot
        return pltpu.make_async_remote_copy(
            src_ref=self.x, dst_ref=self.out.at[y, c], send_sem=self.ys.at[k], recv_sem=self.yr.at[k],
            device_id=g.device(a, b, wrap(y + k, g.ny), c), device_id_type=MESH,
        )

    def core_copy(self, k):
        g, (a, b, y, c) = self.grid, self.spot
        spot = wrap(y + g.ny - k, g.ny)
        return pltpu.make_async_remote_copy(
            src_ref=self.x if k == 0 else self.out.at[spot, c], dst_ref=self.out.at[spot, c],
            send_sem=self.core_s.at[k], recv_sem=self.core_r.at[k],
            device_id=g.device(a, b, y, 1 - c), device_id_type=MESH,
        )

    def start(self):
        self.own().start()
        for k in range(1, self.grid.ny):
            self.y_copy(k).start()
        self.core_copy(0).start()

    def middle(self, i):
        if i == 1:
            for k in range(1, self.grid.ny):
                pltpu.make_async_copy(self.x, self.x, self.yr.at[k]).wait()
                self.core_copy(k).start()

    def last(self):
        self.own().wait()
        for k in range(self.grid.ny):
            pltpu.make_async_copy(self.x, self.x, self.core_r.at[k]).wait()
        for k in range(self.grid.ny):
            if k:
                self.y_copy(k).wait_send()
            self.core_copy(k).wait_send()


class PlaneReduce:
    count = 9

    @staticmethod
    def scratch(grid, r, width):
        na, nb = grid.na, grid.nb
        sems = lambda *s: pltpu.SemaphoreType.DMA(s)
        vm = lambda *s: pltpu.VMEM(s, jnp.bfloat16)
        return [
            vm(na, r, width), vm(nb - 1, na, r, width), vm(na - 1, r, width),
            sems(1), sems(nb - 1), sems(nb - 1), sems(na - 1), sems(na - 1), sems(1),
        ]

    def __init__(self, grid, source, out, scratch):
        self.grid, self.source, self.out = grid, source, out
        self.acc, self.b_in, self.a_in, self.load_sem, self.sb, self.rb, self.sa, self.ra, _ = scratch
        self.spot = grid.here()

    def load(self):
        return pltpu.make_async_copy(self.source.at[:, self.spot[1]], self.acc, self.load_sem.at[0])

    def copy_b(self, i):
        g, (a, b, y, c) = self.grid, self.spot
        return pltpu.make_async_remote_copy(
            src_ref=self.source.at[:, wrap(b + i, g.nb)], dst_ref=self.b_in.at[i - 1],
            send_sem=self.sb.at[i - 1], recv_sem=self.rb.at[i - 1],
            device_id=g.device(a, wrap(b + i, g.nb), y, c), device_id_type=MESH,
        )

    def copy_a(self, i):
        g, (a, b, y, c) = self.grid, self.spot
        return pltpu.make_async_remote_copy(
            src_ref=self.acc.at[wrap(a + i, g.na)], dst_ref=self.a_in.at[i - 1],
            send_sem=self.sa.at[i - 1], recv_sem=self.ra.at[i - 1],
            device_id=g.device(wrap(a + i, g.na), b, y, c), device_id_type=MESH,
        )

    def start(self):
        for i in range(1, self.grid.nb):
            self.copy_b(i).start()
        self.load().start()

    def middle(self):
        f32 = jnp.float32
        self.load().wait()
        for i in range(1, self.grid.nb):
            ref = self.b_in.at[i - 1]
            pltpu.make_async_copy(ref, ref, self.rb.at[i - 1]).wait()

            def one(m, carry):
                self.acc[m] = (self.acc[m].astype(f32) + ref[m].astype(f32)).astype(self.acc.dtype)
                return carry

            lax.fori_loop(0, self.grid.na, one, 0)
        for i in range(1, self.grid.na):
            self.copy_a(i).start()

    def last(self):
        total = self.acc[self.spot[0]].astype(jnp.float32)
        for i in range(1, self.grid.na):
            ref = self.a_in.at[i - 1]
            pltpu.make_async_copy(ref, ref, self.ra.at[i - 1]).wait()
            total = total + self.a_in[i - 1].astype(jnp.float32)
        self.out[...] = total.astype(self.out.dtype)

    def finish(self):
        for i in range(1, self.grid.nb):
            self.copy_b(i).wait_send()
        for i in range(1, self.grid.na):
            self.copy_a(i).wait_send()


class PlaneGather:
    count = 5

    @staticmethod
    def scratch(grid):
        na, nb = grid.na, grid.nb
        sems = lambda *s: pltpu.SemaphoreType.DMA(s)
        return [sems(1), sems(na - 1), sems(na, nb - 1), sems(na), sems(na, nb - 1)]

    def __init__(self, grid, x, out, scratch):
        self.grid, self.x, self.out = grid, x, out
        self.own_sem, self.sa, self.sb, self.ra, self.rb = scratch
        self.spot = grid.here()

    def own(self):
        return pltpu.make_async_copy(self.x, self.out.at[self.spot[0], self.spot[1]], self.own_sem.at[0])

    def copy_a(self, i):
        g, (a, b, y, c) = self.grid, self.spot
        return pltpu.make_async_remote_copy(
            src_ref=self.x, dst_ref=self.out.at[a, b], send_sem=self.sa.at[i - 1], recv_sem=self.ra.at[i],
            device_id=g.device(wrap(a + i, g.na), b, y, c), device_id_type=MESH,
        )

    def copy_b(self, i, k):
        g, (a, b, y, c) = self.grid, self.spot
        aa = wrap(a + g.na - i, g.na)
        return pltpu.make_async_remote_copy(
            src_ref=self.x if i == 0 else self.out.at[aa, b], dst_ref=self.out.at[aa, b],
            send_sem=self.sb.at[i, k - 1], recv_sem=self.rb.at[i, k - 1],
            device_id=g.device(a, wrap(b + k, g.nb), y, c), device_id_type=MESH,
        )

    def start(self):
        self.own().start()
        for i in range(1, self.grid.na):
            self.copy_a(i).start()
        for k in range(1, self.grid.nb):
            self.copy_b(0, k).start()

    def middle(self, i):
        ref = self.out.at[wrap(self.spot[0] + self.grid.na - i, self.grid.na), self.spot[1]]
        pltpu.make_async_copy(ref, ref, self.ra.at[i]).wait()
        for k in range(1, self.grid.nb):
            self.copy_b(i, k).start()

    def last(self):
        self.own().wait()
        ref = self.x
        for i in range(self.grid.na):
            for k in range(1, self.grid.nb):
                pltpu.make_async_copy(ref, ref, self.rb.at[i, k - 1]).wait()
        for i in range(1, self.grid.na):
            self.copy_a(i).wait_send()
        for i in range(self.grid.na):
            for k in range(1, self.grid.nb):
                self.copy_b(i, k).wait_send()


def last_kernel(grid, x_ref, w_ref, t_ref, out_ref, w_out, t_out, own_sem, ss, rs, cs, cr, *scratch):
    gathers = [
        TensorGather(grid, t_ref, t_out, scratch[: TensorGather.count]),
        PlaneGather(grid, w_ref, w_out, scratch[TensorGather.count :]),
    ]
    gather_kernel(grid, x_ref, out_ref, own_sem, ss, rs, cs, cr, gathers)


def last_call(grid, x, w, t, collective_id):
    r, n = x.shape
    blocks = grid.na * grid.nb * grid.ny
    any_space = pl.BlockSpec(memory_space=pl.ANY)
    outs = pl.pallas_call(
        functools.partial(last_kernel, grid),
        out_shape=[
            jax.ShapeDtypeStruct((grid.size, r, n), x.dtype),
            jax.ShapeDtypeStruct((grid.na, grid.nb) + w.shape, w.dtype),
            jax.ShapeDtypeStruct((grid.ny, 2) + t.shape, t.dtype),
        ],
        in_specs=[any_space] * 3,
        out_specs=[any_space] * 3,
        scratch_shapes=[
            pltpu.SemaphoreType.DMA,
            pltpu.SemaphoreType.DMA((gather_sends(grid),)),
            pltpu.SemaphoreType.DMA((2 * blocks,)),
            pltpu.SemaphoreType.DMA((2 * blocks,)),
            pltpu.SemaphoreType.DMA((2 * blocks,)),
        ]
        + TensorGather.scratch(grid)
        + PlaneGather.scratch(grid),
        cost_estimate=microseconds(36),
        compiler_params=pltpu.CompilerParams(collective_id=collective_id, has_side_effects=True),
    )(x, w, t)
    whole = lambda v: v.reshape(-1, v.shape[-1])
    return outs[0], whole(outs[1]), whole(outs[2])


def dot_rows(left_side, right_side):
    return lax.dot_general(
        left_side, right_side, (((1,), (1,)), ((), ())), preferred_element_type=jnp.float32
    )


def dot_plain(left_side, right_side):
    return jnp.dot(left_side, right_side, preferred_element_type=jnp.float32)


def round_up(value, unit):
    return -(-value // unit) * unit


def experts_kernel(
    grid,
    pieces,
    x_ref,
    dz_ref,
    gate_ref,
    eg_hbm,
    eu_hbm,
    ed_hbm,
    sg_hbm,
    su_hbm,
    sd_hbm,
    all_ref,
    grad_ref,
    y_ref,
    acts_ref,
    gates,
    egu,
    ed,
    sgu,
    sd,
    dabuf,
    xbuf,
    dzbuf,
    gated,
    dcat,
    act,
    dsh,
    ybuf,
    dx,
    dx_out,
    core_in,
    d1_in0,
    d1_in1,
    d2_in0,
    d2_in1,
    a_in,
    gate_sem,
    weight_sem,
    own_sem,
    x_sem,
    dz_sem,
    out_sem,
    fill_sem,
    send_sem,
    recv_sem,
    share_send,
    share_recv,
    core_s,
    core_r,
    s10,
    r10,
    s11,
    r11,
    s20,
    r20,
    s21,
    r21,
    sa,
    ra,
):
    na, nb, ny = grid.na, grid.nb, grid.ny
    a, b, y, c = grid.here()
    r, n = x_ref.shape
    half, width, rows = r // 2, n // pieces, na * r
    pairs = nb * ny
    steps = 2 * pairs
    device = a * nb + b
    f, fs = ed_hbm.shape[1], sd_hbm.shape[0]
    wide, wide_s = egu.shape[0] // (2 * EXP_DEV), sd.shape[0]
    ef = EXP_DEV * wide
    columns = columns_of(ef, wide_s)
    f32, bf = jnp.float32, jnp.bfloat16
    fills = [(ed_hbm.at[e], ed, e * wide, f, wide) for e in range(EXP_DEV)]
    fills += [(sd_hbm, sd, 0, fs, wide_s)]
    fills += [(eg_hbm.at[e], egu, e * wide, f, wide) for e in range(EXP_DEV)]
    fills += [(eu_hbm.at[e], egu, ef + e * wide, f, wide) for e in range(EXP_DEV)]
    fills += [(sg_hbm, sgu, 0, fs, wide_s), (su_hbm, sgu, wide_s, fs, wide_s)]
    loads = [
        pltpu.make_async_copy(src, dst.at[pl.ds(at, real)], weight_sem.at[i])
        for i, (src, dst, at, real, _) in enumerate(fills)
    ]
    for load in loads:
        load.start()
    gate_load = pltpu.make_async_copy(gate_ref.at[:, :, :, :, :, pl.ds(LATENT, 128)], gates, gate_sem)
    gate_load.start()
    greet(grid)

    counts = [0]

    def place(bb, yy, cc, aa, h):
        return all_ref.at[aa, bb, yy, cc, pl.ds(h * half, half)]

    def slot(bb, yy, aa, h):
        return ((bb * ny + yy) * na + aa) * 2 + h

    def push(src, bb, yy, aa, h, where, send, recv):
        pltpu.make_async_remote_copy(
            src_ref=src,
            dst_ref=place(bb, yy, c, aa, h),
            send_sem=send,
            recv_sem=recv.at[slot(bb, yy, aa, h)],
            device_id=where,
            device_id_type=MESH,
        ).start()

    def line(i):
        if na != 4:
            return wrap(a + i, na)
        if i == 0:
            return a
        if i == 1:
            return a + 1 - 2 * lax.rem(a, 2)
        return (i - lax.div(a, 2)) if i == 2 else (3 - 3 * lax.div(a, 2))

    def onward(src, bb, yy, aa, h, dims):
        for d in dims:
            size = {"a": na, "b": nb, "y": ny}[d]
            for i in range(1, size):
                where = {
                    "a": lambda: grid.device(line(i), b, y, c),
                    "b": lambda: grid.device(a, wrap(b + i, nb), y, c),
                    "y": lambda: grid.device(a, b, wrap(y + i, ny), c),
                }[d]()
                push(src, bb, yy, aa, h, where, send_sem.at[counts[0]], recv_sem)
                counts[0] += 1
        push(
            src, bb, yy, aa, h, grid.device(a, b, y, 1 - c), share_send.at[slot(bb, yy, aa, h)], share_recv
        )

    def landed(bb, yy, cc, aa, h, sem):
        ref = place(bb, yy, cc, aa, h)
        pltpu.make_async_copy(ref, ref, sem.at[slot(bb, yy, aa, h)]).wait()
        return ref

    orders = (("b", "y"), ("y", "b"))

    def relay(j, k, i, h, dims):
        bb, yy, aa = wrap(b + j, nb), wrap(y + k, ny), line(i)
        onward(landed(bb, yy, c, aa, h, recv_sem), bb, yy, aa, h, dims)

    own = pltpu.make_async_copy(x_ref, all_ref.at[a, b, y, c], own_sem)
    own.start()
    for h in range(2):
        onward(x_ref.at[pl.ds(h * half, half)], b, y, a, h, ("a",) + orders[h])

    hooks = {}
    early = []
    for i in range(na):
        if i:
            early += [(0, 0, i, h, orders[h]) for h in range(2)]
        if i:
            early += [(j, 0, i - 1, 0, orders[0][1:]) for j in range(1, nb)]
            early += [(0, k, i - 1, 1, orders[1][1:]) for k in range(1, ny)]
    early += [(j, 0, na - 1, 0, orders[0][1:]) for j in range(1, nb)]
    early += [(0, k, na - 1, 1, orders[1][1:]) for k in range(1, ny)]
    for m, event in enumerate(early):
        place_at = 1 + m * (2 * steps - 1) // len(early)
        hooks.setdefault(("early", place_at // 2, place_at % 2), []).append(event)
    for pair in range(1, pairs):
        j, k = pair // ny, pair % ny
        late = [(j, k, i, h, ()) for i in range(na) for h in range(2) if (k if h == 0 else j)]
        for m, event in enumerate(late):
            hooks.setdefault(("main", pair, m * 2 // len(late)), []).append(event)

    def hook(stage, step, spot):
        for (when_stage, when, when_spot), events in hooks.items():
            if when_stage == stage and when_spot == spot:

                @pl.when(step == when)
                def _():
                    for event in events:
                        relay(*event)

    def spots(step):
        pair, l = lax.div(step, 2), 1 - lax.rem(step, 2)
        j, k = lax.div(pair, ny), lax.rem(pair, ny)
        return j, k, l, wrap(b + j, nb), wrap(y + k, ny), wrap(c + l, 2)

    def flat(value):
        return value.reshape(rows, value.shape[-1])

    def fold(value):
        return value.reshape(na, r, value.shape[-1])

    def dz_load(step):
        _, _, _, bb, yy, cc = spots(step)
        s = lax.rem(step, 2)
        return pltpu.make_async_copy(dz_ref.at[:, bb, yy, cc], dzbuf.at[s], dz_sem.at[s])

    dz_load(a * 0).start()
    for _, dst, at, real, padded in fills:
        if padded > real:
            dst[at + real : at + padded] = jnp.zeros((padded - real, n), bf)
    for load in loads[: EXP_DEV + 1]:
        load.wait()

    def early_body(step, carry):
        s = lax.rem(step, 2)

        @pl.when(step + 1 < steps)
        def _():
            dz_load(step + 1).start()

        dz_load(step).wait()
        dz = flat(dzbuf[s])
        dabuf[step, :, :ef] = dot_rows(dz, ed[...]).astype(bf)
        hook("early", step, 0)
        dabuf[step, :, ef:] = dot_rows(dz, sd[...]).astype(bf)
        hook("early", step, 1)
        return carry

    lax.fori_loop(0, steps, early_body, 0)
    for load in loads[EXP_DEV + 1 :]:
        load.wait()
    own.wait()
    gate_load.wait()

    def x_load(step):
        _, _, _, bb, yy, cc = spots(step)
        s = lax.rem(step, 2)
        return pltpu.make_async_copy(all_ref.at[:, bb, yy, cc], xbuf.at[s], x_sem.at[s])

    def await_shared(step):
        _, _, _, bb, yy, cc = spots(step)
        for i in range(na):
            for h in range(2):
                landed(bb, yy, cc, line(i), h, share_recv)

    def stores(step):
        _, _, _, bb, yy, cc = spots(step)
        s = lax.rem(step, 2)
        return [
            pltpu.make_async_copy(
                gated.at[s], acts_ref.at[:, bb, yy, cc, :, pl.ds(columns[2], ef)], out_sem.at[s, 0]
            ),
            pltpu.make_async_copy(
                dcat.at[s], acts_ref.at[:, bb, yy, cc, :, pl.ds(columns[0], 2 * ef)], out_sem.at[s, 1]
            ),
        ]

    def remote(src, dst, ss, rs, where):
        return pltpu.make_async_remote_copy(
            src_ref=src, dst_ref=dst, send_sem=ss, recv_sem=rs, device_id=where, device_id_type=MESH
        )

    def cols(p):
        return pl.ds(p * width, width)

    upper = (pl.ds(0, half), pl.ds(half, half))

    def send_core(pair):
        j, k = lax.div(pair, ny), lax.rem(pair, ny)
        return remote(
            dx_out.at[lax.rem(pair, 2)], core_in.at[j, k], core_s.at[lax.rem(pair, 2)],
            core_r.at[j, k], grid.device(a, b, y, 1 - c),
        )

    def send_10(p, j, k):
        return remote(
            dx.at[j, k, :, upper[0], cols(p)], d1_in0.at[p, j, k - 1], s10.at[p, j, k - 1],
            r10.at[p, j, k - 1], grid.device(a, b, wrap(y + k, ny), c),
        )

    def send_11(p, j, k):
        return remote(
            dx.at[j, k, :, upper[1], cols(p)], d1_in1.at[p, k, j - 1], s11.at[p, k, j - 1],
            r11.at[p, k, j - 1], grid.device(a, wrap(b + j, nb), y, c),
        )

    def await_in(ref, sem):
        pltpu.make_async_copy(ref, ref, sem).wait()

    def add(dst, src):
        dst[...] = (dst[...].astype(f32) + src[...].astype(f32)).astype(dst.dtype)

    def shared_front(step, x, s):
        g = dot_rows(x, sgu[:wide_s])
        u = dot_rows(x, sgu[wide_s:])
        d = dabuf[step, :, ef:].astype(f32)
        sig = 1.0 / (1.0 + jnp.exp(-g))
        swish = g * sig
        act[s] = fold((swish * u).astype(bf))
        dsh[s, :, :, :wide_s] = fold((d * u * (sig + swish * (1.0 - sig))).astype(bf))
        dsh[s, :, :, wide_s:] = fold((d * swish).astype(bf))

    def is_mine(bb, yy, cc):
        return lax.rem((bb * ny + yy) * 2 + cc, na * nb) == device

    chunk = min(n, 1024)

    def main_body(step, carry):
        j, k, l, bb, yy, cc = spots(step)
        s = lax.rem(step, 2)

        @pl.when(step >= 2)
        def _():
            for store in stores(step - 2):
                store.wait()

        x_load(step).wait()
        x = flat(xbuf[s])
        g = dot_rows(x, egu[:ef])
        u = dot_rows(x, egu[ef:])
        gate = flat(gates[:, bb, yy, cc]).astype(f32)
        lane = lax.broadcasted_iota(jnp.int32, gate.shape, 1) - (ROPE + EXP_DEV * device)
        experts_all = EXP_DEV * na * nb
        for e in range(EXP_DEV):
            at = pl.ds(e * wide, wide)
            hit = (lane == e) | (lane == e + experts_all)
            scale = jnp.sum(jnp.where(hit, gate, 0.0), axis=-1, keepdims=True)
            ge, ue = g[:, e * wide : (e + 1) * wide], u[:, e * wide : (e + 1) * wide]
            d = dabuf[step, :, at].astype(f32) * scale
            sig = 1.0 / (1.0 + jnp.exp(-ge))
            swish = ge * sig
            gated[s, :, :, at] = fold((scale * (swish * ue)).astype(bf))
            dcat[s, :, :, at] = fold((d * ue * (sig + swish * (1.0 - sig))).astype(bf))
            dcat[s, :, :, pl.ds(ef + e * wide, wide)] = fold((d * swish).astype(bf))
        hook("main", step, 0)
        mine = is_mine(bb, yy, cc)

        @pl.when(mine)
        def _():
            shared_front(step, x, 0)

        hook("main", step, 1)

        @pl.when((l == 0) & (step + 1 < steps))
        def _():
            await_shared(step + 1)

        @pl.when(step + 1 < steps)
        def _():
            x_load(step + 1).start()

        def column(target):
            for q in range(n // chunk):
                at = pl.ds(q * chunk, chunk)
                total = dot_plain(flat(dcat[s]), egu[:, at])
                target[:, :, at] = fold(total.astype(bf))

            @pl.when(mine)
            def _():
                for q in range(n // chunk):
                    at = pl.ds(q * chunk, chunk)
                    more = dot_plain(flat(dsh[0]), sgu[:, at])
                    target[:, :, at] = fold((flat(target[:, :, at]).astype(f32) + more).astype(bf))

        for store in stores(step):
            store.start()

        @pl.when(l == 1)
        def _():
            pair = lax.div(step, 2)

            @pl.when(pair >= 2)
            def _():
                send_core(pair - 2).wait_send()

            column(dx_out.at[lax.rem(pair, 2)])
            send_core(pair).start()

        @pl.when(l == 0)
        def _():
            column(dx.at[j, k])
            await_in(core_in.at[j, k], core_r.at[j, k])

            def one(i, carry):
                add(dx.at[j, k, i], core_in.at[j, k, i])
                return carry

            lax.fori_loop(0, na, one, 0)

            @pl.when(k > 0)
            def _():
                for p in range(pieces):
                    send_10(p, j, k).start()

            @pl.when(j > 0)
            def _():
                for p in range(pieces):
                    send_11(p, j, k).start()

        return carry

    await_shared(a * 0)
    x_load(a * 0).start()
    lax.fori_loop(0, steps, main_body, 0)
    for step in (steps - 2, steps - 1):
        for store in stores(a * 0 + step):
            store.wait()

    def send_20(p, j):
        return remote(
            dx.at[j, 0, :, upper[0], cols(p)], d2_in0.at[p, j - 1], s20.at[p, j - 1],
            r20.at[p, j - 1], grid.device(a, wrap(b + j, nb), y, c),
        )

    def send_21(p, k):
        return remote(
            dx.at[0, k, :, upper[1], cols(p)], d2_in1.at[p, k - 1], s21.at[p, k - 1],
            r21.at[p, k - 1], grid.device(a, b, wrap(y + k, ny), c),
        )

    def send_a(p, i):
        return remote(
            dx.at[0, 0, wrap(a + i, na), :, cols(p)], a_in.at[p, i - 1], sa.at[p, i - 1],
            ra.at[p, i - 1], grid.device(wrap(a + i, na), b, y, c),
        )

    def sum_first(p):
        for j in reversed(range(nb)):
            for k in range(1, ny):
                await_in(d1_in0.at[p, j, k - 1], r10.at[p, j, k - 1])
                for i in range(na):
                    add(dx.at[j, 0, i, upper[0], cols(p)], d1_in0.at[p, j, k - 1, i])
            if j:
                send_20(p, j).start()
        for k in reversed(range(ny)):
            for j in range(1, nb):
                await_in(d1_in1.at[p, k, j - 1], r11.at[p, k, j - 1])
                for i in range(na):
                    add(dx.at[0, k, i, upper[1], cols(p)], d1_in1.at[p, k, j - 1, i])
            if k:
                send_21(p, k).start()

    def sum_second(p):
        for j in range(1, nb):
            await_in(d2_in0.at[p, j - 1], r20.at[p, j - 1])
            for i in range(na):
                add(dx.at[0, 0, i, upper[0], cols(p)], d2_in0.at[p, j - 1, i])
        for k in range(1, ny):
            await_in(d2_in1.at[p, k - 1], r21.at[p, k - 1])
            for i in range(na):
                add(dx.at[0, 0, i, upper[1], cols(p)], d2_in1.at[p, k - 1, i])
        for i in range(1, na):
            send_a(p, i).start()

    def sum_last(p):
        total = dx[0, 0, a, :, cols(p)].astype(f32)
        for i in range(1, na):
            await_in(a_in.at[p, i - 1], ra.at[p, i - 1])
            total = total + a_in[p, i - 1].astype(f32)
        grad_ref[:, cols(p)] = total

    work = [(sum_first, p) for p in range(pieces)] + [(sum_second, p) for p in range(pieces)]
    turns = {}
    for m, item in enumerate(work):
        turns.setdefault(min(steps - 1, 1 + m * (steps - 1) // len(work)), []).append(item)

    def fill_loads(step):
        _, _, _, bb, yy, cc = spots(step)
        s = lax.rem(step, 2)
        return [
            pltpu.make_async_copy(all_ref.at[:, bb, yy, cc], xbuf.at[s], x_sem.at[s]),
            pltpu.make_async_copy(
                acts_ref.at[:, bb, yy, cc, :, pl.ds(columns[2], ef)], gated.at[s], fill_sem.at[s]
            ),
        ]

    def fill_stores(step):
        _, _, _, bb, yy, cc = spots(step)
        s = lax.rem(step, 2)
        pairs_of = [
            (act.at[s], acts_ref.at[:, bb, yy, cc, :, pl.ds(columns[3], wide_s)]),
            (dsh.at[s], acts_ref.at[:, bb, yy, cc, :, pl.ds(columns[1], 2 * wide_s)]),
            (ybuf.at[s], y_ref.at[:, bb, yy, cc]),
        ]
        return [
            pltpu.make_async_copy(src, dst, out_sem.at[s, i])
            for i, (src, dst) in enumerate(pairs_of)
        ]

    for load in fill_loads(a * 0):
        load.start()

    def fill_body(step, carry):
        j, k, l, bb, yy, cc = spots(step)
        s = lax.rem(step, 2)

        @pl.when(step + 1 < steps)
        def _():
            for load in fill_loads(step + 1):
                load.start()

        @pl.when(step >= 2)
        def _():
            for store in fill_stores(step - 2):
                store.wait()

        for load in fill_loads(step):
            load.wait()
        x = flat(xbuf[s])
        shared_front(step, x, s)
        for q in range(n // chunk):
            at = pl.ds(q * chunk, chunk)
            ybuf[s, :, :, at] = fold(dot_plain(flat(gated[s]), ed[:, at]).astype(bf))

        @pl.when(is_mine(bb, yy, cc))
        def _():
            for q in range(n // chunk):
                at = pl.ds(q * chunk, chunk)
                more = dot_plain(flat(act[s]), sd[:, at])
                ybuf[s, :, :, at] = fold((flat(ybuf[s, :, :, at]).astype(f32) + more).astype(bf))

        for store in fill_stores(step):
            store.start()
        for when, items in turns.items():

            @pl.when(step == when)
            def _():
                for item, p in items:
                    item(p)

        return carry

    lax.fori_loop(0, steps, fill_body, 0)
    for p in range(pieces):
        sum_last(p)

    for step in (steps - 2, steps - 1):
        for store in fill_stores(a * 0 + step):
            store.wait()
    some = place(b, y, c, a, 0)
    for i in range(counts[0]):
        pltpu.make_async_copy(some, some, send_sem.at[i]).wait()
    for i in range(2 * na * pairs):
        pltpu.make_async_copy(some, some, share_send.at[i]).wait()
    for pair in range(max(0, pairs - 2), pairs):
        send_core(a * 0 + pair).wait_send()
    for p in range(pieces):
        for j in range(nb):
            for k in range(ny):
                if k:
                    send_10(p, j, k).wait_send()
                if j:
                    send_11(p, j, k).wait_send()
        for j in range(1, nb):
            send_20(p, j).wait_send()
        for k in range(1, ny):
            send_21(p, k).wait_send()
        for i in range(1, na):
            send_a(p, i).wait_send()


def columns_of(ef, wide_s):
    return (0, 2 * ef, 2 * ef + 2 * wide_s, 3 * ef + 2 * wide_s, 3 * ef + 3 * wide_s)


def experts_call(
    grid, x, dz, gates, expert_gate, expert_up, expert_down, shared_gate, shared_up, shared_down,
    collective_id, pieces=2,
):
    r, n = x.shape
    na, nb, ny = grid.na, grid.nb, grid.ny
    f, fs = expert_down.shape[1], shared_down.shape[0]
    wide, wide_s = round_up(f, 128), round_up(fs, 128)
    ef = EXP_DEV * wide
    half, width, rows = r // 2, n // pieces, na * r
    steps = 2 * nb * ny
    lay = (na, nb, ny, 2, r)
    bf = jnp.bfloat16
    sems = lambda *s: pltpu.SemaphoreType.DMA(s)
    vm = lambda *s: pltpu.VMEM(s, bf)
    sends = 2 * (na - 1 + na * (nb - 1) + na * (ny - 1) + na * (nb - 1) * (ny - 1))
    any_space = pl.BlockSpec(memory_space=pl.ANY)
    in_vmem = pl.BlockSpec(memory_space=pltpu.VMEM)
    outs = pl.pallas_call(
        functools.partial(experts_kernel, grid, pieces),
        out_shape=[
            jax.ShapeDtypeStruct(lay + (n,), bf),
            jax.ShapeDtypeStruct((r, n), jnp.float32),
            jax.ShapeDtypeStruct(lay + (n,), bf),
            jax.ShapeDtypeStruct(lay + (columns_of(ef, wide_s)[-1],), bf),
        ],
        in_specs=[any_space] * 9,
        out_specs=[any_space, in_vmem] + [any_space] * 2,
        scratch_shapes=[
            vm(*lay, 128), vm(2 * ef, n), vm(ef, n), vm(2 * wide_s, n), vm(wide_s, n),
            vm(steps, rows, ef + wide_s),
            vm(2, na, r, n), vm(2, na, r, n),
            vm(2, na, r, ef), vm(2, na, r, 2 * ef),
            vm(2, na, r, wide_s), vm(2, na, r, 2 * wide_s),
            vm(2, na, r, n),
            vm(nb, ny, na, r, n),
            vm(2, na, r, n),
            vm(nb, ny, na, r, n),
            vm(pieces, nb, ny - 1, na, half, width),
            vm(pieces, ny, nb - 1, na, half, width),
            vm(pieces, nb - 1, na, half, width),
            vm(pieces, ny - 1, na, half, width),
            vm(pieces, na - 1, r, width),
            pltpu.SemaphoreType.DMA, sems(3 * EXP_DEV + 3), pltpu.SemaphoreType.DMA, sems(2), sems(2),
            sems(2, 4), sems(2),
            sems(sends), sems(2 * na * nb * ny), sems(2 * na * nb * ny), sems(2 * na * nb * ny),
            sems(2), sems(nb, ny),
            sems(pieces, nb, ny - 1), sems(pieces, nb, ny - 1),
            sems(pieces, ny, nb - 1), sems(pieces, ny, nb - 1),
            sems(pieces, nb - 1), sems(pieces, nb - 1),
            sems(pieces, ny - 1), sems(pieces, ny - 1),
            sems(pieces, na - 1), sems(pieces, na - 1),
        ],
        cost_estimate=microseconds(130),
        compiler_params=pltpu.CompilerParams(
            collective_id=collective_id, has_side_effects=True, vmem_limit_bytes=63 << 20
        ),
    )(
        x,
        dz.reshape(lay + (n,)),
        gates.reshape(lay + (gates.shape[-1],)),
        jnp.swapaxes(expert_gate, 1, 2), jnp.swapaxes(expert_up, 1, 2), expert_down,
        shared_gate.T, shared_up.T, shared_down,
    )
    tokens = grid.size * r
    rows_all, grad, out_rows, acts = outs
    return rows_all.reshape(tokens, n), grad, out_rows.reshape(tokens, n), acts.reshape(tokens, -1)


class Reduce:
    @staticmethod
    def scratch(grid, r, width):
        na, nb, ny = grid.na, grid.nb, grid.ny
        head = Reduce.head(r)
        sems = lambda *s: pltpu.SemaphoreType.DMA(s)
        vm = lambda *s: pltpu.VMEM(s, jnp.bfloat16)
        return [
            vm(nb, ny, na, r, width), vm(nb, ny, na, r, width),
            vm(nb, ny - 1, na, head, width), vm(ny, nb - 1, na, max(16, r - head), width),
            vm(nb - 1, na, head, width), vm(ny - 1, na, max(16, r - head), width), vm(na - 1, r, width),
            sems(nb, ny), sems(nb, ny), sems(nb, ny),
            sems(nb, ny - 1), sems(nb, ny - 1), sems(ny, nb - 1), sems(ny, nb - 1),
            sems(nb - 1), sems(nb - 1), sems(ny - 1), sems(ny - 1), sems(na - 1), sems(na - 1),
        ]

    count = 20

    @staticmethod
    def head(r):
        return r

    @staticmethod
    def schedule(sums):
        stages = [[one.core, one.first, one.second] for one in sums]
        work = []
        for beat in range(len(sums) + 2):
            for back in range(3):
                if 0 <= beat - back < len(sums):
                    work.append(stages[beat - back][back])
        return work

    def __init__(self, grid, source, out, scratch):
        self.grid, self.source, self.out = grid, source, out
        (
            self.acc, self.core_in, self.in10, self.in11, self.in20, self.in21, self.a_in,
            self.load_sem, self.core_s, self.core_r, self.s10, self.r10, self.s11, self.r11,
            self.s20, self.r20, self.s21, self.r21, self.sa, self.ra,
        ) = scratch
        self.spot = grid.here()
        r = self.acc.shape[3]
        head = Reduce.head(r)
        self.both = head < r
        self.upper = (pl.ds(0, head), pl.ds(head, r - head) if self.both else None)
        self.spots = [(j, k) for j in reversed(range(grid.nb)) for k in reversed(range(grid.ny))]

    def remote(self, src, dst, ss, rs, where):
        return pltpu.make_async_remote_copy(
            src_ref=src, dst_ref=dst, send_sem=ss, recv_sem=rs, device_id=where, device_id_type=MESH
        )

    def core_copy(self, j, k):
        g, (a, b, y, c) = self.grid, self.spot
        return self.remote(
            self.source.at[:, wrap(b + j, g.nb), wrap(y + k, g.ny), 1 - c], self.core_in.at[j, k],
            self.core_s.at[j, k], self.core_r.at[j, k], g.device(a, b, y, 1 - c),
        )

    def load(self, j, k):
        g, (a, b, y, c) = self.grid, self.spot
        return pltpu.make_async_copy(
            self.source.at[:, wrap(b + j, g.nb), wrap(y + k, g.ny), c], self.acc.at[j, k], self.load_sem.at[j, k]
        )

    def copy10(self, j, k):
        g, (a, b, y, c) = self.grid, self.spot
        return self.remote(
            self.acc.at[j, k, :, self.upper[0]], self.in10.at[j, k - 1], self.s10.at[j, k - 1],
            self.r10.at[j, k - 1], g.device(a, b, wrap(y + k, g.ny), c),
        )

    def copy11(self, j, k):
        g, (a, b, y, c) = self.grid, self.spot
        return self.remote(
            self.acc.at[j, k, :, self.upper[1]], self.in11.at[k, j - 1], self.s11.at[k, j - 1],
            self.r11.at[k, j - 1], g.device(a, wrap(b + j, g.nb), y, c),
        )

    def copy20(self, j):
        g, (a, b, y, c) = self.grid, self.spot
        return self.remote(
            self.acc.at[j, 0, :, self.upper[0]], self.in20.at[j - 1], self.s20.at[j - 1],
            self.r20.at[j - 1], g.device(a, wrap(b + j, g.nb), y, c),
        )

    def copy21(self, k):
        g, (a, b, y, c) = self.grid, self.spot
        return self.remote(
            self.acc.at[0, k, :, self.upper[1]], self.in21.at[k - 1], self.s21.at[k - 1],
            self.r21.at[k - 1], g.device(a, b, wrap(y + k, g.ny), c),
        )

    def copy_a(self, i):
        g, (a, b, y, c) = self.grid, self.spot
        return self.remote(
            self.acc.at[0, 0, wrap(a + i, g.na)], self.a_in.at[i - 1], self.sa.at[i - 1],
            self.ra.at[i - 1], g.device(wrap(a + i, g.na), b, y, c),
        )

    def add(self, into, rows, ref, sem):
        pltpu.make_async_copy(ref, ref, sem).wait()
        f32 = jnp.float32

        def one(i, carry):
            total = into[i, rows].astype(f32) + ref[i].astype(f32)
            into[i, rows] = total.astype(into.dtype)
            return carry

        lax.fori_loop(0, self.grid.na, one, 0)

    def start(self):
        for j, k in self.spots:
            self.core_copy(j, k).start()
            self.load(j, k).start()

    def core(self):
        whole = pl.ds(0, self.acc.shape[3])
        for j, k in self.spots:
            self.load(j, k).wait()
            self.add(self.acc.at[j, k], whole, self.core_in.at[j, k], self.core_r.at[j, k])
            if k:
                self.copy10(j, k).start()
            if j and self.both:
                self.copy11(j, k).start()

    def first(self):
        nb, ny = self.grid.nb, self.grid.ny
        for j in reversed(range(nb)):
            for k in range(1, ny):
                self.add(self.acc.at[j, 0], self.upper[0], self.in10.at[j, k - 1], self.r10.at[j, k - 1])
            if j:
                self.copy20(j).start()
        for k in reversed(range(ny if self.both else 0)):
            for j in range(1, nb):
                self.add(self.acc.at[0, k], self.upper[1], self.in11.at[k, j - 1], self.r11.at[k, j - 1])
            if k:
                self.copy21(k).start()

    def second(self):
        for j in range(1, self.grid.nb):
            self.add(self.acc.at[0, 0], self.upper[0], self.in20.at[j - 1], self.r20.at[j - 1])
        for k in range(1, self.grid.ny if self.both else 0):
            self.add(self.acc.at[0, 0], self.upper[1], self.in21.at[k - 1], self.r21.at[k - 1])
        for i in range(1, self.grid.na):
            self.copy_a(i).start()

    def last(self):
        total = self.acc[0, 0, self.spot[0]].astype(jnp.float32)
        for i in range(1, self.grid.na):
            pltpu.make_async_copy(self.a_in.at[i - 1], self.a_in.at[i - 1], self.ra.at[i - 1]).wait()
            total = total + self.a_in[i - 1].astype(jnp.float32)
        self.out[...] = total.astype(self.out.dtype)

    def finish(self):
        for j, k in self.spots:
            self.core_copy(j, k).wait_send()
            if k:
                self.copy10(j, k).wait_send()
            if j and self.both:
                self.copy11(j, k).wait_send()
        for j in range(1, self.grid.nb):
            self.copy20(j).wait_send()
        for k in range(1, self.grid.ny if self.both else 0):
            self.copy21(k).wait_send()
        for i in range(1, self.grid.na):
            self.copy_a(i).wait_send()


W_PIECES = 1


def gradients_kernel(grid, pieces, unit, places, *refs):
    (y_ref, k_ref, w_ref, t_ref, q_ref, x_ref, dz_ref, acts_ref), refs = refs[:8], refs[8:]
    (y_out, k_out, w_out, t_out, q_out), refs = refs[:5], refs[5:]
    outs, refs = refs[:6], refs[6:]
    (big, left, right, big_sem, left_sem, out_sem), refs = refs[:6], refs[6:]
    width = y_ref.shape[-1] // pieces
    sources = [(k_ref, k_out)]
    for p in range(pieces):
        at = pl.ds(p * width, width)
        sources.append((y_ref.at[:, :, :, :, :, at], y_out.at[:, at]))
    sums = [
        Reduce(grid, src, out, refs[m * Reduce.count : (m + 1) * Reduce.count])
        for m, (src, out) in enumerate(sources)
    ]
    refs = refs[len(sums) * Reduce.count :]
    w_width = w_ref.shape[-1] // W_PIECES
    flat_sums = []
    for p in range(W_PIECES):
        at = pl.ds(p * w_width, w_width)
        part = refs[p * PlaneReduce.count : (p + 1) * PlaneReduce.count]
        flat_sums.append(PlaneReduce(grid, w_ref.at[:, :, :, at], w_out.at[:, at], part))
    refs = refs[W_PIECES * PlaneReduce.count :]
    flat_sums.append(TensorReduce(grid, t_ref, t_out, refs[: TensorReduce.count]))
    q_gather = PlaneGather(grid, q_ref, q_out, refs[TensorReduce.count :])
    tiles = len(places)
    turn = sum(1 for place in places if place[0] != 2 and place[0] != 5)
    slots = big.shape[0]

    def left_load(m):
        s = lax.rem(m, 2)
        at = pl.ds(pl.multiple_of(m * unit, unit), unit)
        return pltpu.make_async_copy(acts_ref.at[:, at], left.at[s], left_sem.at[s])

    big_loads = [
        pltpu.make_async_copy(src, big.at[s % slots], big_sem.at[s]) for s, src in enumerate((x_ref, dz_ref))
    ]
    big_loads[0].start()
    greet(grid)
    for one in sums + flat_sums + [q_gather]:
        one.start()
    left_load(grid.here()[0] * 0).start()
    if slots > 1:
        big_loads[1].start()
    big_loads[0].wait()

    work = Reduce.schedule(sums)
    for p, one in enumerate(flat_sums):
        work.insert(min(len(work), 3 + 3 * p), one.middle)
    for i in range(1, grid.na):
        work.insert(min(len(work), 3 + 3 * i), functools.partial(q_gather.middle, i))
    turns = {}
    for n, item in enumerate(work):
        turns.setdefault(n * tiles // len(work), []).append(item)

    def store(m):
        which, head, first, rows = places[m]
        dst = outs[which]
        dst = dst.at[pl.ds(first, rows)] if head is None else dst.at[head, pl.ds(first, rows)]
        return pltpu.make_async_copy(right.at[m % 2, pl.ds(0, rows)], dst, out_sem.at[m % 2])

    def tile_body(m, carry):
        s = lax.rem(m, 2)

        @pl.when(m + 1 < tiles)
        def _():
            left_load(m + 1).start()

        for n in range(2, tiles):

            @pl.when(m == n)
            def _():
                store(n - 2).wait()

        @pl.when(m == turn)
        def _():
            if slots == 1:
                big_loads[1].start()
            big_loads[1].wait()

        left_load(m).wait()
        operand = big.at[lax.div(m, turn) if slots > 1 else 0]
        right[s] = lax.dot_general(
            left[s], operand[...], (((0,), (0,)), ((), ())), preferred_element_type=jnp.float32
        ).astype(right.dtype)
        for n in range(tiles):

            @pl.when(m == n)
            def _():
                store(n).start()
                for item in turns.get(n, ()):
                    item()

        return carry

    lax.fori_loop(0, tiles, tile_body, 0)
    for one in sums + flat_sums:
        one.last()
    for n in range(max(0, tiles - 2), tiles):
        store(n).wait()
    for one in sums + flat_sums:
        one.finish()
    q_gather.last()


def gradients_call(grid, out_rows, key_rows, weight_rows, tensor_rows, query_rows, x, dz, acts, f, fs, collective_id, pieces=4):
    tokens, n = x.shape
    r = tokens // grid.size
    lay = (grid.na, grid.nb, grid.ny, 2, r)
    wide, wide_s = round_up(f, 128), round_up(fs, 128)
    unit = math.gcd(wide, wide_s)
    places = []
    for which, heads, real, padded in (
        (0, EXP_DEV, f, wide), (1, EXP_DEV, f, wide), (3, 0, fs, wide_s), (4, 0, fs, wide_s),
        (2, EXP_DEV, f, wide), (5, 0, fs, wide_s),
    ):
        for head in range(max(heads, 1)):
            for first in range(0, padded, unit):
                places.append((which, head if heads else None, first, min(unit, real - first)))
    slots = 2 if 2 * tokens * n * 2 <= (24 << 20) else 1
    any_space = pl.BlockSpec(memory_space=pl.ANY)
    in_vmem = pl.BlockSpec(memory_space=pltpu.VMEM)
    f32 = jnp.float32
    scratch = [
        pltpu.VMEM((slots, tokens, n), x.dtype),
        pltpu.VMEM((2, tokens, unit), x.dtype),
        pltpu.VMEM((2, unit, n), x.dtype),
        pltpu.SemaphoreType.DMA((2,)),
        pltpu.SemaphoreType.DMA((2,)),
        pltpu.SemaphoreType.DMA((2,)),
    ]
    kw = key_rows.shape[1]
    for width in [kw] + [n // pieces] * pieces:
        scratch += Reduce.scratch(grid, r, width)
    wr, ww = weight_rows.shape[0] // (grid.na * grid.nb), weight_rows.shape[1]
    scratch += PlaneReduce.scratch(grid, wr, ww // W_PIECES) * W_PIECES
    tr, tw = tensor_rows.shape[0] // (2 * grid.ny), tensor_rows.shape[1]
    scratch += TensorReduce.scratch(grid, tr, tw) + PlaneGather.scratch(grid)
    outs = pl.pallas_call(
        functools.partial(gradients_kernel, grid, pieces, unit, places),
        out_shape=[
            jax.ShapeDtypeStruct((r, n), f32),
            jax.ShapeDtypeStruct((r, kw), f32),
            jax.ShapeDtypeStruct((wr, ww), x.dtype),
            jax.ShapeDtypeStruct((tr, tw), f32),
            jax.ShapeDtypeStruct((grid.na, grid.nb) + query_rows.shape, x.dtype),
            jax.ShapeDtypeStruct((EXP_DEV, f, n), x.dtype),
            jax.ShapeDtypeStruct((EXP_DEV, f, n), x.dtype),
            jax.ShapeDtypeStruct((EXP_DEV, f, n), x.dtype),
            jax.ShapeDtypeStruct((fs, n), x.dtype),
            jax.ShapeDtypeStruct((fs, n), x.dtype),
            jax.ShapeDtypeStruct((fs, n), x.dtype),
        ],
        in_specs=[any_space] * 8,
        out_specs=[in_vmem] * 4 + [any_space] * 7,
        scratch_shapes=scratch,
        cost_estimate=microseconds(90),
        compiler_params=pltpu.CompilerParams(
            collective_id=collective_id, has_side_effects=True, vmem_limit_bytes=62 << 20
        ),
    )(
        out_rows.reshape(lay + (n,)),
        key_rows.reshape(lay + (kw,)),
        weight_rows.reshape(grid.na, grid.nb, wr, ww),
        tensor_rows.reshape(grid.ny, 2, tr, tw),
        query_rows,
        x,
        dz,
        acts,
    )
    y_sum, k_sum, w_sum, t_sum, q_all = outs[:5]
    eg, eu, ed, sg, su, sd = (out.astype(f32) for out in outs[5:])
    q_all = q_all.reshape(tokens, -1)
    weights = (jnp.swapaxes(eg, 1, 2), jnp.swapaxes(eu, 1, 2), ed, sg.T, su.T, sd)
    return y_sum, k_sum, w_sum, t_sum, q_all, weights


class GatherAll:
    @staticmethod
    def scratch(grid):
        blocks = 2 * grid.na * grid.nb * grid.ny
        sems = lambda n: pltpu.SemaphoreType.DMA((n,))
        return [sems(1), sems(gather_sends(grid)), sems(blocks), sems(blocks), sems(blocks)]

    def __init__(self, grid, x, out, scratch, halves=2):
        self.grid, self.x, self.out, self.halves = grid, x, out, halves
        self.own_sem, self.sends, self.recvs, self.share_s, self.share_r = scratch
        self.spot = grid.here()
        self.half = x.shape[0] // halves
        self.count = 0
        na, nb, ny = grid.na, grid.nb, grid.ny
        self.orders = (("b", "y"), ("y", "b"))
        near = [(0, k, 0, 0, ()) for k in range(1, ny)] + [(0, k, 0, 1, ("b",)) for k in range(1, ny)]
        first = [(0, 0, i, h, self.orders[h]) for i in range(1, na) for h in range(2)]
        second = []
        for i in range(na):
            second += [(j, 0, i, 0, ("y",)) for j in range(1, nb)]
            second += [(0, k, i, 1, ("b",)) for k in range(1, ny) if i]
        third = []
        for i in range(na):
            third += [(0, k, i, 0, ()) for k in range(1, ny) if i]
            third += [(j, 0, i, 1, ()) for j in range(1, nb)]
        for i in range(na):
            third += [(j, k, i, h, ()) for j in range(1, nb) for k in range(1, ny) for h in range(2)]
        self.near = [event for event in near if event[3] < halves]
        self.others = [event for event in first + second + third if event[3] < halves]

    def line(self, i):
        a = self.spot[0]
        if self.grid.na != 4:
            return wrap(a + i, self.grid.na)
        if i == 0:
            return a
        if i == 1:
            return a + 1 - 2 * lax.rem(a, 2)
        return (i - lax.div(a, 2)) if i == 2 else (3 - 3 * lax.div(a, 2))

    def place(self, bb, yy, cc, aa, h):
        return self.out.at[aa, bb, yy, cc, pl.ds(h * self.half, self.half)]

    def slot(self, bb, yy, aa, h):
        return ((bb * self.grid.ny + yy) * self.grid.na + aa) * 2 + h

    def push(self, src, bb, yy, aa, h, where, send, recv):
        pltpu.make_async_remote_copy(
            src_ref=src, dst_ref=self.place(bb, yy, self.spot[3], aa, h), send_sem=send,
            recv_sem=recv.at[self.slot(bb, yy, aa, h)], device_id=where, device_id_type=MESH,
        ).start()

    def onward(self, src, bb, yy, aa, h, dims):
        g, (a, b, y, c) = self.grid, self.spot
        for d in dims:
            for i in range(1, {"a": g.na, "b": g.nb, "y": g.ny}[d]):
                if d == "a":
                    where = g.device(self.line(i), b, y, c)
                elif d == "b":
                    where = g.device(a, wrap(b + i, g.nb), y, c)
                else:
                    where = g.device(a, b, wrap(y + i, g.ny), c)
                self.push(src, bb, yy, aa, h, where, self.sends.at[self.count], self.recvs)
                self.count += 1
        where = g.device(a, b, y, 1 - c)
        self.push(src, bb, yy, aa, h, where, self.share_s.at[self.slot(bb, yy, aa, h)], self.share_r)

    def landed(self, bb, yy, cc, aa, h, sem):
        ref = self.place(bb, yy, cc, aa, h)
        pltpu.make_async_copy(ref, ref, sem.at[self.slot(bb, yy, aa, h)]).wait()
        return ref

    def own(self):
        a, b, y, c = self.spot
        return pltpu.make_async_copy(self.x, self.out.at[a, b, y, c], self.own_sem.at[0])

    def start(self):
        a, b, y, c = self.spot
        self.own().start()
        for h in range(self.halves):
            src = self.x.at[pl.ds(h * self.half, self.half)]
            self.onward(src, b, y, a, h, ("y", "a", "b") if h == 0 else ("y", "b", "a"))

    def relay(self, j, k, i, h, dims):
        g, (a, b, y, c) = self.grid, self.spot
        bb, yy, aa = wrap(b + j, g.nb), wrap(y + k, g.ny), self.line(i)
        self.onward(self.landed(bb, yy, c, aa, h, self.recvs), bb, yy, aa, h, dims)

    def shared(self, j, k, i):
        g, (a, b, y, c) = self.grid, self.spot
        for h in range(self.halves):
            self.landed(wrap(b + j, g.nb), wrap(y + k, g.ny), 1 - c, self.line(i), h, self.share_r)

    def group(self):
        for event in self.near:
            self.relay(*event)
        for k in range(self.grid.ny):
            self.shared(0, k, 0)
        self.own().wait()

    def finish(self):
        g, (a, b, y, c) = self.grid, self.spot
        for j in range(g.nb):
            for k in range(g.ny):
                for i in range(g.na):
                    if i or j:
                        self.shared(j, k, i)
        some = self.place(b, y, c, a, 0)
        for i in range(self.count):
            pltpu.make_async_copy(some, some, self.sends.at[i]).wait()
        for i in range(g.na * g.nb * g.ny):
            for h in range(self.halves):
                pltpu.make_async_copy(some, some, self.share_s.at[2 * i + h]).wait()


def turn_back(values, cosines, sines):
    quarter = ROPE // 2
    lane = lax.broadcasted_iota(jnp.int32, values.shape, 1)
    swapped = jnp.where(
        lane < quarter,
        pltpu.roll(values, values.shape[1] - quarter, 1),
        pltpu.roll(values, quarter, 1),
    )
    return values * cosines + swapped * sines


def attention_back_kernel(
    grid,
    pieces,
    x_ref,
    wo_hbm,
    q_hbm,
    kv_hbm,
    packed_hbm,
    we_hbm,
    ctx_ref,
    log_ref,
    seg_ref,
    own_seg_ref,
    cos_ref,
    sin_ref,
    dq_ref,
    keys_ref,
    part_ref,
    wo_ref,
    wo,
    q,
    kv,
    packed,
    we,
    grads,
    kcat,
    bias,
    dkv,
    drope,
    wo_part,
    load_sem,
    *scratch,
):
    f32, bf = jnp.float32, jnp.bfloat16
    rows, tokens = q.shape[0], kv.shape[0]
    heads = q.shape[1] // 256
    scale = (NOPE + ROPE) ** (-0.5)
    a, b, y, c = grid.here()
    pairs = ((wo_hbm, wo), (q_hbm, q), (kv_hbm, kv), (packed_hbm, packed), (we_hbm, we))
    loads = [pltpu.make_async_copy(src, dst, load_sem.at[i]) for i, (src, dst) in enumerate(pairs)]
    for load in loads:
        load.start()
    greet(grid)
    group = TensorGather(grid, x_ref, grads, scratch[: TensorGather.count])
    group.start()
    sums = []
    width = wo.shape[1] // pieces
    for p in range(pieces):
        first = TensorGather.count + p * PlaneReduce.count
        at = pl.ds(p * width, width)
        sums.append(
            PlaneReduce(
                grid, wo_part.at[:, :, :, at], wo_ref.at[:, at], scratch[first : first + PlaneReduce.count]
            )
        )
    first_row = (a * grid.nb + b) * rows
    ordinal = first_row + lax.broadcasted_iota(jnp.int32, (rows, tokens), 0)
    key = lax.broadcasted_iota(jnp.int32, (rows, tokens), 1)
    seg = seg_ref[...]
    seen = (key <= ordinal) & ((seg == own_seg_ref[...]) | (seg == 0))
    bias[...] = jnp.where(seen, 0.0, masked_out)
    for load in loads:
        load.wait()
    kcat[:, NOPE:] = packed[:, LATENT : LATENT + 128]
    lane = lax.broadcasted_iota(jnp.int32, (tokens, 128), 1)
    kcat[:, NOPE:] = jnp.where(lane < ROPE, kcat[:, NOPE:].astype(f32), 0.0).astype(bf)

    group.middle(1)
    group.last()
    rows_in = grads[...].reshape(rows, grads.shape[-1])
    for p in range(pieces):
        at = pl.ds(p * width, width)
        wo_part[:, :, :, at] = (
            lax.dot_general(
                ctx_ref[...], rows_in[:, p * width : (p + 1) * width], (((0,), (0,)), ((), ())),
                preferred_element_type=f32,
            )
            .astype(bf)
            .reshape(wo_part.shape[:3] + (width,))
        )
        sums[p].start()
    dctx = dot_rows(rows_in, wo[...]).astype(bf)

    points = 3 * heads + 1
    at_point = {}
    for p in range(pieces):
        at_point.setdefault((p + 1) * points // (pieces + 2), []).append(sums[p].middle)
    done = [0]

    def hook():
        for event in at_point.get(done[0], ()):
            event()
        done[0] += 1

    hook()
    for h in range(heads):
        qh = q[:, h * 256 : (h + 1) * 256]
        kcat[:, :NOPE] = kv[:, h * 256 : h * 256 + NOPE]
        s = dot_rows(qh, kcat[...]) * scale + bias[...]
        p = jnp.exp(s - log_ref[h])
        dh = dctx[:, h * VDIM : (h + 1) * VDIM]
        dp = dot_rows(dh, kv[:, h * 256 + NOPE : (h + 1) * 256])
        ds = (p * (dp - jnp.sum(p * dp, axis=-1, keepdims=True))).astype(bf)
        p = p.astype(bf)
        hook()
        dq = dot_plain(ds, kcat[...]) * scale
        dq_ref[:, h * 256 : h * 256 + NOPE] = dq[:, :NOPE].astype(bf)
        dq_ref[:, h * 256 + NOPE : (h + 1) * 256] = turn_back(
            dq[:, NOPE:], cos_ref[...], sin_ref[...]
        ).astype(bf)
        hook()
        dkv[:, h * 256 + NOPE : (h + 1) * 256] = lax.dot_general(
            p, dh, (((0,), (0,)), ((), ())), preferred_element_type=f32
        ).astype(bf)
        dk = scale * lax.dot_general(ds, qh, (((0,), (0,)), ((), ())), preferred_element_type=f32)
        dkv[:, h * 256 : h * 256 + NOPE] = dk[:, :NOPE].astype(bf)
        if h == 0:
            drope[...] = dk[:, NOPE:]
        else:
            drope[...] += dk[:, NOPE:]
        hook()
    keys_ref[:, :LATENT] = dot_rows(dkv[...], we[...]).astype(bf)
    keys_ref[:, LATENT:] = drope[...].astype(bf)
    part_ref[...] = lax.dot_general(
        packed[:, :LATENT], dkv[...], (((0,), (0,)), ((), ())), preferred_element_type=f32
    ).astype(bf)
    for one in sums:
        one.last()
    for one in sums:
        one.finish()


def attention_back_call(
    grid, x, wo, q, kv, packed, we, context, log_total, seg, own_seg, cosines, sines, collective_id, pieces=4
):
    r, n = x.shape
    rows, tokens, heads = q.shape[0], kv.shape[0], q.shape[1] // 256
    bf, f32 = jnp.bfloat16, jnp.float32
    any_space = pl.BlockSpec(memory_space=pl.ANY)
    in_vmem = pl.BlockSpec(memory_space=pltpu.VMEM)
    share = wo.shape[0] // (grid.na * grid.nb)
    return pl.pallas_call(
        functools.partial(attention_back_kernel, grid, pieces),
        out_shape=[
            jax.ShapeDtypeStruct(q.shape, bf),
            jax.ShapeDtypeStruct((tokens, LATENT + 128), bf),
            jax.ShapeDtypeStruct(we.shape, bf),
            jax.ShapeDtypeStruct((share, n), bf),
        ],
        in_specs=[any_space] * 6 + [in_vmem] * 6,
        out_specs=[in_vmem] * 4,
        scratch_shapes=[
            pltpu.VMEM(wo.shape, bf),
            pltpu.VMEM(q.shape, bf),
            pltpu.VMEM(kv.shape, bf),
            pltpu.VMEM(packed.shape, bf),
            pltpu.VMEM(we.shape, bf),
            pltpu.VMEM((grid.ny, 2, r, n), bf),
            pltpu.VMEM((tokens, 256), bf),
            pltpu.VMEM((rows, tokens), f32),
            pltpu.VMEM(kv.shape, bf),
            pltpu.VMEM((tokens, 128), f32),
            pltpu.VMEM((grid.na, grid.nb, share, n), bf),
            pltpu.SemaphoreType.DMA((5,)),
        ]
        + TensorGather.scratch(grid)
        + PlaneReduce.scratch(grid, share, n // pieces) * pieces,
        cost_estimate=microseconds(50),
        compiler_params=pltpu.CompilerParams(
            collective_id=collective_id, has_side_effects=True, vmem_limit_bytes=62 << 20
        ),
    )(x, wo, q, kv, packed, we, context, log_total, seg, own_seg, cosines, sines)


def front_kernel(
    grid,
    hidden_ref,
    gain_ref,
    lgain_ref,
    mgain_ref,
    gate_ref,
    route_ref,
    cos_ref,
    sin_ref,
    seg_ref,
    own_seg_ref,
    cot_hbm,
    wl_hbm,
    wq_hbm,
    we_hbm,
    wo_hbm,
    packed_hbm,
    cot_all,
    kv_ref,
    q,
    normed_ref,
    comp_ref,
    log_ref,
    ctx_ref,
    res_ref,
    moe_ref,
    wl,
    wq,
    we,
    wo,
    normed,
    mine,
    packed,
    kv,
    kcat,
    bias,
    part,
    total,
    load_sem,
    kv_sem,
    packed_sem,
    *scratch,
):
    f32, bf = jnp.float32, jnp.bfloat16
    rows, few, tokens = hidden_ref.shape[0], mine.shape[0], kv.shape[0]
    heads = q.shape[1] // 256
    scale = (NOPE + ROPE) ** (-0.5)
    a, b, y, c = grid.here()
    pairs = (
        (wl_hbm, wl.at[pl.ds(0, LATENT + ROPE)]), (wq_hbm, wq), (we_hbm, we), (wo_hbm, wo),
    )
    loads = [pltpu.make_async_copy(src, dst, load_sem.at[i]) for i, (src, dst) in enumerate(pairs)]
    for load in loads:
        load.start()
    wl[LATENT + ROPE :] = jnp.zeros((wl.shape[0] - LATENT - ROPE, wl.shape[1]), bf)
    greet(grid)
    at = pl.ds(pl.multiple_of((y * 2 + c) * few, few), few)

    def rms(v, gain):
        return v * lax.rsqrt(jnp.mean(v * v, axis=-1, keepdims=True) + epsilon) * gain

    hidden_few = hidden_ref[at].astype(f32)
    normed_few = rms(hidden_few, gain_ref[...]).astype(bf)
    normed_ref[...] = normed_few
    loads[0].wait()
    comp = dot_rows(normed_few, wl[...])
    comp_ref[...] = comp
    mine[:, :LATENT] = rms(comp[:, :LATENT], lgain_ref[...]).astype(bf)
    tail = turn_back(comp[:, LATENT:], cos_ref[at], -sin_ref[at])
    lane = lax.broadcasted_iota(jnp.int32, tail.shape, 1) - ROPE
    routes, gates = route_ref[at], gate_ref[at]
    for k in range(TOP):
        expert, gate = routes[:, k : k + 1], gates[:, k : k + 1]
        high = gate.astype(bf).astype(f32)
        tail += jnp.where(lane == expert, high, 0.0)
        tail += jnp.where(lane == expert + EXP_DEV * grid.na * grid.nb, gate - high, 0.0)
    mine[:, LATENT:] = tail.astype(bf)
    gather = GatherAll(grid, mine, packed_hbm, scratch[:5], halves=1)
    gather.start()
    cots = GatherAll(grid, cot_hbm.at[at], cot_all, scratch[5:10])
    cots.start()
    normed[...] = rms(hidden_ref[...].astype(f32), gain_ref[...]).astype(bf)
    loads[1].wait()
    gather.group()
    third = len(gather.others) // 3
    for event in gather.others[:third]:
        gather.relay(*event)
    raw = dot_plain(normed[...], wq[...])
    width = raw.shape[1]
    for h in range(heads):
        step = h * (NOPE + ROPE)
        moved = raw if step == 0 else pltpu.roll(raw, width - step, 1)
        q[:, h * 256 : h * 256 + NOPE] = moved[:, :NOPE].astype(bf)
        q[:, h * 256 + NOPE : (h + 1) * 256] = turn_back(
            moved[:, NOPE : NOPE + 128], cos_ref[...], -sin_ref[...]
        ).astype(bf)
    for event in gather.others[third:]:
        gather.relay(*event)
    early = 2 * (grid.na - 1)
    for event in cots.near + cots.others[:early]:
        cots.relay(*event)
    ordinal = (a * grid.nb + b) * rows + lax.broadcasted_iota(jnp.int32, (rows, tokens), 0)
    key = lax.broadcasted_iota(jnp.int32, (rows, tokens), 1)
    seg = seg_ref[...]
    seen = (key <= ordinal) & ((seg == own_seg_ref[...]) | (seg == 0))
    bias[...] = jnp.where(seen, 0.0, masked_out)
    gather.finish()
    load = pltpu.make_async_copy(packed_hbm, packed, packed_sem)
    load.start()

    passing = [functools.partial(cots.relay, *event) for event in cots.others[early:]]
    at_point = {}
    for m, event in enumerate(passing):
        at_point.setdefault(m * (heads + 1) // len(passing), []).append(event)

    def hook(point):
        for event in at_point.get(point, ()):
            event()

    load.wait()
    hook(0)
    flat = packed[...].reshape(tokens, packed.shape[-1])
    lane = lax.broadcasted_iota(jnp.int32, (tokens, 128), 1)
    kcat[:, NOPE:] = jnp.where(lane < ROPE, flat[:, LATENT:].astype(f32), 0.0).astype(bf)
    loads[2].wait()
    kv[...] = dot_plain(flat[:, :LATENT], we[...]).astype(bf)
    store = pltpu.make_async_copy(kv, kv_ref, kv_sem)
    store.start()
    hook(1)
    for h in range(heads):
        kcat[:, :NOPE] = kv[:, h * 256 : h * 256 + NOPE]
        s = dot_rows(q[:, h * 256 : (h + 1) * 256], kcat[...]) * scale + bias[...]
        peak = jnp.max(s, axis=-1, keepdims=True)
        w = jnp.exp(s - peak)
        tot = jnp.sum(w, axis=-1, keepdims=True)
        log_ref[h] = peak + jnp.log(tot)
        p = (w * (1.0 / tot)).astype(bf)
        ctx_ref[:, h * VDIM : (h + 1) * VDIM] = dot_plain(
            p, kv[:, h * 256 + NOPE : (h + 1) * 256]
        ).astype(bf)
        hook(2 + h)
    loads[3].wait()
    part[...] = dot_plain(ctx_ref[...], wo[...]).astype(bf).reshape(part.shape)
    reduce = TensorReduce(grid, part, total, scratch[10:])
    reduce.start()
    reduce.middle()
    reduce.last()
    residual = hidden_ref[at].astype(f32) + total[...]
    res_ref[...] = residual
    moe_ref[...] = rms(residual, mgain_ref[...]).astype(bf)
    store.wait()
    for k in range(grid.ny):
        cots.shared(0, k, 0)
    cots.own().wait()
    cots.finish()
    reduce.finish()


def front_call(
    grid, hidden, cotangent, attn_gain, latent_gain, moe_gain, gates, routes, cosines, sines, seg, own_seg,
    latent_weight, query_weight, expand_weight, output_weight, collective_id,
):
    rows, n = hidden.shape
    few = rows // (2 * grid.ny)
    tokens = grid.size * few
    heads = query_weight.shape[1] // (NOPE + ROPE)
    bf, f32 = jnp.bfloat16, jnp.float32
    any_space = pl.BlockSpec(memory_space=pl.ANY)
    in_vmem = pl.BlockSpec(memory_space=pltpu.VMEM)
    width = LATENT + 128
    lay = (grid.na, grid.nb, grid.ny, 2, few)
    outs = pl.pallas_call(
        functools.partial(front_kernel, grid),
        out_shape=[
            jax.ShapeDtypeStruct(lay + (width,), bf),
            jax.ShapeDtypeStruct(lay + (n,), bf),
            jax.ShapeDtypeStruct((tokens, heads * 256), bf),
            jax.ShapeDtypeStruct((rows, heads * 256), bf),
            jax.ShapeDtypeStruct((few, n), bf),
            jax.ShapeDtypeStruct((few, width), f32),
            jax.ShapeDtypeStruct((heads, rows, 1), f32),
            jax.ShapeDtypeStruct((rows, heads * VDIM), bf),
            jax.ShapeDtypeStruct((few, n), f32),
            jax.ShapeDtypeStruct((few, n), bf),
        ],
        in_specs=[in_vmem] * 10 + [any_space] * 5,
        out_specs=[any_space] * 3 + [in_vmem] * 7,
        scratch_shapes=[
            pltpu.VMEM((width, n), bf),
            pltpu.VMEM(query_weight.shape, bf),
            pltpu.VMEM(expand_weight.shape, bf),
            pltpu.VMEM(output_weight.shape, bf),
            pltpu.VMEM((rows, n), bf),
            pltpu.VMEM((few, width), bf),
            pltpu.VMEM(lay + (width,), bf),
            pltpu.VMEM((tokens, heads * 256), bf),
            pltpu.VMEM((tokens, 256), bf),
            pltpu.VMEM((rows, tokens), f32),
            pltpu.VMEM((grid.ny, 2, few, n), bf),
            pltpu.VMEM((few, n), f32),
            pltpu.SemaphoreType.DMA((4,)),
            pltpu.SemaphoreType.DMA,
            pltpu.SemaphoreType.DMA,
        ]
        + GatherAll.scratch(grid) * 2
        + TensorReduce.scratch(grid, few, n),
        cost_estimate=microseconds(74),
        compiler_params=pltpu.CompilerParams(
            collective_id=collective_id, has_side_effects=True, vmem_limit_bytes=62 << 20
        ),
    )(
        hidden, attn_gain[None], latent_gain[None], moe_gain[None], gates, routes, cosines, sines,
        seg, own_seg, cotangent, latent_weight.T, query_weight, expand_weight, output_weight,
    )
    return [outs[0].reshape(tokens, width), outs[1].reshape(tokens, n), *outs[2:]]


def rms_scale(values, gain_vec):
    return (
        values * lax.rsqrt(jnp.mean(values * values, axis=-1, keepdims=True) + epsilon) * gain_vec
    )


def rotate(values, places):
    halfway = values.shape[-1] // 2
    frequency = 10000.0 ** (-jnp.arange(halfway, dtype=jnp.float32) / halfway)
    angles = places.astype(jnp.float32)[:, None] * frequency[None, :]
    cosine = jnp.cos(angles)
    sine_part = jnp.sin(angles)
    if values.ndim == 3:
        cosine = cosine[:, None, :]
        sine_part = sine_part[:, None, :]
    first_half = values[..., :halfway]
    second = values[..., halfway:]
    return jnp.concatenate(
        [first_half * cosine - second * sine_part, second * cosine + first_half * sine_part],
        axis=-1,
    )


def seq_places(segments):
    total_rows = segments.shape[0]
    ordinal = jnp.arange(total_rows, dtype=jnp.int32)
    starts = jnp.concatenate(
        [jnp.ones((1,), jnp.int32), (segments[1:] != segments[:-1]).astype(jnp.int32)]
    )
    seg_start = lax.cummax(jnp.where(starts > 0, ordinal, 0), axis=0)
    return jnp.where(segments == 0, ordinal, total_rows // 2 + ordinal - seg_start)


def silu_product(gate_pre, up_pre):
    return jax.nn.silu(gate_pre) * up_pre


def score_block(queries, key_plain, rope_all, visible):
    scale_factor = (NOPE + ROPE) ** (-0.5)
    raw_scores = jnp.einsum(
        "thc,shc->hts", queries[..., :NOPE], key_plain, preferred_element_type=jnp.float32
    )
    raw_scores = raw_scores + jnp.einsum(
        "thr,sr->hts", queries[..., NOPE:], rope_all, preferred_element_type=jnp.float32
    )
    return jnp.where(visible[None], scale_factor * raw_scores, masked_out)


def dot(left_side, right_side):
    return jnp.dot(left_side, right_side, preferred_element_type=jnp.float32)


def pad_columns(values):
    return jnp.pad(values, ((0, 0), (0, -values.shape[1] % 128)))


def low(values):
    return values.astype(jnp.bfloat16)


def shards(
    grid,
    hidden_in,
    attn_gain,
    query_weight,
    latent_weight,
    latent_gain,
    expand_weight,
    output_weight,
    moe_gain,
    shared_gate,
    shared_up,
    shared_down,
    expert_gate,
    expert_up,
    expert_down,
    gate_values,
    expert_routes,
    segments,
    cotangent,
):
    tok_rows, model_width = hidden_in.shape
    groups = lax.axis_size("expert")
    parts = lax.axis_size("tensor")
    device = lax.axis_index("expert")
    part = lax.axis_index("tensor")
    total_rows = segments.shape[0]
    few = tok_rows // parts
    start_row = device * tok_rows
    scale_factor = (NOPE + ROPE) ** (-0.5)

    def quarter(values):
        return lax.dynamic_slice_in_dim(values, part * few, few)

    def own_group(values):
        return lax.dynamic_slice_in_dim(values, start_row, tok_rows)

    places = own_group(seq_places(segments))
    own_seg = own_group(segments)
    halfway = ROPE // 2
    frequency = 10000.0 ** (-jnp.arange(halfway, dtype=jnp.float32) / halfway)
    angles = places.astype(jnp.float32)[:, None] * frequency[None, :]
    nothing = jnp.zeros((tok_rows, 128 - ROPE), jnp.float32)
    cosines, sines = jnp.cos(angles), jnp.sin(angles)
    cosines = jnp.concatenate([cosines, cosines, nothing], axis=1)
    sines = jnp.concatenate([sines, -sines, nothing], axis=1)
    hidden_few = quarter(hidden_in)

    (
        packed_all, cot_all, expanded, queries, normed_few, compressed, log_total, merged, residual, moe_in,
    ) = front_call(
        grid, hidden_in, cotangent, attn_gain, latent_gain, moe_gain, gate_values, expert_routes,
        cosines, sines, segments[None, :], own_seg[:, None],
        latent_weight, query_weight, expand_weight, output_weight, 0,
    )
    hidden_f = hidden_few.astype(jnp.float32)

    moe_all, grad_moe_in, out_rows, acts = experts_call(
        grid, moe_in, cot_all, packed_all, expert_gate, expert_up, expert_down,
        shared_gate, shared_up, shared_down, 2,
    )
    normed_later, _ = lax.optimization_barrier((normed_few, moe_in[:8]))
    normed_all = lax.all_gather(normed_later, ALL, axis=0, tiled=True)

    grad_moe_in, normed_all = lax.optimization_barrier((grad_moe_in, normed_all))
    _, pull_moe = jax.vjp(rms_scale, residual, moe_gain)
    grad_residual, grad_moe_gain = pull_moe(grad_moe_in)
    grad_residual = grad_residual + quarter(cotangent).astype(jnp.float32)
    grad_q, key_rows, expand_part, output_rows = attention_back_call(
        grid,
        low(grad_residual),
        output_weight,
        queries,
        expanded,
        packed_all,
        expand_weight,
        merged,
        log_total,
        segments[None, :],
        own_seg[:, None],
        cosines,
        sines,
        5,
    )
    grad_q_low = grad_q.reshape(tok_rows, -1, 256)[:, :, : NOPE + ROPE].reshape(tok_rows, -1)
    normed_rows = low(dot(grad_q_low, query_weight.T))

    moe_out, grad_keys, weight_rows, grad_normed, grad_q_all, expert_grads = gradients_call(
        grid, out_rows, key_rows, expand_part, normed_rows, grad_q_low, moe_all, cot_all, acts,
        expert_down.shape[1], shared_down.shape[0], 3,
    )
    output_rows, weight_rows = lax.optimization_barrier((output_rows, weight_rows))
    output_rows = lax.all_gather(output_rows, "expert", axis=0, tiled=True)
    grad_expert_gate, grad_expert_up, grad_expert_down = expert_grads[:3]
    grad_shared_gate, grad_shared_up, grad_shared_down = expert_grads[3:]
    layer_out = low(residual + moe_out)
    places_few = quarter(places)
    compressed_few = compressed[:, : LATENT + ROPE]
    _, pull_latent = jax.vjp(rms_scale, compressed_few[:, :LATENT], latent_gain)
    grad_plain_latent, grad_latent_gain = pull_latent(grad_keys[:, :LATENT])
    _, pull_krope = jax.vjp(partial(rotate, places=places_few), compressed_few[:, LATENT:])
    (grad_k_turned,) = pull_krope(grad_keys[:, LATENT : LATENT + ROPE])
    grad_comp_low = low(jnp.concatenate([grad_plain_latent, grad_k_turned], axis=-1))
    grad_normed = grad_normed + dot(grad_comp_low, latent_weight.T)
    _, pull_input = jax.vjp(rms_scale, hidden_f, attn_gain)
    grad_input_norm, grad_attn_gain = pull_input(grad_normed)
    gains = jnp.concatenate([grad_attn_gain, grad_latent_gain, grad_moe_gain])
    gains = jnp.pad(gains, (0, -gains.shape[0] % few)).reshape(few, -1)
    gains_high = low(gains)
    gains_low = low(gains - gains_high.astype(jnp.float32))
    spread = gains.shape[1]
    both = jnp.concatenate([layer_out, low(grad_residual + grad_input_norm)], axis=1)
    last, weight_rows, both = last_call(
        grid,
        pad_columns(jnp.concatenate([grad_comp_low, gains_high, gains_low], axis=1)),
        weight_rows,
        both,
        8,
    )
    grad_comp_all = last.reshape(total_rows, -1)[:, : LATENT + ROPE]
    gains = jnp.sum(last[:, :, LATENT + ROPE : LATENT + ROPE + 2 * spread].astype(jnp.float32), axis=0)
    gains = (gains[:, :spread] + gains[:, spread:]).reshape(-1)
    grad_latent_weight = dot(normed_all.T, grad_comp_all)
    grad_query_weight = dot(normed_all.T, grad_q_all)
    layer_out, grad_hidden = both[:, :model_width], both[:, model_width:].astype(jnp.float32)
    grad_output_weight = output_rows.astype(jnp.float32)
    grad_expand_weight = weight_rows.astype(jnp.float32)
    return (
        layer_out,
        grad_hidden,
        gains[:model_width],
        grad_query_weight,
        grad_latent_weight,
        gains[model_width : model_width + LATENT],
        grad_expand_weight,
        grad_output_weight,
        gains[model_width + LATENT : 2 * model_width + LATENT],
        grad_shared_gate,
        grad_shared_up,
        grad_shared_down,
        grad_expert_gate,
        grad_expert_up,
        grad_expert_down,
    )


def solution(mesh):
    grid = Grid(mesh.shape["expert"], mesh.shape["tensor"])
    placed = (
        P("expert", None),
        P(),
        P(None, "tensor"),
        P(),
        P(),
        P(None, "tensor"),
        P("tensor", None),
        P(),
        P(None, "tensor"),
        P(None, "tensor"),
        P("tensor", None),
        P("expert", None, "tensor"),
        P("expert", None, "tensor"),
        P("expert", "tensor", None),
        P("expert", None),
        P("expert", None),
        P(),
        P("expert", None),
    )
    return jax.shard_map(
        partial(shards, grid),
        mesh=mesh,
        in_specs=placed,
        out_specs=(
            P("expert", None),
            P("expert", None),
            P(),
            P(None, "tensor"),
            P(),
            P(),
            P(None, "tensor"),
            P("tensor", None),
            P(),
            P(None, "tensor"),
            P(None, "tensor"),
            P("tensor", None),
            P("expert", None, "tensor"),
            P("expert", None, "tensor"),
            P("expert", "tensor", None),
        ),
        check_vma=False,
    )
```

```python
import functools
import math
from functools import partial

import jax
import jax.numpy as jnp
from jax import lax
from jax.experimental import pallas as pl
from jax.experimental.pallas import tpu as pltpu
from jax.sharding import PartitionSpec as P

NOPE = 128
ROPE = 64
VDIM = 128
LATENT = 512
TOP = 6
EXP_DEV = 2
ALL = ("expert", "tensor")
MESH = pl.DeviceIdType.MESH

epsilon = 1e-06
masked_out = -1e30


class Grid:
    def __init__(self, expert, tensor):
        self.na = 4 if expert % 4 == 0 else 1
        self.nb = expert // self.na
        self.ny = tensor // 2
        self.size = expert * tensor

    def here(self):
        e, t = lax.axis_index("expert"), lax.axis_index("tensor")
        return (lax.div(e, self.nb), lax.rem(e, self.nb), lax.div(t, 2), lax.rem(t, 2))

    def device(self, a, b, y, c):
        return {"expert": a * self.nb + b, "tensor": y * 2 + c}

    def block(self, a, b, y, c):
        return ((a * self.nb + b) * self.ny + y) * 2 + c


def microseconds(time):
    return pl.CostEstimate(flops=time * 1000**3, bytes_accessed=0, transcendentals=0)


def wrap(i, n):
    return lax.rem(i, n)


def greet(grid):
    a, b, y, c = grid.here()
    barrier = pltpu.get_barrier_semaphore()
    others = (
        [grid.device(wrap(a + i, grid.na), b, y, c) for i in range(1, grid.na)]
        + [grid.device(a, wrap(b + i, grid.nb), y, c) for i in range(1, grid.nb)]
        + [grid.device(a, b, wrap(y + i, grid.ny), c) for i in range(1, grid.ny)]
        + [grid.device(a, b, y, 1 - c)]
    )
    for other in others:
        pl.semaphore_signal(barrier, inc=1, device_id=other, device_id_type=MESH)
    pl.semaphore_wait(barrier, len(others))


def gather_kernel(
    grid, x_ref, out_ref, own_sem, send_sem, recv_sem, core_send, core_recv, extra=()
):
    na, nb, ny = grid.na, grid.nb, grid.ny
    a, b, y, c = grid.here()
    half = x_ref.shape[0] // 2
    greet(grid)
    waits = []

    def dst(bb, yy, cc, aa, h):
        return out_ref.at[grid.block(aa, bb, yy, cc), pl.ds(h * half, half)]

    def slot(bb, yy, aa, h):
        return ((bb * ny + yy) * na + aa) * 2 + h

    def push(src, bb, yy, aa, h, where, kind):
        copy = pltpu.make_async_remote_copy(
            src_ref=src,
            dst_ref=dst(bb, yy, c, aa, h),
            send_sem=core_send.at[slot(bb, yy, aa, h)] if kind == "c" else send_sem.at[len(waits)],
            recv_sem=(core_recv if kind == "c" else recv_sem).at[slot(bb, yy, aa, h)],
            device_id=where,
            device_id_type=MESH,
        )
        copy.start()
        if kind != "c":
            waits.append(copy)
        else:
            core_waits.append(copy)

    core_waits = []

    def onward(src, bb, yy, aa, h, dims):
        for d in dims:
            if d == "a":
                for i in range(1, na):
                    push(src, bb, yy, aa, h, grid.device(wrap(a + i, na), b, y, c), d)
            if d == "b":
                for i in range(1, nb):
                    push(src, bb, yy, aa, h, grid.device(a, wrap(b + i, nb), y, c), d)
            if d == "y":
                for i in range(1, ny):
                    push(src, bb, yy, aa, h, grid.device(a, b, wrap(y + i, ny), c), d)
        push(src, bb, yy, aa, h, grid.device(a, b, y, 1 - c), "c")

    def landed(bb, yy, cc, aa, h, sem):
        ref = dst(bb, yy, cc, aa, h)
        pltpu.make_async_copy(ref, ref, sem.at[slot(bb, yy, aa, h)]).wait()
        return ref

    own = pltpu.make_async_copy(x_ref, out_ref.at[grid.block(a, b, y, c)], own_sem)
    own.start()
    orders = (("b", "y"), ("y", "b"))
    for h in range(2):
        onward(x_ref.at[pl.ds(h * half, half)], b, y, a, h, ("a",) + orders[h])
    for one in extra:
        one.start()
    for i in range(1, na):
        aa = wrap(a + na - i, na)
        for h in range(2):
            onward(landed(b, y, c, aa, h, recv_sem), b, y, aa, h, orders[h])
    for i in range(na):
        aa = wrap(a + na - i, na)
        for h in range(2):
            n1 = (nb, ny)[h]
            for j in range(1, n1):
                bb, yy = (wrap(b + nb - j, nb), y) if h == 0 else (b, wrap(y + ny - j, ny))
                onward(landed(bb, yy, c, aa, h, recv_sem), bb, yy, aa, h, orders[h][1:])
    for i in range(na):
        aa = wrap(a + na - i, na)
        for h in range(2):
            for j in range(nb):
                for k in range(1, ny):
                    if h == 0:
                        bb, yy = wrap(b + nb - j, nb), wrap(y + ny - k, ny)
                        onward(landed(bb, yy, c, aa, h, recv_sem), bb, yy, aa, h, ())
            for j in range(ny):
                for k in range(1, nb):
                    if h == 1:
                        bb, yy = wrap(b + nb - k, nb), wrap(y + ny - j, ny)
                        onward(landed(bb, yy, c, aa, h, recv_sem), bb, yy, aa, h, ())
    for i in range(1, na):
        for one in extra:
            one.middle(i)
    for j in range(nb):
        for k in range(ny):
            for i in range(na):
                for h in range(2):
                    landed(wrap(b + nb - j, nb), wrap(y + ny - k, ny), 1 - c, wrap(a + na - i, na), h, core_recv)
    own.wait()
    for copy in waits + core_waits:
        copy.wait_send()
    for one in extra:
        one.last()


def gather_sends(grid):
    na, nb, ny = grid.na, grid.nb, grid.ny
    return 2 * (na - 1 + na * (nb - 1) + na * (ny - 1) + na * (nb - 1) * (ny - 1))


def gather_all(grid, x, collective_id):
    r, n = x.shape
    blocks = grid.na * grid.nb * grid.ny
    return pl.pallas_call(
        functools.partial(gather_kernel, grid),
        out_shape=jax.ShapeDtypeStruct((grid.size, r, n), x.dtype),
        in_specs=[pl.BlockSpec(memory_space=pl.ANY)],
        out_specs=pl.BlockSpec(memory_space=pl.ANY),
        scratch_shapes=[
            pltpu.SemaphoreType.DMA,
            pltpu.SemaphoreType.DMA((gather_sends(grid),)),
            pltpu.SemaphoreType.DMA((2 * blocks,)),
            pltpu.SemaphoreType.DMA((2 * blocks,)),
            pltpu.SemaphoreType.DMA((2 * blocks,)),
        ],
        compiler_params=pltpu.CompilerParams(collective_id=collective_id, has_side_effects=True),
    )(x)


def scatter_kernel(grid, pieces, p_ref, out_ref, acc, core_in, d1_in0, d1_in1, d2_in0, d2_in1, a_in,
                   load_sem, core_s, core_r, s10, r10, s11, r11, s20, r20, s21, r21, sa, ra):
    na, nb, ny = grid.na, grid.nb, grid.ny
    a, b, y, c = grid.here()
    half = p_ref.shape[4] // 2
    width = p_ref.shape[5] // pieces
    greet(grid)
    pending = []

    def send(src, dst, ss, rs, where):
        copy = pltpu.make_async_remote_copy(src_ref=src, dst_ref=dst, send_sem=ss, recv_sem=rs, device_id=where, device_id_type=MESH)
        copy.start()
        pending.append(copy)

    def await_in(ref, sem):
        pltpu.make_async_copy(ref, ref, sem).wait()

    def add(dst, src):
        dst[...] = (dst[...].astype(jnp.float32) + src[...].astype(jnp.float32)).astype(dst.dtype)

    def cols(p):
        return pl.ds(p * width, width)

    spots = [(j, k) for j in reversed(range(nb)) for k in reversed(range(ny))]
    loads = {}
    for p in range(pieces):
        for n, (j, k) in enumerate(spots):
            bb, yy = wrap(b + j, nb), wrap(y + k, ny)
            send(p_ref.at[:, bb, yy, 1 - c, :, cols(p)], core_in.at[p, j, k], core_s.at[p, n], core_r.at[p, n],
                 grid.device(a, b, y, 1 - c))
            load = pltpu.make_async_copy(p_ref.at[:, bb, yy, c, :, cols(p)], acc.at[p, j, k], load_sem.at[p, n])
            load.start()
            loads[p, n] = load
    rows = (pl.ds(0, half), pl.ds(half, half))
    for p in range(pieces):
        for n, (j, k) in enumerate(spots):
            loads[p, n].wait()
            await_in(core_in.at[p, j, k], core_r.at[p, n])
            for i in range(na):
                add(acc.at[p, j, k, i], core_in.at[p, j, k, i])
            if k:
                send(acc.at[p, j, k, :, rows[0]], d1_in0.at[p, j, k - 1], s10.at[p, j, k - 1], r10.at[p, j, k - 1],
                     grid.device(a, b, wrap(y + k, ny), c))
            if j:
                send(acc.at[p, j, k, :, rows[1]], d1_in1.at[p, k, j - 1], s11.at[p, k, j - 1], r11.at[p, k, j - 1],
                     grid.device(a, wrap(b + j, nb), y, c))
    for p in range(pieces):
        for j in reversed(range(nb)):
            for k in range(1, ny):
                await_in(d1_in0.at[p, j, k - 1], r10.at[p, j, k - 1])
                for i in range(na):
                    add(acc.at[p, j, 0, i, rows[0]], d1_in0.at[p, j, k - 1, i])
            if j:
                send(acc.at[p, j, 0, :, rows[0]], d2_in0.at[p, j - 1], s20.at[p, j - 1], r20.at[p, j - 1],
                     grid.device(a, wrap(b + j, nb), y, c))
        for k in reversed(range(ny)):
            for j in range(1, nb):
                await_in(d1_in1.at[p, k, j - 1], r11.at[p, k, j - 1])
                for i in range(na):
                    add(acc.at[p, 0, k, i, rows[1]], d1_in1.at[p, k, j - 1, i])
            if k:
                send(acc.at[p, 0, k, :, rows[1]], d2_in1.at[p, k - 1], s21.at[p, k - 1], r21.at[p, k - 1],
                     grid.device(a, b, wrap(y + k, ny), c))
    for p in range(pieces):
        for j in range(1, nb):
            await_in(d2_in0.at[p, j - 1], r20.at[p, j - 1])
            for i in range(na):
                add(acc.at[p, 0, 0, i, rows[0]], d2_in0.at[p, j - 1, i])
        for k in range(1, ny):
            await_in(d2_in1.at[p, k - 1], r21.at[p, k - 1])
            for i in range(na):
                add(acc.at[p, 0, 0, i, rows[1]], d2_in1.at[p, k - 1, i])
        for i in range(1, na):
            aa = wrap(a + i, na)
            send(acc.at[p, 0, 0, aa], a_in.at[p, i - 1], sa.at[p, i - 1], ra.at[p, i - 1], grid.device(aa, b, y, c))
    for p in range(pieces):
        total = acc[p, 0, 0, a].astype(jnp.float32)
        for i in range(1, na):
            await_in(a_in.at[p, i - 1], ra.at[p, i - 1])
            total = total + a_in[p, i - 1].astype(jnp.float32)
        out_ref[:, cols(p)] = total.astype(out_ref.dtype)
    for copy in pending:
        copy.wait_send()


def scatter_all(grid, p, dtype, collective_id, pieces=2):
    r, n = p.shape[0] // grid.size, p.shape[1]
    na, nb, ny = grid.na, grid.nb, grid.ny
    half, width = r // 2, n // pieces
    sems = lambda *s: pltpu.SemaphoreType.DMA(s)
    vm = lambda *s: pltpu.VMEM(s, jnp.bfloat16)
    return pl.pallas_call(
        functools.partial(scatter_kernel, grid, pieces),
        out_shape=jax.ShapeDtypeStruct((r, n), dtype),
        in_specs=[pl.BlockSpec(memory_space=pl.ANY)],
        out_specs=pl.BlockSpec(memory_space=pltpu.VMEM),
        scratch_shapes=[
            vm(pieces, nb, ny, na, r, width),
            vm(pieces, nb, ny, na, r, width),
            vm(pieces, nb, ny - 1, na, half, width),
            vm(pieces, ny, nb - 1, na, half, width),
            vm(pieces, nb - 1, na, half, width),
            vm(pieces, ny - 1, na, half, width),
            vm(pieces, na - 1, r, width),
            sems(pieces, nb * ny), sems(pieces, nb * ny), sems(pieces, nb * ny),
            sems(pieces, nb, ny - 1), sems(pieces, nb, ny - 1),
            sems(pieces, ny, nb - 1), sems(pieces, ny, nb - 1),
            sems(pieces, nb - 1), sems(pieces, nb - 1),
            sems(pieces, ny - 1), sems(pieces, ny - 1),
            sems(pieces, na - 1), sems(pieces, na - 1),
        ],
        compiler_params=pltpu.CompilerParams(collective_id=collective_id, has_side_effects=True, vmem_limit_bytes=40 << 20),
    )(p.reshape(na, nb, ny, 2, r, n))


def greet_tensor(grid):
    a, b, y, c = grid.here()
    barrier = pltpu.get_barrier_semaphore()
    others = [grid.device(a, b, wrap(y + i, grid.ny), c) for i in range(1, grid.ny)]
    others.append(grid.device(a, b, y, 1 - c))
    for other in others:
        pl.semaphore_signal(barrier, inc=1, device_id=other, device_id_type=MESH)
    pl.semaphore_wait(barrier, len(others))


def tensor_scatter_kernel(grid, p_ref, out_ref, acc, core_in, y_in, core_s, core_r, ys, yr):
    ny = grid.ny
    a, b, y, c = grid.here()
    greet_tensor(grid)
    pending = []
    for k in reversed(range(ny)):
        copy = pltpu.make_async_remote_copy(
            src_ref=p_ref.at[wrap(y + k, ny), 1 - c], dst_ref=core_in.at[k], send_sem=core_s.at[k], recv_sem=core_r.at[k],
            device_id=grid.device(a, b, y, 1 - c), device_id_type=MESH,
        )
        copy.start()
        pending.append(copy)
    for k in reversed(range(ny)):
        pltpu.make_async_copy(core_in.at[k], core_in.at[k], core_r.at[k]).wait()
        total = p_ref[wrap(y + k, ny), c].astype(jnp.float32) + core_in[k].astype(jnp.float32)
        if k:
            acc[k - 1] = total.astype(acc.dtype)
            copy = pltpu.make_async_remote_copy(
                src_ref=acc.at[k - 1], dst_ref=y_in.at[k - 1], send_sem=ys.at[k - 1], recv_sem=yr.at[k - 1],
                device_id=grid.device(a, b, wrap(y + k, ny), c), device_id_type=MESH,
            )
            copy.start()
            pending.append(copy)
        else:
            out_ref[...] = total
    for k in range(1, ny):
        pltpu.make_async_copy(y_in.at[k - 1], y_in.at[k - 1], yr.at[k - 1]).wait()
        out_ref[...] += y_in[k - 1].astype(jnp.float32)
    for copy in pending:
        copy.wait_send()


def tensor_scatter(grid, p, collective_id):
    ny = grid.ny
    r, n = p.shape[0] // (2 * ny), p.shape[1]
    return pl.pallas_call(
        functools.partial(tensor_scatter_kernel, grid),
        out_shape=jax.ShapeDtypeStruct((r, n), jnp.float32),
        in_specs=[pl.BlockSpec(memory_space=pltpu.VMEM)],
        out_specs=pl.BlockSpec(memory_space=pltpu.VMEM),
        scratch_shapes=[
            pltpu.VMEM((max(ny - 1, 1), r, n), p.dtype),
            pltpu.VMEM((ny, r, n), p.dtype),
            pltpu.VMEM((max(ny - 1, 1), r, n), p.dtype),
            pltpu.SemaphoreType.DMA((ny,)),
            pltpu.SemaphoreType.DMA((ny,)),
            pltpu.SemaphoreType.DMA((max(ny - 1, 1),)),
            pltpu.SemaphoreType.DMA((max(ny - 1, 1),)),
        ],
        compiler_params=pltpu.CompilerParams(
            collective_id=collective_id, has_side_effects=True, vmem_limit_bytes=16 << 20
        ),
    )(p.reshape(ny, 2, r, n))


def tensor_gather_kernel(grid, x_ref, out_ref, own_sem, ys, yr, core_s, core_r):
    ny = grid.ny
    a, b, y, c = grid.here()
    greet_tensor(grid)
    own = pltpu.make_async_copy(x_ref, out_ref.at[y, c], own_sem)
    own.start()
    pending = []

    def push(src, spot, ss, rs, where):
        copy = pltpu.make_async_remote_copy(
            src_ref=src, dst_ref=out_ref.at[spot, c], send_sem=ss, recv_sem=rs, device_id=where, device_id_type=MESH
        )
        copy.start()
        pending.append(copy)

    for k in range(1, ny):
        push(x_ref, y, ys.at[k], yr.at[k], grid.device(a, b, wrap(y + k, ny), c))
    push(x_ref, y, core_s.at[0], core_r.at[0], grid.device(a, b, y, 1 - c))
    for k in range(1, ny):
        spot = wrap(y + ny - k, ny)
        ref = out_ref.at[spot, c]
        pltpu.make_async_copy(ref, ref, yr.at[k]).wait()
        push(ref, spot, core_s.at[k], core_r.at[k], grid.device(a, b, y, 1 - c))
    for k in range(ny):
        ref = out_ref.at[wrap(y + ny - k, ny), 1 - c]
        pltpu.make_async_copy(ref, ref, core_r.at[k]).wait()
    own.wait()
    for copy in pending:
        copy.wait_send()


def tensor_gather(grid, x, collective_id):
    ny = grid.ny
    r, n = x.shape
    out = pl.pallas_call(
        functools.partial(tensor_gather_kernel, grid),
        out_shape=jax.ShapeDtypeStruct((ny, 2, r, n), x.dtype),
        in_specs=[pl.BlockSpec(memory_space=pltpu.VMEM)],
        out_specs=pl.BlockSpec(memory_space=pltpu.VMEM),
        scratch_shapes=[pltpu.SemaphoreType.DMA] + [pltpu.SemaphoreType.DMA((ny,))] * 4,
        compiler_params=pltpu.CompilerParams(
            collective_id=collective_id, has_side_effects=True, vmem_limit_bytes=16 << 20
        ),
    )(x)
    return out.reshape(2 * ny * r, n)


class TensorReduce:
    count = 8

    @staticmethod
    def scratch(grid, r, width):
        ny = grid.ny
        sems = lambda *s: pltpu.SemaphoreType.DMA(s)
        vm = lambda *s: pltpu.VMEM(s, jnp.bfloat16)
        return [
            vm(ny, r, width), vm(ny, r, width), vm(ny - 1, r, width),
            sems(ny), sems(ny), sems(ny), sems(ny - 1), sems(ny - 1),
        ]

    def __init__(self, grid, source, out, scratch):
        self.grid, self.source, self.out = grid, source, out
        (
            self.acc, self.core_in, self.y_in, self.load_sem, self.core_s, self.core_r, self.ys, self.yr,
        ) = scratch
        self.spot = grid.here()

    def load(self, k):
        g, (a, b, y, c) = self.grid, self.spot
        return pltpu.make_async_copy(self.source.at[wrap(y + k, g.ny), c], self.acc.at[k], self.load_sem.at[k])

    def core_copy(self, k):
        g, (a, b, y, c) = self.grid, self.spot
        return pltpu.make_async_remote_copy(
            src_ref=self.source.at[wrap(y + k, g.ny), 1 - c], dst_ref=self.core_in.at[k],
            send_sem=self.core_s.at[k], recv_sem=self.core_r.at[k],
            device_id=g.device(a, b, y, 1 - c), device_id_type=MESH,
        )

    def y_copy(self, k):
        g, (a, b, y, c) = self.grid, self.spot
        return pltpu.make_async_remote_copy(
            src_ref=self.acc.at[k], dst_ref=self.y_in.at[k - 1], send_sem=self.ys.at[k - 1],
            recv_sem=self.yr.at[k - 1], device_id=g.device(a, b, wrap(y + k, g.ny), c), device_id_type=MESH,
        )

    def start(self):
        for k in reversed(range(self.grid.ny)):
            self.core_copy(k).start()
            self.load(k).start()

    def middle(self):
        f32 = jnp.float32
        for k in reversed(range(self.grid.ny)):
            self.load(k).wait()
            ref = self.core_in.at[k]
            pltpu.make_async_copy(ref, ref, self.core_r.at[k]).wait()
            total = self.acc[k].astype(f32) + self.core_in[k].astype(f32)
            self.acc[k] = total.astype(self.acc.dtype)
            if k:
                self.y_copy(k).start()

    def last(self):
        total = self.acc[0].astype(jnp.float32)
        for k in range(1, self.grid.ny):
            ref = self.y_in.at[k - 1]
            pltpu.make_async_copy(ref, ref, self.yr.at[k - 1]).wait()
            total = total + self.y_in[k - 1].astype(jnp.float32)
        self.out[...] = total

    def finish(self):
        for k in range(self.grid.ny):
            self.core_copy(k).wait_send()
            if k:
                self.y_copy(k).wait_send()


class TensorGather:
    count = 5

    @staticmethod
    def scratch(grid):
        return [pltpu.SemaphoreType.DMA((1,))] + [pltpu.SemaphoreType.DMA((grid.ny,))] * 4

    def __init__(self, grid, x, out, scratch):
        self.grid, self.x, self.out = grid, x, out
        self.own_sem, self.ys, self.yr, self.core_s, self.core_r = scratch
        self.spot = grid.here()

    def own(self):
        return pltpu.make_async_copy(self.x, self.out.at[self.spot[2], self.spot[3]], self.own_sem.at[0])

    def y_copy(self, k):
        g, (a, b, y, c) = self.grid, self.spot
        return pltpu.make_async_remote_copy(
            src_ref=self.x, dst_ref=self.out.at[y, c], send_sem=self.ys.at[k], recv_sem=self.yr.at[k],
            device_id=g.device(a, b, wrap(y + k, g.ny), c), device_id_type=MESH,
        )

    def core_copy(self, k):
        g, (a, b, y, c) = self.grid, self.spot
        spot = wrap(y + g.ny - k, g.ny)
        return pltpu.make_async_remote_copy(
            src_ref=self.x if k == 0 else self.out.at[spot, c], dst_ref=self.out.at[spot, c],
            send_sem=self.core_s.at[k], recv_sem=self.core_r.at[k],
            device_id=g.device(a, b, y, 1 - c), device_id_type=MESH,
        )

    def start(self):
        self.own().start()
        for k in range(1, self.grid.ny):
            self.y_copy(k).start()
        self.core_copy(0).start()

    def middle(self, i):
        if i == 1:
            for k in range(1, self.grid.ny):
                pltpu.make_async_copy(self.x, self.x, self.yr.at[k]).wait()
                self.core_copy(k).start()

    def last(self):
        self.own().wait()
        for k in range(self.grid.ny):
            pltpu.make_async_copy(self.x, self.x, self.core_r.at[k]).wait()
        for k in range(self.grid.ny):
            if k:
                self.y_copy(k).wait_send()
            self.core_copy(k).wait_send()


class PlaneReduce:
    count = 9

    @staticmethod
    def scratch(grid, r, width):
        na, nb = grid.na, grid.nb
        sems = lambda *s: pltpu.SemaphoreType.DMA(s)
        vm = lambda *s: pltpu.VMEM(s, jnp.bfloat16)
        return [
            vm(na, r, width), vm(nb - 1, na, r, width), vm(na - 1, r, width),
            sems(1), sems(nb - 1), sems(nb - 1), sems(na - 1), sems(na - 1), sems(1),
        ]

    def __init__(self, grid, source, out, scratch):
        self.grid, self.source, self.out = grid, source, out
        self.acc, self.b_in, self.a_in, self.load_sem, self.sb, self.rb, self.sa, self.ra, _ = scratch
        self.spot = grid.here()

    def load(self):
        return pltpu.make_async_copy(self.source.at[:, self.spot[1]], self.acc, self.load_sem.at[0])

    def copy_b(self, i):
        g, (a, b, y, c) = self.grid, self.spot
        return pltpu.make_async_remote_copy(
            src_ref=self.source.at[:, wrap(b + i, g.nb)], dst_ref=self.b_in.at[i - 1],
            send_sem=self.sb.at[i - 1], recv_sem=self.rb.at[i - 1],
            device_id=g.device(a, wrap(b + i, g.nb), y, c), device_id_type=MESH,
        )

    def copy_a(self, i):
        g, (a, b, y, c) = self.grid, self.spot
        return pltpu.make_async_remote_copy(
            src_ref=self.acc.at[wrap(a + i, g.na)], dst_ref=self.a_in.at[i - 1],
            send_sem=self.sa.at[i - 1], recv_sem=self.ra.at[i - 1],
            device_id=g.device(wrap(a + i, g.na), b, y, c), device_id_type=MESH,
        )

    def start(self):
        for i in range(1, self.grid.nb):
            self.copy_b(i).start()
        self.load().start()

    def middle(self):
        f32 = jnp.float32
        self.load().wait()
        for i in range(1, self.grid.nb):
            ref = self.b_in.at[i - 1]
            pltpu.make_async_copy(ref, ref, self.rb.at[i - 1]).wait()

            def one(m, carry):
                self.acc[m] = (self.acc[m].astype(f32) + ref[m].astype(f32)).astype(self.acc.dtype)
                return carry

            lax.fori_loop(0, self.grid.na, one, 0)
        for i in range(1, self.grid.na):
            self.copy_a(i).start()

    def last(self):
        total = self.acc[self.spot[0]].astype(jnp.float32)
        for i in range(1, self.grid.na):
            ref = self.a_in.at[i - 1]
            pltpu.make_async_copy(ref, ref, self.ra.at[i - 1]).wait()
            total = total + self.a_in[i - 1].astype(jnp.float32)
        self.out[...] = total.astype(self.out.dtype)

    def finish(self):
        for i in range(1, self.grid.nb):
            self.copy_b(i).wait_send()
        for i in range(1, self.grid.na):
            self.copy_a(i).wait_send()


class PlaneGather:
    count = 5

    @staticmethod
    def scratch(grid):
        na, nb = grid.na, grid.nb
        sems = lambda *s: pltpu.SemaphoreType.DMA(s)
        return [sems(1), sems(na - 1), sems(na, nb - 1), sems(na), sems(na, nb - 1)]

    def __init__(self, grid, x, out, scratch):
        self.grid, self.x, self.out = grid, x, out
        self.own_sem, self.sa, self.sb, self.ra, self.rb = scratch
        self.spot = grid.here()

    def own(self):
        return pltpu.make_async_copy(self.x, self.out.at[self.spot[0], self.spot[1]], self.own_sem.at[0])

    def copy_a(self, i):
        g, (a, b, y, c) = self.grid, self.spot
        return pltpu.make_async_remote_copy(
            src_ref=self.x, dst_ref=self.out.at[a, b], send_sem=self.sa.at[i - 1], recv_sem=self.ra.at[i],
            device_id=g.device(wrap(a + i, g.na), b, y, c), device_id_type=MESH,
        )

    def copy_b(self, i, k):
        g, (a, b, y, c) = self.grid, self.spot
        aa = wrap(a + g.na - i, g.na)
        return pltpu.make_async_remote_copy(
            src_ref=self.x if i == 0 else self.out.at[aa, b], dst_ref=self.out.at[aa, b],
            send_sem=self.sb.at[i, k - 1], recv_sem=self.rb.at[i, k - 1],
            device_id=g.device(a, wrap(b + k, g.nb), y, c), device_id_type=MESH,
        )

    def start(self):
        self.own().start()
        for i in range(1, self.grid.na):
            self.copy_a(i).start()
        for k in range(1, self.grid.nb):
            self.copy_b(0, k).start()

    def middle(self, i):
        ref = self.out.at[wrap(self.spot[0] + self.grid.na - i, self.grid.na), self.spot[1]]
        pltpu.make_async_copy(ref, ref, self.ra.at[i]).wait()
        for k in range(1, self.grid.nb):
            self.copy_b(i, k).start()

    def last(self):
        self.own().wait()
        ref = self.x
        for i in range(self.grid.na):
            for k in range(1, self.grid.nb):
                pltpu.make_async_copy(ref, ref, self.rb.at[i, k - 1]).wait()
        for i in range(1, self.grid.na):
            self.copy_a(i).wait_send()
        for i in range(self.grid.na):
            for k in range(1, self.grid.nb):
                self.copy_b(i, k).wait_send()


def last_kernel(grid, x_ref, w_ref, t_ref, out_ref, w_out, t_out, own_sem, ss, rs, cs, cr, *scratch):
    gathers = [
        TensorGather(grid, t_ref, t_out, scratch[: TensorGather.count]),
        PlaneGather(grid, w_ref, w_out, scratch[TensorGather.count :]),
    ]
    gather_kernel(grid, x_ref, out_ref, own_sem, ss, rs, cs, cr, gathers)


def last_call(grid, x, w, t, collective_id):
    r, n = x.shape
    blocks = grid.na * grid.nb * grid.ny
    any_space = pl.BlockSpec(memory_space=pl.ANY)
    outs = pl.pallas_call(
        functools.partial(last_kernel, grid),
        out_shape=[
            jax.ShapeDtypeStruct((grid.size, r, n), x.dtype),
            jax.ShapeDtypeStruct((grid.na, grid.nb) + w.shape, w.dtype),
            jax.ShapeDtypeStruct((grid.ny, 2) + t.shape, t.dtype),
        ],
        in_specs=[any_space] * 3,
        out_specs=[any_space] * 3,
        scratch_shapes=[
            pltpu.SemaphoreType.DMA,
            pltpu.SemaphoreType.DMA((gather_sends(grid),)),
            pltpu.SemaphoreType.DMA((2 * blocks,)),
            pltpu.SemaphoreType.DMA((2 * blocks,)),
            pltpu.SemaphoreType.DMA((2 * blocks,)),
        ]
        + TensorGather.scratch(grid)
        + PlaneGather.scratch(grid),
        cost_estimate=microseconds(36),
        compiler_params=pltpu.CompilerParams(collective_id=collective_id, has_side_effects=True),
    )(x, w, t)
    whole = lambda v: v.reshape(-1, v.shape[-1])
    return outs[0], whole(outs[1]), whole(outs[2])


def dot_rows(left_side, right_side):
    return lax.dot_general(
        left_side, right_side, (((1,), (1,)), ((), ())), preferred_element_type=jnp.float32
    )


def dot_plain(left_side, right_side):
    return jnp.dot(left_side, right_side, preferred_element_type=jnp.float32)


def round_up(value, unit):
    return -(-value // unit) * unit


def experts_kernel(
    grid,
    pieces,
    x_ref,
    dz_ref,
    gate_ref,
    eg_hbm,
    eu_hbm,
    ed_hbm,
    sg_hbm,
    su_hbm,
    sd_hbm,
    all_ref,
    grad_ref,
    y_ref,
    acts_ref,
    gates,
    egu,
    ed,
    sgu,
    sd,
    dabuf,
    xbuf,
    dzbuf,
    gated,
    dcat,
    act,
    dsh,
    ybuf,
    dx,
    dx_out,
    core_in,
    d1_in0,
    d1_in1,
    d2_in0,
    d2_in1,
    a_in,
    gate_sem,
    weight_sem,
    own_sem,
    x_sem,
    dz_sem,
    out_sem,
    fill_sem,
    send_sem,
    recv_sem,
    share_send,
    share_recv,
    core_s,
    core_r,
    s10,
    r10,
    s11,
    r11,
    s20,
    r20,
    s21,
    r21,
    sa,
    ra,
):
    na, nb, ny = grid.na, grid.nb, grid.ny
    a, b, y, c = grid.here()
    r, n = x_ref.shape
    half, width, rows = r // 2, n // pieces, na * r
    pairs = nb * ny
    steps = 2 * pairs
    device = a * nb + b
    f, fs = ed_hbm.shape[1], sd_hbm.shape[0]
    wide, wide_s = egu.shape[0] // (2 * EXP_DEV), sd.shape[0]
    ef = EXP_DEV * wide
    columns = columns_of(ef, wide_s)
    f32, bf = jnp.float32, jnp.bfloat16
    fills = [(ed_hbm.at[e], ed, e * wide, f, wide) for e in range(EXP_DEV)]
    fills += [(sd_hbm, sd, 0, fs, wide_s)]
    fills += [(eg_hbm.at[e], egu, e * wide, f, wide) for e in range(EXP_DEV)]
    fills += [(eu_hbm.at[e], egu, ef + e * wide, f, wide) for e in range(EXP_DEV)]
    fills += [(sg_hbm, sgu, 0, fs, wide_s), (su_hbm, sgu, wide_s, fs, wide_s)]
    loads = [
        pltpu.make_async_copy(src, dst.at[pl.ds(at, real)], weight_sem.at[i])
        for i, (src, dst, at, real, _) in enumerate(fills)
    ]
    for load in loads:
        load.start()
    gate_load = pltpu.make_async_copy(gate_ref.at[:, :, :, :, :, pl.ds(LATENT, 128)], gates, gate_sem)
    gate_load.start()
    greet(grid)

    counts = [0]

    def place(bb, yy, cc, aa, h):
        return all_ref.at[aa, bb, yy, cc, pl.ds(h * half, half)]

    def slot(bb, yy, aa, h):
        return ((bb * ny + yy) * na + aa) * 2 + h

    def push(src, bb, yy, aa, h, where, send, recv):
        pltpu.make_async_remote_copy(
            src_ref=src,
            dst_ref=place(bb, yy, c, aa, h),
            send_sem=send,
            recv_sem=recv.at[slot(bb, yy, aa, h)],
            device_id=where,
            device_id_type=MESH,
        ).start()

    def line(i):
        if na != 4:
            return wrap(a + i, na)
        if i == 0:
            return a
        if i == 1:
            return a + 1 - 2 * lax.rem(a, 2)
        return (i - lax.div(a, 2)) if i == 2 else (3 - 3 * lax.div(a, 2))

    def onward(src, bb, yy, aa, h, dims):
        for d in dims:
            size = {"a": na, "b": nb, "y": ny}[d]
            for i in range(1, size):
                where = {
                    "a": lambda: grid.device(line(i), b, y, c),
                    "b": lambda: grid.device(a, wrap(b + i, nb), y, c),
                    "y": lambda: grid.device(a, b, wrap(y + i, ny), c),
                }[d]()
                push(src, bb, yy, aa, h, where, send_sem.at[counts[0]], recv_sem)
                counts[0] += 1
        push(
            src, bb, yy, aa, h, grid.device(a, b, y, 1 - c), share_send.at[slot(bb, yy, aa, h)], share_recv
        )

    def landed(bb, yy, cc, aa, h, sem):
        ref = place(bb, yy, cc, aa, h)
        pltpu.make_async_copy(ref, ref, sem.at[slot(bb, yy, aa, h)]).wait()
        return ref

    orders = (("b", "y"), ("y", "b"))

    def relay(j, k, i, h, dims):
        bb, yy, aa = wrap(b + j, nb), wrap(y + k, ny), line(i)
        onward(landed(bb, yy, c, aa, h, recv_sem), bb, yy, aa, h, dims)

    own = pltpu.make_async_copy(x_ref, all_ref.at[a, b, y, c], own_sem)
    own.start()
    for h in range(2):
        onward(x_ref.at[pl.ds(h * half, half)], b, y, a, h, ("a",) + orders[h])

    hooks = {}
    early = []
    for i in range(na):
        if i:
            early += [(0, 0, i, h, orders[h]) for h in range(2)]
        if i:
            early += [(j, 0, i - 1, 0, orders[0][1:]) for j in range(1, nb)]
            early += [(0, k, i - 1, 1, orders[1][1:]) for k in range(1, ny)]
    early += [(j, 0, na - 1, 0, orders[0][1:]) for j in range(1, nb)]
    early += [(0, k, na - 1, 1, orders[1][1:]) for k in range(1, ny)]
    for m, event in enumerate(early):
        place_at = 1 + m * (2 * steps - 1) // len(early)
        hooks.setdefault(("early", place_at // 2, place_at % 2), []).append(event)
    for pair in range(1, pairs):
        j, k = pair // ny, pair % ny
        late = [(j, k, i, h, ()) for i in range(na) for h in range(2) if (k if h == 0 else j)]
        for m, event in enumerate(late):
            hooks.setdefault(("main", pair, m * 2 // len(late)), []).append(event)

    def hook(stage, step, spot):
        for (when_stage, when, when_spot), events in hooks.items():
            if when_stage == stage and when_spot == spot:

                @pl.when(step == when)
                def _():
                    for event in events:
                        relay(*event)

    def spots(step):
        pair, l = lax.div(step, 2), 1 - lax.rem(step, 2)
        j, k = lax.div(pair, ny), lax.rem(pair, ny)
        return j, k, l, wrap(b + j, nb), wrap(y + k, ny), wrap(c + l, 2)

    def flat(value):
        return value.reshape(rows, value.shape[-1])

    def fold(value):
        return value.reshape(na, r, value.shape[-1])

    def dz_load(step):
        _, _, _, bb, yy, cc = spots(step)
        s = lax.rem(step, 2)
        return pltpu.make_async_copy(dz_ref.at[:, bb, yy, cc], dzbuf.at[s], dz_sem.at[s])

    dz_load(a * 0).start()
    for _, dst, at, real, padded in fills:
        if padded > real:
            dst[at + real : at + padded] = jnp.zeros((padded - real, n), bf)
    for load in loads[: EXP_DEV + 1]:
        load.wait()

    def early_body(step, carry):
        s = lax.rem(step, 2)

        @pl.when(step + 1 < steps)
        def _():
            dz_load(step + 1).start()

        dz_load(step).wait()
        dz = flat(dzbuf[s])
        dabuf[step, :, :ef] = dot_rows(dz, ed[...]).astype(bf)
        hook("early", step, 0)
        dabuf[step, :, ef:] = dot_rows(dz, sd[...]).astype(bf)
        hook("early", step, 1)
        return carry

    lax.fori_loop(0, steps, early_body, 0)
    for load in loads[EXP_DEV + 1 :]:
        load.wait()
    own.wait()
    gate_load.wait()

    def x_load(step):
        _, _, _, bb, yy, cc = spots(step)
        s = lax.rem(step, 2)
        return pltpu.make_async_copy(all_ref.at[:, bb, yy, cc], xbuf.at[s], x_sem.at[s])

    def await_shared(step):
        _, _, _, bb, yy, cc = spots(step)
        for i in range(na):
            for h in range(2):
                landed(bb, yy, cc, line(i), h, share_recv)

    def stores(step):
        _, _, _, bb, yy, cc = spots(step)
        s = lax.rem(step, 2)
        return [
            pltpu.make_async_copy(
                gated.at[s], acts_ref.at[:, bb, yy, cc, :, pl.ds(columns[2], ef)], out_sem.at[s, 0]
            ),
            pltpu.make_async_copy(
                dcat.at[s], acts_ref.at[:, bb, yy, cc, :, pl.ds(columns[0], 2 * ef)], out_sem.at[s, 1]
            ),
        ]

    def remote(src, dst, ss, rs, where):
        return pltpu.make_async_remote_copy(
            src_ref=src, dst_ref=dst, send_sem=ss, recv_sem=rs, device_id=where, device_id_type=MESH
        )

    def cols(p):
        return pl.ds(p * width, width)

    upper = (pl.ds(0, half), pl.ds(half, half))

    def send_core(pair):
        j, k = lax.div(pair, ny), lax.rem(pair, ny)
        return remote(
            dx_out.at[lax.rem(pair, 2)], core_in.at[j, k], core_s.at[lax.rem(pair, 2)],
            core_r.at[j, k], grid.device(a, b, y, 1 - c),
        )

    def send_10(p, j, k):
        return remote(
            dx.at[j, k, :, upper[0], cols(p)], d1_in0.at[p, j, k - 1], s10.at[p, j, k - 1],
            r10.at[p, j, k - 1], grid.device(a, b, wrap(y + k, ny), c),
        )

    def send_11(p, j, k):
        return remote(
            dx.at[j, k, :, upper[1], cols(p)], d1_in1.at[p, k, j - 1], s11.at[p, k, j - 1],
            r11.at[p, k, j - 1], grid.device(a, wrap(b + j, nb), y, c),
        )

    def await_in(ref, sem):
        pltpu.make_async_copy(ref, ref, sem).wait()

    def add(dst, src):
        dst[...] = (dst[...].astype(f32) + src[...].astype(f32)).astype(dst.dtype)

    def shared_front(step, x, s):
        g = dot_rows(x, sgu[:wide_s])
        u = dot_rows(x, sgu[wide_s:])
        d = dabuf[step, :, ef:].astype(f32)
        sig = 1.0 / (1.0 + jnp.exp(-g))
        swish = g * sig
        act[s] = fold((swish * u).astype(bf))
        dsh[s, :, :, :wide_s] = fold((d * u * (sig + swish * (1.0 - sig))).astype(bf))
        dsh[s, :, :, wide_s:] = fold((d * swish).astype(bf))

    def is_mine(bb, yy, cc):
        return lax.rem((bb * ny + yy) * 2 + cc, na * nb) == device

    chunk = min(n, 1024)

    def main_body(step, carry):
        j, k, l, bb, yy, cc = spots(step)
        s = lax.rem(step, 2)

        @pl.when(step >= 2)
        def _():
            for store in stores(step - 2):
                store.wait()

        x_load(step).wait()
        x = flat(xbuf[s])
        g = dot_rows(x, egu[:ef])
        u = dot_rows(x, egu[ef:])
        gate = flat(gates[:, bb, yy, cc]).astype(f32)
        lane = lax.broadcasted_iota(jnp.int32, gate.shape, 1) - (ROPE + EXP_DEV * device)
        experts_all = EXP_DEV * na * nb
        for e in range(EXP_DEV):
            at = pl.ds(e * wide, wide)
            hit = (lane == e) | (lane == e + experts_all)
            scale = jnp.sum(jnp.where(hit, gate, 0.0), axis=-1, keepdims=True)
            ge, ue = g[:, e * wide : (e + 1) * wide], u[:, e * wide : (e + 1) * wide]
            d = dabuf[step, :, at].astype(f32) * scale
            sig = 1.0 / (1.0 + jnp.exp(-ge))
            swish = ge * sig
            gated[s, :, :, at] = fold((scale * (swish * ue)).astype(bf))
            dcat[s, :, :, at] = fold((d * ue * (sig + swish * (1.0 - sig))).astype(bf))
            dcat[s, :, :, pl.ds(ef + e * wide, wide)] = fold((d * swish).astype(bf))
        hook("main", step, 0)
        mine = is_mine(bb, yy, cc)

        @pl.when(mine)
        def _():
            shared_front(step, x, 0)

        hook("main", step, 1)

        @pl.when((l == 0) & (step + 1 < steps))
        def _():
            await_shared(step + 1)

        @pl.when(step + 1 < steps)
        def _():
            x_load(step + 1).start()

        def column(target):
            for q in range(n // chunk):
                at = pl.ds(q * chunk, chunk)
                total = dot_plain(flat(dcat[s]), egu[:, at])
                target[:, :, at] = fold(total.astype(bf))

            @pl.when(mine)
            def _():
                for q in range(n // chunk):
                    at = pl.ds(q * chunk, chunk)
                    more = dot_plain(flat(dsh[0]), sgu[:, at])
                    target[:, :, at] = fold((flat(target[:, :, at]).astype(f32) + more).astype(bf))

        for store in stores(step):
            store.start()

        @pl.when(l == 1)
        def _():
            pair = lax.div(step, 2)

            @pl.when(pair >= 2)
            def _():
                send_core(pair - 2).wait_send()

            column(dx_out.at[lax.rem(pair, 2)])
            send_core(pair).start()

        @pl.when(l == 0)
        def _():
            column(dx.at[j, k])
            await_in(core_in.at[j, k], core_r.at[j, k])

            def one(i, carry):
                add(dx.at[j, k, i], core_in.at[j, k, i])
                return carry

            lax.fori_loop(0, na, one, 0)

            @pl.when(k > 0)
            def _():
                for p in range(pieces):
                    send_10(p, j, k).start()

            @pl.when(j > 0)
            def _():
                for p in range(pieces):
                    send_11(p, j, k).start()

        return carry

    await_shared(a * 0)
    x_load(a * 0).start()
    lax.fori_loop(0, steps, main_body, 0)
    for step in (steps - 2, steps - 1):
        for store in stores(a * 0 + step):
            store.wait()

    def send_20(p, j):
        return remote(
            dx.at[j, 0, :, upper[0], cols(p)], d2_in0.at[p, j - 1], s20.at[p, j - 1],
            r20.at[p, j - 1], grid.device(a, wrap(b + j, nb), y, c),
        )

    def send_21(p, k):
        return remote(
            dx.at[0, k, :, upper[1], cols(p)], d2_in1.at[p, k - 1], s21.at[p, k - 1],
            r21.at[p, k - 1], grid.device(a, b, wrap(y + k, ny), c),
        )

    def send_a(p, i):
        return remote(
            dx.at[0, 0, wrap(a + i, na), :, cols(p)], a_in.at[p, i - 1], sa.at[p, i - 1],
            ra.at[p, i - 1], grid.device(wrap(a + i, na), b, y, c),
        )

    def sum_first(p):
        for j in reversed(range(nb)):
            for k in range(1, ny):
                await_in(d1_in0.at[p, j, k - 1], r10.at[p, j, k - 1])
                for i in range(na):
                    add(dx.at[j, 0, i, upper[0], cols(p)], d1_in0.at[p, j, k - 1, i])
            if j:
                send_20(p, j).start()
        for k in reversed(range(ny)):
            for j in range(1, nb):
                await_in(d1_in1.at[p, k, j - 1], r11.at[p, k, j - 1])
                for i in range(na):
                    add(dx.at[0, k, i, upper[1], cols(p)], d1_in1.at[p, k, j - 1, i])
            if k:
                send_21(p, k).start()

    def sum_second(p):
        for j in range(1, nb):
            await_in(d2_in0.at[p, j - 1], r20.at[p, j - 1])
            for i in range(na):
                add(dx.at[0, 0, i, upper[0], cols(p)], d2_in0.at[p, j - 1, i])
        for k in range(1, ny):
            await_in(d2_in1.at[p, k - 1], r21.at[p, k - 1])
            for i in range(na):
                add(dx.at[0, 0, i, upper[1], cols(p)], d2_in1.at[p, k - 1, i])
        for i in range(1, na):
            send_a(p, i).start()

    def sum_last(p):
        total = dx[0, 0, a, :, cols(p)].astype(f32)
        for i in range(1, na):
            await_in(a_in.at[p, i - 1], ra.at[p, i - 1])
            total = total + a_in[p, i - 1].astype(f32)
        grad_ref[:, cols(p)] = total

    work = [(sum_first, p) for p in range(pieces)] + [(sum_second, p) for p in range(pieces)]
    turns = {}
    for m, item in enumerate(work):
        turns.setdefault(min(steps - 1, 1 + m * (steps - 1) // len(work)), []).append(item)

    def fill_loads(step):
        _, _, _, bb, yy, cc = spots(step)
        s = lax.rem(step, 2)
        return [
            pltpu.make_async_copy(all_ref.at[:, bb, yy, cc], xbuf.at[s], x_sem.at[s]),
            pltpu.make_async_copy(
                acts_ref.at[:, bb, yy, cc, :, pl.ds(columns[2], ef)], gated.at[s], fill_sem.at[s]
            ),
        ]

    def fill_stores(step):
        _, _, _, bb, yy, cc = spots(step)
        s = lax.rem(step, 2)
        pairs_of = [
            (act.at[s], acts_ref.at[:, bb, yy, cc, :, pl.ds(columns[3], wide_s)]),
            (dsh.at[s], acts_ref.at[:, bb, yy, cc, :, pl.ds(columns[1], 2 * wide_s)]),
            (ybuf.at[s], y_ref.at[:, bb, yy, cc]),
        ]
        return [
            pltpu.make_async_copy(src, dst, out_sem.at[s, i])
            for i, (src, dst) in enumerate(pairs_of)
        ]

    for load in fill_loads(a * 0):
        load.start()

    def fill_body(step, carry):
        j, k, l, bb, yy, cc = spots(step)
        s = lax.rem(step, 2)

        @pl.when(step + 1 < steps)
        def _():
            for load in fill_loads(step + 1):
                load.start()

        @pl.when(step >= 2)
        def _():
            for store in fill_stores(step - 2):
                store.wait()

        for load in fill_loads(step):
            load.wait()
        x = flat(xbuf[s])
        shared_front(step, x, s)
        for q in range(n // chunk):
            at = pl.ds(q * chunk, chunk)
            ybuf[s, :, :, at] = fold(dot_plain(flat(gated[s]), ed[:, at]).astype(bf))

        @pl.when(is_mine(bb, yy, cc))
        def _():
            for q in range(n // chunk):
                at = pl.ds(q * chunk, chunk)
                more = dot_plain(flat(act[s]), sd[:, at])
                ybuf[s, :, :, at] = fold((flat(ybuf[s, :, :, at]).astype(f32) + more).astype(bf))

        for store in fill_stores(step):
            store.start()
        for when, items in turns.items():

            @pl.when(step == when)
            def _():
                for item, p in items:
                    item(p)

        return carry

    lax.fori_loop(0, steps, fill_body, 0)
    for p in range(pieces):
        sum_last(p)

    for step in (steps - 2, steps - 1):
        for store in fill_stores(a * 0 + step):
            store.wait()
    some = place(b, y, c, a, 0)
    for i in range(counts[0]):
        pltpu.make_async_copy(some, some, send_sem.at[i]).wait()
    for i in range(2 * na * pairs):
        pltpu.make_async_copy(some, some, share_send.at[i]).wait()
    for pair in range(max(0, pairs - 2), pairs):
        send_core(a * 0 + pair).wait_send()
    for p in range(pieces):
        for j in range(nb):
            for k in range(ny):
                if k:
                    send_10(p, j, k).wait_send()
                if j:
                    send_11(p, j, k).wait_send()
        for j in range(1, nb):
            send_20(p, j).wait_send()
        for k in range(1, ny):
            send_21(p, k).wait_send()
        for i in range(1, na):
            send_a(p, i).wait_send()


def columns_of(ef, wide_s):
    return (0, 2 * ef, 2 * ef + 2 * wide_s, 3 * ef + 2 * wide_s, 3 * ef + 3 * wide_s)


def experts_call(
    grid, x, dz, gates, expert_gate, expert_up, expert_down, shared_gate, shared_up, shared_down,
    collective_id, pieces=2,
):
    r, n = x.shape
    na, nb, ny = grid.na, grid.nb, grid.ny
    f, fs = expert_down.shape[1], shared_down.shape[0]
    wide, wide_s = round_up(f, 128), round_up(fs, 128)
    ef = EXP_DEV * wide
    half, width, rows = r // 2, n // pieces, na * r
    steps = 2 * nb * ny
    lay = (na, nb, ny, 2, r)
    bf = jnp.bfloat16
    sems = lambda *s: pltpu.SemaphoreType.DMA(s)
    vm = lambda *s: pltpu.VMEM(s, bf)
    sends = 2 * (na - 1 + na * (nb - 1) + na * (ny - 1) + na * (nb - 1) * (ny - 1))
    any_space = pl.BlockSpec(memory_space=pl.ANY)
    in_vmem = pl.BlockSpec(memory_space=pltpu.VMEM)
    outs = pl.pallas_call(
        functools.partial(experts_kernel, grid, pieces),
        out_shape=[
            jax.ShapeDtypeStruct(lay + (n,), bf),
            jax.ShapeDtypeStruct((r, n), jnp.float32),
            jax.ShapeDtypeStruct(lay + (n,), bf),
            jax.ShapeDtypeStruct(lay + (columns_of(ef, wide_s)[-1],), bf),
        ],
        in_specs=[any_space] * 9,
        out_specs=[any_space, in_vmem] + [any_space] * 2,
        scratch_shapes=[
            vm(*lay, 128), vm(2 * ef, n), vm(ef, n), vm(2 * wide_s, n), vm(wide_s, n),
            vm(steps, rows, ef + wide_s),
            vm(2, na, r, n), vm(2, na, r, n),
            vm(2, na, r, ef), vm(2, na, r, 2 * ef),
            vm(2, na, r, wide_s), vm(2, na, r, 2 * wide_s),
            vm(2, na, r, n),
            vm(nb, ny, na, r, n),
            vm(2, na, r, n),
            vm(nb, ny, na, r, n),
            vm(pieces, nb, ny - 1, na, half, width),
            vm(pieces, ny, nb - 1, na, half, width),
            vm(pieces, nb - 1, na, half, width),
            vm(pieces, ny - 1, na, half, width),
            vm(pieces, na - 1, r, width),
            pltpu.SemaphoreType.DMA, sems(3 * EXP_DEV + 3), pltpu.SemaphoreType.DMA, sems(2), sems(2),
            sems(2, 4), sems(2),
            sems(sends), sems(2 * na * nb * ny), sems(2 * na * nb * ny), sems(2 * na * nb * ny),
            sems(2), sems(nb, ny),
            sems(pieces, nb, ny - 1), sems(pieces, nb, ny - 1),
            sems(pieces, ny, nb - 1), sems(pieces, ny, nb - 1),
            sems(pieces, nb - 1), sems(pieces, nb - 1),
            sems(pieces, ny - 1), sems(pieces, ny - 1),
            sems(pieces, na - 1), sems(pieces, na - 1),
        ],
        cost_estimate=microseconds(130),
        compiler_params=pltpu.CompilerParams(
            collective_id=collective_id, has_side_effects=True, vmem_limit_bytes=63 << 20
        ),
    )(
        x,
        dz.reshape(lay + (n,)),
        gates.reshape(lay + (gates.shape[-1],)),
        jnp.swapaxes(expert_gate, 1, 2), jnp.swapaxes(expert_up, 1, 2), expert_down,
        shared_gate.T, shared_up.T, shared_down,
    )
    tokens = grid.size * r
    rows_all, grad, out_rows, acts = outs
    return rows_all.reshape(tokens, n), grad, out_rows.reshape(tokens, n), acts.reshape(tokens, -1)


class Reduce:
    @staticmethod
    def scratch(grid, r, width):
        na, nb, ny = grid.na, grid.nb, grid.ny
        head = Reduce.head(r)
        sems = lambda *s: pltpu.SemaphoreType.DMA(s)
        vm = lambda *s: pltpu.VMEM(s, jnp.bfloat16)
        return [
            vm(nb, ny, na, r, width), vm(nb, ny, na, r, width),
            vm(nb, ny - 1, na, head, width), vm(ny, nb - 1, na, max(16, r - head), width),
            vm(nb - 1, na, head, width), vm(ny - 1, na, max(16, r - head), width), vm(na - 1, r, width),
            sems(nb, ny), sems(nb, ny), sems(nb, ny),
            sems(nb, ny - 1), sems(nb, ny - 1), sems(ny, nb - 1), sems(ny, nb - 1),
            sems(nb - 1), sems(nb - 1), sems(ny - 1), sems(ny - 1), sems(na - 1), sems(na - 1),
        ]

    count = 20

    @staticmethod
    def head(r):
        return r

    @staticmethod
    def schedule(sums):
        stages = [[one.core, one.first, one.second] for one in sums]
        work = []
        for beat in range(len(sums) + 2):
            for back in range(3):
                if 0 <= beat - back < len(sums):
                    work.append(stages[beat - back][back])
        return work

    def __init__(self, grid, source, out, scratch):
        self.grid, self.source, self.out = grid, source, out
        (
            self.acc, self.core_in, self.in10, self.in11, self.in20, self.in21, self.a_in,
            self.load_sem, self.core_s, self.core_r, self.s10, self.r10, self.s11, self.r11,
            self.s20, self.r20, self.s21, self.r21, self.sa, self.ra,
        ) = scratch
        self.spot = grid.here()
        r = self.acc.shape[3]
        head = Reduce.head(r)
        self.both = head < r
        self.upper = (pl.ds(0, head), pl.ds(head, r - head) if self.both else None)
        self.spots = [(j, k) for j in reversed(range(grid.nb)) for k in reversed(range(grid.ny))]

    def remote(self, src, dst, ss, rs, where):
        return pltpu.make_async_remote_copy(
            src_ref=src, dst_ref=dst, send_sem=ss, recv_sem=rs, device_id=where, device_id_type=MESH
        )

    def core_copy(self, j, k):
        g, (a, b, y, c) = self.grid, self.spot
        return self.remote(
            self.source.at[:, wrap(b + j, g.nb), wrap(y + k, g.ny), 1 - c], self.core_in.at[j, k],
            self.core_s.at[j, k], self.core_r.at[j, k], g.device(a, b, y, 1 - c),
        )

    def load(self, j, k):
        g, (a, b, y, c) = self.grid, self.spot
        return pltpu.make_async_copy(
            self.source.at[:, wrap(b + j, g.nb), wrap(y + k, g.ny), c], self.acc.at[j, k], self.load_sem.at[j, k]
        )

    def copy10(self, j, k):
        g, (a, b, y, c) = self.grid, self.spot
        return self.remote(
            self.acc.at[j, k, :, self.upper[0]], self.in10.at[j, k - 1], self.s10.at[j, k - 1],
            self.r10.at[j, k - 1], g.device(a, b, wrap(y + k, g.ny), c),
        )

    def copy11(self, j, k):
        g, (a, b, y, c) = self.grid, self.spot
        return self.remote(
            self.acc.at[j, k, :, self.upper[1]], self.in11.at[k, j - 1], self.s11.at[k, j - 1],
            self.r11.at[k, j - 1], g.device(a, wrap(b + j, g.nb), y, c),
        )

    def copy20(self, j):
        g, (a, b, y, c) = self.grid, self.spot
        return self.remote(
            self.acc.at[j, 0, :, self.upper[0]], self.in20.at[j - 1], self.s20.at[j - 1],
            self.r20.at[j - 1], g.device(a, wrap(b + j, g.nb), y, c),
        )

    def copy21(self, k):
        g, (a, b, y, c) = self.grid, self.spot
        return self.remote(
            self.acc.at[0, k, :, self.upper[1]], self.in21.at[k - 1], self.s21.at[k - 1],
            self.r21.at[k - 1], g.device(a, b, wrap(y + k, g.ny), c),
        )

    def copy_a(self, i):
        g, (a, b, y, c) = self.grid, self.spot
        return self.remote(
            self.acc.at[0, 0, wrap(a + i, g.na)], self.a_in.at[i - 1], self.sa.at[i - 1],
            self.ra.at[i - 1], g.device(wrap(a + i, g.na), b, y, c),
        )

    def add(self, into, rows, ref, sem):
        pltpu.make_async_copy(ref, ref, sem).wait()
        f32 = jnp.float32

        def one(i, carry):
            total = into[i, rows].astype(f32) + ref[i].astype(f32)
            into[i, rows] = total.astype(into.dtype)
            return carry

        lax.fori_loop(0, self.grid.na, one, 0)

    def start(self):
        for j, k in self.spots:
            self.core_copy(j, k).start()
            self.load(j, k).start()

    def core(self):
        whole = pl.ds(0, self.acc.shape[3])
        for j, k in self.spots:
            self.load(j, k).wait()
            self.add(self.acc.at[j, k], whole, self.core_in.at[j, k], self.core_r.at[j, k])
            if k:
                self.copy10(j, k).start()
            if j and self.both:
                self.copy11(j, k).start()

    def first(self):
        nb, ny = self.grid.nb, self.grid.ny
        for j in reversed(range(nb)):
            for k in range(1, ny):
                self.add(self.acc.at[j, 0], self.upper[0], self.in10.at[j, k - 1], self.r10.at[j, k - 1])
            if j:
                self.copy20(j).start()
        for k in reversed(range(ny if self.both else 0)):
            for j in range(1, nb):
                self.add(self.acc.at[0, k], self.upper[1], self.in11.at[k, j - 1], self.r11.at[k, j - 1])
            if k:
                self.copy21(k).start()

    def second(self):
        for j in range(1, self.grid.nb):
            self.add(self.acc.at[0, 0], self.upper[0], self.in20.at[j - 1], self.r20.at[j - 1])
        for k in range(1, self.grid.ny if self.both else 0):
            self.add(self.acc.at[0, 0], self.upper[1], self.in21.at[k - 1], self.r21.at[k - 1])
        for i in range(1, self.grid.na):
            self.copy_a(i).start()

    def last(self):
        total = self.acc[0, 0, self.spot[0]].astype(jnp.float32)
        for i in range(1, self.grid.na):
            pltpu.make_async_copy(self.a_in.at[i - 1], self.a_in.at[i - 1], self.ra.at[i - 1]).wait()
            total = total + self.a_in[i - 1].astype(jnp.float32)
        self.out[...] = total.astype(self.out.dtype)

    def finish(self):
        for j, k in self.spots:
            self.core_copy(j, k).wait_send()
            if k:
                self.copy10(j, k).wait_send()
            if j and self.both:
                self.copy11(j, k).wait_send()
        for j in range(1, self.grid.nb):
            self.copy20(j).wait_send()
        for k in range(1, self.grid.ny if self.both else 0):
            self.copy21(k).wait_send()
        for i in range(1, self.grid.na):
            self.copy_a(i).wait_send()


W_PIECES = 1


def gradients_kernel(grid, pieces, unit, places, *refs):
    (y_ref, k_ref, w_ref, t_ref, q_ref, x_ref, dz_ref, acts_ref), refs = refs[:8], refs[8:]
    (y_out, k_out, w_out, t_out, q_out), refs = refs[:5], refs[5:]
    outs, refs = refs[:6], refs[6:]
    (big, left, right, big_sem, left_sem, out_sem), refs = refs[:6], refs[6:]
    width = y_ref.shape[-1] // pieces
    sources = [(k_ref, k_out)]
    for p in range(pieces):
        at = pl.ds(p * width, width)
        sources.append((y_ref.at[:, :, :, :, :, at], y_out.at[:, at]))
    sums = [
        Reduce(grid, src, out, refs[m * Reduce.count : (m + 1) * Reduce.count])
        for m, (src, out) in enumerate(sources)
    ]
    refs = refs[len(sums) * Reduce.count :]
    w_width = w_ref.shape[-1] // W_PIECES
    flat_sums = []
    for p in range(W_PIECES):
        at = pl.ds(p * w_width, w_width)
        part = refs[p * PlaneReduce.count : (p + 1) * PlaneReduce.count]
        flat_sums.append(PlaneReduce(grid, w_ref.at[:, :, :, at], w_out.at[:, at], part))
    refs = refs[W_PIECES * PlaneReduce.count :]
    flat_sums.append(TensorReduce(grid, t_ref, t_out, refs[: TensorReduce.count]))
    q_gather = PlaneGather(grid, q_ref, q_out, refs[TensorReduce.count :])
    tiles = len(places)
    turn = sum(1 for place in places if place[0] != 2 and place[0] != 5)
    slots = big.shape[0]

    def left_load(m):
        s = lax.rem(m, 2)
        at = pl.ds(pl.multiple_of(m * unit, unit), unit)
        return pltpu.make_async_copy(acts_ref.at[:, at], left.at[s], left_sem.at[s])

    big_loads = [
        pltpu.make_async_copy(src, big.at[s % slots], big_sem.at[s]) for s, src in enumerate((x_ref, dz_ref))
    ]
    big_loads[0].start()
    greet(grid)
    for one in [q_gather] + flat_sums + sums:
        one.start()
    left_load(grid.here()[0] * 0).start()
    if slots > 1:
        big_loads[1].start()
    big_loads[0].wait()

    work = Reduce.schedule(sums)
    for p, one in enumerate(flat_sums):
        work.insert(min(len(work), 3 + 3 * p), one.middle)
    for i in range(1, grid.na):
        work.insert(min(len(work), 2 + 2 * i), functools.partial(q_gather.middle, i))
    turns = {}
    for n, item in enumerate(work):
        turns.setdefault(n * tiles // len(work), []).append(item)

    def store(m):
        which, head, first, rows = places[m]
        dst = outs[which]
        dst = dst.at[pl.ds(first, rows)] if head is None else dst.at[head, pl.ds(first, rows)]
        return pltpu.make_async_copy(right.at[m % 2, pl.ds(0, rows)], dst, out_sem.at[m % 2])

    def tile_body(m, carry):
        s = lax.rem(m, 2)

        @pl.when(m + 1 < tiles)
        def _():
            left_load(m + 1).start()

        for n in range(2, tiles):

            @pl.when(m == n)
            def _():
                store(n - 2).wait()

        @pl.when(m == turn)
        def _():
            if slots == 1:
                big_loads[1].start()
            big_loads[1].wait()

        left_load(m).wait()
        operand = big.at[lax.div(m, turn) if slots > 1 else 0]
        right[s] = lax.dot_general(
            left[s], operand[...], (((0,), (0,)), ((), ())), preferred_element_type=jnp.float32
        ).astype(right.dtype)
        for n in range(tiles):

            @pl.when(m == n)
            def _():
                store(n).start()
                for item in turns.get(n, ()):
                    item()

        return carry

    lax.fori_loop(0, tiles, tile_body, 0)
    for one in sums + flat_sums:
        one.last()
    for n in range(max(0, tiles - 2), tiles):
        store(n).wait()
    for one in sums + flat_sums:
        one.finish()
    q_gather.last()


def gradients_call(grid, out_rows, key_rows, weight_rows, tensor_rows, query_rows, x, dz, acts, f, fs, collective_id, pieces=4):
    tokens, n = x.shape
    r = tokens // grid.size
    lay = (grid.na, grid.nb, grid.ny, 2, r)
    wide, wide_s = round_up(f, 128), round_up(fs, 128)
    unit = math.gcd(wide, wide_s)
    places = []
    for which, heads, real, padded in (
        (0, EXP_DEV, f, wide), (1, EXP_DEV, f, wide), (3, 0, fs, wide_s), (4, 0, fs, wide_s),
        (2, EXP_DEV, f, wide), (5, 0, fs, wide_s),
    ):
        for head in range(max(heads, 1)):
            for first in range(0, padded, unit):
                places.append((which, head if heads else None, first, min(unit, real - first)))
    slots = 2 if 2 * tokens * n * 2 <= (24 << 20) else 1
    any_space = pl.BlockSpec(memory_space=pl.ANY)
    in_vmem = pl.BlockSpec(memory_space=pltpu.VMEM)
    f32 = jnp.float32
    scratch = [
        pltpu.VMEM((slots, tokens, n), x.dtype),
        pltpu.VMEM((2, tokens, unit), x.dtype),
        pltpu.VMEM((2, unit, n), x.dtype),
        pltpu.SemaphoreType.DMA((2,)),
        pltpu.SemaphoreType.DMA((2,)),
        pltpu.SemaphoreType.DMA((2,)),
    ]
    kw = key_rows.shape[1]
    for width in [kw] + [n // pieces] * pieces:
        scratch += Reduce.scratch(grid, r, width)
    wr, ww = weight_rows.shape[0] // (grid.na * grid.nb), weight_rows.shape[1]
    scratch += PlaneReduce.scratch(grid, wr, ww // W_PIECES) * W_PIECES
    tr, tw = tensor_rows.shape[0] // (2 * grid.ny), tensor_rows.shape[1]
    scratch += TensorReduce.scratch(grid, tr, tw) + PlaneGather.scratch(grid)
    outs = pl.pallas_call(
        functools.partial(gradients_kernel, grid, pieces, unit, places),
        out_shape=[
            jax.ShapeDtypeStruct((r, n), f32),
            jax.ShapeDtypeStruct((r, kw), f32),
            jax.ShapeDtypeStruct((wr, ww), x.dtype),
            jax.ShapeDtypeStruct((tr, tw), f32),
            jax.ShapeDtypeStruct((grid.na, grid.nb) + query_rows.shape, x.dtype),
            jax.ShapeDtypeStruct((EXP_DEV, f, n), x.dtype),
            jax.ShapeDtypeStruct((EXP_DEV, f, n), x.dtype),
            jax.ShapeDtypeStruct((EXP_DEV, f, n), x.dtype),
            jax.ShapeDtypeStruct((fs, n), x.dtype),
            jax.ShapeDtypeStruct((fs, n), x.dtype),
            jax.ShapeDtypeStruct((fs, n), x.dtype),
        ],
        in_specs=[any_space] * 8,
        out_specs=[in_vmem] * 4 + [any_space] * 7,
        scratch_shapes=scratch,
        cost_estimate=microseconds(90),
        compiler_params=pltpu.CompilerParams(
            collective_id=collective_id, has_side_effects=True, vmem_limit_bytes=62 << 20
        ),
    )(
        out_rows.reshape(lay + (n,)),
        key_rows.reshape(lay + (kw,)),
        weight_rows.reshape(grid.na, grid.nb, wr, ww),
        tensor_rows.reshape(grid.ny, 2, tr, tw),
        query_rows,
        x,
        dz,
        acts,
    )
    y_sum, k_sum, w_sum, t_sum, q_all = outs[:5]
    eg, eu, ed, sg, su, sd = (out.astype(f32) for out in outs[5:])
    q_all = q_all.reshape(tokens, -1)
    weights = (jnp.swapaxes(eg, 1, 2), jnp.swapaxes(eu, 1, 2), ed, sg.T, su.T, sd)
    return y_sum, k_sum, w_sum, t_sum, q_all, weights


class GatherAll:
    @staticmethod
    def scratch(grid):
        blocks = 2 * grid.na * grid.nb * grid.ny
        sems = lambda n: pltpu.SemaphoreType.DMA((n,))
        return [sems(1), sems(gather_sends(grid)), sems(blocks), sems(blocks), sems(blocks)]

    def __init__(self, grid, x, out, scratch, halves=2):
        self.grid, self.x, self.out, self.halves = grid, x, out, halves
        self.own_sem, self.sends, self.recvs, self.share_s, self.share_r = scratch
        self.spot = grid.here()
        self.half = x.shape[0] // halves
        self.count = 0
        na, nb, ny = grid.na, grid.nb, grid.ny
        self.orders = (("b", "y"), ("y", "b"))
        near = [(0, k, 0, 0, ()) for k in range(1, ny)] + [(0, k, 0, 1, ("b",)) for k in range(1, ny)]
        first = [(0, 0, i, h, self.orders[h]) for i in range(1, na) for h in range(2)]
        second = []
        for i in range(na):
            second += [(j, 0, i, 0, ("y",)) for j in range(1, nb)]
            second += [(0, k, i, 1, ("b",)) for k in range(1, ny) if i]
        third = []
        for i in range(na):
            third += [(0, k, i, 0, ()) for k in range(1, ny) if i]
            third += [(j, 0, i, 1, ()) for j in range(1, nb)]
        for i in range(na):
            third += [(j, k, i, h, ()) for j in range(1, nb) for k in range(1, ny) for h in range(2)]
        self.near = [event for event in near if event[3] < halves]
        self.others = [event for event in first + second + third if event[3] < halves]

    def line(self, i):
        a = self.spot[0]
        if self.grid.na != 4:
            return wrap(a + i, self.grid.na)
        if i == 0:
            return a
        if i == 1:
            return a + 1 - 2 * lax.rem(a, 2)
        return (i - lax.div(a, 2)) if i == 2 else (3 - 3 * lax.div(a, 2))

    def place(self, bb, yy, cc, aa, h):
        return self.out.at[aa, bb, yy, cc, pl.ds(h * self.half, self.half)]

    def slot(self, bb, yy, aa, h):
        return ((bb * self.grid.ny + yy) * self.grid.na + aa) * 2 + h

    def push(self, src, bb, yy, aa, h, where, send, recv):
        pltpu.make_async_remote_copy(
            src_ref=src, dst_ref=self.place(bb, yy, self.spot[3], aa, h), send_sem=send,
            recv_sem=recv.at[self.slot(bb, yy, aa, h)], device_id=where, device_id_type=MESH,
        ).start()

    def onward(self, src, bb, yy, aa, h, dims):
        g, (a, b, y, c) = self.grid, self.spot
        for d in dims:
            for i in range(1, {"a": g.na, "b": g.nb, "y": g.ny}[d]):
                if d == "a":
                    where = g.device(self.line(i), b, y, c)
                elif d == "b":
                    where = g.device(a, wrap(b + i, g.nb), y, c)
                else:
                    where = g.device(a, b, wrap(y + i, g.ny), c)
                self.push(src, bb, yy, aa, h, where, self.sends.at[self.count], self.recvs)
                self.count += 1
        where = g.device(a, b, y, 1 - c)
        self.push(src, bb, yy, aa, h, where, self.share_s.at[self.slot(bb, yy, aa, h)], self.share_r)

    def landed(self, bb, yy, cc, aa, h, sem):
        ref = self.place(bb, yy, cc, aa, h)
        pltpu.make_async_copy(ref, ref, sem.at[self.slot(bb, yy, aa, h)]).wait()
        return ref

    def own(self):
        a, b, y, c = self.spot
        return pltpu.make_async_copy(self.x, self.out.at[a, b, y, c], self.own_sem.at[0])

    def start(self):
        a, b, y, c = self.spot
        self.own().start()
        for h in range(self.halves):
            src = self.x.at[pl.ds(h * self.half, self.half)]
            self.onward(src, b, y, a, h, ("y", "a", "b") if h == 0 else ("y", "b", "a"))

    def relay(self, j, k, i, h, dims):
        g, (a, b, y, c) = self.grid, self.spot
        bb, yy, aa = wrap(b + j, g.nb), wrap(y + k, g.ny), self.line(i)
        self.onward(self.landed(bb, yy, c, aa, h, self.recvs), bb, yy, aa, h, dims)

    def shared(self, j, k, i):
        g, (a, b, y, c) = self.grid, self.spot
        for h in range(self.halves):
            self.landed(wrap(b + j, g.nb), wrap(y + k, g.ny), 1 - c, self.line(i), h, self.share_r)

    def group(self):
        for event in self.near:
            self.relay(*event)
        for k in range(self.grid.ny):
            self.shared(0, k, 0)
        self.own().wait()

    def finish(self):
        g, (a, b, y, c) = self.grid, self.spot
        for j in range(g.nb):
            for k in range(g.ny):
                for i in range(g.na):
                    if i or j:
                        self.shared(j, k, i)
        some = self.place(b, y, c, a, 0)
        for i in range(self.count):
            pltpu.make_async_copy(some, some, self.sends.at[i]).wait()
        for i in range(g.na * g.nb * g.ny):
            for h in range(self.halves):
                pltpu.make_async_copy(some, some, self.share_s.at[2 * i + h]).wait()


def turn_back(values, cosines, sines):
    quarter = ROPE // 2
    lane = lax.broadcasted_iota(jnp.int32, values.shape, 1)
    swapped = jnp.where(
        lane < quarter,
        pltpu.roll(values, values.shape[1] - quarter, 1),
        pltpu.roll(values, quarter, 1),
    )
    return values * cosines + swapped * sines


def attention_back_kernel(
    grid,
    pieces,
    x_ref,
    wo_hbm,
    q_hbm,
    kv_hbm,
    packed_hbm,
    we_hbm,
    ctx_ref,
    log_ref,
    seg_ref,
    own_seg_ref,
    cos_ref,
    sin_ref,
    dq_ref,
    keys_ref,
    part_ref,
    wo_ref,
    wo,
    q,
    kv,
    packed,
    we,
    grads,
    kcat,
    bias,
    dkv,
    drope,
    wo_part,
    load_sem,
    *scratch,
):
    f32, bf = jnp.float32, jnp.bfloat16
    rows, tokens = q.shape[0], kv.shape[0]
    heads = q.shape[1] // 256
    scale = (NOPE + ROPE) ** (-0.5)
    a, b, y, c = grid.here()
    pairs = ((wo_hbm, wo), (q_hbm, q), (kv_hbm, kv), (packed_hbm, packed), (we_hbm, we))
    loads = [pltpu.make_async_copy(src, dst, load_sem.at[i]) for i, (src, dst) in enumerate(pairs)]
    for load in loads:
        load.start()
    greet(grid)
    group = TensorGather(grid, x_ref, grads, scratch[: TensorGather.count])
    group.start()
    sums = []
    width = wo.shape[1] // pieces
    for p in range(pieces):
        first = TensorGather.count + p * PlaneReduce.count
        at = pl.ds(p * width, width)
        sums.append(
            PlaneReduce(
                grid, wo_part.at[:, :, :, at], wo_ref.at[:, at], scratch[first : first + PlaneReduce.count]
            )
        )
    first_row = (a * grid.nb + b) * rows
    ordinal = first_row + lax.broadcasted_iota(jnp.int32, (rows, tokens), 0)
    key = lax.broadcasted_iota(jnp.int32, (rows, tokens), 1)
    seg = seg_ref[...]
    seen = (key <= ordinal) & ((seg == own_seg_ref[...]) | (seg == 0))
    bias[...] = jnp.where(seen, 0.0, masked_out)
    for load in loads:
        load.wait()
    kcat[:, NOPE:] = packed[:, LATENT : LATENT + 128]
    lane = lax.broadcasted_iota(jnp.int32, (tokens, 128), 1)
    kcat[:, NOPE:] = jnp.where(lane < ROPE, kcat[:, NOPE:].astype(f32), 0.0).astype(bf)

    group.middle(1)
    group.last()
    rows_in = grads[...].reshape(rows, grads.shape[-1])
    for p in range(pieces):
        at = pl.ds(p * width, width)
        wo_part[:, :, :, at] = (
            lax.dot_general(
                ctx_ref[...], rows_in[:, p * width : (p + 1) * width], (((0,), (0,)), ((), ())),
                preferred_element_type=f32,
            )
            .astype(bf)
            .reshape(wo_part.shape[:3] + (width,))
        )
        sums[p].start()
    dctx = dot_rows(rows_in, wo[...]).astype(bf)

    points = 3 * heads + 1
    at_point = {}
    for p in range(pieces):
        at_point.setdefault((p + 1) * points // (pieces + 2), []).append(sums[p].middle)
    done = [0]

    def hook():
        for event in at_point.get(done[0], ()):
            event()
        done[0] += 1

    hook()
    for h in range(heads):
        qh = q[:, h * 256 : (h + 1) * 256]
        kcat[:, :NOPE] = kv[:, h * 256 : h * 256 + NOPE]
        s = dot_rows(qh, kcat[...]) * scale + bias[...]
        p = jnp.exp(s - log_ref[h])
        dh = dctx[:, h * VDIM : (h + 1) * VDIM]
        dp = dot_rows(dh, kv[:, h * 256 + NOPE : (h + 1) * 256])
        ds = (p * (dp - jnp.sum(p * dp, axis=-1, keepdims=True))).astype(bf)
        p = p.astype(bf)
        hook()
        dq = dot_plain(ds, kcat[...]) * scale
        dq_ref[:, h * 256 : h * 256 + NOPE] = dq[:, :NOPE].astype(bf)
        dq_ref[:, h * 256 + NOPE : (h + 1) * 256] = turn_back(
            dq[:, NOPE:], cos_ref[...], sin_ref[...]
        ).astype(bf)
        hook()
        dkv[:, h * 256 + NOPE : (h + 1) * 256] = lax.dot_general(
            p, dh, (((0,), (0,)), ((), ())), preferred_element_type=f32
        ).astype(bf)
        dk = scale * lax.dot_general(ds, qh, (((0,), (0,)), ((), ())), preferred_element_type=f32)
        dkv[:, h * 256 : h * 256 + NOPE] = dk[:, :NOPE].astype(bf)
        if h == 0:
            drope[...] = dk[:, NOPE:]
        else:
            drope[...] += dk[:, NOPE:]
        hook()
    keys_ref[:, :LATENT] = dot_rows(dkv[...], we[...]).astype(bf)
    keys_ref[:, LATENT:] = drope[...].astype(bf)
    part_ref[...] = lax.dot_general(
        packed[:, :LATENT], dkv[...], (((0,), (0,)), ((), ())), preferred_element_type=f32
    ).astype(bf)
    for one in sums:
        one.last()
    for one in sums:
        one.finish()


def attention_back_call(
    grid, x, wo, q, kv, packed, we, context, log_total, seg, own_seg, cosines, sines, collective_id, pieces=4
):
    r, n = x.shape
    rows, tokens, heads = q.shape[0], kv.shape[0], q.shape[1] // 256
    bf, f32 = jnp.bfloat16, jnp.float32
    any_space = pl.BlockSpec(memory_space=pl.ANY)
    in_vmem = pl.BlockSpec(memory_space=pltpu.VMEM)
    share = wo.shape[0] // (grid.na * grid.nb)
    return pl.pallas_call(
        functools.partial(attention_back_kernel, grid, pieces),
        out_shape=[
            jax.ShapeDtypeStruct(q.shape, bf),
            jax.ShapeDtypeStruct((tokens, LATENT + 128), bf),
            jax.ShapeDtypeStruct(we.shape, bf),
            jax.ShapeDtypeStruct((share, n), bf),
        ],
        in_specs=[any_space] * 6 + [in_vmem] * 6,
        out_specs=[in_vmem] * 4,
        scratch_shapes=[
            pltpu.VMEM(wo.shape, bf),
            pltpu.VMEM(q.shape, bf),
            pltpu.VMEM(kv.shape, bf),
            pltpu.VMEM(packed.shape, bf),
            pltpu.VMEM(we.shape, bf),
            pltpu.VMEM((grid.ny, 2, r, n), bf),
            pltpu.VMEM((tokens, 256), bf),
            pltpu.VMEM((rows, tokens), f32),
            pltpu.VMEM(kv.shape, bf),
            pltpu.VMEM((tokens, 128), f32),
            pltpu.VMEM((grid.na, grid.nb, share, n), bf),
            pltpu.SemaphoreType.DMA((5,)),
        ]
        + TensorGather.scratch(grid)
        + PlaneReduce.scratch(grid, share, n // pieces) * pieces,
        cost_estimate=microseconds(50),
        compiler_params=pltpu.CompilerParams(
            collective_id=collective_id, has_side_effects=True, vmem_limit_bytes=62 << 20
        ),
    )(x, wo, q, kv, packed, we, context, log_total, seg, own_seg, cosines, sines)


def front_kernel(
    grid,
    hidden_ref,
    gain_ref,
    lgain_ref,
    mgain_ref,
    gate_ref,
    route_ref,
    cos_ref,
    sin_ref,
    seg_ref,
    own_seg_ref,
    cot_hbm,
    wl_hbm,
    wq_hbm,
    we_hbm,
    wo_hbm,
    packed_hbm,
    cot_all,
    kv_ref,
    q,
    normed_ref,
    comp_ref,
    log_ref,
    ctx_ref,
    res_ref,
    moe_ref,
    wl,
    wq,
    we,
    wo,
    normed,
    mine,
    packed,
    kv,
    kcat,
    bias,
    part,
    total,
    load_sem,
    kv_sem,
    packed_sem,
    *scratch,
):
    f32, bf = jnp.float32, jnp.bfloat16
    rows, few, tokens = hidden_ref.shape[0], mine.shape[0], kv.shape[0]
    heads = q.shape[1] // 256
    scale = (NOPE + ROPE) ** (-0.5)
    a, b, y, c = grid.here()
    pairs = (
        (wl_hbm, wl.at[pl.ds(0, LATENT + ROPE)]), (wq_hbm, wq), (we_hbm, we), (wo_hbm, wo),
    )
    loads = [pltpu.make_async_copy(src, dst, load_sem.at[i]) for i, (src, dst) in enumerate(pairs)]
    for load in loads:
        load.start()
    wl[LATENT + ROPE :] = jnp.zeros((wl.shape[0] - LATENT - ROPE, wl.shape[1]), bf)
    greet(grid)
    at = pl.ds(pl.multiple_of((y * 2 + c) * few, few), few)

    def rms(v, gain):
        return v * lax.rsqrt(jnp.mean(v * v, axis=-1, keepdims=True) + epsilon) * gain

    hidden_few = hidden_ref[at].astype(f32)
    normed_few = rms(hidden_few, gain_ref[...]).astype(bf)
    normed_ref[...] = normed_few
    loads[0].wait()
    comp = dot_rows(normed_few, wl[...])
    comp_ref[...] = comp
    mine[:, :LATENT] = rms(comp[:, :LATENT], lgain_ref[...]).astype(bf)
    tail = turn_back(comp[:, LATENT:], cos_ref[at], -sin_ref[at])
    lane = lax.broadcasted_iota(jnp.int32, tail.shape, 1) - ROPE
    routes, gates = route_ref[at], gate_ref[at]
    for k in range(TOP):
        expert, gate = routes[:, k : k + 1], gates[:, k : k + 1]
        high = gate.astype(bf).astype(f32)
        tail += jnp.where(lane == expert, high, 0.0)
        tail += jnp.where(lane == expert + EXP_DEV * grid.na * grid.nb, gate - high, 0.0)
    mine[:, LATENT:] = tail.astype(bf)
    gather = GatherAll(grid, mine, packed_hbm, scratch[:5], halves=1)
    gather.start()
    cots = GatherAll(grid, cot_hbm.at[at], cot_all, scratch[5:10])
    cots.start()
    normed[...] = rms(hidden_ref[...].astype(f32), gain_ref[...]).astype(bf)
    loads[1].wait()
    gather.group()
    third = len(gather.others) // 3
    for event in gather.others[:third]:
        gather.relay(*event)
    raw = dot_plain(normed[...], wq[...])
    width = raw.shape[1]
    for h in range(heads):
        step = h * (NOPE + ROPE)
        moved = raw if step == 0 else pltpu.roll(raw, width - step, 1)
        q[:, h * 256 : h * 256 + NOPE] = moved[:, :NOPE].astype(bf)
        q[:, h * 256 + NOPE : (h + 1) * 256] = turn_back(
            moved[:, NOPE : NOPE + 128], cos_ref[...], -sin_ref[...]
        ).astype(bf)
    for event in gather.others[third:]:
        gather.relay(*event)
    early = 2 * (grid.na - 1)
    for event in cots.near + cots.others[:early]:
        cots.relay(*event)
    ordinal = (a * grid.nb + b) * rows + lax.broadcasted_iota(jnp.int32, (rows, tokens), 0)
    key = lax.broadcasted_iota(jnp.int32, (rows, tokens), 1)
    seg = seg_ref[...]
    seen = (key <= ordinal) & ((seg == own_seg_ref[...]) | (seg == 0))
    bias[...] = jnp.where(seen, 0.0, masked_out)
    gather.finish()
    load = pltpu.make_async_copy(packed_hbm, packed, packed_sem)
    load.start()

    passing = [functools.partial(cots.relay, *event) for event in cots.others[early:]]
    at_point = {}
    for m, event in enumerate(passing):
        at_point.setdefault(m * (heads + 1) // len(passing), []).append(event)

    def hook(point):
        for event in at_point.get(point, ()):
            event()

    load.wait()
    hook(0)
    flat = packed[...].reshape(tokens, packed.shape[-1])
    lane = lax.broadcasted_iota(jnp.int32, (tokens, 128), 1)
    kcat[:, NOPE:] = jnp.where(lane < ROPE, flat[:, LATENT:].astype(f32), 0.0).astype(bf)
    loads[2].wait()
    kv[...] = dot_plain(flat[:, :LATENT], we[...]).astype(bf)
    store = pltpu.make_async_copy(kv, kv_ref, kv_sem)
    store.start()
    hook(1)
    for h in range(heads):
        kcat[:, :NOPE] = kv[:, h * 256 : h * 256 + NOPE]
        s = dot_rows(q[:, h * 256 : (h + 1) * 256], kcat[...]) * scale + bias[...]
        peak = jnp.max(s, axis=-1, keepdims=True)
        w = jnp.exp(s - peak)
        tot = jnp.sum(w, axis=-1, keepdims=True)
        log_ref[h] = peak + jnp.log(tot)
        p = (w * (1.0 / tot)).astype(bf)
        ctx_ref[:, h * VDIM : (h + 1) * VDIM] = dot_plain(
            p, kv[:, h * 256 + NOPE : (h + 1) * 256]
        ).astype(bf)
        hook(2 + h)
    loads[3].wait()
    part[...] = dot_plain(ctx_ref[...], wo[...]).astype(bf).reshape(part.shape)
    reduce = TensorReduce(grid, part, total, scratch[10:])
    reduce.start()
    reduce.middle()
    reduce.last()
    residual = hidden_ref[at].astype(f32) + total[...]
    res_ref[...] = residual
    moe_ref[...] = rms(residual, mgain_ref[...]).astype(bf)
    store.wait()
    for k in range(grid.ny):
        cots.shared(0, k, 0)
    cots.own().wait()
    cots.finish()
    reduce.finish()


def front_call(
    grid, hidden, cotangent, attn_gain, latent_gain, moe_gain, gates, routes, cosines, sines, seg, own_seg,
    latent_weight, query_weight, expand_weight, output_weight, collective_id,
):
    rows, n = hidden.shape
    few = rows // (2 * grid.ny)
    tokens = grid.size * few
    heads = query_weight.shape[1] // (NOPE + ROPE)
    bf, f32 = jnp.bfloat16, jnp.float32
    any_space = pl.BlockSpec(memory_space=pl.ANY)
    in_vmem = pl.BlockSpec(memory_space=pltpu.VMEM)
    width = LATENT + 128
    lay = (grid.na, grid.nb, grid.ny, 2, few)
    outs = pl.pallas_call(
        functools.partial(front_kernel, grid),
        out_shape=[
            jax.ShapeDtypeStruct(lay + (width,), bf),
            jax.ShapeDtypeStruct(lay + (n,), bf),
            jax.ShapeDtypeStruct((tokens, heads * 256), bf),
            jax.ShapeDtypeStruct((rows, heads * 256), bf),
            jax.ShapeDtypeStruct((few, n), bf),
            jax.ShapeDtypeStruct((few, width), f32),
            jax.ShapeDtypeStruct((heads, rows, 1), f32),
            jax.ShapeDtypeStruct((rows, heads * VDIM), bf),
            jax.ShapeDtypeStruct((few, n), f32),
            jax.ShapeDtypeStruct((few, n), bf),
        ],
        in_specs=[in_vmem] * 10 + [any_space] * 5,
        out_specs=[any_space] * 3 + [in_vmem] * 7,
        scratch_shapes=[
            pltpu.VMEM((width, n), bf),
            pltpu.VMEM(query_weight.shape, bf),
            pltpu.VMEM(expand_weight.shape, bf),
            pltpu.VMEM(output_weight.shape, bf),
            pltpu.VMEM((rows, n), bf),
            pltpu.VMEM((few, width), bf),
            pltpu.VMEM(lay + (width,), bf),
            pltpu.VMEM((tokens, heads * 256), bf),
            pltpu.VMEM((tokens, 256), bf),
            pltpu.VMEM((rows, tokens), f32),
            pltpu.VMEM((grid.ny, 2, few, n), bf),
            pltpu.VMEM((few, n), f32),
            pltpu.SemaphoreType.DMA((4,)),
            pltpu.SemaphoreType.DMA,
            pltpu.SemaphoreType.DMA,
        ]
        + GatherAll.scratch(grid) * 2
        + TensorReduce.scratch(grid, few, n),
        cost_estimate=microseconds(74),
        compiler_params=pltpu.CompilerParams(
            collective_id=collective_id, has_side_effects=True, vmem_limit_bytes=62 << 20
        ),
    )(
        hidden, attn_gain[None], latent_gain[None], moe_gain[None], gates, routes, cosines, sines,
        seg, own_seg, cotangent, latent_weight.T, query_weight, expand_weight, output_weight,
    )
    return [outs[0].reshape(tokens, width), outs[1].reshape(tokens, n), *outs[2:]]


def rms_scale(values, gain_vec):
    return (
        values * lax.rsqrt(jnp.mean(values * values, axis=-1, keepdims=True) + epsilon) * gain_vec
    )


def rotate(values, places):
    halfway = values.shape[-1] // 2
    frequency = 10000.0 ** (-jnp.arange(halfway, dtype=jnp.float32) / halfway)
    angles = places.astype(jnp.float32)[:, None] * frequency[None, :]
    cosine = jnp.cos(angles)
    sine_part = jnp.sin(angles)
    if values.ndim == 3:
        cosine = cosine[:, None, :]
        sine_part = sine_part[:, None, :]
    first_half = values[..., :halfway]
    second = values[..., halfway:]
    return jnp.concatenate(
        [first_half * cosine - second * sine_part, second * cosine + first_half * sine_part],
        axis=-1,
    )


def seq_places(segments):
    total_rows = segments.shape[0]
    ordinal = jnp.arange(total_rows, dtype=jnp.int32)
    starts = jnp.concatenate(
        [jnp.ones((1,), jnp.int32), (segments[1:] != segments[:-1]).astype(jnp.int32)]
    )
    seg_start = lax.cummax(jnp.where(starts > 0, ordinal, 0), axis=0)
    return jnp.where(segments == 0, ordinal, total_rows // 2 + ordinal - seg_start)


def silu_product(gate_pre, up_pre):
    return jax.nn.silu(gate_pre) * up_pre


def score_block(queries, key_plain, rope_all, visible):
    scale_factor = (NOPE + ROPE) ** (-0.5)
    raw_scores = jnp.einsum(
        "thc,shc->hts", queries[..., :NOPE], key_plain, preferred_element_type=jnp.float32
    )
    raw_scores = raw_scores + jnp.einsum(
        "thr,sr->hts", queries[..., NOPE:], rope_all, preferred_element_type=jnp.float32
    )
    return jnp.where(visible[None], scale_factor * raw_scores, masked_out)


def dot(left_side, right_side):
    return jnp.dot(left_side, right_side, preferred_element_type=jnp.float32)


def pad_columns(values):
    return jnp.pad(values, ((0, 0), (0, -values.shape[1] % 128)))


def low(values):
    return values.astype(jnp.bfloat16)


def shards(
    grid,
    hidden_in,
    attn_gain,
    query_weight,
    latent_weight,
    latent_gain,
    expand_weight,
    output_weight,
    moe_gain,
    shared_gate,
    shared_up,
    shared_down,
    expert_gate,
    expert_up,
    expert_down,
    gate_values,
    expert_routes,
    segments,
    cotangent,
):
    tok_rows, model_width = hidden_in.shape
    groups = lax.axis_size("expert")
    parts = lax.axis_size("tensor")
    device = lax.axis_index("expert")
    part = lax.axis_index("tensor")
    total_rows = segments.shape[0]
    few = tok_rows // parts
    start_row = device * tok_rows
    scale_factor = (NOPE + ROPE) ** (-0.5)

    def quarter(values):
        return lax.dynamic_slice_in_dim(values, part * few, few)

    def own_group(values):
        return lax.dynamic_slice_in_dim(values, start_row, tok_rows)

    places = own_group(seq_places(segments))
    own_seg = own_group(segments)
    halfway = ROPE // 2
    frequency = 10000.0 ** (-jnp.arange(halfway, dtype=jnp.float32) / halfway)
    angles = places.astype(jnp.float32)[:, None] * frequency[None, :]
    nothing = jnp.zeros((tok_rows, 128 - ROPE), jnp.float32)
    cosines, sines = jnp.cos(angles), jnp.sin(angles)
    cosines = jnp.concatenate([cosines, cosines, nothing], axis=1)
    sines = jnp.concatenate([sines, -sines, nothing], axis=1)
    hidden_few = quarter(hidden_in)

    (
        packed_all, cot_all, expanded, queries, normed_few, compressed, log_total, merged, residual, moe_in,
    ) = front_call(
        grid, hidden_in, cotangent, attn_gain, latent_gain, moe_gain, gate_values, expert_routes,
        cosines, sines, segments[None, :], own_seg[:, None],
        latent_weight, query_weight, expand_weight, output_weight, 0,
    )
    hidden_f = hidden_few.astype(jnp.float32)

    moe_all, grad_moe_in, out_rows, acts = experts_call(
        grid, moe_in, cot_all, packed_all, expert_gate, expert_up, expert_down,
        shared_gate, shared_up, shared_down, 2,
    )
    normed_later, _ = lax.optimization_barrier((normed_few, moe_in[:8]))
    normed_all = lax.all_gather(normed_later, ALL, axis=0, tiled=True)

    grad_moe_in, normed_all = lax.optimization_barrier((grad_moe_in, normed_all))
    _, pull_moe = jax.vjp(rms_scale, residual, moe_gain)
    grad_residual, grad_moe_gain = pull_moe(grad_moe_in)
    grad_residual = grad_residual + quarter(cotangent).astype(jnp.float32)
    grad_q, key_rows, expand_part, output_rows = attention_back_call(
        grid,
        low(grad_residual),
        output_weight,
        queries,
        expanded,
        packed_all,
        expand_weight,
        merged,
        log_total,
        segments[None, :],
        own_seg[:, None],
        cosines,
        sines,
        5,
    )
    grad_q_low = grad_q.reshape(tok_rows, -1, 256)[:, :, : NOPE + ROPE].reshape(tok_rows, -1)
    normed_rows = low(dot(grad_q_low, query_weight.T))

    moe_out, grad_keys, weight_rows, grad_normed, grad_q_all, expert_grads = gradients_call(
        grid, out_rows, key_rows, expand_part, normed_rows, grad_q_low, moe_all, cot_all, acts,
        expert_down.shape[1], shared_down.shape[0], 3,
    )
    output_rows, weight_rows = lax.optimization_barrier((output_rows, weight_rows))
    output_rows = lax.all_gather(output_rows, "expert", axis=0, tiled=True)
    grad_expert_gate, grad_expert_up, grad_expert_down = expert_grads[:3]
    grad_shared_gate, grad_shared_up, grad_shared_down = expert_grads[3:]
    layer_out = low(residual + moe_out)
    places_few = quarter(places)
    compressed_few = compressed[:, : LATENT + ROPE]
    _, pull_latent = jax.vjp(rms_scale, compressed_few[:, :LATENT], latent_gain)
    grad_plain_latent, grad_latent_gain = pull_latent(grad_keys[:, :LATENT])
    _, pull_krope = jax.vjp(partial(rotate, places=places_few), compressed_few[:, LATENT:])
    (grad_k_turned,) = pull_krope(grad_keys[:, LATENT : LATENT + ROPE])
    grad_comp_low = low(jnp.concatenate([grad_plain_latent, grad_k_turned], axis=-1))
    grad_normed = grad_normed + dot(grad_comp_low, latent_weight.T)
    _, pull_input = jax.vjp(rms_scale, hidden_f, attn_gain)
    grad_input_norm, grad_attn_gain = pull_input(grad_normed)
    gains = jnp.concatenate([grad_attn_gain, grad_latent_gain, grad_moe_gain])
    gains = jnp.pad(gains, (0, -gains.shape[0] % few)).reshape(few, -1)
    gains_high = low(gains)
    gains_low = low(gains - gains_high.astype(jnp.float32))
    spread = gains.shape[1]
    both = jnp.concatenate([layer_out, low(grad_residual + grad_input_norm)], axis=1)
    last, weight_rows, both = last_call(
        grid,
        pad_columns(jnp.concatenate([grad_comp_low, gains_high, gains_low], axis=1)),
        weight_rows,
        both,
        8,
    )
    grad_comp_all = last.reshape(total_rows, -1)[:, : LATENT + ROPE]
    gains = jnp.sum(last[:, :, LATENT + ROPE : LATENT + ROPE + 2 * spread].astype(jnp.float32), axis=0)
    gains = (gains[:, :spread] + gains[:, spread:]).reshape(-1)
    grad_latent_weight = dot(normed_all.T, grad_comp_all)
    grad_query_weight = dot(normed_all.T, grad_q_all)
    layer_out, grad_hidden = both[:, :model_width], both[:, model_width:].astype(jnp.float32)
    grad_output_weight = output_rows.astype(jnp.float32)
    grad_expand_weight = weight_rows.astype(jnp.float32)
    return (
        layer_out,
        grad_hidden,
        gains[:model_width],
        grad_query_weight,
        grad_latent_weight,
        gains[model_width : model_width + LATENT],
        grad_expand_weight,
        grad_output_weight,
        gains[model_width + LATENT : 2 * model_width + LATENT],
        grad_shared_gate,
        grad_shared_up,
        grad_shared_down,
        grad_expert_gate,
        grad_expert_up,
        grad_expert_down,
    )


def solution(mesh):
    grid = Grid(mesh.shape["expert"], mesh.shape["tensor"])
    placed = (
        P("expert", None),
        P(),
        P(None, "tensor"),
        P(),
        P(),
        P(None, "tensor"),
        P("tensor", None),
        P(),
        P(None, "tensor"),
        P(None, "tensor"),
        P("tensor", None),
        P("expert", None, "tensor"),
        P("expert", None, "tensor"),
        P("expert", "tensor", None),
        P("expert", None),
        P("expert", None),
        P(),
        P("expert", None),
    )
    return jax.shard_map(
        partial(shards, grid),
        mesh=mesh,
        in_specs=placed,
        out_specs=(
            P("expert", None),
            P("expert", None),
            P(),
            P(None, "tensor"),
            P(),
            P(),
            P(None, "tensor"),
            P("tensor", None),
            P(),
            P(None, "tensor"),
            P(None, "tensor"),
            P("tensor", None),
            P("expert", None, "tensor"),
            P("expert", None, "tensor"),
            P("expert", "tensor", None),
        ),
        check_vma=False,
    )
```
